32 devices in a mesh: pb: 4 (over x, core), lab: 8 (over z, y).
Axes of the slice: x: 2, y: 2, z: 4, core: 2. Of those that a mesh axis runs over, the one named last changes fastest.
Arguments:
- queries: bfloat16 [1024, 768], P(('pb', 'lab')), may hold values from -6 to 6
- label_weights: bfloat16 [8192, 768], P('lab'), may hold values from -0.21875 to 0.21875
- sibling_blocks: int32 [1024, 8], P('pb'), may hold values from 0 to 63, as said below
- positive_slot: int32 [1024], P('pb'), may hold values from 0 to 1023
Outputs:
- query_grad: float32 [1024, 768], P(('pb', 'lab'))
- weight_grad: bfloat16 [8192, 768], P('lab')
The draws below stay inside these ranges and needn't reach their ends.
Inputs may be any that keep to these rules, and one draw needn't show every extreme that they name: `sibling_blocks`: each row names 8 different cluster blocks, lying in 8 different runs of 8 blocks (block // 8 differs). Rows are taken in aligned runs of 32 (one device's queries): within each run, exactly 32 rows name a block of each run of 8 blocks. Within each query group (aligned blocks of 256 rows) no block is named by more than 32 rows, and some block is named by exactly 32 rows.
All inputs are finite; a program needn't handle non-finite values.
Results may differ from the reference program's by a relative error of at most 0.0047.
Values may be sent and summed in bfloat16 or wider, within the bound.
No kernel may reach another device: no remote copies, remote signals or barrier semaphores. Data moves between devices by JAX's collectives and lax.ppermute only.
A program may use at most 64 MiB of HBM per device.

```python
import jax
import jax.numpy as jnp
from jax import lax

D = 768
BLOCK = 128
K = 8
Q_DEV = 32
BPD = 8
GROUPS = 4
Q_GRP = 256
NQ = 1024
NB = 64
L = 8192
CAP = 32
N_LAB = 8


def draw_sibling_blocks(key, part):
    key_off, key_rows, key_blk = jax.random.split(key, 3)
    offset = jax.random.randint(key_off, (GROUPS, N_LAB, 1, 1), 0, N_LAB)
    row_keys = jax.random.split(key_rows, GROUPS * N_LAB)
    row_perm = jax.vmap(lambda one: jax.random.permutation(one, Q_DEV))(row_keys)
    row_perm = row_perm.reshape(GROUPS, N_LAB, Q_DEV, 1).astype(jnp.int32)
    steps_k = jnp.arange(K, dtype=jnp.int32).reshape(1, 1, 1, K)
    device = (offset + row_perm * K + steps_k) % N_LAB
    home = jnp.arange(N_LAB, dtype=jnp.int32).reshape(1, N_LAB, 1, 1)
    pick = jnp.broadcast_to(jnp.minimum(home % (2 * BPD), BPD - 1), device.shape)
    blk_keys = jax.random.split(key_blk, GROUPS * N_LAB)
    blk_perm = jax.vmap(lambda one: jax.random.permutation(one, BPD))(blk_keys)
    blk_perm = blk_perm.reshape(GROUPS, N_LAB, BPD).astype(jnp.int32)
    group_idx = jnp.broadcast_to(jnp.arange(GROUPS, dtype=jnp.int32).reshape(GROUPS, 1, 1, 1), device.shape)
    local = blk_perm[group_idx, device, pick]
    return (device * BPD + local).reshape(NQ, K).astype(jnp.int32)


def with_ends(result, stream_key, smallest, high):
    extent = result.shape
    place = [jax.random.randint(jax.random.fold_in(stream_key, axis), (), 0, extent[axis]) for axis in range(len(extent))]
    result = result.at[tuple(place)].set(smallest)
    longest = extent.index(max(extent))
    place[longest] = (place[longest] + 1) % extent[longest]
    return result.at[tuple(place)].set(high)


def level_of(key, dims, shards, smallest, largest):
    gain, own = 1.0, jax.random.fold_in(key, 6)
    for dim, shards_of in shards:
        heights = jnp.exp(jax.random.uniform(jax.random.fold_in(own, dim), (shards_of,), jnp.float32, smallest / len(shards), largest / len(shards)))
        gain = gain * jnp.repeat(heights, dims[dim] // shards_of).reshape([-1 if axis == dim else 1 for axis in range(len(dims))])
    return gain


def noise(own_key, extent, spread, most, cuts=(), held_as=jnp.bfloat16):
    gain = level_of(own_key, extent, cuts, -0.22, 0.18) if cuts else 1.0
    array = jax.random.normal(own_key, extent, jnp.float32) * spread * gain
    return jnp.minimum(jnp.maximum(array, -most), most).astype(held_as)


def setup_inputs(seed: int = 0) -> dict:
    splits = jax.random.split(jax.random.key(seed), 5)
    return {
        "queries": noise(splits[0], (NQ, D), 1.0, 6.0, ((0, 32),)),
        "label_weights": noise(splits[1], (L, D), D ** -0.5, 0.21875, ((0, 8),)),
        "sibling_blocks": draw_sibling_blocks(jax.random.fold_in(splits[4], 71), 0),
        "positive_slot": with_ends(jax.random.randint(splits[3], (NQ,), 0, K * BLOCK), jax.random.fold_in(splits[3], 1), 0, (K * BLOCK) - 1).astype(jnp.int32),
    }


def group_terms(q_grp, sel_grp, pos_grp, w_blocks):
    nblk = w_blocks.shape[0]
    qcount = q_grp.shape[0]
    block_ids = jnp.arange(nblk, dtype=jnp.int32)
    hit = jnp.any(sel_grp[:, :, None] == block_ids[None, None, :], axis=1).astype(jnp.int32)
    rank = jnp.cumsum(hit, axis=0) - 1
    slot = jnp.take_along_axis(rank, sel_grp, axis=1)
    query_ids = jnp.broadcast_to(jnp.arange(qcount, dtype=jnp.int32)[:, None], sel_grp.shape)
    table = jnp.zeros((nblk, CAP), jnp.int32).at[sel_grp, slot].set(query_ids)
    valid = jnp.zeros((nblk, CAP), jnp.float32).at[sel_grp, slot].set(1.0)
    pblock = jnp.take_along_axis(sel_grp, (pos_grp // BLOCK)[:, None], axis=1)[:, 0]
    positive = pblock * BLOCK + pos_grp % BLOCK
    rows = q_grp[table].astype(jnp.float32)
    wide_w = w_blocks.astype(jnp.float32)
    scores = jnp.einsum('bcd,bld->bcl', rows, wide_w)
    label_ids = block_ids[:, None] * BLOCK + jnp.arange(BLOCK, dtype=jnp.int32)[None, :]
    target = (label_ids[:, None, :] == positive[table][:, :, None]).astype(jnp.float32)
    slope = (valid[:, :, None] * (jax.nn.sigmoid(scores) - target)).astype(jnp.bfloat16).astype(jnp.float32)
    w_part = jnp.einsum('bcl,bcd->bld', slope, rows)
    dq_parts = jnp.einsum('bcl,bld->bcd', slope, wide_w)
    dq = jnp.zeros((qcount, q_grp.shape[1]), jnp.float32).at[table].add(dq_parts)
    return dq, w_part.reshape(nblk * BLOCK, q_grp.shape[1])


def reference(queries, label_weights, sibling_blocks, positive_slot):
    qs = queries.reshape(GROUPS, Q_GRP, D)
    sels = sibling_blocks.reshape(GROUPS, Q_GRP, K)
    poss = positive_slot.reshape(GROUPS, Q_GRP)
    w_blocks = label_weights.reshape(NB, BLOCK, D)

    def step(w_sum, items):
        dq, w_part = group_terms(items[0], items[1], items[2], w_blocks)
        return w_sum + w_part, dq

    w_sum, dqs = lax.scan(step, jnp.zeros((L, D), jnp.float32), (qs, sels, poss))
    return dqs.reshape(NQ, D), (w_sum / GROUPS).astype(jnp.bfloat16)
```

```python
import jax
import jax.numpy as jnp
from jax import lax
from jax.sharding import PartitionSpec as P

BLOCK = 128
K = 8


def pack_index(touched, width_slots, fill_value):
    homes, count = touched.shape
    rank = jnp.cumsum(touched.astype(jnp.int32), axis=1) - 1
    place = jnp.where(touched, rank, width_slots)
    home_ids = jnp.broadcast_to(jnp.arange(homes, dtype=jnp.int32)[:, None], touched.shape)
    row_ids = jnp.broadcast_to(jnp.arange(count, dtype=jnp.int32)[None, :], touched.shape)
    table = (
        jnp.full((homes, width_slots + 1), fill_value, jnp.int32).at[home_ids, place].set(row_ids)
    )
    return table[:, :width_slots]


def sparse_shards(queries, label_weights, sibling_blocks, positive_slot):
    width = queries.shape[1]
    qcount = sibling_blocks.shape[0]
    lab_dev = label_weights.shape[0]
    blocks_dev = lab_dev // BLOCK
    first = lax.axis_index("lab") * blocks_dev
    local_ids = first + jnp.arange(blocks_dev, dtype=jnp.int32)
    pblock = jnp.take_along_axis(sibling_blocks, (positive_slot // BLOCK)[:, None], axis=1)[:, 0]
    positive = pblock * BLOCK + positive_slot % BLOCK
    label_ids = local_ids[:, None] * BLOCK + jnp.arange(BLOCK, dtype=jnp.int32)[None, :]
    chosen_all = jnp.any(sibling_blocks[:, :, None] == local_ids[None, None, :], axis=1)
    piece = lax.all_gather(queries, "lab", axis=0, tiled=True)
    count = piece.shape[0]
    scores = jnp.dot(piece, label_weights.T, preferred_element_type=jnp.float32)
    scores = scores.reshape(count, blocks_dev, BLOCK)
    target = (label_ids[None, :, :] == positive[:, None, None]).astype(jnp.float32)
    slope = jnp.where(chosen_all[:, :, None], jax.nn.sigmoid(scores) - target, 0.0)
    slope = slope.astype(jnp.bfloat16).reshape(count, lab_dev)
    dq_all = jnp.dot(slope, label_weights, preferred_element_type=jnp.float32)
    w_acc = lax.dot_general(
        slope, piece, (((0,), (0,)), ((), ())), preferred_element_type=jnp.float32
    )
    homes = lax.axis_size("lab")
    q_home = qcount // homes
    slots = q_home * K // homes
    touched = jnp.any(chosen_all, axis=1).reshape(homes, q_home)
    send_idx = pack_index(touched, slots, q_home)
    padded = jnp.concatenate(
        [dq_all.reshape(homes, q_home, width), jnp.zeros((homes, 1, width), jnp.float32)], axis=1
    )
    outgoing = jnp.take_along_axis(padded, send_idx[:, :, None], axis=1)
    incoming = lax.all_to_all(outgoing, "lab", split_axis=0, concat_axis=0, tiled=True)
    own_blocks = lax.dynamic_slice_in_dim(sibling_blocks, lax.axis_index("lab") * q_home, q_home, 0)
    source_ids = jnp.arange(homes, dtype=jnp.int32)
    own_touch = jnp.any(
        (own_blocks // blocks_dev)[:, :, None] == source_ids[None, None, :], axis=1
    ).T
    recv_idx = pack_index(own_touch, slots, q_home)
    query_grad = (
        jnp.zeros((q_home + 1, width), jnp.float32)
        .at[recv_idx.reshape(-1)]
        .add(incoming.reshape(-1, width))[:q_home]
    )
    groups = lax.axis_size("pb")
    total = lax.psum(w_acc, "pb")
    weight_grad = (total / groups).astype(jnp.bfloat16)
    return (query_grad, weight_grad)


def swap(value, axis, bit):
    count = lax.axis_size(axis)
    return lax.ppermute(value, axis, [(i, i ^ bit) for i in range(count)])


def codes(sibling_blocks, positive_slot, blocks_dev):
    first = lax.axis_index("lab") * blocks_dev
    local = sibling_blocks.T - first
    inside = (local >= 0) & (local < blocks_dev)
    chosen = jnp.max(jnp.where(inside, local, -1), axis=0)
    steps = jnp.arange(local.shape[0], dtype=jnp.int32)[:, None]
    pblock = jnp.sum(jnp.where(steps == (positive_slot // BLOCK)[None, :], local, 0), axis=0)
    return jnp.stack([chosen, pblock * BLOCK + positive_slot % BLOCK])


def slopes(rows, weights, code):
    lab_dev = weights.shape[0]
    scores = lax.dot_general(
        weights, rows, (((1,), (1,)), ((), ())), preferred_element_type=jnp.float32
    )
    ids = jnp.arange(lab_dev, dtype=jnp.int32)[:, None]
    target = (ids == code[1][None, :]).astype(jnp.float32)
    slope = jnp.where(ids // BLOCK == code[0][None, :], jax.nn.sigmoid(scores) - target, 0.0)
    return slope.astype(jnp.bfloat16)


def dense_shards(queries, label_weights, sibling_blocks, positive_slot):
    q_home, width = queries.shape
    blocks_dev = label_weights.shape[0] // BLOCK
    homes = lax.axis_size("lab")
    groups = lax.axis_size("pb")
    code = codes(sibling_blocks, positive_slot, blocks_dev)
    copies = jnp.broadcast_to(queries[None], (homes, q_home, width))
    own = lax.all_to_all(copies, "lab", split_axis=0, concat_axis=0, tiled=True)
    parts = [own.reshape(homes * q_home, width)]
    notes = [code]
    bit = groups // 2
    while bit:
        parts = parts + [swap(part, "pb", bit) for part in parts]
        notes = notes + [swap(note, "pb", bit) for note in notes]
        bit //= 2
    slope = slopes(parts[0], label_weights, notes[0])
    dq = lax.dot_general(
        slope, label_weights, (((0,), (0,)), ((), ())), preferred_element_type=jnp.float32
    )
    dq = dq.astype(jnp.bfloat16).reshape(homes, q_home, width)
    incoming = lax.all_to_all(dq, "lab", split_axis=0, concat_axis=0, tiled=True)
    query_grad = jnp.sum(incoming.astype(jnp.float32), axis=0)
    rows = jnp.concatenate(parts, axis=0)
    note = jnp.concatenate(notes, axis=1)
    every = slopes(rows, label_weights, note)
    total = jnp.dot(every, rows, preferred_element_type=jnp.float32)
    weight_grad = (total / groups).astype(jnp.bfloat16)
    return (query_grad, weight_grad)


def solution(mesh):
    groups, homes = mesh.shape["pb"], mesh.shape["lab"]

    def shards(queries, label_weights, sibling_blocks, positive_slot):
        every_row_everywhere = homes == K
        few = groups * sibling_blocks.shape[0] <= 2 * label_weights.shape[0]
        paired = groups & (groups - 1) == 0
        one_block = label_weights.shape[0] // BLOCK <= K
        plan = dense_shards if every_row_everywhere and few and paired and one_block else sparse_shards
        return plan(queries, label_weights, sibling_blocks, positive_slot)

    in_specs = (P(("pb", "lab"), None), P("lab", None), P("pb", None), P("pb"))
    out_specs = (P(("pb", "lab"), None), P("lab", None))
    return jax.shard_map(shards, mesh=mesh, in_specs=in_specs, out_specs=out_specs, check_vma=False)
```

```python
import jax
import jax.numpy as jnp
from jax import lax
from jax.sharding import PartitionSpec as P

BLOCK = 128
K = 8


def pack_index(touched, width_slots, fill_value):
    homes, count = touched.shape
    rank = jnp.cumsum(touched.astype(jnp.int32), axis=1) - 1
    place = jnp.where(touched, rank, width_slots)
    home_ids = jnp.broadcast_to(jnp.arange(homes, dtype=jnp.int32)[:, None], touched.shape)
    row_ids = jnp.broadcast_to(jnp.arange(count, dtype=jnp.int32)[None, :], touched.shape)
    table = (
        jnp.full((homes, width_slots + 1), fill_value, jnp.int32).at[home_ids, place].set(row_ids)
    )
    return table[:, :width_slots]


def sparse_shards(queries, label_weights, sibling_blocks, positive_slot):
    width = queries.shape[1]
    qcount = sibling_blocks.shape[0]
    lab_dev = label_weights.shape[0]
    blocks_dev = lab_dev // BLOCK
    first = lax.axis_index("lab") * blocks_dev
    local_ids = first + jnp.arange(blocks_dev, dtype=jnp.int32)
    pblock = jnp.take_along_axis(sibling_blocks, (positive_slot // BLOCK)[:, None], axis=1)[:, 0]
    positive = pblock * BLOCK + positive_slot % BLOCK
    label_ids = local_ids[:, None] * BLOCK + jnp.arange(BLOCK, dtype=jnp.int32)[None, :]
    chosen_all = jnp.any(sibling_blocks[:, :, None] == local_ids[None, None, :], axis=1)
    piece = lax.all_gather(queries, "lab", axis=0, tiled=True)
    count = piece.shape[0]
    scores = jnp.dot(piece, label_weights.T, preferred_element_type=jnp.float32)
    scores = scores.reshape(count, blocks_dev, BLOCK)
    target = (label_ids[None, :, :] == positive[:, None, None]).astype(jnp.float32)
    slope = jnp.where(chosen_all[:, :, None], jax.nn.sigmoid(scores) - target, 0.0)
    slope = slope.astype(jnp.bfloat16).reshape(count, lab_dev)
    dq_all = jnp.dot(slope, label_weights, preferred_element_type=jnp.float32)
    w_acc = lax.dot_general(
        slope, piece, (((0,), (0,)), ((), ())), preferred_element_type=jnp.float32
    )
    homes = lax.axis_size("lab")
    q_home = qcount // homes
    slots = q_home * K // homes
    touched = jnp.any(chosen_all, axis=1).reshape(homes, q_home)
    send_idx = pack_index(touched, slots, q_home)
    padded = jnp.concatenate(
        [dq_all.reshape(homes, q_home, width), jnp.zeros((homes, 1, width), jnp.float32)], axis=1
    )
    outgoing = jnp.take_along_axis(padded, send_idx[:, :, None], axis=1)
    incoming = lax.all_to_all(outgoing, "lab", split_axis=0, concat_axis=0, tiled=True)
    own_blocks = lax.dynamic_slice_in_dim(sibling_blocks, lax.axis_index("lab") * q_home, q_home, 0)
    source_ids = jnp.arange(homes, dtype=jnp.int32)
    own_touch = jnp.any(
        (own_blocks // blocks_dev)[:, :, None] == source_ids[None, None, :], axis=1
    ).T
    recv_idx = pack_index(own_touch, slots, q_home)
    query_grad = (
        jnp.zeros((q_home + 1, width), jnp.float32)
        .at[recv_idx.reshape(-1)]
        .add(incoming.reshape(-1, width))[:q_home]
    )
    groups = lax.axis_size("pb")
    total = lax.psum(w_acc, "pb")
    weight_grad = (total / groups).astype(jnp.bfloat16)
    return (query_grad, weight_grad)


def swap(value, axis, bit):
    count = lax.axis_size(axis)
    return lax.ppermute(value, axis, [(i, i ^ bit) for i in range(count)])


def codes(sibling_blocks, positive_slot, blocks_dev):
    first = lax.axis_index("lab") * blocks_dev
    local = sibling_blocks.T - first
    inside = (local >= 0) & (local < blocks_dev)
    chosen = jnp.max(jnp.where(inside, local, -1), axis=0)
    steps = jnp.arange(local.shape[0], dtype=jnp.int32)[:, None]
    pblock = jnp.sum(jnp.where(steps == (positive_slot // BLOCK)[None, :], local, 0), axis=0)
    return jnp.stack([chosen, pblock * BLOCK + positive_slot % BLOCK])


def slopes(rows, weights, code):
    lab_dev = weights.shape[0]
    scores = lax.dot_general(
        weights, rows, (((1,), (1,)), ((), ())), preferred_element_type=jnp.float32
    )
    ids = jnp.arange(lab_dev, dtype=jnp.int32)[:, None]
    target = (ids == code[1][None, :]).astype(jnp.float32)
    slope = jnp.where(ids // BLOCK == code[0][None, :], jax.nn.sigmoid(scores) - target, 0.0)
    return slope.astype(jnp.bfloat16)


def flip_to(value, index, count):
    bit = 1
    while bit < count:
        split = value.reshape((count // (2 * bit), 2, bit) + value.shape[1:])
        turned = jnp.concatenate([split[:, 1:], split[:, :1]], axis=1)
        value = jnp.where((index & bit) != 0, turned, split).reshape(value.shape)
        bit *= 2
    return value


def dense_shards(queries, label_weights, sibling_blocks, positive_slot):
    q_home, width = queries.shape
    blocks_dev = label_weights.shape[0] // BLOCK
    homes = lax.axis_size("lab")
    groups = lax.axis_size("pb")
    me = lax.axis_index("lab")
    arrived = [queries] + [swap(queries, "lab", step) for step in range(1, homes)]
    sibling = flip_to(sibling_blocks.reshape(homes, q_home, -1), me, homes)
    slot = flip_to(positive_slot.reshape(homes, q_home), me, homes)
    code = codes(sibling.reshape(sibling_blocks.shape), slot.reshape(-1), blocks_dev)
    parts = [jnp.concatenate(arrived, axis=0)]
    notes = [code]
    bit = groups // 2
    while bit:
        parts = parts + [swap(part, "pb", bit) for part in parts]
        notes = notes + [swap(note, "pb", bit) for note in notes]
        bit //= 2
    slope = slopes(parts[0], label_weights, notes[0])
    dq = lax.dot_general(
        slope, label_weights, (((0,), (0,)), ((), ())), preferred_element_type=jnp.float32
    )
    dq = dq.reshape(homes, q_home, width)
    incoming = [dq[0]]
    for step in range(1, homes):
        incoming.append(swap(dq[step].astype(jnp.bfloat16), "lab", step))
    rows = jnp.concatenate(parts, axis=0)
    note = jnp.concatenate(notes, axis=1)
    every = slopes(rows, label_weights, note)
    total = jnp.dot(every, rows, preferred_element_type=jnp.float32)
    weight_grad = (total / groups).astype(jnp.bfloat16)
    *incoming, weight_grad = lax.optimization_barrier((*incoming, weight_grad))
    query_grad = incoming[0]
    for term in incoming[1:]:
        query_grad = query_grad + term.astype(jnp.float32)
    return (query_grad, weight_grad)


def solution(mesh):
    groups, homes = mesh.shape["pb"], mesh.shape["lab"]

    def shards(queries, label_weights, sibling_blocks, positive_slot):
        every_row_everywhere = homes == K
        few = groups * sibling_blocks.shape[0] <= 2 * label_weights.shape[0]
        paired = groups & (groups - 1) == 0
        one_block = label_weights.shape[0] // BLOCK <= K
        plan = dense_shards if every_row_everywhere and few and paired and one_block else sparse_shards
        return plan(queries, label_weights, sibling_blocks, positive_slot)

    in_specs = (P(("pb", "lab"), None), P("lab", None), P("pb", None), P("pb"))
    out_specs = (P(("pb", "lab"), None), P("lab", None))
    return jax.shard_map(shards, mesh=mesh, in_specs=in_specs, out_specs=out_specs, check_vma=False)
```

```python
import jax
import jax.numpy as jnp
from jax import lax
from jax.sharding import PartitionSpec as P

BLOCK = 128
K = 8


def pack_index(touched, width_slots, fill_value):
    homes, count = touched.shape
    rank = jnp.cumsum(touched.astype(jnp.int32), axis=1) - 1
    place = jnp.where(touched, rank, width_slots)
    home_ids = jnp.broadcast_to(jnp.arange(homes, dtype=jnp.int32)[:, None], touched.shape)
    row_ids = jnp.broadcast_to(jnp.arange(count, dtype=jnp.int32)[None, :], touched.shape)
    table = (
        jnp.full((homes, width_slots + 1), fill_value, jnp.int32).at[home_ids, place].set(row_ids)
    )
    return table[:, :width_slots]


def sparse_shards(queries, label_weights, sibling_blocks, positive_slot):
    width = queries.shape[1]
    qcount = sibling_blocks.shape[0]
    lab_dev = label_weights.shape[0]
    blocks_dev = lab_dev // BLOCK
    first = lax.axis_index("lab") * blocks_dev
    local_ids = first + jnp.arange(blocks_dev, dtype=jnp.int32)
    pblock = jnp.take_along_axis(sibling_blocks, (positive_slot // BLOCK)[:, None], axis=1)[:, 0]
    positive = pblock * BLOCK + positive_slot % BLOCK
    label_ids = local_ids[:, None] * BLOCK + jnp.arange(BLOCK, dtype=jnp.int32)[None, :]
    chosen_all = jnp.any(sibling_blocks[:, :, None] == local_ids[None, None, :], axis=1)
    piece = lax.all_gather(queries, "lab", axis=0, tiled=True)
    count = piece.shape[0]
    scores = jnp.dot(piece, label_weights.T, preferred_element_type=jnp.float32)
    scores = scores.reshape(count, blocks_dev, BLOCK)
    target = (label_ids[None, :, :] == positive[:, None, None]).astype(jnp.float32)
    slope = jnp.where(chosen_all[:, :, None], jax.nn.sigmoid(scores) - target, 0.0)
    slope = slope.astype(jnp.bfloat16).reshape(count, lab_dev)
    dq_all = jnp.dot(slope, label_weights, preferred_element_type=jnp.float32)
    w_acc = lax.dot_general(
        slope, piece, (((0,), (0,)), ((), ())), preferred_element_type=jnp.float32
    )
    homes = lax.axis_size("lab")
    q_home = qcount // homes
    slots = q_home * K // homes
    touched = jnp.any(chosen_all, axis=1).reshape(homes, q_home)
    send_idx = pack_index(touched, slots, q_home)
    padded = jnp.concatenate(
        [dq_all.reshape(homes, q_home, width), jnp.zeros((homes, 1, width), jnp.float32)], axis=1
    )
    outgoing = jnp.take_along_axis(padded, send_idx[:, :, None], axis=1)
    incoming = lax.all_to_all(outgoing, "lab", split_axis=0, concat_axis=0, tiled=True)
    own_blocks = lax.dynamic_slice_in_dim(sibling_blocks, lax.axis_index("lab") * q_home, q_home, 0)
    source_ids = jnp.arange(homes, dtype=jnp.int32)
    own_touch = jnp.any(
        (own_blocks // blocks_dev)[:, :, None] == source_ids[None, None, :], axis=1
    ).T
    recv_idx = pack_index(own_touch, slots, q_home)
    query_grad = (
        jnp.zeros((q_home + 1, width), jnp.float32)
        .at[recv_idx.reshape(-1)]
        .add(incoming.reshape(-1, width))[:q_home]
    )
    groups = lax.axis_size("pb")
    total = lax.psum(w_acc, "pb")
    weight_grad = (total / groups).astype(jnp.bfloat16)
    return (query_grad, weight_grad)


def slopes(rows, weights, code):
    lab_dev = weights.shape[0]
    scores = lax.dot_general(
        weights, rows, (((1,), (1,)), ((), ())), preferred_element_type=jnp.float32
    )
    ids = jnp.arange(lab_dev, dtype=jnp.int32)[:, None]
    target = (ids == code[1][None, :]).astype(jnp.float32)
    slope = jnp.where(ids // BLOCK == code[0][None, :], jax.nn.sigmoid(scores) - target, 0.0)
    return slope.astype(jnp.bfloat16)


def dense_shards(queries, label_weights, sibling_blocks, positive_slot):
    q_home, width = queries.shape
    qcount, picks = sibling_blocks.shape
    blocks_dev = label_weights.shape[0] // BLOCK
    homes = lax.axis_size("lab")
    groups = lax.axis_size("pb")
    me = lax.axis_index("lab")
    own_blocks = lax.dynamic_slice_in_dim(sibling_blocks, me * q_home, q_home, 0)
    own_slot = lax.dynamic_slice_in_dim(positive_slot, me * q_home, q_home, 0)[:, None]
    columns = jnp.concatenate([own_blocks, own_slot // BLOCK, own_slot % BLOCK], axis=1)
    columns = jnp.pad(columns, ((0, 0), (0, BLOCK - columns.shape[1])))
    carried = jnp.concatenate([queries, columns.astype(jnp.bfloat16)], axis=1)
    every = lax.all_gather(carried, ("pb", "lab"), axis=0, tiled=True)
    rows = every[:, :width]
    ints = every[:, width : width + picks + 2].astype(jnp.int32).T
    local = ints[:picks] - me * blocks_dev
    inside = (local >= 0) & (local < blocks_dev)
    chosen = jnp.max(jnp.where(inside, local, -1), axis=0)
    steps = jnp.arange(picks, dtype=jnp.int32)[:, None]
    pblock = jnp.sum(jnp.where(steps == ints[picks], local, 0), axis=0)
    code = jnp.stack([chosen, pblock * BLOCK + ints[picks + 1]])
    slope = slopes(rows, label_weights, code)
    mine = lax.dynamic_slice_in_dim(slope, lax.axis_index("pb") * qcount, qcount, 1)
    dq = lax.dot_general(
        mine, label_weights, (((0,), (0,)), ((), ())), preferred_element_type=jnp.float32
    )
    query_grad = lax.psum_scatter(dq, "lab", scatter_dimension=0, tiled=True)
    total = jnp.dot(slope, rows, preferred_element_type=jnp.float32)
    weight_grad = (total / groups).astype(jnp.bfloat16)
    return (query_grad, weight_grad)


def solution(mesh):
    groups, homes = mesh.shape["pb"], mesh.shape["lab"]

    def shards(queries, label_weights, sibling_blocks, positive_slot):
        every_row_everywhere = homes == K
        few = groups * sibling_blocks.shape[0] <= 2 * label_weights.shape[0]
        paired = groups & (groups - 1) == 0
        one_block = label_weights.shape[0] // BLOCK <= K
        plan = dense_shards if every_row_everywhere and few and paired and one_block else sparse_shards
        return plan(queries, label_weights, sibling_blocks, positive_slot)

    in_specs = (P(("pb", "lab"), None), P("lab", None), P("pb", None), P("pb"))
    out_specs = (P(("pb", "lab"), None), P("lab", None))
    return jax.shard_map(shards, mesh=mesh, in_specs=in_specs, out_specs=out_specs, check_vma=False)
```

```python
import jax
import jax.numpy as jnp
from jax import lax
from jax.experimental import pallas as pl
from jax.experimental.pallas import tpu as pltpu
from jax.sharding import PartitionSpec as P

BLOCK = 128
K = 8
NOTE = 16
VMEM_LIMIT = 24 * 1024 * 1024


def pack_index(touched, width_slots, fill_value):
    homes, count = touched.shape
    rank = jnp.cumsum(touched.astype(jnp.int32), axis=1) - 1
    place = jnp.where(touched, rank, width_slots)
    home_ids = jnp.broadcast_to(jnp.arange(homes, dtype=jnp.int32)[:, None], touched.shape)
    row_ids = jnp.broadcast_to(jnp.arange(count, dtype=jnp.int32)[None, :], touched.shape)
    table = (
        jnp.full((homes, width_slots + 1), fill_value, jnp.int32).at[home_ids, place].set(row_ids)
    )
    return table[:, :width_slots]


def sparse_shards(queries, label_weights, sibling_blocks, positive_slot):
    width = queries.shape[1]
    qcount = sibling_blocks.shape[0]
    lab_dev = label_weights.shape[0]
    blocks_dev = lab_dev // BLOCK
    first = lax.axis_index("lab") * blocks_dev
    local_ids = first + jnp.arange(blocks_dev, dtype=jnp.int32)
    pblock = jnp.take_along_axis(sibling_blocks, (positive_slot // BLOCK)[:, None], axis=1)[:, 0]
    positive = pblock * BLOCK + positive_slot % BLOCK
    label_ids = local_ids[:, None] * BLOCK + jnp.arange(BLOCK, dtype=jnp.int32)[None, :]
    chosen_all = jnp.any(sibling_blocks[:, :, None] == local_ids[None, None, :], axis=1)
    piece = lax.all_gather(queries, "lab", axis=0, tiled=True)
    count = piece.shape[0]
    scores = jnp.dot(piece, label_weights.T, preferred_element_type=jnp.float32)
    scores = scores.reshape(count, blocks_dev, BLOCK)
    target = (label_ids[None, :, :] == positive[:, None, None]).astype(jnp.float32)
    slope = jnp.where(chosen_all[:, :, None], jax.nn.sigmoid(scores) - target, 0.0)
    slope = slope.astype(jnp.bfloat16).reshape(count, lab_dev)
    dq_all = jnp.dot(slope, label_weights, preferred_element_type=jnp.float32)
    w_acc = lax.dot_general(
        slope, piece, (((0,), (0,)), ((), ())), preferred_element_type=jnp.float32
    )
    homes = lax.axis_size("lab")
    q_home = qcount // homes
    slots = q_home * K // homes
    touched = jnp.any(chosen_all, axis=1).reshape(homes, q_home)
    send_idx = pack_index(touched, slots, q_home)
    padded = jnp.concatenate(
        [dq_all.reshape(homes, q_home, width), jnp.zeros((homes, 1, width), jnp.float32)], axis=1
    )
    outgoing = jnp.take_along_axis(padded, send_idx[:, :, None], axis=1)
    incoming = lax.all_to_all(outgoing, "lab", split_axis=0, concat_axis=0, tiled=True)
    own_blocks = lax.dynamic_slice_in_dim(sibling_blocks, lax.axis_index("lab") * q_home, q_home, 0)
    source_ids = jnp.arange(homes, dtype=jnp.int32)
    own_touch = jnp.any(
        (own_blocks // blocks_dev)[:, :, None] == source_ids[None, None, :], axis=1
    ).T
    recv_idx = pack_index(own_touch, slots, q_home)
    query_grad = (
        jnp.zeros((q_home + 1, width), jnp.float32)
        .at[recv_idx.reshape(-1)]
        .add(incoming.reshape(-1, width))[:q_home]
    )
    groups = lax.axis_size("pb")
    total = lax.psum(w_acc, "pb")
    weight_grad = (total / groups).astype(jnp.bfloat16)
    return (query_grad, weight_grad)


def swap(value, axis, bit):
    count = lax.axis_size(axis)
    return lax.ppermute(value, axis, [(i, i ^ bit) for i in range(count)])


def local_call(body, outs, args, flops=0):
    scalars = [arg for arg in args if arg.dtype == jnp.int32]
    size = sum(a.size * a.dtype.itemsize for a in list(args) + list(outs))
    specs = [
        pl.BlockSpec(memory_space=pltpu.SMEM if arg.dtype == jnp.int32 else pltpu.VMEM)
        for arg in args
    ]
    del scalars
    return pl.pallas_call(
        body,
        out_shape=outs,
        in_specs=specs,
        out_specs=[pl.BlockSpec(memory_space=pltpu.VMEM)] * len(outs),
        cost_estimate=pl.CostEstimate(flops=flops, bytes_accessed=size, transcendentals=0),
        compiler_params=pltpu.CompilerParams(vmem_limit_bytes=VMEM_LIMIT),
    )(*args)


def like(rows, width, dtype):
    return jax.ShapeDtypeStruct((rows, width), dtype)


def join_body(side_ref, own_ref, came_ref, out_ref):
    rows = own_ref.shape[0]
    side = side_ref[0]
    out_ref[pl.ds(pl.multiple_of(side * rows, rows), rows), :] = own_ref[...]
    out_ref[pl.ds(pl.multiple_of((1 - side) * rows, rows), rows), :] = came_ref[...]


def join_note_body(side_ref, own_ref, came_ref, note_ref, out_ref, noted_ref):
    rows = own_ref.shape[0]
    join_body(side_ref, own_ref, came_ref, out_ref)
    noted_ref[: 2 * rows, :] = out_ref[...]
    noted_ref[2 * rows :, :] = note_ref[...]


def slope_of(rows, weights_ref, chosen, place):
    count = rows.shape[0]
    blocks = weights_ref.shape[0] // BLOCK
    scores = lax.dot_general(
        weights_ref[...], rows, (((1,), (1,)), ((), ())), preferred_element_type=jnp.float32
    )
    named = jnp.zeros((BLOCK, count), jnp.float32)
    for block in range(blocks):
        named = jnp.where(chosen == block, scores[block * BLOCK : (block + 1) * BLOCK], named)
    ids = lax.broadcasted_iota(jnp.int32, (BLOCK, count), 0)
    slope = jax.nn.sigmoid(named) - jnp.where(ids == place, 1.0, 0.0)
    parts = [jnp.where(chosen == block, slope, 0.0).astype(jnp.bfloat16) for block in range(blocks)]
    return jnp.concatenate(parts, axis=0)


def read_note(note, which, count):
    chosen = note[2 * which : 2 * which + 1, :count].astype(jnp.int32)
    place = note[2 * which + 1 : 2 * which + 2, :count].astype(jnp.int32)
    return chosen, place


def grad_body(which, rows_ref, weights_ref, note_ref, dq_ref, slope_ref):
    rows = rows_ref[...]
    note = note_ref[...].astype(jnp.float32)
    slope = slope_of(rows, weights_ref, *read_note(note, which, rows.shape[0]))
    slope_ref[...] = slope
    dq = lax.dot_general(
        slope, weights_ref[...], (((0,), (0,)), ((), ())), preferred_element_type=jnp.float32
    )
    dq_ref[...] = dq.astype(dq_ref.dtype)


def near_body(rows_ref, weights_ref, note_ref, dq_ref, slope_ref):
    grad_body(0, rows_ref, weights_ref, note_ref, dq_ref, slope_ref)


def far_body(near_ref, rows_ref, weights_ref, note_ref, dq_ref, slope_ref, all_ref):
    grad_body(1, rows_ref, weights_ref, note_ref, dq_ref, slope_ref)
    noted = near_ref.shape[0]
    all_ref[:noted, :] = near_ref[...]
    all_ref[noted:, :] = rows_ref[...]


def fold_body(side_ref, kept_ref, came_ref, keep_ref, send_ref):
    rows = keep_ref.shape[0]
    side = side_ref[0]
    mine = pl.ds(pl.multiple_of(side * rows, rows), rows)
    other = pl.ds(pl.multiple_of((1 - side) * rows, rows), rows)
    keep_ref[...] = kept_ref[mine, :] + came_ref[mine, :].astype(jnp.float32)
    send = kept_ref[other, :] + came_ref[other, :].astype(jnp.float32)
    send_ref[...] = send.astype(send_ref.dtype)


def last_body(kept_ref, came_ref, out_ref):
    out_ref[...] = kept_ref[...] + came_ref[...].astype(jnp.float32)


def slopes_of_set(near_rows, far_rows, note, weights_ref):
    half = near_rows.shape[0]
    rows = jnp.concatenate([near_rows, far_rows], axis=0)
    codes = [read_note(note, which, half) for which in range(2)]
    chosen = jnp.concatenate([codes[0][0], codes[1][0]], axis=1)
    place = jnp.concatenate([codes[0][1], codes[1][1]], axis=1)
    return rows, slope_of(rows, weights_ref, chosen, place)


def early_body(near_ref, far_ref, near_slope_ref, far_slope_ref, set_ref, weights_ref, acc_ref):
    half = near_ref.shape[0]
    note = set_ref[half : half + NOTE, :].astype(jnp.float32)
    rows, slope = slopes_of_set(set_ref[:half, :], set_ref[half + NOTE :, :], note, weights_ref)
    rows = jnp.concatenate([near_ref[...], far_ref[...], rows], axis=0)
    slope = jnp.concatenate([near_slope_ref[...], far_slope_ref[...], slope], axis=1)
    acc_ref[...] = jnp.dot(slope, rows, preferred_element_type=jnp.float32)


def late_body(groups, *refs):
    *set_refs, weights_ref, acc_ref, out_ref = refs
    rows, slopes = [], []
    for near_ref, far_ref in zip(set_refs[::2], set_refs[1::2]):
        half = far_ref.shape[0]
        note = near_ref[half:, :].astype(jnp.float32)
        part, slope = slopes_of_set(near_ref[:half, :], far_ref[...], note, weights_ref)
        rows.append(part)
        slopes.append(slope)
    total = acc_ref[...] + jnp.dot(
        jnp.concatenate(slopes, axis=1),
        jnp.concatenate(rows, axis=0),
        preferred_element_type=jnp.float32,
    )
    out_ref[...] = (total / groups).astype(out_ref.dtype)


def make_note(sibling_blocks, positive_slot, blocks_dev, homes, width):
    me = lax.axis_index("lab")
    local = sibling_blocks.T - me * blocks_dev
    inside = (local >= 0) & (local < blocks_dev)
    chosen = jnp.max(jnp.where(inside, local, -1), axis=0)
    steps = jnp.arange(local.shape[0], dtype=jnp.int32)[:, None]
    pblock = jnp.sum(jnp.where(steps == (positive_slot // BLOCK)[None, :], local, 0), axis=0)
    place = jnp.where(pblock == chosen, positive_slot % BLOCK, -1)
    code = jnp.stack([chosen, place]).astype(jnp.bfloat16)
    bits = homes.bit_length() - 1
    code = code.reshape((2,) + (2,) * bits + (-1,))
    code = code.transpose((bits, 0) + tuple(range(bits - 1, 0, -1)) + (bits + 1,))
    code = code.reshape(2, 2, -1)
    code = jnp.where(me % 2 == 0, code, code[::-1]).reshape(4, -1)
    return jnp.pad(code, ((0, NOTE - 4), (0, width - code.shape[1])))


def dense_shards(queries, label_weights, sibling_blocks, positive_slot):
    q_home, width = queries.shape
    qcount = sibling_blocks.shape[0]
    half = qcount // 2
    lab_dev = label_weights.shape[0]
    homes = lax.axis_size("lab")
    groups = lax.axis_size("pb")
    me = lax.axis_index("lab")
    f32, bf16 = jnp.float32, jnp.bfloat16

    def side(bit):
        return jnp.reshape((me // bit) % 2, (1,)).astype(jnp.int32)

    note = make_note(sibling_blocks, positive_slot, lab_dev // BLOCK, homes, width)
    near, bit = queries, homes // 2
    while bit > 2:
        near = local_call(
            join_body, [like(2 * near.shape[0], width, bf16)], [side(bit), near, swap(near, "lab", bit)]
        )[0]
        bit //= 2
    near, noted = local_call(
        join_note_body,
        [like(half, width, bf16), like(half + NOTE, width, bf16)],
        [side(2), near, swap(near, "lab", 2), note],
    )
    far = swap(near, "lab", 1)
    work = 4 * half * lab_dev * width
    near_dq, near_slope = local_call(
        near_body,
        [like(half, width, f32), like(lab_dev, half, bf16)],
        [near, label_weights, note],
        work,
    )
    far_dq, far_slope, whole = local_call(
        far_body,
        [like(half, width, bf16), like(lab_dev, half, bf16), like(qcount + NOTE, width, bf16)],
        [noted, far, label_weights, note],
        work,
    )
    kept, came, bit = near_dq, swap(far_dq, "lab", 1), 2
    while bit < homes:
        rows = kept.shape[0] // 2
        kept, send = local_call(
            fold_body, [like(rows, width, f32), like(rows, width, bf16)], [side(bit), kept, came]
        )
        came = swap(send, "lab", bit)
        bit *= 2
    query_grad = local_call(last_body, [like(q_home, width, f32)], [kept, came])[0]
    sets = [(swap(noted, "pb", groups // 2), swap(far, "pb", groups // 2))]
    bit = groups // 4
    mate = swap(whole, "pb", 1)
    while bit:
        sets = sets + [(swap(a, "pb", bit), swap(b, "pb", bit)) for a, b in sets]
        bit //= 2
    acc = local_call(
        early_body,
        [like(lab_dev, width, f32)],
        [near, far, near_slope, far_slope, mate, label_weights],
        3 * work,
    )[0]
    flat = [part for pair in sets for part in pair]
    weight_grad = local_call(
        lambda *refs: late_body(groups, *refs),
        [like(lab_dev, width, bf16)],
        flat + [label_weights, acc],
        4 * work,
    )[0]
    return (query_grad, weight_grad)


def solution(mesh):
    groups, homes = mesh.shape["pb"], mesh.shape["lab"]

    def shards(queries, label_weights, sibling_blocks, positive_slot):
        every_row_everywhere = homes == K
        few = groups * sibling_blocks.shape[0] <= 2 * label_weights.shape[0]
        paired = groups == 4 and homes & (homes - 1) == 0
        one_block = label_weights.shape[0] // BLOCK <= K
        plan = dense_shards if every_row_everywhere and few and paired and one_block else sparse_shards
        return plan(queries, label_weights, sibling_blocks, positive_slot)

    in_specs = (P(("pb", "lab"), None), P("lab", None), P("pb", None), P("pb"))
    out_specs = (P(("pb", "lab"), None), P("lab", None))
    return jax.shard_map(shards, mesh=mesh, in_specs=in_specs, out_specs=out_specs, check_vma=False)
```

```python
import jax
import jax.numpy as jnp
from jax import lax
from jax.experimental import pallas as pl
from jax.experimental.pallas import tpu as pltpu
from jax.sharding import PartitionSpec as P

BLOCK = 128
K = 8
NOTE = 16
VMEM_LIMIT = 24 * 1024 * 1024


def pack_index(touched, width_slots, fill_value):
    homes, count = touched.shape
    rank = jnp.cumsum(touched.astype(jnp.int32), axis=1) - 1
    place = jnp.where(touched, rank, width_slots)
    home_ids = jnp.broadcast_to(jnp.arange(homes, dtype=jnp.int32)[:, None], touched.shape)
    row_ids = jnp.broadcast_to(jnp.arange(count, dtype=jnp.int32)[None, :], touched.shape)
    table = (
        jnp.full((homes, width_slots + 1), fill_value, jnp.int32).at[home_ids, place].set(row_ids)
    )
    return table[:, :width_slots]


def sparse_shards(queries, label_weights, sibling_blocks, positive_slot):
    width = queries.shape[1]
    qcount = sibling_blocks.shape[0]
    lab_dev = label_weights.shape[0]
    blocks_dev = lab_dev // BLOCK
    first = lax.axis_index("lab") * blocks_dev
    local_ids = first + jnp.arange(blocks_dev, dtype=jnp.int32)
    pblock = jnp.take_along_axis(sibling_blocks, (positive_slot // BLOCK)[:, None], axis=1)[:, 0]
    positive = pblock * BLOCK + positive_slot % BLOCK
    label_ids = local_ids[:, None] * BLOCK + jnp.arange(BLOCK, dtype=jnp.int32)[None, :]
    chosen_all = jnp.any(sibling_blocks[:, :, None] == local_ids[None, None, :], axis=1)
    piece = lax.all_gather(queries, "lab", axis=0, tiled=True)
    count = piece.shape[0]
    scores = jnp.dot(piece, label_weights.T, preferred_element_type=jnp.float32)
    scores = scores.reshape(count, blocks_dev, BLOCK)
    target = (label_ids[None, :, :] == positive[:, None, None]).astype(jnp.float32)
    slope = jnp.where(chosen_all[:, :, None], jax.nn.sigmoid(scores) - target, 0.0)
    slope = slope.astype(jnp.bfloat16).reshape(count, lab_dev)
    dq_all = jnp.dot(slope, label_weights, preferred_element_type=jnp.float32)
    w_acc = lax.dot_general(
        slope, piece, (((0,), (0,)), ((), ())), preferred_element_type=jnp.float32
    )
    homes = lax.axis_size("lab")
    q_home = qcount // homes
    slots = q_home * K // homes
    touched = jnp.any(chosen_all, axis=1).reshape(homes, q_home)
    send_idx = pack_index(touched, slots, q_home)
    padded = jnp.concatenate(
        [dq_all.reshape(homes, q_home, width), jnp.zeros((homes, 1, width), jnp.float32)], axis=1
    )
    outgoing = jnp.take_along_axis(padded, send_idx[:, :, None], axis=1)
    incoming = lax.all_to_all(outgoing, "lab", split_axis=0, concat_axis=0, tiled=True)
    own_blocks = lax.dynamic_slice_in_dim(sibling_blocks, lax.axis_index("lab") * q_home, q_home, 0)
    source_ids = jnp.arange(homes, dtype=jnp.int32)
    own_touch = jnp.any(
        (own_blocks // blocks_dev)[:, :, None] == source_ids[None, None, :], axis=1
    ).T
    recv_idx = pack_index(own_touch, slots, q_home)
    query_grad = (
        jnp.zeros((q_home + 1, width), jnp.float32)
        .at[recv_idx.reshape(-1)]
        .add(incoming.reshape(-1, width))[:q_home]
    )
    groups = lax.axis_size("pb")
    total = lax.psum(w_acc, "pb")
    weight_grad = (total / groups).astype(jnp.bfloat16)
    return (query_grad, weight_grad)


def swap(value, axis, bit):
    count = lax.axis_size(axis)
    return lax.ppermute(value, axis, [(i, i ^ bit) for i in range(count)])


def local_call(body, outs, args, flops=0, follows=()):
    specs = [
        pl.BlockSpec(memory_space=pltpu.SMEM if arg.dtype == jnp.int32 else pltpu.VMEM)
        for arg in args
    ]
    given, later = len(args), len(args) + len(follows)
    return pl.pallas_call(
        lambda *refs: body(*refs[:given], *refs[later:]),
        out_shape=outs,
        in_specs=specs + [pl.BlockSpec(memory_space=pl.ANY)] * len(follows),
        out_specs=[pl.BlockSpec(memory_space=pltpu.VMEM)] * len(outs),
        cost_estimate=pl.CostEstimate(flops=flops, bytes_accessed=0, transcendentals=0),
        compiler_params=pltpu.CompilerParams(vmem_limit_bytes=VMEM_LIMIT),
    )(*args, *follows)


def like(rows, width, dtype):
    return jax.ShapeDtypeStruct((rows, width), dtype)


def join_body(side_ref, own_ref, came_ref, out_ref):
    rows = own_ref.shape[0]
    side = side_ref[0]
    out_ref[pl.ds(pl.multiple_of(side * rows, rows), rows), :] = own_ref[...]
    out_ref[pl.ds(pl.multiple_of((1 - side) * rows, rows), rows), :] = came_ref[...]


def hold_body(rows_ref, held_ref):
    held_ref[...] = rows_ref[...]


def join_mark_body(side_ref, own_ref, came_ref, out_ref, mark_ref):
    join_body(side_ref, own_ref, came_ref, out_ref)
    mark_ref[...] = jnp.zeros_like(mark_ref)


def slope_of(rows, weights_ref, chosen, place):
    count = rows.shape[0]
    blocks = weights_ref.shape[0] // BLOCK
    scores = lax.dot_general(
        weights_ref[...], rows, (((1,), (1,)), ((), ())), preferred_element_type=jnp.float32
    )
    named = jnp.zeros((BLOCK, count), jnp.float32)
    for block in range(blocks):
        named = jnp.where(chosen == block, scores[block * BLOCK : (block + 1) * BLOCK], named)
    ids = lax.broadcasted_iota(jnp.int32, (BLOCK, count), 0)
    slope = jax.nn.sigmoid(named) - jnp.where(ids == place, 1.0, 0.0)
    parts = [jnp.where(chosen == block, slope, 0.0).astype(jnp.bfloat16) for block in range(blocks)]
    return jnp.concatenate(parts, axis=0)


def read_note(note, which, count):
    chosen = note[2 * which : 2 * which + 1, :count].astype(jnp.int32)
    place = note[2 * which + 1 : 2 * which + 2, :count].astype(jnp.int32)
    return chosen, place


def grad_body(which, rows_ref, weights_ref, note_ref, dq_ref, slope_ref):
    rows = rows_ref[...]
    note = note_ref[...].astype(jnp.float32)
    slope = slope_of(rows, weights_ref, *read_note(note, which, rows.shape[0]))
    slope_ref[...] = slope
    dq = lax.dot_general(
        slope, weights_ref[...], (((0,), (0,)), ((), ())), preferred_element_type=jnp.float32
    )
    dq_ref[...] = dq.astype(dq_ref.dtype)


def near_body(rows_ref, weights_ref, note_ref, dq_ref, slope_ref, noted_ref, held_ref):
    held_ref[...] = weights_ref[...]
    grad_body(0, rows_ref, weights_ref, note_ref, dq_ref, slope_ref)
    half = rows_ref.shape[0]
    noted_ref[:half, :] = rows_ref[...]
    noted_ref[half:, :] = note_ref[...]


def far_body(rows_ref, weights_ref, note_ref, dq_ref, slope_ref, far_out):
    grad_body(1, rows_ref, weights_ref, note_ref, dq_ref, slope_ref)
    far_out[...] = rows_ref[...]


def fold_body(side_ref, kept_ref, came_ref, keep_ref, send_ref):
    rows = keep_ref.shape[0]
    side = side_ref[0]
    mine = pl.ds(pl.multiple_of(side * rows, rows), rows)
    other = pl.ds(pl.multiple_of((1 - side) * rows, rows), rows)
    keep_ref[...] = kept_ref[mine, :] + came_ref[mine, :].astype(jnp.float32)
    send = kept_ref[other, :] + came_ref[other, :].astype(jnp.float32)
    send_ref[...] = send.astype(send_ref.dtype)


def last_body(kept_ref, came_ref, out_ref):
    out_ref[...] = kept_ref[...] + came_ref[...].astype(jnp.float32)


def slopes_of_set(near_rows, far_rows, note, weights_ref):
    half = near_rows.shape[0]
    rows = jnp.concatenate([near_rows, far_rows], axis=0)
    codes = [read_note(note, which, half) for which in range(2)]
    chosen = jnp.concatenate([codes[0][0], codes[1][0]], axis=1)
    place = jnp.concatenate([codes[0][1], codes[1][1]], axis=1)
    return rows, slope_of(rows, weights_ref, chosen, place)


def own_body(near_ref, far_ref, near_slope_ref, far_slope_ref, noted_ref, acc_ref, whole_ref):
    noted = noted_ref.shape[0]
    whole_ref[:noted, :] = noted_ref[...]
    whole_ref[noted:, :] = far_ref[...]
    rows = jnp.concatenate([near_ref[...], far_ref[...]], axis=0)
    slope = jnp.concatenate([near_slope_ref[...], far_slope_ref[...]], axis=1)
    acc_ref[...] = jnp.dot(slope, rows, preferred_element_type=jnp.float32)


def split_set(set_ref):
    half = (set_ref.shape[0] - NOTE) // 2
    return set_ref[:half, :], set_ref[half + NOTE :, :], set_ref[half : half + NOTE, :]


def pack_body(near_ref, far_ref, out_ref):
    noted = near_ref.shape[0]
    out_ref[:noted, :] = near_ref[...]
    out_ref[noted:, :] = far_ref[...]


def add_sets(acc_ref, weights_ref, set_refs):
    rows, slopes = [], []
    for set_ref in set_refs:
        near, far, note = split_set(set_ref)
        part, slope = slopes_of_set(near, far, note.astype(jnp.float32), weights_ref)
        rows.append(part)
        slopes.append(slope)
    return acc_ref[...] + jnp.dot(
        jnp.concatenate(slopes, axis=1),
        jnp.concatenate(rows, axis=0),
        preferred_element_type=jnp.float32,
    )


def mate_body(set_ref, weights_ref, acc_ref, out_ref):
    out_ref[...] = add_sets(acc_ref, weights_ref, [set_ref])


def late_body(groups, one_ref, two_ref, weights_ref, acc_ref, out_ref, mark_ref):
    mark_ref[...] = jnp.zeros_like(mark_ref)
    total = add_sets(acc_ref, weights_ref, [one_ref, two_ref])
    out_ref[...] = (total / groups).astype(out_ref.dtype)


def make_note(sibling_blocks, positive_slot, mark, blocks_dev, homes, width):
    sibling_blocks, positive_slot = sibling_blocks + mark, positive_slot + mark
    me = lax.axis_index("lab")
    local = sibling_blocks.T - me * blocks_dev
    inside = (local >= 0) & (local < blocks_dev)
    chosen = jnp.max(jnp.where(inside, local, -1), axis=0)
    steps = jnp.arange(local.shape[0], dtype=jnp.int32)[:, None]
    pblock = jnp.sum(jnp.where(steps == (positive_slot // BLOCK)[None, :], local, 0), axis=0)
    place = jnp.where(pblock == chosen, positive_slot % BLOCK, -1)
    code = jnp.stack([chosen, place]).astype(jnp.bfloat16)
    bits = homes.bit_length() - 1
    code = code.reshape((2,) + (2,) * bits + (-1,))
    code = code.transpose((bits, 0) + tuple(range(bits - 1, 0, -1)) + (bits + 1,))
    code = code.reshape(2, 2, -1)
    code = jnp.where(me % 2 == 0, code, code[::-1]).reshape(4, -1)
    return jnp.pad(code, ((0, NOTE - 4), (0, width - code.shape[1])))


def dense_shards(queries, label_weights, sibling_blocks, positive_slot):
    q_home, width = queries.shape
    qcount = sibling_blocks.shape[0]
    half = qcount // 2
    lab_dev = label_weights.shape[0]
    homes = lax.axis_size("lab")
    groups = lax.axis_size("pb")
    me = lax.axis_index("lab")
    f32, bf16 = jnp.float32, jnp.bfloat16

    def side(bit):
        return jnp.reshape((me // bit) % 2, (1,)).astype(jnp.int32)

    far_bit = groups // 2
    bit = homes // 2
    came = swap(queries, "lab", bit)
    near = local_call(hold_body, [like(q_home, width, bf16)], [queries])[0]
    while True:
        near, mark = local_call(
            join_mark_body,
            [like(2 * near.shape[0], width, bf16), like(1, BLOCK, jnp.int32)],
            [side(bit), near, came],
        )
        bit //= 2
        if bit == 1:
            break
        note = make_note(
            sibling_blocks, positive_slot, mark[0, 0], lab_dev // BLOCK, homes, width
        )
        came = swap(near, "lab", bit)
    far = swap(near, "lab", 1)
    work = 4 * half * lab_dev * width
    near_dq, near_slope, noted, weights = local_call(
        near_body,
        [
            like(half, width, f32),
            like(lab_dev, half, bf16),
            like(half + NOTE, width, bf16),
            like(lab_dev, width, bf16),
        ],
        [near, label_weights, note],
        work,
    )
    cross_near = swap(noted, "pb", far_bit)
    far_dq, far_slope, far_copy = local_call(
        far_body,
        [like(half, width, bf16), like(lab_dev, half, bf16), like(half, width, bf16)],
        [far, weights, note],
        work,
        [near_dq],
    )
    came = swap(far_dq, "lab", 1)
    acc, whole = local_call(
        own_body,
        [like(lab_dev, width, f32), like(qcount + NOTE, width, bf16)],
        [near, far, near_slope, far_slope, noted],
        work,
        [cross_near],
    )
    cross_far = swap(far_copy, "pb", far_bit)
    mate = swap(whole, "pb", 1)
    rows = half // 2
    kept, send = local_call(
        fold_body, [like(rows, width, f32), like(rows, width, bf16)], [side(2), near_dq, came], 0, [acc]
    )
    came = swap(send, "lab", 2)
    cross = local_call(
        pack_body, [like(qcount + NOTE, width, bf16)], [cross_near, cross_far], 0, [kept]
    )[0]
    acc = local_call(
        mate_body, [like(lab_dev, width, f32)], [mate, weights, acc], 40 * work, [cross]
    )[0]
    cross_mate = swap(cross, "pb", 1)
    bit = 4
    while bit < homes:
        rows //= 2
        kept, send = local_call(
            fold_body,
            [like(rows, width, f32), like(rows, width, bf16)],
            [side(bit), kept, came],
            0,
            [acc],
        )
        came = swap(send, "lab", bit)
        bit *= 2
    weight_grad, mark = local_call(
        lambda *refs: late_body(groups, *refs),
        [like(lab_dev, width, bf16), like(1, BLOCK, jnp.int32)],
        [cross, cross_mate, weights, acc],
        4 * work,
        [kept],
    )
    query_grad = local_call(
        last_body, [like(q_home, width, f32)], [kept, came], 0, [mark]
    )[0]
    return (query_grad, weight_grad)


def solution(mesh):
    groups, homes = mesh.shape["pb"], mesh.shape["lab"]

    def shards(queries, label_weights, sibling_blocks, positive_slot):
        every_row_everywhere = homes == K
        few = groups * sibling_blocks.shape[0] <= 2 * label_weights.shape[0]
        paired = groups == 4 and homes & (homes - 1) == 0
        one_block = label_weights.shape[0] // BLOCK <= K
        plan = dense_shards if every_row_everywhere and few and paired and one_block else sparse_shards
        return plan(queries, label_weights, sibling_blocks, positive_slot)

    in_specs = (P(("pb", "lab"), None), P("lab", None), P("pb", None), P("pb"))
    out_specs = (P(("pb", "lab"), None), P("lab", None))
    return jax.shard_map(shards, mesh=mesh, in_specs=in_specs, out_specs=out_specs, check_vma=False)
```

```python
import jax
import jax.numpy as jnp
from jax import lax
from jax.experimental import pallas as pl
from jax.experimental.pallas import tpu as pltpu
from jax.sharding import PartitionSpec as P

BLOCK = 128
K = 8
NOTE = 16
VMEM_LIMIT = 24 * 1024 * 1024


def pack_index(touched, width_slots, fill_value):
    homes, count = touched.shape
    rank = jnp.cumsum(touched.astype(jnp.int32), axis=1) - 1
    place = jnp.where(touched, rank, width_slots)
    home_ids = jnp.broadcast_to(jnp.arange(homes, dtype=jnp.int32)[:, None], touched.shape)
    row_ids = jnp.broadcast_to(jnp.arange(count, dtype=jnp.int32)[None, :], touched.shape)
    table = (
        jnp.full((homes, width_slots + 1), fill_value, jnp.int32).at[home_ids, place].set(row_ids)
    )
    return table[:, :width_slots]


def sparse_shards(queries, label_weights, sibling_blocks, positive_slot):
    width = queries.shape[1]
    qcount = sibling_blocks.shape[0]
    lab_dev = label_weights.shape[0]
    blocks_dev = lab_dev // BLOCK
    first = lax.axis_index("lab") * blocks_dev
    local_ids = first + jnp.arange(blocks_dev, dtype=jnp.int32)
    pblock = jnp.take_along_axis(sibling_blocks, (positive_slot // BLOCK)[:, None], axis=1)[:, 0]
    positive = pblock * BLOCK + positive_slot % BLOCK
    label_ids = local_ids[:, None] * BLOCK + jnp.arange(BLOCK, dtype=jnp.int32)[None, :]
    chosen_all = jnp.any(sibling_blocks[:, :, None] == local_ids[None, None, :], axis=1)
    piece = lax.all_gather(queries, "lab", axis=0, tiled=True)
    count = piece.shape[0]
    scores = jnp.dot(piece, label_weights.T, preferred_element_type=jnp.float32)
    scores = scores.reshape(count, blocks_dev, BLOCK)
    target = (label_ids[None, :, :] == positive[:, None, None]).astype(jnp.float32)
    slope = jnp.where(chosen_all[:, :, None], jax.nn.sigmoid(scores) - target, 0.0)
    slope = slope.astype(jnp.bfloat16).reshape(count, lab_dev)
    dq_all = jnp.dot(slope, label_weights, preferred_element_type=jnp.float32)
    w_acc = lax.dot_general(
        slope, piece, (((0,), (0,)), ((), ())), preferred_element_type=jnp.float32
    )
    homes = lax.axis_size("lab")
    q_home = qcount // homes
    slots = q_home * K // homes
    touched = jnp.any(chosen_all, axis=1).reshape(homes, q_home)
    send_idx = pack_index(touched, slots, q_home)
    padded = jnp.concatenate(
        [dq_all.reshape(homes, q_home, width), jnp.zeros((homes, 1, width), jnp.float32)], axis=1
    )
    outgoing = jnp.take_along_axis(padded, send_idx[:, :, None], axis=1)
    incoming = lax.all_to_all(outgoing, "lab", split_axis=0, concat_axis=0, tiled=True)
    own_blocks = lax.dynamic_slice_in_dim(sibling_blocks, lax.axis_index("lab") * q_home, q_home, 0)
    source_ids = jnp.arange(homes, dtype=jnp.int32)
    own_touch = jnp.any(
        (own_blocks // blocks_dev)[:, :, None] == source_ids[None, None, :], axis=1
    ).T
    recv_idx = pack_index(own_touch, slots, q_home)
    query_grad = (
        jnp.zeros((q_home + 1, width), jnp.float32)
        .at[recv_idx.reshape(-1)]
        .add(incoming.reshape(-1, width))[:q_home]
    )
    groups = lax.axis_size("pb")
    total = lax.psum(w_acc, "pb")
    weight_grad = (total / groups).astype(jnp.bfloat16)
    return (query_grad, weight_grad)


def swap(value, axis, bit):
    count = lax.axis_size(axis)
    return lax.ppermute(value, axis, [(i, i ^ bit) for i in range(count)])


def local_call(body, outs, args, flops=0, follows=()):
    specs = [
        pl.BlockSpec(memory_space=pltpu.SMEM if arg.dtype == jnp.int32 else pltpu.VMEM)
        for arg in args
    ]
    given, later = len(args), len(args) + len(follows)
    return pl.pallas_call(
        lambda *refs: body(*refs[:given], *refs[later:]),
        out_shape=outs,
        in_specs=specs + [pl.BlockSpec(memory_space=pl.ANY)] * len(follows),
        out_specs=[pl.BlockSpec(memory_space=pltpu.VMEM)] * len(outs),
        cost_estimate=pl.CostEstimate(flops=flops, bytes_accessed=0, transcendentals=0),
        compiler_params=pltpu.CompilerParams(vmem_limit_bytes=VMEM_LIMIT),
    )(*args, *follows)


def like(rows, width, dtype):
    return jax.ShapeDtypeStruct((rows, width), dtype)


def join_body(side_ref, own_ref, came_ref, out_ref):
    rows = own_ref.shape[0]
    side = side_ref[0]
    out_ref[pl.ds(pl.multiple_of(side * rows, rows), rows), :] = own_ref[...]
    out_ref[pl.ds(pl.multiple_of((1 - side) * rows, rows), rows), :] = came_ref[...]


def hold_body(rows_ref, held_ref):
    held_ref[...] = rows_ref[...]


def join_mark_body(side_ref, own_ref, came_ref, out_ref, mark_ref):
    join_body(side_ref, own_ref, came_ref, out_ref)
    mark_ref[...] = jnp.zeros_like(mark_ref)


def join_note_body(side_ref, own_ref, came_ref, note_ref, out_ref, noted_ref):
    rows = out_ref.shape[0]
    join_body(side_ref, own_ref, came_ref, out_ref)
    noted_ref[:rows, :] = out_ref[...]
    noted_ref[rows:, :] = note_ref[...]


def slope_of(rows, weights_ref, chosen, place):
    count = rows.shape[0]
    blocks = weights_ref.shape[0] // BLOCK
    scores = lax.dot_general(
        weights_ref[...], rows, (((1,), (1,)), ((), ())), preferred_element_type=jnp.float32
    )
    named = jnp.zeros((BLOCK, count), jnp.float32)
    for block in range(blocks):
        named = jnp.where(chosen == block, scores[block * BLOCK : (block + 1) * BLOCK], named)
    ids = lax.broadcasted_iota(jnp.int32, (BLOCK, count), 0)
    slope = jax.nn.sigmoid(named) - jnp.where(ids == place, 1.0, 0.0)
    parts = [jnp.where(chosen == block, slope, 0.0).astype(jnp.bfloat16) for block in range(blocks)]
    return jnp.concatenate(parts, axis=0)


def read_note(note, which, count):
    chosen = note[2 * which : 2 * which + 1, :count].astype(jnp.int32)
    place = note[2 * which + 1 : 2 * which + 2, :count].astype(jnp.int32)
    return chosen, place


def grad_body(which, rows_ref, weights_ref, note_ref, dq_ref, slope_ref):
    rows = rows_ref[...]
    note = note_ref[...].astype(jnp.float32)
    slope = slope_of(rows, weights_ref, *read_note(note, which, rows.shape[0]))
    slope_ref[...] = slope
    dq = lax.dot_general(
        slope, weights_ref[...], (((0,), (0,)), ((), ())), preferred_element_type=jnp.float32
    )
    dq_ref[...] = dq.astype(dq_ref.dtype)


def near_body(rows_ref, weights_ref, note_ref, dq_ref, slope_ref, held_ref):
    held_ref[...] = weights_ref[...]
    grad_body(0, rows_ref, weights_ref, note_ref, dq_ref, slope_ref)


def far_body(rows_ref, weights_ref, note_ref, dq_ref, slope_ref, far_out):
    grad_body(1, rows_ref, weights_ref, note_ref, dq_ref, slope_ref)
    far_out[...] = rows_ref[...]


def fold_body(side_ref, kept_ref, came_ref, keep_ref, send_ref):
    rows = keep_ref.shape[0]
    side = side_ref[0]
    mine = pl.ds(pl.multiple_of(side * rows, rows), rows)
    other = pl.ds(pl.multiple_of((1 - side) * rows, rows), rows)
    keep_ref[...] = kept_ref[mine, :] + came_ref[mine, :].astype(jnp.float32)
    send = kept_ref[other, :] + came_ref[other, :].astype(jnp.float32)
    send_ref[...] = send.astype(send_ref.dtype)


def last_body(kept_ref, came_ref, out_ref):
    out_ref[...] = kept_ref[...] + came_ref[...].astype(jnp.float32)


def slopes_of_set(near_rows, far_rows, note, weights_ref):
    half = near_rows.shape[0]
    rows = jnp.concatenate([near_rows, far_rows], axis=0)
    codes = [read_note(note, which, half) for which in range(2)]
    chosen = jnp.concatenate([codes[0][0], codes[1][0]], axis=1)
    place = jnp.concatenate([codes[0][1], codes[1][1]], axis=1)
    return rows, slope_of(rows, weights_ref, chosen, place)


def own_body(near_ref, far_ref, near_slope_ref, far_slope_ref, noted_ref, acc_ref, whole_ref):
    noted = noted_ref.shape[0]
    whole_ref[:noted, :] = noted_ref[...]
    whole_ref[noted:, :] = far_ref[...]
    rows = jnp.concatenate([near_ref[...], far_ref[...]], axis=0)
    slope = jnp.concatenate([near_slope_ref[...], far_slope_ref[...]], axis=1)
    acc_ref[...] = jnp.dot(slope, rows, preferred_element_type=jnp.float32)


def split_set(set_ref):
    half = (set_ref.shape[0] - NOTE) // 2
    return set_ref[:half, :], set_ref[half + NOTE :, :], set_ref[half : half + NOTE, :]


def fold_pack_body(side_ref, kept_ref, came_ref, near_ref, far_ref, keep_ref, send_ref, set_ref):
    noted = near_ref.shape[0]
    fold_body(side_ref, kept_ref, came_ref, keep_ref, send_ref)
    set_ref[:noted, :] = near_ref[...]
    set_ref[noted:, :] = far_ref[...]


def add_sets(acc_ref, weights_ref, set_refs):
    rows, slopes = [], []
    for set_ref in set_refs:
        near, far, note = split_set(set_ref)
        part, slope = slopes_of_set(near, far, note.astype(jnp.float32), weights_ref)
        rows.append(part)
        slopes.append(slope)
    return acc_ref[...] + jnp.dot(
        jnp.concatenate(slopes, axis=1),
        jnp.concatenate(rows, axis=0),
        preferred_element_type=jnp.float32,
    )


def mate_body(set_ref, weights_ref, acc_ref, out_ref):
    out_ref[...] = add_sets(acc_ref, weights_ref, [set_ref])


def late_body(groups, one_ref, two_ref, weights_ref, acc_ref, out_ref, mark_ref):
    mark_ref[...] = jnp.zeros_like(mark_ref)
    total = add_sets(acc_ref, weights_ref, [one_ref, two_ref])
    out_ref[...] = (total / groups).astype(out_ref.dtype)


def make_note(sibling_blocks, positive_slot, mark, blocks_dev, homes, width):
    sibling_blocks, positive_slot = sibling_blocks + mark, positive_slot + mark
    me = lax.axis_index("lab")
    local = sibling_blocks.T - me * blocks_dev
    inside = (local >= 0) & (local < blocks_dev)
    chosen = jnp.max(jnp.where(inside, local, -1), axis=0)
    steps = jnp.arange(local.shape[0], dtype=jnp.int32)[:, None]
    pblock = jnp.sum(jnp.where(steps == (positive_slot // BLOCK)[None, :], local, 0), axis=0)
    place = jnp.where(pblock == chosen, positive_slot % BLOCK, -1)
    code = jnp.stack([chosen, place]).astype(jnp.bfloat16)
    bits = homes.bit_length() - 1
    code = code.reshape((2,) + (2,) * bits + (-1,))
    code = code.transpose((bits, 0) + tuple(range(bits - 1, 0, -1)) + (bits + 1,))
    code = code.reshape(2, 2, -1)
    code = jnp.where(me % 2 == 0, code, code[::-1]).reshape(4, -1)
    return jnp.pad(code, ((0, NOTE - 4), (0, width - code.shape[1])))


def dense_shards(queries, label_weights, sibling_blocks, positive_slot):
    q_home, width = queries.shape
    qcount = sibling_blocks.shape[0]
    half = qcount // 2
    lab_dev = label_weights.shape[0]
    homes = lax.axis_size("lab")
    groups = lax.axis_size("pb")
    me = lax.axis_index("lab")
    f32, bf16 = jnp.float32, jnp.bfloat16

    def side(bit):
        return jnp.reshape((me // bit) % 2, (1,)).astype(jnp.int32)

    far_bit = groups // 2
    bit = homes // 2
    came = swap(queries, "lab", bit)
    near = local_call(hold_body, [like(q_home, width, bf16)], [queries])[0]
    while bit > 2:
        near, mark = local_call(
            join_mark_body,
            [like(2 * near.shape[0], width, bf16), like(1, BLOCK, jnp.int32)],
            [side(bit), near, came],
        )
        bit //= 2
        came = swap(near, "lab", bit)
    note = make_note(sibling_blocks, positive_slot, mark[0, 0], lab_dev // BLOCK, homes, width)
    near, noted = local_call(
        join_note_body,
        [like(half, width, bf16), like(half + NOTE, width, bf16)],
        [side(bit), near, came, note],
    )
    far = swap(near, "lab", 1)
    work = 4 * half * lab_dev * width
    near_dq, near_slope, weights = local_call(
        near_body,
        [like(half, width, f32), like(lab_dev, half, bf16), like(lab_dev, width, bf16)],
        [near, label_weights, note],
        work,
    )
    cross_near = swap(noted, "pb", far_bit)
    far_dq, far_slope, far_copy = local_call(
        far_body,
        [like(half, width, bf16), like(lab_dev, half, bf16), like(half, width, bf16)],
        [far, weights, note],
        work,
        [near_dq],
    )
    came = swap(far_dq, "lab", 1)
    acc, whole = local_call(
        own_body,
        [like(lab_dev, width, f32), like(qcount + NOTE, width, bf16)],
        [near, far, near_slope, far_slope, noted],
        work,
        [cross_near],
    )
    cross_far = swap(far_copy, "pb", far_bit)
    mate = swap(whole, "pb", 1)
    rows = half // 2
    kept, send, cross = local_call(
        fold_pack_body,
        [like(rows, width, f32), like(rows, width, bf16), like(qcount + NOTE, width, bf16)],
        [side(2), near_dq, came, cross_near, cross_far],
        0,
        [acc],
    )
    came = swap(send, "lab", 2)
    acc = local_call(
        mate_body, [like(lab_dev, width, f32)], [mate, weights, acc], 2 * work, [kept]
    )[0]
    cross_mate = swap(cross, "pb", 1)
    bit = 4
    while bit < homes:
        rows //= 2
        kept, send = local_call(
            fold_body,
            [like(rows, width, f32), like(rows, width, bf16)],
            [side(bit), kept, came],
            0,
            [acc],
        )
        came = swap(send, "lab", bit)
        bit *= 2
    weight_grad, mark = local_call(
        lambda *refs: late_body(groups, *refs),
        [like(lab_dev, width, bf16), like(1, BLOCK, jnp.int32)],
        [cross, cross_mate, weights, acc],
        4 * work,
        [kept],
    )
    query_grad = local_call(
        last_body, [like(q_home, width, f32)], [kept, came], 0, [mark]
    )[0]
    return (query_grad, weight_grad)


def solution(mesh):
    groups, homes = mesh.shape["pb"], mesh.shape["lab"]

    def shards(queries, label_weights, sibling_blocks, positive_slot):
        every_row_everywhere = homes == K
        few = groups * sibling_blocks.shape[0] <= 2 * label_weights.shape[0]
        paired = groups == 4 and homes & (homes - 1) == 0
        one_block = label_weights.shape[0] // BLOCK <= K
        plan = dense_shards if every_row_everywhere and few and paired and one_block else sparse_shards
        return plan(queries, label_weights, sibling_blocks, positive_slot)

    in_specs = (P(("pb", "lab"), None), P("lab", None), P("pb", None), P("pb"))
    out_specs = (P(("pb", "lab"), None), P("lab", None))
    return jax.shard_map(shards, mesh=mesh, in_specs=in_specs, out_specs=out_specs, check_vma=False)
```

```python
import jax
import jax.numpy as jnp
from jax import lax
from jax.experimental import pallas as pl
from jax.experimental.pallas import tpu as pltpu
from jax.sharding import PartitionSpec as P

BLOCK = 128
K = 8
NOTE = 16
VMEM_LIMIT = 24 * 1024 * 1024


def pack_index(touched, width_slots, fill_value):
    homes, count = touched.shape
    rank = jnp.cumsum(touched.astype(jnp.int32), axis=1) - 1
    place = jnp.where(touched, rank, width_slots)
    home_ids = jnp.broadcast_to(jnp.arange(homes, dtype=jnp.int32)[:, None], touched.shape)
    row_ids = jnp.broadcast_to(jnp.arange(count, dtype=jnp.int32)[None, :], touched.shape)
    table = (
        jnp.full((homes, width_slots + 1), fill_value, jnp.int32).at[home_ids, place].set(row_ids)
    )
    return table[:, :width_slots]


def sparse_shards(queries, label_weights, sibling_blocks, positive_slot):
    width = queries.shape[1]
    qcount = sibling_blocks.shape[0]
    lab_dev = label_weights.shape[0]
    blocks_dev = lab_dev // BLOCK
    first = lax.axis_index("lab") * blocks_dev
    local_ids = first + jnp.arange(blocks_dev, dtype=jnp.int32)
    pblock = jnp.take_along_axis(sibling_blocks, (positive_slot // BLOCK)[:, None], axis=1)[:, 0]
    positive = pblock * BLOCK + positive_slot % BLOCK
    label_ids = local_ids[:, None] * BLOCK + jnp.arange(BLOCK, dtype=jnp.int32)[None, :]
    chosen_all = jnp.any(sibling_blocks[:, :, None] == local_ids[None, None, :], axis=1)
    piece = lax.all_gather(queries, "lab", axis=0, tiled=True)
    count = piece.shape[0]
    scores = jnp.dot(piece, label_weights.T, preferred_element_type=jnp.float32)
    scores = scores.reshape(count, blocks_dev, BLOCK)
    target = (label_ids[None, :, :] == positive[:, None, None]).astype(jnp.float32)
    slope = jnp.where(chosen_all[:, :, None], jax.nn.sigmoid(scores) - target, 0.0)
    slope = slope.astype(jnp.bfloat16).reshape(count, lab_dev)
    dq_all = jnp.dot(slope, label_weights, preferred_element_type=jnp.float32)
    w_acc = lax.dot_general(
        slope, piece, (((0,), (0,)), ((), ())), preferred_element_type=jnp.float32
    )
    homes = lax.axis_size("lab")
    q_home = qcount // homes
    slots = q_home * K // homes
    touched = jnp.any(chosen_all, axis=1).reshape(homes, q_home)
    send_idx = pack_index(touched, slots, q_home)
    padded = jnp.concatenate(
        [dq_all.reshape(homes, q_home, width), jnp.zeros((homes, 1, width), jnp.float32)], axis=1
    )
    outgoing = jnp.take_along_axis(padded, send_idx[:, :, None], axis=1)
    incoming = lax.all_to_all(outgoing, "lab", split_axis=0, concat_axis=0, tiled=True)
    own_blocks = lax.dynamic_slice_in_dim(sibling_blocks, lax.axis_index("lab") * q_home, q_home, 0)
    source_ids = jnp.arange(homes, dtype=jnp.int32)
    own_touch = jnp.any(
        (own_blocks // blocks_dev)[:, :, None] == source_ids[None, None, :], axis=1
    ).T
    recv_idx = pack_index(own_touch, slots, q_home)
    query_grad = (
        jnp.zeros((q_home + 1, width), jnp.float32)
        .at[recv_idx.reshape(-1)]
        .add(incoming.reshape(-1, width))[:q_home]
    )
    groups = lax.axis_size("pb")
    total = lax.psum(w_acc, "pb")
    weight_grad = (total / groups).astype(jnp.bfloat16)
    return (query_grad, weight_grad)


def swap(value, axis, bit):
    count = lax.axis_size(axis)
    return lax.ppermute(value, axis, [(i, i ^ bit) for i in range(count)])


def diagonal(value, group_bit, home_bit):
    groups, homes = lax.axis_size("pb"), lax.axis_size("lab")
    pairs = [
        (g * homes + h, (g ^ group_bit) * homes + (h ^ home_bit))
        for g in range(groups)
        for h in range(homes)
    ]
    return lax.ppermute(value, ("pb", "lab"), pairs)


def local_call(body, outs, args, flops=0, follows=()):
    specs = [
        pl.BlockSpec(memory_space=pltpu.SMEM if arg.dtype == jnp.int32 else pltpu.VMEM)
        for arg in args
    ]
    given, later = len(args), len(args) + len(follows)
    return pl.pallas_call(
        lambda *refs: body(*refs[:given], *refs[later:]),
        out_shape=outs,
        in_specs=specs + [pl.BlockSpec(memory_space=pl.ANY)] * len(follows),
        out_specs=[pl.BlockSpec(memory_space=pltpu.VMEM)] * len(outs),
        cost_estimate=pl.CostEstimate(flops=flops, bytes_accessed=0, transcendentals=0),
        compiler_params=pltpu.CompilerParams(vmem_limit_bytes=VMEM_LIMIT),
    )(*args, *follows)


def like(rows, width, dtype):
    return jax.ShapeDtypeStruct((rows, width), dtype)


def join_body(place_ref, own_ref, *refs):
    *came_refs, note_ref, out_ref, noted_ref = refs
    rows, place = own_ref.shape[0], place_ref[0]
    for step, ref in enumerate([own_ref, *came_refs]):
        start = pl.multiple_of((place ^ step) * rows, rows)
        out_ref[pl.ds(start, rows), :] = ref[...]
    half = out_ref.shape[0]
    noted_ref[:half, :] = out_ref[...]
    noted_ref[half:, :] = note_ref[...]


def hold_body(rows_ref, held_ref):
    held_ref[...] = rows_ref[...]


def slope_of(rows, weights_ref, chosen, place):
    count = rows.shape[0]
    blocks = weights_ref.shape[0] // BLOCK
    scores = lax.dot_general(
        weights_ref[...], rows, (((1,), (1,)), ((), ())), preferred_element_type=jnp.float32
    )
    named = jnp.zeros((BLOCK, count), jnp.float32)
    for block in range(blocks):
        named = jnp.where(chosen == block, scores[block * BLOCK : (block + 1) * BLOCK], named)
    ids = lax.broadcasted_iota(jnp.int32, (BLOCK, count), 0)
    slope = jax.nn.sigmoid(named) - jnp.where(ids == place, 1.0, 0.0)
    parts = [jnp.where(chosen == block, slope, 0.0).astype(jnp.bfloat16) for block in range(blocks)]
    return jnp.concatenate(parts, axis=0)


def read_note(note, which, count):
    chosen = note[2 * which : 2 * which + 1, :count].astype(jnp.int32)
    place = note[2 * which + 1 : 2 * which + 2, :count].astype(jnp.int32)
    return chosen, place


def grad_body(which, rows_ref, weights_ref, note_ref, dq_ref, slope_ref):
    rows = rows_ref[...]
    note = note_ref[...].astype(jnp.float32)
    slope = slope_of(rows, weights_ref, *read_note(note, which, rows.shape[0]))
    slope_ref[...] = slope
    dq = lax.dot_general(
        slope, weights_ref[...], (((0,), (0,)), ((), ())), preferred_element_type=jnp.float32
    )
    dq_ref[...] = dq.astype(dq_ref.dtype)


def near_body(rows_ref, weights_ref, note_ref, dq_ref, slope_ref, held_ref):
    held_ref[...] = weights_ref[...]
    grad_body(0, rows_ref, weights_ref, note_ref, dq_ref, slope_ref)


def far_body(side_ref, rows_ref, weights_ref, note_ref, near_ref, dq_ref, slope_ref):
    rows = rows_ref[...]
    half = rows.shape[0]
    planes, homes, q_home = 2, dq_ref.shape[0], dq_ref.shape[1]
    side = side_ref[0]
    note = note_ref[...].astype(jnp.float32)
    slope = slope_of(rows, weights_ref, *read_note(note, 1, half))
    slope_ref[...] = slope
    far = lax.dot_general(
        slope, weights_ref[...], (((0,), (0,)), ((), ())), preferred_element_type=jnp.float32
    ).astype(dq_ref.dtype)
    near = near_ref[...]
    for z in range(homes // planes):
        part = slice(z * q_home, (z + 1) * q_home)
        dq_ref[planes * z + side] = near[part, :]
        dq_ref[planes * z + 1 - side] = far[part, :]


def sum_body(terms_ref, out_ref):
    total = terms_ref[0].astype(jnp.float32)
    for source in range(1, terms_ref.shape[0]):
        total = total + terms_ref[source].astype(jnp.float32)
    out_ref[...] = total


def slopes_of_set(near_rows, far_rows, note, weights_ref):
    half = near_rows.shape[0]
    rows = jnp.concatenate([near_rows, far_rows], axis=0)
    codes = [read_note(note, which, half) for which in range(2)]
    chosen = jnp.concatenate([codes[0][0], codes[1][0]], axis=1)
    place = jnp.concatenate([codes[0][1], codes[1][1]], axis=1)
    return rows, slope_of(rows, weights_ref, chosen, place)


def own_body(near_ref, far_ref, near_slope_ref, far_slope_ref, noted_ref, acc_ref, whole_ref):
    noted = noted_ref.shape[0]
    whole_ref[:noted, :] = noted_ref[...]
    whole_ref[noted:, :] = far_ref[...]
    rows = jnp.concatenate([near_ref[...], far_ref[...]], axis=0)
    slope = jnp.concatenate([near_slope_ref[...], far_slope_ref[...]], axis=1)
    acc_ref[...] = jnp.dot(slope, rows, preferred_element_type=jnp.float32)


def split_set(set_ref):
    half = (set_ref.shape[0] - NOTE) // 2
    return set_ref[:half, :], set_ref[half + NOTE :, :], set_ref[half : half + NOTE, :]


def pack_body(near_ref, far_ref, out_ref):
    noted = near_ref.shape[0]
    out_ref[:noted, :] = near_ref[...]
    out_ref[noted:, :] = far_ref[...]


def add_sets(acc_ref, weights_ref, set_refs):
    rows, slopes = [], []
    for set_ref in set_refs:
        near, far, note = split_set(set_ref)
        part, slope = slopes_of_set(near, far, note.astype(jnp.float32), weights_ref)
        rows.append(part)
        slopes.append(slope)
    return acc_ref[...] + jnp.dot(
        jnp.concatenate(slopes, axis=1),
        jnp.concatenate(rows, axis=0),
        preferred_element_type=jnp.float32,
    )


def mate_body(set_ref, weights_ref, acc_ref, out_ref):
    out_ref[...] = add_sets(acc_ref, weights_ref, [set_ref])


def late_body(groups, one_ref, two_ref, weights_ref, acc_ref, out_ref, mark_ref):
    mark_ref[...] = jnp.zeros_like(mark_ref)
    total = add_sets(acc_ref, weights_ref, [one_ref, two_ref])
    out_ref[...] = (total / groups).astype(out_ref.dtype)


def make_note(sibling_blocks, positive_slot, blocks_dev, homes, width):
    me = lax.axis_index("lab")
    local = sibling_blocks.T - me * blocks_dev
    inside = (local >= 0) & (local < blocks_dev)
    chosen = jnp.max(jnp.where(inside, local, -1), axis=0)
    steps = jnp.arange(local.shape[0], dtype=jnp.int32)[:, None]
    pblock = jnp.sum(jnp.where(steps == (positive_slot // BLOCK)[None, :], local, 0), axis=0)
    place = jnp.where(pblock == chosen, positive_slot % BLOCK, -1)
    code = jnp.stack([chosen, place]).astype(jnp.bfloat16)
    code = code.reshape(2, homes // 2, 2, -1).transpose(2, 0, 1, 3).reshape(2, 2, -1)
    code = jnp.where(me % 2 == 0, code, code[::-1]).reshape(4, -1)
    return jnp.pad(code, ((0, NOTE - 4), (0, width - code.shape[1])))


def dense_shards(queries, label_weights, sibling_blocks, positive_slot):
    q_home, width = queries.shape
    qcount = sibling_blocks.shape[0]
    half = qcount // 2
    lab_dev = label_weights.shape[0]
    homes = lax.axis_size("lab")
    groups = lax.axis_size("pb")
    me = lax.axis_index("lab")
    f32, bf16 = jnp.float32, jnp.bfloat16

    place = jnp.reshape(me // 2, (1,)).astype(jnp.int32)
    side = jnp.reshape(me % 2, (1,)).astype(jnp.int32)
    far_bit = groups // 2
    came = [swap(queries, "lab", 2 * step) for step in range(1, homes // 2)]
    held = local_call(hold_body, [like(q_home, width, bf16)], [queries])[0]
    note = make_note(sibling_blocks, positive_slot, lab_dev // BLOCK, homes, width)
    near, noted = local_call(
        join_body,
        [like(half, width, bf16), like(half + NOTE, width, bf16)],
        [place, held, *came, note],
    )
    far = swap(near, "lab", 1)
    work = 4 * half * lab_dev * width
    near_dq, near_slope, weights = local_call(
        near_body,
        [like(half, width, bf16), like(lab_dev, half, bf16), like(lab_dev, width, bf16)],
        [near, label_weights, note],
        work,
    )
    cross_near = swap(noted, "pb", far_bit)
    cross_far = diagonal(near, far_bit, 1)
    dq, far_slope = local_call(
        far_body,
        [jax.ShapeDtypeStruct((homes, q_home, width), bf16), like(lab_dev, half, bf16)],
        [side, far, weights, note, near_dq],
        work,
    )
    terms = lax.all_to_all(dq, "lab", split_axis=0, concat_axis=0, tiled=True)
    acc, whole = local_call(
        own_body,
        [like(lab_dev, width, f32), like(qcount + NOTE, width, bf16)],
        [near, far, near_slope, far_slope, noted],
        work,
        [],
    )
    mate = swap(whole, "pb", 1)
    cross = local_call(
        pack_body, [like(qcount + NOTE, width, bf16)], [cross_near, cross_far], 0, [acc]
    )[0]
    cross_mate = swap(cross, "pb", 1)
    acc = local_call(
        mate_body, [like(lab_dev, width, f32)], [mate, weights, acc], 2 * work, [cross]
    )[0]
    weight_grad, mark = local_call(
        lambda *refs: late_body(groups, *refs),
        [like(lab_dev, width, bf16), like(1, BLOCK, jnp.int32)],
        [cross, cross_mate, weights, acc],
        4 * work,
    )
    query_grad = local_call(sum_body, [like(q_home, width, f32)], [terms], 0, [mark])[0]
    return (query_grad, weight_grad)


def solution(mesh):
    groups, homes = mesh.shape["pb"], mesh.shape["lab"]

    def shards(queries, label_weights, sibling_blocks, positive_slot):
        every_row_everywhere = homes == K
        few = groups * sibling_blocks.shape[0] <= 2 * label_weights.shape[0]
        paired = groups == 4 and homes & (homes - 1) == 0
        one_block = label_weights.shape[0] // BLOCK <= K
        plan = dense_shards if every_row_everywhere and few and paired and one_block else sparse_shards
        return plan(queries, label_weights, sibling_blocks, positive_slot)

    in_specs = (P(("pb", "lab"), None), P("lab", None), P("pb", None), P("pb"))
    out_specs = (P(("pb", "lab"), None), P("lab", None))
    return jax.shard_map(shards, mesh=mesh, in_specs=in_specs, out_specs=out_specs, check_vma=False)
```

```python
import jax
import jax.numpy as jnp
from jax import lax
from jax.experimental import pallas as pl
from jax.experimental.pallas import tpu as pltpu
from jax.sharding import PartitionSpec as P

BLOCK = 128
K = 8
NOTE = 16
VMEM_LIMIT = 24 * 1024 * 1024


def pack_index(touched, width_slots, fill_value):
    homes, count = touched.shape
    rank = jnp.cumsum(touched.astype(jnp.int32), axis=1) - 1
    place = jnp.where(touched, rank, width_slots)
    home_ids = jnp.broadcast_to(jnp.arange(homes, dtype=jnp.int32)[:, None], touched.shape)
    row_ids = jnp.broadcast_to(jnp.arange(count, dtype=jnp.int32)[None, :], touched.shape)
    table = (
        jnp.full((homes, width_slots + 1), fill_value, jnp.int32).at[home_ids, place].set(row_ids)
    )
    return table[:, :width_slots]


def sparse_shards(queries, label_weights, sibling_blocks, positive_slot):
    width = queries.shape[1]
    qcount = sibling_blocks.shape[0]
    lab_dev = label_weights.shape[0]
    blocks_dev = lab_dev // BLOCK
    first = lax.axis_index("lab") * blocks_dev
    local_ids = first + jnp.arange(blocks_dev, dtype=jnp.int32)
    pblock = jnp.take_along_axis(sibling_blocks, (positive_slot // BLOCK)[:, None], axis=1)[:, 0]
    positive = pblock * BLOCK + positive_slot % BLOCK
    label_ids = local_ids[:, None] * BLOCK + jnp.arange(BLOCK, dtype=jnp.int32)[None, :]
    chosen_all = jnp.any(sibling_blocks[:, :, None] == local_ids[None, None, :], axis=1)
    piece = lax.all_gather(queries, "lab", axis=0, tiled=True)
    count = piece.shape[0]
    scores = jnp.dot(piece, label_weights.T, preferred_element_type=jnp.float32)
    scores = scores.reshape(count, blocks_dev, BLOCK)
    target = (label_ids[None, :, :] == positive[:, None, None]).astype(jnp.float32)
    slope = jnp.where(chosen_all[:, :, None], jax.nn.sigmoid(scores) - target, 0.0)
    slope = slope.astype(jnp.bfloat16).reshape(count, lab_dev)
    dq_all = jnp.dot(slope, label_weights, preferred_element_type=jnp.float32)
    w_acc = lax.dot_general(
        slope, piece, (((0,), (0,)), ((), ())), preferred_element_type=jnp.float32
    )
    homes = lax.axis_size("lab")
    q_home = qcount // homes
    slots = q_home * K // homes
    touched = jnp.any(chosen_all, axis=1).reshape(homes, q_home)
    send_idx = pack_index(touched, slots, q_home)
    padded = jnp.concatenate(
        [dq_all.reshape(homes, q_home, width), jnp.zeros((homes, 1, width), jnp.float32)], axis=1
    )
    outgoing = jnp.take_along_axis(padded, send_idx[:, :, None], axis=1)
    incoming = lax.all_to_all(outgoing, "lab", split_axis=0, concat_axis=0, tiled=True)
    own_blocks = lax.dynamic_slice_in_dim(sibling_blocks, lax.axis_index("lab") * q_home, q_home, 0)
    source_ids = jnp.arange(homes, dtype=jnp.int32)
    own_touch = jnp.any(
        (own_blocks // blocks_dev)[:, :, None] == source_ids[None, None, :], axis=1
    ).T
    recv_idx = pack_index(own_touch, slots, q_home)
    query_grad = (
        jnp.zeros((q_home + 1, width), jnp.float32)
        .at[recv_idx.reshape(-1)]
        .add(incoming.reshape(-1, width))[:q_home]
    )
    groups = lax.axis_size("pb")
    total = lax.psum(w_acc, "pb")
    weight_grad = (total / groups).astype(jnp.bfloat16)
    return (query_grad, weight_grad)


def swap(value, axis, bit):
    count = lax.axis_size(axis)
    return lax.ppermute(value, axis, [(i, i ^ bit) for i in range(count)])


def local_call(body, outs, args, flops=0, follows=()):
    specs = [
        pl.BlockSpec(memory_space=pltpu.SMEM if arg.dtype == jnp.int32 else pltpu.VMEM)
        for arg in args
    ]
    given, later = len(args), len(args) + len(follows)
    return pl.pallas_call(
        lambda *refs: body(*refs[:given], *refs[later:]),
        out_shape=outs,
        in_specs=specs + [pl.BlockSpec(memory_space=pl.ANY)] * len(follows),
        out_specs=[pl.BlockSpec(memory_space=pltpu.VMEM)] * len(outs),
        cost_estimate=pl.CostEstimate(flops=flops, bytes_accessed=0, transcendentals=0),
        compiler_params=pltpu.CompilerParams(vmem_limit_bytes=VMEM_LIMIT),
    )(*args, *follows)


def like(rows, width, dtype):
    return jax.ShapeDtypeStruct((rows, width), dtype)


def join_body(*refs):
    *came_refs, note_ref, out_ref, noted_ref = refs
    rows = came_refs[0].shape[0]
    for step, ref in enumerate(came_refs):
        out_ref[step * rows : (step + 1) * rows, :] = ref[...]
    half = out_ref.shape[0]
    noted_ref[:half, :] = out_ref[...]
    noted_ref[half:, :] = note_ref[...]


def prep_body(
    me_ref, queries_ref, weights_ref, sibling_ref, slot_ref,
    own_ref, held_ref, note_ref, sibling, slot, sems,
):
    pairs = [(sibling_ref, sibling), (slot_ref, slot), (queries_ref, own_ref), (weights_ref, held_ref)]
    copies = [pltpu.make_async_copy(*pair, sems.at[i]) for i, pair in enumerate(pairs)]
    for copy in copies:
        copy.start()
    for copy in copies[:2]:
        copy.wait()
    me, q_home = me_ref[0], queries_ref.shape[0]
    blocks_dev = weights_ref.shape[0] // BLOCK
    count = slot.shape[1]
    local = sibling[...] - me * blocks_dev
    inside = (local >= 0) & (local < blocks_dev)
    chosen = jnp.max(jnp.where(inside, local, -1), axis=0, keepdims=True)
    steps = lax.broadcasted_iota(jnp.int32, local.shape, 0)
    named = steps == lax.shift_right_logical(slot[...], BLOCK.bit_length() - 1)
    pblock = jnp.sum(jnp.where(named, local, 0), axis=0, keepdims=True)
    place = jnp.where(pblock == chosen, slot[...] & (BLOCK - 1), -1)
    rows = lax.broadcasted_iota(jnp.int32, (NOTE, count), 0)
    code = jnp.where(rows == 0, chosen, jnp.where(rows == 1, place, 0))
    shift, half = q_home.bit_length() - 1, count // 2
    lane = lax.broadcasted_iota(jnp.int32, (count, count), 1)
    source = lax.broadcasted_iota(jnp.int32, (count, count), 0)
    plane = (lane >= half).astype(jnp.int32)
    step = lax.shift_right_logical(lane & (half - 1), shift)
    home = (2 * step + plane) ^ me
    wanted = home * q_home + (lane & (q_home - 1))
    order = jnp.where(source == wanted, 1.0, 0.0).astype(jnp.bfloat16)
    note = jnp.dot(code.astype(jnp.bfloat16), order, preferred_element_type=jnp.float32)
    note_ref[...] = jnp.zeros_like(note_ref)
    note_ref[:, :count] = note.astype(note_ref.dtype)
    for copy in copies[2:]:
        copy.wait()


def prepare(me, queries, weights, sibling, slot):
    return pl.pallas_call(
        prep_body,
        out_shape=[
            like(*queries.shape, queries.dtype),
            like(*weights.shape, weights.dtype),
            like(NOTE, queries.shape[1], jnp.bfloat16),
        ],
        in_specs=[pl.BlockSpec(memory_space=pltpu.SMEM)] + [pl.BlockSpec(memory_space=pl.ANY)] * 4,
        out_specs=[pl.BlockSpec(memory_space=pltpu.VMEM)] * 3,
        scratch_shapes=[
            pltpu.VMEM(sibling.shape, jnp.int32),
            pltpu.VMEM(slot.shape, jnp.int32),
            pltpu.SemaphoreType.DMA((4,)),
        ],
        cost_estimate=pl.CostEstimate(flops=0, bytes_accessed=0, transcendentals=0),
    )(me, queries, weights, sibling, slot)


def slope_of(rows, weights_ref, chosen, place):
    count = rows.shape[0]
    blocks = weights_ref.shape[0] // BLOCK
    scores = lax.dot_general(
        weights_ref[...], rows, (((1,), (1,)), ((), ())), preferred_element_type=jnp.float32
    )
    named = jnp.zeros((BLOCK, count), jnp.float32)
    for block in range(blocks):
        named = jnp.where(chosen == block, scores[block * BLOCK : (block + 1) * BLOCK], named)
    ids = lax.broadcasted_iota(jnp.int32, (BLOCK, count), 0)
    slope = jax.nn.sigmoid(named) - jnp.where(ids == place, 1.0, 0.0)
    parts = [jnp.where(chosen == block, slope, 0.0).astype(jnp.bfloat16) for block in range(blocks)]
    return jnp.concatenate(parts, axis=0)


def read_note(note, first, count):
    code = note[:2, first : first + count].astype(jnp.float32).astype(jnp.int32)
    return code[:1], code[1:]


def grad_terms(first, rows_ref, weights_ref, note_ref, slope_ref):
    rows = rows_ref[...]
    slope = slope_of(rows, weights_ref, *read_note(note_ref[...], first, rows.shape[0]))
    slope_ref[...] = slope
    return lax.dot_general(
        slope, weights_ref[...], (((0,), (0,)), ((), ())), preferred_element_type=jnp.float32
    )


def near_body(place_ref, rows_ref, weights_ref, note_ref, slope_ref, terms_ref):
    dq = grad_terms(0, rows_ref, weights_ref, note_ref, slope_ref).astype(terms_ref.dtype)
    count = terms_ref.shape[1]
    for step in range(terms_ref.shape[0]):
        terms_ref[step ^ place_ref[0]] = dq[step * count : (step + 1) * count]


def far_body(rows_ref, weights_ref, note_ref, slope_ref, *term_refs):
    dq = grad_terms(rows_ref.shape[0], rows_ref, weights_ref, note_ref, slope_ref)
    count = term_refs[0].shape[0]
    for step, ref in enumerate(term_refs):
        ref[...] = dq[step * count : (step + 1) * count].astype(ref.dtype)


def sum_body(near_ref, *refs):
    *term_refs, out_ref, mark_ref = refs
    mark_ref[...] = jnp.zeros_like(mark_ref)
    total = near_ref[0].astype(jnp.float32)
    for step in range(1, near_ref.shape[0]):
        total = total + near_ref[step].astype(jnp.float32)
    for ref in term_refs:
        total = total + ref[...].astype(jnp.float32)
    out_ref[...] = total


def slopes_of_set(near_rows, far_rows, note, weights_ref):
    rows = jnp.concatenate([near_rows, far_rows], axis=0)
    return rows, slope_of(rows, weights_ref, *read_note(note, 0, rows.shape[0]))


def own_body(near_ref, far_ref, near_slope_ref, far_slope_ref, acc_ref):
    rows = jnp.concatenate([near_ref[...], far_ref[...]], axis=0)
    slope = jnp.concatenate([near_slope_ref[...], far_slope_ref[...]], axis=1)
    acc_ref[...] = jnp.dot(slope, rows, preferred_element_type=jnp.float32)


def pack_body(own_near_ref, own_far_ref, near_ref, far_ref, out_ref):
    start = 0
    for ref in (own_near_ref, own_far_ref, near_ref, far_ref):
        out_ref[start : start + ref.shape[0], :] = ref[...]
        start += ref.shape[0]


def add_set(acc_ref, weights_ref, set_ref, start):
    half = (set_ref.shape[0] // 2 - NOTE) // 2
    middle = start + half + NOTE
    rows, slope = slopes_of_set(
        set_ref[start : start + half, :],
        set_ref[middle : middle + half, :],
        set_ref[start + half : middle, :],
        weights_ref,
    )
    return acc_ref[...] + jnp.dot(slope, rows, preferred_element_type=jnp.float32)


def add_body(start, set_ref, weights_ref, acc_ref, out_ref):
    out_ref[...] = add_set(acc_ref, weights_ref, set_ref, start)


def late_body(groups, start, set_ref, weights_ref, acc_ref, out_ref):
    total = add_set(acc_ref, weights_ref, set_ref, start)
    out_ref[...] = (total / groups).astype(out_ref.dtype)


def dense_shards(queries, label_weights, sibling_blocks, positive_slot):
    q_home, width = queries.shape
    qcount = sibling_blocks.shape[0]
    half = qcount // 2
    lab_dev = label_weights.shape[0]
    homes = lax.axis_size("lab")
    groups = lax.axis_size("pb")
    f32, bf16 = jnp.float32, jnp.bfloat16
    far_bit = groups // 2
    me = jnp.reshape(lax.axis_index("lab"), (1,)).astype(jnp.int32)
    came = [swap(queries, "lab", step) for step in range(2, homes, 2)]
    held, weights, note = prepare(
        me, queries, label_weights, sibling_blocks.T, positive_slot.reshape(1, qcount)
    )
    near, noted = local_call(
        join_body, [like(half, width, bf16), like(half + NOTE, width, bf16)], [held, *came, note]
    )
    far = swap(near, "lab", 1)
    cross_near = swap(noted, "pb", far_bit)
    work = 4 * half * lab_dev * width
    slope = like(lab_dev, half, bf16)
    near_slope, near_dq = local_call(
        near_body,
        [slope, jax.ShapeDtypeStruct((homes // 2, q_home, width), bf16)],
        [me // 2, near, weights, note],
        work,
    )
    planes = [list(range(plane, homes, 2)) for plane in range(2)]
    near_terms = lax.all_to_all(
        near_dq, "lab", split_axis=0, concat_axis=0, axis_index_groups=planes, tiled=True
    )
    cross_far = swap(far, "pb", far_bit)
    far_slope, *far_terms = local_call(
        far_body,
        [slope] + [like(q_home, width, bf16)] * (homes // 2),
        [far, weights, note],
        work,
        [near_dq],
    )
    terms = [swap(out, "lab", 2 * step + 1) for step, out in enumerate(far_terms)]
    acc = local_call(
        own_body, [like(lab_dev, width, f32)], [near, far, near_slope, far_slope], work
    )[0]
    span = qcount + NOTE
    pack = local_call(
        pack_body, [like(2 * span, width, bf16)], [noted, far, cross_near, cross_far], 0, [acc]
    )[0]
    mate = swap(pack, "pb", 1)
    grown = like(lab_dev, width, f32)
    acc = local_call(
        lambda *refs: add_body(span, *refs), [grown], [pack, weights, acc], 100 * work
    )[0]
    acc = local_call(
        lambda *refs: add_body(0, *refs), [grown], [mate, weights, acc], 2 * work
    )[0]
    query_grad, mark = local_call(
        sum_body,
        [like(q_home, width, f32), like(1, BLOCK, jnp.int32)],
        [near_terms, *terms],
        0,
        [acc],
    )
    weight_grad = local_call(
        lambda *refs: late_body(groups, span, *refs),
        [like(lab_dev, width, bf16)],
        [mate, weights, acc],
        2 * work,
        [mark],
    )[0]
    return (query_grad, weight_grad)


def solution(mesh):
    groups, homes = mesh.shape["pb"], mesh.shape["lab"]

    def shards(queries, label_weights, sibling_blocks, positive_slot):
        every_row_everywhere = homes == K
        few = groups * sibling_blocks.shape[0] <= 2 * label_weights.shape[0]
        paired = groups == 4 and homes & (homes - 1) == 0
        one_block = label_weights.shape[0] // BLOCK <= K
        plan = dense_shards if every_row_everywhere and few and paired and one_block else sparse_shards
        return plan(queries, label_weights, sibling_blocks, positive_slot)

    in_specs = (P(("pb", "lab"), None), P("lab", None), P("pb", None), P("pb"))
    out_specs = (P(("pb", "lab"), None), P("lab", None))
    return jax.shard_map(shards, mesh=mesh, in_specs=in_specs, out_specs=out_specs, check_vma=False)
```

```python
import jax
import jax.numpy as jnp
from jax import lax
from jax.experimental import pallas as pl
from jax.experimental.pallas import tpu as pltpu
from jax.sharding import PartitionSpec as P

BLOCK = 128
K = 8
NOTE = 16
VMEM_LIMIT = 24 * 1024 * 1024


def pack_index(touched, width_slots, fill_value):
    homes, count = touched.shape
    rank = jnp.cumsum(touched.astype(jnp.int32), axis=1) - 1
    place = jnp.where(touched, rank, width_slots)
    home_ids = jnp.broadcast_to(jnp.arange(homes, dtype=jnp.int32)[:, None], touched.shape)
    row_ids = jnp.broadcast_to(jnp.arange(count, dtype=jnp.int32)[None, :], touched.shape)
    table = (
        jnp.full((homes, width_slots + 1), fill_value, jnp.int32).at[home_ids, place].set(row_ids)
    )
    return table[:, :width_slots]


def sparse_shards(queries, label_weights, sibling_blocks, positive_slot):
    width = queries.shape[1]
    qcount = sibling_blocks.shape[0]
    lab_dev = label_weights.shape[0]
    blocks_dev = lab_dev // BLOCK
    first = lax.axis_index("lab") * blocks_dev
    local_ids = first + jnp.arange(blocks_dev, dtype=jnp.int32)
    pblock = jnp.take_along_axis(sibling_blocks, (positive_slot // BLOCK)[:, None], axis=1)[:, 0]
    positive = pblock * BLOCK + positive_slot % BLOCK
    label_ids = local_ids[:, None] * BLOCK + jnp.arange(BLOCK, dtype=jnp.int32)[None, :]
    chosen_all = jnp.any(sibling_blocks[:, :, None] == local_ids[None, None, :], axis=1)
    piece = lax.all_gather(queries, "lab", axis=0, tiled=True)
    count = piece.shape[0]
    scores = jnp.dot(piece, label_weights.T, preferred_element_type=jnp.float32)
    scores = scores.reshape(count, blocks_dev, BLOCK)
    target = (label_ids[None, :, :] == positive[:, None, None]).astype(jnp.float32)
    slope = jnp.where(chosen_all[:, :, None], jax.nn.sigmoid(scores) - target, 0.0)
    slope = slope.astype(jnp.bfloat16).reshape(count, lab_dev)
    dq_all = jnp.dot(slope, label_weights, preferred_element_type=jnp.float32)
    w_acc = lax.dot_general(
        slope, piece, (((0,), (0,)), ((), ())), preferred_element_type=jnp.float32
    )
    homes = lax.axis_size("lab")
    q_home = qcount // homes
    slots = q_home * K // homes
    touched = jnp.any(chosen_all, axis=1).reshape(homes, q_home)
    send_idx = pack_index(touched, slots, q_home)
    padded = jnp.concatenate(
        [dq_all.reshape(homes, q_home, width), jnp.zeros((homes, 1, width), jnp.float32)], axis=1
    )
    outgoing = jnp.take_along_axis(padded, send_idx[:, :, None], axis=1)
    incoming = lax.all_to_all(outgoing, "lab", split_axis=0, concat_axis=0, tiled=True)
    own_blocks = lax.dynamic_slice_in_dim(sibling_blocks, lax.axis_index("lab") * q_home, q_home, 0)
    source_ids = jnp.arange(homes, dtype=jnp.int32)
    own_touch = jnp.any(
        (own_blocks // blocks_dev)[:, :, None] == source_ids[None, None, :], axis=1
    ).T
    recv_idx = pack_index(own_touch, slots, q_home)
    query_grad = (
        jnp.zeros((q_home + 1, width), jnp.float32)
        .at[recv_idx.reshape(-1)]
        .add(incoming.reshape(-1, width))[:q_home]
    )
    groups = lax.axis_size("pb")
    total = lax.psum(w_acc, "pb")
    weight_grad = (total / groups).astype(jnp.bfloat16)
    return (query_grad, weight_grad)


def swap(value, axis, bit):
    count = lax.axis_size(axis)
    return lax.ppermute(value, axis, [(i, i ^ bit) for i in range(count)])


def local_call(body, outs, args, flops=0, follows=()):
    specs = [
        pl.BlockSpec(memory_space=pltpu.SMEM if arg.dtype == jnp.int32 else pltpu.VMEM)
        for arg in args
    ]
    given, later = len(args), len(args) + len(follows)
    return pl.pallas_call(
        lambda *refs: body(*refs[:given], *refs[later:]),
        out_shape=outs,
        in_specs=specs + [pl.BlockSpec(memory_space=pl.ANY)] * len(follows),
        out_specs=[pl.BlockSpec(memory_space=pltpu.VMEM)] * len(outs),
        cost_estimate=pl.CostEstimate(flops=flops, bytes_accessed=0, transcendentals=0),
        compiler_params=pltpu.CompilerParams(vmem_limit_bytes=VMEM_LIMIT),
    )(*args, *follows)


def like(rows, width, dtype):
    return jax.ShapeDtypeStruct((rows, width), dtype)


def stack_body(*refs):
    *came_refs, out_ref = refs
    start = 0
    for ref in came_refs:
        out_ref[start : start + ref.shape[0], : ref.shape[1]] = ref[...]
        start += ref.shape[0]


def grad_body(near_ref, far_ref, weights_ref, note_ref, kept_ref, slope_ref, *term_refs):
    rows = jnp.concatenate([near_ref[...], far_ref[...]], axis=0)
    weights = weights_ref[...]
    count, blocks = rows.shape[0], weights.shape[0] // BLOCK
    code = note_ref[:2, :count].astype(jnp.float32).astype(jnp.int32)
    chosen, place = code[:1], code[1:]
    scores = lax.dot_general(
        weights, rows, (((1,), (1,)), ((), ())), preferred_element_type=jnp.float32
    )
    named = jnp.zeros((BLOCK, count), jnp.float32)
    for block in range(blocks):
        named = jnp.where(chosen == block, scores[block * BLOCK : (block + 1) * BLOCK], named)
    ids = lax.broadcasted_iota(jnp.int32, (BLOCK, count), 0)
    slope = (jax.nn.sigmoid(named) - jnp.where(ids == place, 1.0, 0.0)).astype(jnp.bfloat16)
    slope_ref[:BLOCK, :] = slope
    slope_ref[BLOCK:, :] = note_ref[:, :count]
    dq = lax.dot_general(
        spread(slope, chosen, range(blocks)),
        weights,
        (((0,), (0,)), ((), ())),
        preferred_element_type=jnp.float32,
    )
    q_home = kept_ref.shape[0]
    kept_ref[...] = dq[:q_home]
    half = count // q_home // 2
    for step, ref in enumerate(term_refs, 1):
        start = (step // 2 + (step % 2) * half) * q_home
        ref[...] = dq[start : start + q_home].astype(ref.dtype)


def spread(slope, chosen, blocks):
    wide = slope.astype(jnp.float32)
    parts = [jnp.where(chosen == block, wide, 0.0).astype(slope.dtype) for block in blocks]
    return jnp.concatenate(parts, axis=0)


def read_slope(slope):
    chosen = slope[BLOCK : BLOCK + 1].astype(jnp.float32).astype(jnp.int32)
    return slope[:BLOCK], chosen


def own_body(near_ref, far_ref, slope_ref, acc_ref):
    rows = jnp.concatenate([near_ref[...], far_ref[...]], axis=0)
    wide = spread(*read_slope(slope_ref[...]), range(acc_ref.shape[0] // BLOCK))
    acc_ref[...] = jnp.dot(wide, rows, preferred_element_type=jnp.float32)


def add_body(near_ref, far_ref, slope_ref, acc_ref, out_ref):
    own_body(near_ref, far_ref, slope_ref, out_ref)
    out_ref[...] += acc_ref[...]


def late_body(groups, set_ref, acc_ref, out_ref, held, sems):
    count = set_ref.shape[0] - BLOCK - NOTE
    rows = set_ref[:count, :]
    slope, chosen = read_slope(set_ref[count:, :count])
    blocks = acc_ref.shape[0] // BLOCK
    chunk = blocks // sems.shape[0]
    copies = []
    for part in range(sems.shape[0]):
        here = pl.ds(part * chunk * BLOCK, chunk * BLOCK)
        wide = spread(slope, chosen, range(part * chunk, (part + 1) * chunk))
        total = acc_ref[here, :] + jnp.dot(wide, rows, preferred_element_type=jnp.float32)
        held[here, :] = (total / groups).astype(held.dtype)
        copy = pltpu.make_async_copy(held.at[here, :], out_ref.at[here, :], sems.at[part])
        copy.start()
        copies.append(copy)
    for copy in copies:
        copy.wait()


def late(groups, swapped, acc, mark):
    lab_dev, width = acc.shape
    out = like(lab_dev, width, swapped.dtype)
    chunks = 4
    return pl.pallas_call(
        lambda set_ref, acc_ref, mark_ref, *refs: late_body(groups, set_ref, acc_ref, *refs),
        out_shape=out,
        in_specs=[pl.BlockSpec(memory_space=pltpu.VMEM)] * 2 + [pl.BlockSpec(memory_space=pl.ANY)],
        out_specs=pl.BlockSpec(memory_space=pl.ANY),
        scratch_shapes=[pltpu.VMEM(out.shape, out.dtype), pltpu.SemaphoreType.DMA((chunks,))],
        cost_estimate=pl.CostEstimate(flops=0, bytes_accessed=0, transcendentals=0),
        compiler_params=pltpu.CompilerParams(vmem_limit_bytes=VMEM_LIMIT),
    )(swapped, acc, mark)


def sum_body(kept_ref, *refs):
    *term_refs, out_ref, mark_ref = refs
    mark_ref[...] = jnp.zeros_like(mark_ref)
    total = kept_ref[...]
    for ref in term_refs:
        total = total + ref[...].astype(jnp.float32)
    out_ref[...] = total


def make_note(sibling_blocks, positive_slot, blocks_dev, homes, width):
    me = lax.axis_index("lab")
    local = sibling_blocks.T - me * blocks_dev
    inside = (local >= 0) & (local < blocks_dev)
    chosen = jnp.max(jnp.where(inside, local, -1), axis=0)
    steps = jnp.arange(local.shape[0], dtype=jnp.int32)[:, None]
    pblock = jnp.sum(jnp.where(steps == (positive_slot // BLOCK)[None, :], local, 0), axis=0)
    place = jnp.where(pblock == chosen, positive_slot % BLOCK, -1)
    code = jnp.stack([chosen, place]).astype(jnp.bfloat16)
    return jnp.pad(code, ((0, NOTE - 2), (0, width - code.shape[1])))


def order_body(me_ref, note_ref, q_home_ref, out_ref):
    q_home, count = q_home_ref.shape[0], note_ref.shape[1]
    half = count // 2
    lane = lax.broadcasted_iota(jnp.int32, (count, count), 1)
    source = lax.broadcasted_iota(jnp.int32, (count, count), 0)
    plane = (lane >= half).astype(jnp.int32)
    step = lax.shift_right_logical(lane & (half - 1), q_home.bit_length() - 1)
    wanted = ((2 * step + plane) ^ me_ref[0]) * q_home + (lane & (q_home - 1))
    order = jnp.where(source == wanted, 1.0, 0.0).astype(jnp.bfloat16)
    note = jnp.dot(note_ref[...], order, preferred_element_type=jnp.float32)
    out_ref[...] = note.astype(out_ref.dtype)


def hold_body(rows_ref, held_ref):
    held_ref[...] = rows_ref[...]


def dense_shards(queries, label_weights, sibling_blocks, positive_slot):
    q_home, width = queries.shape
    qcount = sibling_blocks.shape[0]
    half = qcount // 2
    lab_dev = label_weights.shape[0]
    homes = lax.axis_size("lab")
    groups = lax.axis_size("pb")
    f32, bf16 = jnp.float32, jnp.bfloat16
    cross = groups // 2
    me = jnp.reshape(lax.axis_index("lab"), (1,)).astype(jnp.int32)
    came = {step: swap(queries, "lab", step) for step in range(2, homes, 2)}
    came.update({step: swap(queries, "lab", step) for step in range(homes - 1, 0, -2)})
    held = local_call(hold_body, [like(q_home, width, bf16)], [queries])[0]
    note = make_note(sibling_blocks, positive_slot, lab_dev // BLOCK, homes, qcount)
    note = local_call(order_body, [like(NOTE, qcount, bf16)], [me, note, held])[0]
    near = [held] + [came[step] for step in range(2, homes, 2)]
    near = local_call(stack_body, [like(half, width, bf16)], near)[0]
    far = [came[step] for step in range(1, homes, 2)]
    far = local_call(stack_body, [like(half, width, bf16)], far, 0, [near])[0]
    work = 4 * half * lab_dev * width
    slope_like = like(BLOCK + NOTE, qcount, bf16)
    kept, slope, *terms = local_call(
        grad_body,
        [like(q_home, width, f32), slope_like] + [like(q_home, width, bf16)] * (homes - 1),
        [near, far, label_weights, note],
        2 * work,
    )
    terms = {step: swap(term, "lab", step) for step, term in enumerate(terms, 1)}
    cross_near, cross_far = swap(near, "pb", cross), swap(far, "pb", cross)
    cross_slope = swap(slope, "pb", cross)
    grown = like(lab_dev, width, f32)
    acc = local_call(own_body, [grown], [near, far, slope], 10 * work, [cross_near])[0]
    part = local_call(
        sum_part_body,
        [like(q_home, width, f32)],
        [kept] + [terms[step] for step in range(2, homes, 2)],
        0,
        [acc],
    )[0]
    pack = local_call(
        pack_body,
        [like(2 * qcount + BLOCK + NOTE, width, bf16)],
        [slope, cross_slope, near, far, cross_near, cross_far],
        0,
        [part],
    )[0]
    mate = swap(pack, "pb", 1)
    acc = local_call(
        add_body, [grown], [cross_near, cross_far, cross_slope, acc], 100 * work, [part]
    )[0]
    query_grad, mark = local_call(
        sum_body,
        [like(q_home, width, f32), like(1, BLOCK, jnp.int32)],
        [part] + [terms[step] for step in range(1, homes, 2)],
        0,
        [acc],
    )
    weight_grad = late(groups, mate, acc, mark)
    return (query_grad, weight_grad)


def pack_body(slope_ref, came_ref, *refs):
    *rows_refs, out_ref = refs
    stack_body(*rows_refs, out_ref)
    start, count = out_ref.shape[0] - slope_ref.shape[0], slope_ref.shape[1]
    out_ref[start:, :count] = slope_ref[...]
    out_ref[start:, count : 2 * count] = came_ref[...]


def sum_part_body(kept_ref, *refs):
    *term_refs, out_ref = refs
    total = kept_ref[...]
    for ref in term_refs:
        total = total + ref[...].astype(jnp.float32)
    out_ref[...] = total


def solution(mesh):
    groups, homes = mesh.shape["pb"], mesh.shape["lab"]

    def shards(queries, label_weights, sibling_blocks, positive_slot):
        every_row_everywhere = homes == K
        few = groups * sibling_blocks.shape[0] <= 2 * label_weights.shape[0]
        paired = groups == 4 and homes & (homes - 1) == 0
        one_block = label_weights.shape[0] // BLOCK <= K
        plan = dense_shards if every_row_everywhere and few and paired and one_block else sparse_shards
        return plan(queries, label_weights, sibling_blocks, positive_slot)

    in_specs = (P(("pb", "lab"), None), P("lab", None), P("pb", None), P("pb"))
    out_specs = (P(("pb", "lab"), None), P("lab", None))
    return jax.shard_map(shards, mesh=mesh, in_specs=in_specs, out_specs=out_specs, check_vma=False)
```

```python
import jax
import jax.numpy as jnp
from jax import lax
from jax.experimental import pallas as pl
from jax.experimental.pallas import tpu as pltpu
from jax.sharding import PartitionSpec as P

BLOCK = 128
K = 8
NOTE = 16
VMEM_LIMIT = 24 * 1024 * 1024


def pack_index(touched, width_slots, fill_value):
    homes, count = touched.shape
    rank = jnp.cumsum(touched.astype(jnp.int32), axis=1) - 1
    place = jnp.where(touched, rank, width_slots)
    home_ids = jnp.broadcast_to(jnp.arange(homes, dtype=jnp.int32)[:, None], touched.shape)
    row_ids = jnp.broadcast_to(jnp.arange(count, dtype=jnp.int32)[None, :], touched.shape)
    table = (
        jnp.full((homes, width_slots + 1), fill_value, jnp.int32).at[home_ids, place].set(row_ids)
    )
    return table[:, :width_slots]


def sparse_shards(queries, label_weights, sibling_blocks, positive_slot):
    width = queries.shape[1]
    qcount = sibling_blocks.shape[0]
    lab_dev = label_weights.shape[0]
    blocks_dev = lab_dev // BLOCK
    first = lax.axis_index("lab") * blocks_dev
    local_ids = first + jnp.arange(blocks_dev, dtype=jnp.int32)
    pblock = jnp.take_along_axis(sibling_blocks, (positive_slot // BLOCK)[:, None], axis=1)[:, 0]
    positive = pblock * BLOCK + positive_slot % BLOCK
    label_ids = local_ids[:, None] * BLOCK + jnp.arange(BLOCK, dtype=jnp.int32)[None, :]
    chosen_all = jnp.any(sibling_blocks[:, :, None] == local_ids[None, None, :], axis=1)
    piece = lax.all_gather(queries, "lab", axis=0, tiled=True)
    count = piece.shape[0]
    scores = jnp.dot(piece, label_weights.T, preferred_element_type=jnp.float32)
    scores = scores.reshape(count, blocks_dev, BLOCK)
    target = (label_ids[None, :, :] == positive[:, None, None]).astype(jnp.float32)
    slope = jnp.where(chosen_all[:, :, None], jax.nn.sigmoid(scores) - target, 0.0)
    slope = slope.astype(jnp.bfloat16).reshape(count, lab_dev)
    dq_all = jnp.dot(slope, label_weights, preferred_element_type=jnp.float32)
    w_acc = lax.dot_general(
        slope, piece, (((0,), (0,)), ((), ())), preferred_element_type=jnp.float32
    )
    homes = lax.axis_size("lab")
    q_home = qcount // homes
    slots = q_home * K // homes
    touched = jnp.any(chosen_all, axis=1).reshape(homes, q_home)
    send_idx = pack_index(touched, slots, q_home)
    padded = jnp.concatenate(
        [dq_all.reshape(homes, q_home, width), jnp.zeros((homes, 1, width), jnp.float32)], axis=1
    )
    outgoing = jnp.take_along_axis(padded, send_idx[:, :, None], axis=1)
    incoming = lax.all_to_all(outgoing, "lab", split_axis=0, concat_axis=0, tiled=True)
    own_blocks = lax.dynamic_slice_in_dim(sibling_blocks, lax.axis_index("lab") * q_home, q_home, 0)
    source_ids = jnp.arange(homes, dtype=jnp.int32)
    own_touch = jnp.any(
        (own_blocks // blocks_dev)[:, :, None] == source_ids[None, None, :], axis=1
    ).T
    recv_idx = pack_index(own_touch, slots, q_home)
    query_grad = (
        jnp.zeros((q_home + 1, width), jnp.float32)
        .at[recv_idx.reshape(-1)]
        .add(incoming.reshape(-1, width))[:q_home]
    )
    groups = lax.axis_size("pb")
    total = lax.psum(w_acc, "pb")
    weight_grad = (total / groups).astype(jnp.bfloat16)
    return (query_grad, weight_grad)


def swap(value, axis, bit):
    count = lax.axis_size(axis)
    return lax.ppermute(value, axis, [(i, i ^ bit) for i in range(count)])


def diagonal(value, group_bit, home_bit):
    groups, homes = lax.axis_size("pb"), lax.axis_size("lab")
    pairs = [
        (g * homes + h, (g ^ group_bit) * homes + (h ^ home_bit))
        for g in range(groups)
        for h in range(homes)
    ]
    return lax.ppermute(value, ("pb", "lab"), pairs)


def local_call(body, outs, args, flops=0, follows=()):
    specs = [
        pl.BlockSpec(memory_space=pltpu.SMEM if arg.dtype == jnp.int32 else pltpu.VMEM)
        for arg in args
    ]
    given, later = len(args), len(args) + len(follows)
    return pl.pallas_call(
        lambda *refs: body(*refs[:given], *refs[later:]),
        out_shape=outs,
        in_specs=specs + [pl.BlockSpec(memory_space=pl.ANY)] * len(follows),
        out_specs=[pl.BlockSpec(memory_space=pltpu.VMEM)] * len(outs),
        cost_estimate=pl.CostEstimate(flops=flops, bytes_accessed=0, transcendentals=0),
        compiler_params=pltpu.CompilerParams(vmem_limit_bytes=VMEM_LIMIT),
    )(*args, *follows)


def like(rows, width, dtype):
    return jax.ShapeDtypeStruct((rows, width), dtype)


def join_body(place_ref, own_ref, *refs):
    *came_refs, note_ref, out_ref, noted_ref = refs
    rows, place = own_ref.shape[0], place_ref[0]
    for step, ref in enumerate([own_ref, *came_refs]):
        start = pl.multiple_of((place ^ step) * rows, rows)
        out_ref[pl.ds(start, rows), :] = ref[...]
    half = out_ref.shape[0]
    noted_ref[:half, :] = out_ref[...]
    noted_ref[half:, :] = note_ref[...]


def hold_body(rows_ref, held_ref):
    held_ref[...] = rows_ref[...]


def slope_of(rows, weights, chosen, place):
    count, blocks = rows.shape[0], weights.shape[0] // BLOCK
    scores = lax.dot_general(
        weights, rows, (((1,), (1,)), ((), ())), preferred_element_type=jnp.float32
    )
    named = jnp.zeros((BLOCK, count), jnp.float32)
    for block in range(blocks):
        named = jnp.where(chosen == block, scores[block * BLOCK : (block + 1) * BLOCK], named)
    ids = lax.broadcasted_iota(jnp.int32, (BLOCK, count), 0)
    return (jax.nn.sigmoid(named) - jnp.where(ids == place, 1.0, 0.0)).astype(jnp.bfloat16)


def spread(slope, chosen, blocks):
    wide = slope.astype(jnp.float32)
    parts = [jnp.where(chosen == block, wide, 0.0).astype(slope.dtype) for block in blocks]
    return jnp.concatenate(parts, axis=0)


def read_note(note, which, count):
    chosen = note[2 * which : 2 * which + 1, :count].astype(jnp.int32)
    place = note[2 * which + 1 : 2 * which + 2, :count].astype(jnp.int32)
    return chosen, place


def grad_body(which, rows_ref, weights_ref, note_ref, dq_ref, slope_ref):
    rows, weights = rows_ref[...], weights_ref[...]
    note = note_ref[...].astype(jnp.float32)
    chosen, place = read_note(note, which, rows.shape[0])
    slope = slope_of(rows, weights, chosen, place)
    slope_ref[:BLOCK, :] = slope
    slope_ref[BLOCK:, :] = jnp.broadcast_to(chosen, (NOTE, rows.shape[0])).astype(slope.dtype)
    dq = lax.dot_general(
        spread(slope, chosen, range(weights.shape[0] // BLOCK)),
        weights,
        (((0,), (0,)), ((), ())),
        preferred_element_type=jnp.float32,
    )
    dq_ref[...] = dq.astype(dq_ref.dtype)


def near_body(rows_ref, weights_ref, note_ref, dq_ref, slope_ref, held_ref, copy_ref):
    held_ref[...] = weights_ref[...]
    copy_ref[...] = rows_ref[...]
    grad_body(0, rows_ref, weights_ref, note_ref, dq_ref, slope_ref)


def far_body(rows_ref, weights_ref, note_ref, dq_ref, slope_ref):
    grad_body(1, rows_ref, weights_ref, note_ref, dq_ref, slope_ref)


def order_body(side_ref, near_ref, far_ref, out_ref):
    side, q_home = side_ref[0], out_ref.shape[1]
    for z in range(out_ref.shape[0] // 2):
        part = slice(z * q_home, (z + 1) * q_home)
        out_ref[2 * z + side] = near_ref[part, :]
        out_ref[2 * z + 1 - side] = far_ref[part, :]


def sum_body(terms_ref, out_ref):
    total = terms_ref[0].astype(jnp.float32)
    for source in range(1, terms_ref.shape[0]):
        total = total + terms_ref[source].astype(jnp.float32)
    out_ref[...] = total


def stack_body(*refs):
    *came_refs, out_ref = refs
    start = 0
    for ref in came_refs:
        out_ref[start : start + ref.shape[0], : ref.shape[1]] = ref[...]
        start += ref.shape[0]


def read_slope(slope):
    chosen = slope[BLOCK : BLOCK + 1].astype(jnp.float32).astype(jnp.int32)
    return slope[:BLOCK], chosen


def own_body(near_ref, far_ref, near_slope_ref, far_slope_ref, acc_ref, set_ref):
    rows = jnp.concatenate([near_ref[...], far_ref[...]], axis=0)
    slope = jnp.concatenate([near_slope_ref[...], far_slope_ref[...]], axis=1)
    count = rows.shape[0]
    set_ref[:count, :] = rows
    set_ref[count:, :count] = slope
    wide = spread(*read_slope(slope), range(acc_ref.shape[0] // BLOCK))
    acc_ref[...] = jnp.dot(wide, rows, preferred_element_type=jnp.float32)


def mate_body(set_ref, acc_ref, out_ref):
    count = set_ref.shape[0] - BLOCK - NOTE
    slope, chosen = read_slope(set_ref[count:, :count])
    wide = spread(slope, chosen, range(acc_ref.shape[0] // BLOCK))
    out_ref[...] = acc_ref[...] + jnp.dot(
        wide, set_ref[:count, :], preferred_element_type=jnp.float32
    )


def set_slope(set_ref, weights):
    half = (set_ref.shape[0] - NOTE) // 2
    rows = jnp.concatenate([set_ref[:half, :], set_ref[half + NOTE :, :]], axis=0)
    note = set_ref[half : half + NOTE, :].astype(jnp.float32)
    codes = [read_note(note, which, half) for which in range(2)]
    chosen = jnp.concatenate([codes[0][0], codes[1][0]], axis=1)
    place = jnp.concatenate([codes[0][1], codes[1][1]], axis=1)
    return rows, slope_of(rows, weights, chosen, place), chosen


def cross_body(set_ref, weights_ref, acc_ref, out_ref):
    rows, slope, chosen = set_slope(set_ref, weights_ref[...])
    wide = spread(slope, chosen, range(acc_ref.shape[0] // BLOCK))
    out_ref[...] = acc_ref[...] + jnp.dot(wide, rows, preferred_element_type=jnp.float32)


def late_body(groups, set_ref, weights_ref, acc_ref, out_ref, mark_ref, held, sems):
    mark_ref[...] = jnp.zeros_like(mark_ref)
    rows, slope, chosen = set_slope(set_ref, weights_ref[...])
    blocks = acc_ref.shape[0] // BLOCK
    chunk = blocks // sems.shape[0]
    copies = []
    for part in range(sems.shape[0]):
        here = pl.ds(part * chunk * BLOCK, chunk * BLOCK)
        wide = spread(slope, chosen, range(part * chunk, (part + 1) * chunk))
        total = acc_ref[here, :] + jnp.dot(wide, rows, preferred_element_type=jnp.float32)
        held[here, :] = (total / groups).astype(held.dtype)
        copy = pltpu.make_async_copy(held.at[here, :], out_ref.at[here, :], sems.at[part])
        copy.start()
        copies.append(copy)
    for copy in copies:
        copy.wait()


def late(groups, crossed, weights, acc):
    out = like(*weights.shape, weights.dtype)
    chunks = 4
    return pl.pallas_call(
        lambda *refs: late_body(groups, *refs),
        out_shape=[out, like(1, BLOCK, jnp.int32)],
        in_specs=[pl.BlockSpec(memory_space=pltpu.VMEM)] * 3,
        out_specs=[pl.BlockSpec(memory_space=pl.ANY), pl.BlockSpec(memory_space=pltpu.VMEM)],
        scratch_shapes=[pltpu.VMEM(out.shape, out.dtype), pltpu.SemaphoreType.DMA((chunks,))],
        cost_estimate=pl.CostEstimate(flops=0, bytes_accessed=0, transcendentals=0),
        compiler_params=pltpu.CompilerParams(vmem_limit_bytes=VMEM_LIMIT),
    )(crossed, weights, acc)


def make_note(sibling_blocks, positive_slot, blocks_dev, homes, width):
    me = lax.axis_index("lab")
    local = sibling_blocks.T - me * blocks_dev
    inside = (local >= 0) & (local < blocks_dev)
    chosen = jnp.max(jnp.where(inside, local, -1), axis=0)
    steps = jnp.arange(local.shape[0], dtype=jnp.int32)[:, None]
    pblock = jnp.sum(jnp.where(steps == (positive_slot // BLOCK)[None, :], local, 0), axis=0)
    place = jnp.where(pblock == chosen, positive_slot % BLOCK, -1)
    code = jnp.stack([chosen, place]).astype(jnp.bfloat16)
    code = code.reshape(2, homes // 2, 2, -1).transpose(2, 0, 1, 3).reshape(2, 2, -1)
    code = jnp.where(me % 2 == 0, code, code[::-1]).reshape(4, -1)
    return jnp.pad(code, ((0, NOTE - 4), (0, width - code.shape[1])))


def dense_shards(queries, label_weights, sibling_blocks, positive_slot):
    q_home, width = queries.shape
    qcount = sibling_blocks.shape[0]
    half = qcount // 2
    lab_dev = label_weights.shape[0]
    homes = lax.axis_size("lab")
    groups = lax.axis_size("pb")
    me = lax.axis_index("lab")
    f32, bf16 = jnp.float32, jnp.bfloat16

    place = jnp.reshape(me // 2, (1,)).astype(jnp.int32)
    side = jnp.reshape(me % 2, (1,)).astype(jnp.int32)
    far_bit = groups // 2
    came = [swap(queries, "lab", 2 * step) for step in range(1, homes // 2)]
    held = local_call(hold_body, [like(q_home, width, bf16)], [queries])[0]
    note = make_note(sibling_blocks, positive_slot, lab_dev // BLOCK, homes, width)
    near, noted = local_call(
        join_body,
        [like(half, width, bf16), like(half + NOTE, width, bf16)],
        [place, held, *came, note],
    )
    far = swap(near, "lab", 1)
    work = 4 * half * lab_dev * width
    slope_like = like(BLOCK + NOTE, half, bf16)
    near_dq, near_slope, weights, near_copy = local_call(
        near_body,
        [like(half, width, bf16), slope_like, like(lab_dev, width, bf16), like(half, width, bf16)],
        [near, label_weights, note],
        work,
    )
    cross_near = swap(noted, "pb", far_bit)
    cross_far = diagonal(near_copy, far_bit, 1)
    far_dq, far_slope = local_call(
        far_body,
        [like(half, width, bf16), slope_like],
        [far, weights, note],
        work,
        [near_dq],
    )
    dq = local_call(
        order_body, [jax.ShapeDtypeStruct((homes, q_home, width), bf16)], [side, near_dq, far_dq]
    )[0]
    terms = lax.all_to_all(dq, "lab", split_axis=0, concat_axis=0, tiled=True)
    acc, own = local_call(
        own_body,
        [like(lab_dev, width, f32), like(qcount + BLOCK + NOTE, width, bf16)],
        [near, far, near_slope, far_slope],
        work,
        [dq],
    )
    mate = swap(own, "pb", 1)
    cross = local_call(
        stack_body, [like(qcount + NOTE, width, bf16)], [cross_near, cross_far], 0, [acc]
    )[0]
    cross_mate = swap(cross, "pb", 1)
    grown = like(lab_dev, width, f32)
    acc = local_call(mate_body, [grown], [mate, acc], work, [cross])[0]
    acc = local_call(cross_body, [grown], [cross, weights, acc], 2 * work)[0]
    weight_grad, mark = late(groups, cross_mate, weights, acc)
    query_grad = local_call(sum_body, [like(q_home, width, f32)], [terms], 0, [mark])[0]
    return (query_grad, weight_grad)


def solution(mesh):
    groups, homes = mesh.shape["pb"], mesh.shape["lab"]

    def shards(queries, label_weights, sibling_blocks, positive_slot):
        every_row_everywhere = homes == K
        few = groups * sibling_blocks.shape[0] <= 2 * label_weights.shape[0]
        paired = groups == 4 and homes & (homes - 1) == 0
        one_block = label_weights.shape[0] // BLOCK <= K
        plan = dense_shards if every_row_everywhere and few and paired and one_block else sparse_shards
        return plan(queries, label_weights, sibling_blocks, positive_slot)

    in_specs = (P(("pb", "lab"), None), P("lab", None), P("pb", None), P("pb"))
    out_specs = (P(("pb", "lab"), None), P("lab", None))
    return jax.shard_map(shards, mesh=mesh, in_specs=in_specs, out_specs=out_specs, check_vma=False)
```

```python
import jax
import jax.numpy as jnp
from jax import lax
from jax.experimental import pallas as pl
from jax.experimental.pallas import tpu as pltpu
from jax.sharding import PartitionSpec as P

BLOCK = 128
K = 8
NOTE = 16
VMEM_LIMIT = 24 * 1024 * 1024


def pack_index(touched, width_slots, fill_value):
    homes, count = touched.shape
    rank = jnp.cumsum(touched.astype(jnp.int32), axis=1) - 1
    place = jnp.where(touched, rank, width_slots)
    home_ids = jnp.broadcast_to(jnp.arange(homes, dtype=jnp.int32)[:, None], touched.shape)
    row_ids = jnp.broadcast_to(jnp.arange(count, dtype=jnp.int32)[None, :], touched.shape)
    table = (
        jnp.full((homes, width_slots + 1), fill_value, jnp.int32).at[home_ids, place].set(row_ids)
    )
    return table[:, :width_slots]


def sparse_shards(queries, label_weights, sibling_blocks, positive_slot):
    width = queries.shape[1]
    qcount = sibling_blocks.shape[0]
    lab_dev = label_weights.shape[0]
    blocks_dev = lab_dev // BLOCK
    first = lax.axis_index("lab") * blocks_dev
    local_ids = first + jnp.arange(blocks_dev, dtype=jnp.int32)
    pblock = jnp.take_along_axis(sibling_blocks, (positive_slot // BLOCK)[:, None], axis=1)[:, 0]
    positive = pblock * BLOCK + positive_slot % BLOCK
    label_ids = local_ids[:, None] * BLOCK + jnp.arange(BLOCK, dtype=jnp.int32)[None, :]
    chosen_all = jnp.any(sibling_blocks[:, :, None] == local_ids[None, None, :], axis=1)
    piece = lax.all_gather(queries, "lab", axis=0, tiled=True)
    count = piece.shape[0]
    scores = jnp.dot(piece, label_weights.T, preferred_element_type=jnp.float32)
    scores = scores.reshape(count, blocks_dev, BLOCK)
    target = (label_ids[None, :, :] == positive[:, None, None]).astype(jnp.float32)
    slope = jnp.where(chosen_all[:, :, None], jax.nn.sigmoid(scores) - target, 0.0)
    slope = slope.astype(jnp.bfloat16).reshape(count, lab_dev)
    dq_all = jnp.dot(slope, label_weights, preferred_element_type=jnp.float32)
    w_acc = lax.dot_general(
        slope, piece, (((0,), (0,)), ((), ())), preferred_element_type=jnp.float32
    )
    homes = lax.axis_size("lab")
    q_home = qcount // homes
    slots = q_home * K // homes
    touched = jnp.any(chosen_all, axis=1).reshape(homes, q_home)
    send_idx = pack_index(touched, slots, q_home)
    padded = jnp.concatenate(
        [dq_all.reshape(homes, q_home, width), jnp.zeros((homes, 1, width), jnp.float32)], axis=1
    )
    outgoing = jnp.take_along_axis(padded, send_idx[:, :, None], axis=1)
    incoming = lax.all_to_all(outgoing, "lab", split_axis=0, concat_axis=0, tiled=True)
    own_blocks = lax.dynamic_slice_in_dim(sibling_blocks, lax.axis_index("lab") * q_home, q_home, 0)
    source_ids = jnp.arange(homes, dtype=jnp.int32)
    own_touch = jnp.any(
        (own_blocks // blocks_dev)[:, :, None] == source_ids[None, None, :], axis=1
    ).T
    recv_idx = pack_index(own_touch, slots, q_home)
    query_grad = (
        jnp.zeros((q_home + 1, width), jnp.float32)
        .at[recv_idx.reshape(-1)]
        .add(incoming.reshape(-1, width))[:q_home]
    )
    groups = lax.axis_size("pb")
    total = lax.psum(w_acc, "pb")
    weight_grad = (total / groups).astype(jnp.bfloat16)
    return (query_grad, weight_grad)


def swap(value, axis, bit):
    count = lax.axis_size(axis)
    return lax.ppermute(value, axis, [(i, i ^ bit) for i in range(count)])


def diagonal(value, group_bit, home_bit):
    groups, homes = lax.axis_size("pb"), lax.axis_size("lab")
    pairs = [
        (g * homes + h, (g ^ group_bit) * homes + (h ^ home_bit))
        for g in range(groups)
        for h in range(homes)
    ]
    return lax.ppermute(value, ("pb", "lab"), pairs)


def local_call(body, outs, args, flops=0, follows=()):
    specs = [
        pl.BlockSpec(memory_space=pltpu.SMEM if arg.dtype == jnp.int32 else pltpu.VMEM)
        for arg in args
    ]
    given, later = len(args), len(args) + len(follows)
    return pl.pallas_call(
        lambda *refs: body(*refs[:given], *refs[later:]),
        out_shape=outs,
        in_specs=specs + [pl.BlockSpec(memory_space=pl.ANY)] * len(follows),
        out_specs=[pl.BlockSpec(memory_space=pltpu.VMEM)] * len(outs),
        cost_estimate=pl.CostEstimate(flops=flops, bytes_accessed=0, transcendentals=0),
        compiler_params=pltpu.CompilerParams(vmem_limit_bytes=VMEM_LIMIT),
    )(*args, *follows)


def like(rows, width, dtype):
    return jax.ShapeDtypeStruct((rows, width), dtype)


def join_body(place_ref, own_ref, *refs):
    *came_refs, note_ref, out_ref, noted_ref = refs
    rows, place = own_ref.shape[0], place_ref[0]
    for step, ref in enumerate([own_ref, *came_refs]):
        start = pl.multiple_of((place ^ step) * rows, rows)
        out_ref[pl.ds(start, rows), :] = ref[...]
    half = out_ref.shape[0]
    noted_ref[:half, :] = out_ref[...]
    noted_ref[half:, :] = note_ref[...]


def hold_body(rows_ref, held_ref):
    held_ref[...] = rows_ref[...]


def slope_of(rows, weights, chosen, place):
    count, blocks = rows.shape[0], weights.shape[0] // BLOCK
    scores = lax.dot_general(
        weights, rows, (((1,), (1,)), ((), ())), preferred_element_type=jnp.float32
    )
    named = jnp.zeros((BLOCK, count), jnp.float32)
    for block in range(blocks):
        named = jnp.where(chosen == block, scores[block * BLOCK : (block + 1) * BLOCK], named)
    ids = lax.broadcasted_iota(jnp.int32, (BLOCK, count), 0)
    return (jax.nn.sigmoid(named) - jnp.where(ids == place, 1.0, 0.0)).astype(jnp.bfloat16)


def spread(slope, chosen, blocks):
    wide = slope.astype(jnp.float32)
    parts = [jnp.where(chosen == block, wide, 0.0).astype(slope.dtype) for block in blocks]
    return jnp.concatenate(parts, axis=0)


def read_note(note, which, count):
    chosen = note[2 * which : 2 * which + 1, :count].astype(jnp.int32)
    place = note[2 * which + 1 : 2 * which + 2, :count].astype(jnp.int32)
    return chosen, place


def grad_body(which, rows_ref, weights_ref, note_ref, dq_ref, slope_ref):
    rows, weights = rows_ref[...], weights_ref[...]
    note = note_ref[...].astype(jnp.float32)
    chosen, place = read_note(note, which, rows.shape[0])
    slope = slope_of(rows, weights, chosen, place)
    slope_ref[:BLOCK, :] = slope
    slope_ref[BLOCK:, :] = jnp.broadcast_to(chosen, (NOTE, rows.shape[0])).astype(slope.dtype)
    dq = lax.dot_general(
        spread(slope, chosen, range(weights.shape[0] // BLOCK)),
        weights,
        (((0,), (0,)), ((), ())),
        preferred_element_type=jnp.float32,
    )
    dq_ref[...] = dq.astype(dq_ref.dtype)


def near_body(rows_ref, weights_ref, note_ref, dq_ref, slope_ref, held_ref, copy_ref):
    held_ref[...] = weights_ref[...]
    copy_ref[...] = rows_ref[...]
    grad_body(0, rows_ref, weights_ref, note_ref, dq_ref, slope_ref)


def far_body(rows_ref, weights_ref, note_ref, dq_ref, slope_ref):
    grad_body(1, rows_ref, weights_ref, note_ref, dq_ref, slope_ref)


def order_body(side_ref, near_ref, far_ref, out_ref):
    side, q_home = side_ref[0], out_ref.shape[1]
    for z in range(out_ref.shape[0] // 2):
        part = slice(z * q_home, (z + 1) * q_home)
        out_ref[2 * z + side] = near_ref[part, :]
        out_ref[2 * z + 1 - side] = far_ref[part, :]


def sum_body(terms_ref, out_ref):
    total = terms_ref[0].astype(jnp.float32)
    for source in range(1, terms_ref.shape[0]):
        total = total + terms_ref[source].astype(jnp.float32)
    out_ref[...] = total


def stack_body(*refs):
    *came_refs, out_ref = refs
    start = 0
    for ref in came_refs:
        out_ref[start : start + ref.shape[0], : ref.shape[1]] = ref[...]
        start += ref.shape[0]


def read_slope(slope):
    chosen = slope[BLOCK : BLOCK + 1].astype(jnp.float32).astype(jnp.int32)
    return slope[:BLOCK], chosen


def own_body(near_ref, far_ref, near_slope_ref, far_slope_ref, acc_ref, set_ref):
    rows = jnp.concatenate([near_ref[...], far_ref[...]], axis=0)
    slope = jnp.concatenate([near_slope_ref[...], far_slope_ref[...]], axis=1)
    count = rows.shape[0]
    set_ref[:count, :] = rows
    set_ref[count:, :count] = slope
    wide = spread(*read_slope(slope), range(acc_ref.shape[0] // BLOCK))
    acc_ref[...] = jnp.dot(wide, rows, preferred_element_type=jnp.float32)


def mate_body(set_ref, acc_ref, out_ref):
    count = set_ref.shape[0] - BLOCK - NOTE
    slope, chosen = read_slope(set_ref[count:, :count])
    wide = spread(slope, chosen, range(acc_ref.shape[0] // BLOCK))
    out_ref[...] = acc_ref[...] + jnp.dot(
        wide, set_ref[:count, :], preferred_element_type=jnp.float32
    )


def set_slope(set_ref, weights):
    half = (set_ref.shape[0] - NOTE) // 2
    rows = jnp.concatenate([set_ref[:half, :], set_ref[half + NOTE :, :]], axis=0)
    note = set_ref[half : half + NOTE, :].astype(jnp.float32)
    codes = [read_note(note, which, half) for which in range(2)]
    chosen = jnp.concatenate([codes[0][0], codes[1][0]], axis=1)
    place = jnp.concatenate([codes[0][1], codes[1][1]], axis=1)
    return rows, slope_of(rows, weights, chosen, place), chosen


def cross_body(set_ref, weights_ref, acc_ref, out_ref):
    rows, slope, chosen = set_slope(set_ref, weights_ref[...])
    wide = spread(slope, chosen, range(acc_ref.shape[0] // BLOCK))
    out_ref[...] = acc_ref[...] + jnp.dot(wide, rows, preferred_element_type=jnp.float32)


def late_body(groups, set_ref, weights_ref, acc_ref, out_ref, mark_ref, held, sems):
    mark_ref[...] = jnp.zeros_like(mark_ref)
    rows, slope, chosen = set_slope(set_ref, weights_ref[...])
    blocks = acc_ref.shape[0] // BLOCK
    chunk = blocks // sems.shape[0]
    copies = []
    for part in range(sems.shape[0]):
        here = pl.ds(part * chunk * BLOCK, chunk * BLOCK)
        wide = spread(slope, chosen, range(part * chunk, (part + 1) * chunk))
        total = acc_ref[here, :] + jnp.dot(wide, rows, preferred_element_type=jnp.float32)
        held[here, :] = (total / groups).astype(held.dtype)
        copy = pltpu.make_async_copy(held.at[here, :], out_ref.at[here, :], sems.at[part])
        copy.start()
        copies.append(copy)
    for copy in copies:
        copy.wait()


def late(groups, crossed, weights, acc):
    out = like(*weights.shape, weights.dtype)
    chunks = 4
    return pl.pallas_call(
        lambda *refs: late_body(groups, *refs),
        out_shape=[out, like(1, BLOCK, jnp.int32)],
        in_specs=[pl.BlockSpec(memory_space=pltpu.VMEM)] * 3,
        out_specs=[pl.BlockSpec(memory_space=pl.ANY), pl.BlockSpec(memory_space=pltpu.VMEM)],
        scratch_shapes=[pltpu.VMEM(out.shape, out.dtype), pltpu.SemaphoreType.DMA((chunks,))],
        cost_estimate=pl.CostEstimate(flops=0, bytes_accessed=0, transcendentals=0),
        compiler_params=pltpu.CompilerParams(vmem_limit_bytes=VMEM_LIMIT),
    )(crossed, weights, acc)


def make_note(sibling_blocks, positive_slot, blocks_dev, homes, width):
    me = lax.axis_index("lab")
    local = sibling_blocks.T - me * blocks_dev
    inside = (local >= 0) & (local < blocks_dev)
    chosen = jnp.max(jnp.where(inside, local, -1), axis=0)
    steps = jnp.arange(local.shape[0], dtype=jnp.int32)[:, None]
    pblock = jnp.sum(jnp.where(steps == (positive_slot // BLOCK)[None, :], local, 0), axis=0)
    place = jnp.where(pblock == chosen, positive_slot % BLOCK, -1)
    code = jnp.stack([chosen, place]).astype(jnp.bfloat16)
    code = code.reshape(2, homes // 2, 2, -1).transpose(2, 0, 1, 3).reshape(2, 2, -1)
    code = jnp.where(me % 2 == 0, code, code[::-1]).reshape(4, -1)
    return jnp.pad(code, ((0, NOTE - 4), (0, width - code.shape[1])))


def dense_shards(queries, label_weights, sibling_blocks, positive_slot):
    q_home, width = queries.shape
    qcount = sibling_blocks.shape[0]
    half = qcount // 2
    lab_dev = label_weights.shape[0]
    homes = lax.axis_size("lab")
    groups = lax.axis_size("pb")
    me = lax.axis_index("lab")
    f32, bf16 = jnp.float32, jnp.bfloat16

    place = jnp.reshape(me // 2, (1,)).astype(jnp.int32)
    side = jnp.reshape(me % 2, (1,)).astype(jnp.int32)
    far_bit = groups // 2
    came = [swap(queries, "lab", 2 * step) for step in range(1, homes // 2)]
    held = local_call(hold_body, [like(q_home, width, bf16)], [queries])[0]
    note = make_note(sibling_blocks, positive_slot, lab_dev // BLOCK, homes, width)
    near, noted = local_call(
        join_body,
        [like(half, width, bf16), like(half + NOTE, width, bf16)],
        [place, held, *came, note],
    )
    far = swap(near, "lab", 1)
    work = 4 * half * lab_dev * width
    slope_like = like(BLOCK + NOTE, half, bf16)
    near_dq, near_slope, weights, near_copy = local_call(
        near_body,
        [like(half, width, bf16), slope_like, like(lab_dev, width, bf16), like(half, width, bf16)],
        [near, label_weights, note],
        work,
    )
    cross_near = swap(noted, "pb", far_bit)
    cross_far = diagonal(near_copy, far_bit, 1)
    far_dq, far_slope = local_call(
        far_body,
        [like(half, width, bf16), slope_like],
        [far, weights, note],
        work,
        [near_dq],
    )
    dq = local_call(
        order_body, [jax.ShapeDtypeStruct((homes, q_home, width), bf16)], [side, near_dq, far_dq]
    )[0]
    terms = lax.all_to_all(dq, "lab", split_axis=0, concat_axis=0, tiled=True)
    acc, own = local_call(
        own_body,
        [like(lab_dev, width, f32), like(qcount + BLOCK + NOTE, width, bf16)],
        [near, far, near_slope, far_slope],
        work,
    )
    mate = swap(own, "pb", 1)
    cross = local_call(
        stack_body, [like(qcount + NOTE, width, bf16)], [cross_near, cross_far], 0, [acc]
    )[0]
    cross_mate = swap(cross, "pb", 1)
    grown = like(lab_dev, width, f32)
    acc = local_call(cross_body, [grown], [cross, weights, acc], 20 * work)[0]
    acc = local_call(mate_body, [grown], [mate, acc], work)[0]
    weight_grad, mark = late(groups, cross_mate, weights, acc)
    query_grad = local_call(sum_body, [like(q_home, width, f32)], [terms], 0, [mark])[0]
    return (query_grad, weight_grad)


def solution(mesh):
    groups, homes = mesh.shape["pb"], mesh.shape["lab"]

    def shards(queries, label_weights, sibling_blocks, positive_slot):
        every_row_everywhere = homes == K
        few = groups * sibling_blocks.shape[0] <= 2 * label_weights.shape[0]
        paired = groups == 4 and homes & (homes - 1) == 0
        one_block = label_weights.shape[0] // BLOCK <= K
        plan = dense_shards if every_row_everywhere and few and paired and one_block else sparse_shards
        return plan(queries, label_weights, sibling_blocks, positive_slot)

    in_specs = (P(("pb", "lab"), None), P("lab", None), P("pb", None), P("pb"))
    out_specs = (P(("pb", "lab"), None), P("lab", None))
    return jax.shard_map(shards, mesh=mesh, in_specs=in_specs, out_specs=out_specs, check_vma=False)
```

```python
import jax
import jax.numpy as jnp
from jax import lax
from jax.experimental import pallas as pl
from jax.experimental.pallas import tpu as pltpu
from jax.sharding import PartitionSpec as P

BLOCK = 128
K = 8
NOTE = 16
VMEM_LIMIT = 24 * 1024 * 1024


def pack_index(touched, width_slots, fill_value):
    homes, count = touched.shape
    rank = jnp.cumsum(touched.astype(jnp.int32), axis=1) - 1
    place = jnp.where(touched, rank, width_slots)
    home_ids = jnp.broadcast_to(jnp.arange(homes, dtype=jnp.int32)[:, None], touched.shape)
    row_ids = jnp.broadcast_to(jnp.arange(count, dtype=jnp.int32)[None, :], touched.shape)
    table = (
        jnp.full((homes, width_slots + 1), fill_value, jnp.int32).at[home_ids, place].set(row_ids)
    )
    return table[:, :width_slots]


def sparse_shards(queries, label_weights, sibling_blocks, positive_slot):
    width = queries.shape[1]
    qcount = sibling_blocks.shape[0]
    lab_dev = label_weights.shape[0]
    blocks_dev = lab_dev // BLOCK
    first = lax.axis_index("lab") * blocks_dev
    local_ids = first + jnp.arange(blocks_dev, dtype=jnp.int32)
    pblock = jnp.take_along_axis(sibling_blocks, (positive_slot // BLOCK)[:, None], axis=1)[:, 0]
    positive = pblock * BLOCK + positive_slot % BLOCK
    label_ids = local_ids[:, None] * BLOCK + jnp.arange(BLOCK, dtype=jnp.int32)[None, :]
    chosen_all = jnp.any(sibling_blocks[:, :, None] == local_ids[None, None, :], axis=1)
    piece = lax.all_gather(queries, "lab", axis=0, tiled=True)
    count = piece.shape[0]
    scores = jnp.dot(piece, label_weights.T, preferred_element_type=jnp.float32)
    scores = scores.reshape(count, blocks_dev, BLOCK)
    target = (label_ids[None, :, :] == positive[:, None, None]).astype(jnp.float32)
    slope = jnp.where(chosen_all[:, :, None], jax.nn.sigmoid(scores) - target, 0.0)
    slope = slope.astype(jnp.bfloat16).reshape(count, lab_dev)
    dq_all = jnp.dot(slope, label_weights, preferred_element_type=jnp.float32)
    w_acc = lax.dot_general(
        slope, piece, (((0,), (0,)), ((), ())), preferred_element_type=jnp.float32
    )
    homes = lax.axis_size("lab")
    q_home = qcount // homes
    slots = q_home * K // homes
    touched = jnp.any(chosen_all, axis=1).reshape(homes, q_home)
    send_idx = pack_index(touched, slots, q_home)
    padded = jnp.concatenate(
        [dq_all.reshape(homes, q_home, width), jnp.zeros((homes, 1, width), jnp.float32)], axis=1
    )
    outgoing = jnp.take_along_axis(padded, send_idx[:, :, None], axis=1)
    incoming = lax.all_to_all(outgoing, "lab", split_axis=0, concat_axis=0, tiled=True)
    own_blocks = lax.dynamic_slice_in_dim(sibling_blocks, lax.axis_index("lab") * q_home, q_home, 0)
    source_ids = jnp.arange(homes, dtype=jnp.int32)
    own_touch = jnp.any(
        (own_blocks // blocks_dev)[:, :, None] == source_ids[None, None, :], axis=1
    ).T
    recv_idx = pack_index(own_touch, slots, q_home)
    query_grad = (
        jnp.zeros((q_home + 1, width), jnp.float32)
        .at[recv_idx.reshape(-1)]
        .add(incoming.reshape(-1, width))[:q_home]
    )
    groups = lax.axis_size("pb")
    total = lax.psum(w_acc, "pb")
    weight_grad = (total / groups).astype(jnp.bfloat16)
    return (query_grad, weight_grad)


def swap(value, axis, bit):
    count = lax.axis_size(axis)
    return lax.ppermute(value, axis, [(i, i ^ bit) for i in range(count)])


def diagonal(value, group_bit, home_bit):
    groups, homes = lax.axis_size("pb"), lax.axis_size("lab")
    pairs = [
        (g * homes + h, (g ^ group_bit) * homes + (h ^ home_bit))
        for g in range(groups)
        for h in range(homes)
    ]
    return lax.ppermute(value, ("pb", "lab"), pairs)


def local_call(body, outs, args, flops=0, follows=()):
    specs = [
        pl.BlockSpec(memory_space=pltpu.SMEM if arg.dtype == jnp.int32 else pltpu.VMEM)
        for arg in args
    ]
    given, later = len(args), len(args) + len(follows)
    return pl.pallas_call(
        lambda *refs: body(*refs[:given], *refs[later:]),
        out_shape=outs,
        in_specs=specs + [pl.BlockSpec(memory_space=pl.ANY)] * len(follows),
        out_specs=[pl.BlockSpec(memory_space=pltpu.VMEM)] * len(outs),
        cost_estimate=pl.CostEstimate(flops=flops, bytes_accessed=0, transcendentals=0),
        compiler_params=pltpu.CompilerParams(vmem_limit_bytes=VMEM_LIMIT),
    )(*args, *follows)


def like(rows, width, dtype):
    return jax.ShapeDtypeStruct((rows, width), dtype)


def join_body(place_ref, own_ref, *refs):
    *came_refs, note_ref, out_ref, noted_ref = refs
    rows, place = own_ref.shape[0], place_ref[0]
    for step, ref in enumerate([own_ref, *came_refs]):
        start = pl.multiple_of((place ^ step) * rows, rows)
        out_ref[pl.ds(start, rows), :] = ref[...]
    half = out_ref.shape[0]
    noted_ref[:half, :] = out_ref[...]
    noted_ref[half:, :] = note_ref[...]


def hold_body(*refs):
    for source, held in zip(refs[: len(refs) // 2], refs[len(refs) // 2 :]):
        held[...] = source[...]


def slope_of(rows, weights, chosen, place):
    count, blocks = rows.shape[0], weights.shape[0] // BLOCK
    scores = lax.dot_general(
        weights, rows, (((1,), (1,)), ((), ())), preferred_element_type=jnp.float32
    )
    named = jnp.zeros((BLOCK, count), jnp.float32)
    for block in range(blocks):
        named = jnp.where(chosen == block, scores[block * BLOCK : (block + 1) * BLOCK], named)
    ids = lax.broadcasted_iota(jnp.int32, (BLOCK, count), 0)
    return (jax.nn.sigmoid(named) - jnp.where(ids == place, 1.0, 0.0)).astype(jnp.bfloat16)


def spread(slope, chosen, blocks):
    wide = slope.astype(jnp.float32)
    parts = [jnp.where(chosen == block, wide, 0.0).astype(slope.dtype) for block in blocks]
    return jnp.concatenate(parts, axis=0)


def read_note(note, which, count):
    chosen = note[2 * which : 2 * which + 1, :count].astype(jnp.int32)
    place = note[2 * which + 1 : 2 * which + 2, :count].astype(jnp.int32)
    return chosen, place


def grad_body(which, rows_ref, weights_ref, note_ref, dq_ref, slope_ref):
    rows, weights = rows_ref[...], weights_ref[...]
    note = note_ref[...].astype(jnp.float32)
    chosen, place = read_note(note, which, rows.shape[0])
    slope = slope_of(rows, weights, chosen, place)
    slope_ref[:BLOCK, :] = slope
    slope_ref[BLOCK:, :] = jnp.broadcast_to(chosen, (NOTE, rows.shape[0])).astype(slope.dtype)
    dq = lax.dot_general(
        spread(slope, chosen, range(weights.shape[0] // BLOCK)),
        weights,
        (((0,), (0,)), ((), ())),
        preferred_element_type=jnp.float32,
    )
    dq_ref[...] = dq.astype(dq_ref.dtype)


def near_body(rows_ref, weights_ref, note_ref, dq_ref, slope_ref, copy_ref):
    copy_ref[...] = rows_ref[...]
    grad_body(0, rows_ref, weights_ref, note_ref, dq_ref, slope_ref)


def far_body(rows_ref, weights_ref, note_ref, dq_ref, slope_ref):
    grad_body(1, rows_ref, weights_ref, note_ref, dq_ref, slope_ref)


def fold_body(place_ref, near_ref, came_ref, kept_ref, *send_refs):
    rows, place = kept_ref.shape[0], place_ref[0]
    for step, ref in enumerate([kept_ref, *send_refs]):
        part = pl.ds(pl.multiple_of((place ^ step) * rows, rows), rows)
        ref[...] = (near_ref[part, :] + came_ref[part, :].astype(jnp.float32)).astype(ref.dtype)


def sum_body(kept_ref, *refs):
    *term_refs, out_ref = refs
    total = kept_ref[...]
    for ref in term_refs:
        total = total + ref[...].astype(jnp.float32)
    out_ref[...] = total


def stack_body(*refs):
    *came_refs, out_ref = refs
    start = 0
    for ref in came_refs:
        out_ref[start : start + ref.shape[0], : ref.shape[1]] = ref[...]
        start += ref.shape[0]


def read_slope(slope):
    chosen = slope[BLOCK : BLOCK + 1].astype(jnp.float32).astype(jnp.int32)
    return slope[:BLOCK], chosen


def own_body(near_ref, far_ref, near_slope_ref, far_slope_ref, acc_ref, set_ref):
    rows = jnp.concatenate([near_ref[...], far_ref[...]], axis=0)
    slope = jnp.concatenate([near_slope_ref[...], far_slope_ref[...]], axis=1)
    count = rows.shape[0]
    set_ref[:count, :] = rows
    set_ref[count:, :count] = slope
    wide = spread(*read_slope(slope), range(acc_ref.shape[0] // BLOCK))
    acc_ref[...] = jnp.dot(wide, rows, preferred_element_type=jnp.float32)


def mate_body(set_ref, acc_ref, out_ref):
    count = set_ref.shape[0] - BLOCK - NOTE
    slope, chosen = read_slope(set_ref[count:, :count])
    wide = spread(slope, chosen, range(acc_ref.shape[0] // BLOCK))
    out_ref[...] = acc_ref[...] + jnp.dot(
        wide, set_ref[:count, :], preferred_element_type=jnp.float32
    )


def set_slope(set_ref, weights):
    half = (set_ref.shape[0] - NOTE) // 2
    rows = jnp.concatenate([set_ref[:half, :], set_ref[half + NOTE :, :]], axis=0)
    note = set_ref[half : half + NOTE, :].astype(jnp.float32)
    codes = [read_note(note, which, half) for which in range(2)]
    chosen = jnp.concatenate([codes[0][0], codes[1][0]], axis=1)
    place = jnp.concatenate([codes[0][1], codes[1][1]], axis=1)
    return rows, slope_of(rows, weights, chosen, place), chosen


def cross_body(set_ref, weights_ref, acc_ref, out_ref):
    rows, slope, chosen = set_slope(set_ref, weights_ref[...])
    wide = spread(slope, chosen, range(acc_ref.shape[0] // BLOCK))
    out_ref[...] = acc_ref[...] + jnp.dot(wide, rows, preferred_element_type=jnp.float32)


def late_body(groups, set_ref, weights_ref, acc_ref, out_ref, mark_ref, held, sems):
    mark_ref[...] = jnp.zeros_like(mark_ref)
    rows, slope, chosen = set_slope(set_ref, weights_ref[...])
    blocks = acc_ref.shape[0] // BLOCK
    chunk = blocks // sems.shape[0]
    copies = []
    for part in range(sems.shape[0]):
        here = pl.ds(part * chunk * BLOCK, chunk * BLOCK)
        wide = spread(slope, chosen, range(part * chunk, (part + 1) * chunk))
        total = acc_ref[here, :] + jnp.dot(wide, rows, preferred_element_type=jnp.float32)
        held[here, :] = (total / groups).astype(held.dtype)
        copy = pltpu.make_async_copy(held.at[here, :], out_ref.at[here, :], sems.at[part])
        copy.start()
        copies.append(copy)
    for copy in copies:
        copy.wait()


def late(groups, crossed, weights, acc):
    out = like(*weights.shape, weights.dtype)
    chunks = 4
    return pl.pallas_call(
        lambda *refs: late_body(groups, *refs),
        out_shape=[out, like(1, BLOCK, jnp.int32)],
        in_specs=[pl.BlockSpec(memory_space=pltpu.VMEM)] * 3,
        out_specs=[pl.BlockSpec(memory_space=pl.ANY), pl.BlockSpec(memory_space=pltpu.VMEM)],
        scratch_shapes=[pltpu.VMEM(out.shape, out.dtype), pltpu.SemaphoreType.DMA((chunks,))],
        cost_estimate=pl.CostEstimate(flops=0, bytes_accessed=0, transcendentals=0),
        compiler_params=pltpu.CompilerParams(vmem_limit_bytes=VMEM_LIMIT),
    )(crossed, weights, acc)


def note_body(blocks_dev, q_home, me_ref, choice_ref, note_ref):
    choice = choice_ref[...].astype(jnp.int32)
    me, picks, count = me_ref[0], choice.shape[0] - 1, choice.shape[1]
    local, slot = choice[:picks] - me * blocks_dev, choice[picks:]
    inside = (local >= 0) & (local < blocks_dev)
    chosen = jnp.max(jnp.where(inside, local, -1), axis=0, keepdims=True)
    steps = lax.broadcasted_iota(jnp.int32, local.shape, 0)
    named = steps == lax.shift_right_logical(slot, BLOCK.bit_length() - 1)
    pblock = jnp.sum(jnp.where(named, local, 0), axis=0, keepdims=True)
    place = jnp.where(pblock == chosen, slot & (BLOCK - 1), -1)
    row = lax.broadcasted_iota(jnp.int32, (NOTE, count), 0)
    code = jnp.where(row == 0, chosen, jnp.where(row == 1, place, 0))
    half = count // 2
    lane = lax.broadcasted_iota(jnp.int32, (count, count), 1)
    source = lax.broadcasted_iota(jnp.int32, (count, count), 0)
    plane = (lane >= half).astype(jnp.int32) ^ (me & 1)
    step = lax.shift_right_logical(lane & (half - 1), q_home.bit_length() - 1)
    wanted = (2 * step + plane) * q_home + (lane & (q_home - 1))
    order = jnp.where(source == wanted, 1.0, 0.0).astype(jnp.bfloat16)
    code = jnp.dot(code.astype(jnp.bfloat16), order, preferred_element_type=jnp.float32)
    rest = jnp.zeros((NOTE - 4, half), jnp.float32)
    note = jnp.concatenate([code[:2, :half], code[:2, half:], rest], axis=0)
    note_ref[...] = jnp.zeros_like(note_ref)
    note_ref[:, :half] = note.astype(note_ref.dtype)


def dense_shards(queries, label_weights, sibling_blocks, positive_slot):
    q_home, width = queries.shape
    qcount = sibling_blocks.shape[0]
    half = qcount // 2
    lab_dev = label_weights.shape[0]
    homes = lax.axis_size("lab")
    groups = lax.axis_size("pb")
    me = lax.axis_index("lab")
    f32, bf16 = jnp.float32, jnp.bfloat16

    place = jnp.reshape(me // 2, (1,)).astype(jnp.int32)
    far_bit = groups // 2
    came = [swap(queries, "lab", 2 * step) for step in range(1, homes // 2)]
    held, weights = local_call(
        hold_body,
        [like(q_home, width, bf16), like(lab_dev, width, bf16)],
        [queries, label_weights],
    )
    choice = jnp.concatenate([sibling_blocks.T, positive_slot[None]], axis=0).astype(f32)
    note = local_call(
        lambda *refs: note_body(lab_dev // BLOCK, q_home, *refs),
        [like(NOTE, width, bf16)],
        [jnp.reshape(me, (1,)).astype(jnp.int32), choice],
    )[0]
    near, noted = local_call(
        join_body,
        [like(half, width, bf16), like(half + NOTE, width, bf16)],
        [place, held, *came, note],
        0,
        [weights],
    )
    far = swap(near, "lab", 1)
    work = 4 * half * lab_dev * width
    slope_like = like(BLOCK + NOTE, half, bf16)
    near_dq, near_slope, near_copy = local_call(
        near_body,
        [like(half, width, f32), slope_like, like(half, width, bf16)],
        [near, weights, note],
        work,
    )
    cross_near = swap(noted, "pb", far_bit)
    cross_far = diagonal(near_copy, far_bit, 1)
    far_dq, far_slope = local_call(
        far_body,
        [like(half, width, bf16), slope_like],
        [far, weights, note],
        work,
        [near_dq],
    )
    came = swap(far_dq, "lab", 1)
    acc, own = local_call(
        own_body,
        [like(lab_dev, width, f32), like(qcount + BLOCK + NOTE, width, bf16)],
        [near, far, near_slope, far_slope],
        work,
    )
    mate = swap(own, "pb", 1)
    kept, *terms = local_call(
        fold_body,
        [like(q_home, width, f32)] + [like(q_home, width, bf16)] * (homes // 2 - 1),
        [place, near_dq, came],
        0,
        [acc],
    )
    terms = [swap(term, "lab", 2 * step) for step, term in enumerate(terms, 1)]
    cross = local_call(
        stack_body, [like(qcount + NOTE, width, bf16)], [cross_near, cross_far], 0, []
    )[0]
    cross_mate = swap(cross, "pb", 1)
    grown = like(lab_dev, width, f32)
    acc = local_call(cross_body, [grown], [cross, weights, acc], 20 * work)[0]
    acc = local_call(mate_body, [grown], [mate, acc], work)[0]
    weight_grad, mark = late(groups, cross_mate, weights, acc)
    query_grad = local_call(
        sum_body, [like(q_home, width, f32)], [kept, *terms], 0, [mark]
    )[0]
    return (query_grad, weight_grad)


def solution(mesh):
    groups, homes = mesh.shape["pb"], mesh.shape["lab"]

    def shards(queries, label_weights, sibling_blocks, positive_slot):
        every_row_everywhere = homes == K
        few = groups * sibling_blocks.shape[0] <= 2 * label_weights.shape[0]
        paired = groups == 4 and homes & (homes - 1) == 0
        one_block = label_weights.shape[0] // BLOCK <= K
        plan = dense_shards if every_row_everywhere and few and paired and one_block else sparse_shards
        return plan(queries, label_weights, sibling_blocks, positive_slot)

    in_specs = (P(("pb", "lab"), None), P("lab", None), P("pb", None), P("pb"))
    out_specs = (P(("pb", "lab"), None), P("lab", None))
    return jax.shard_map(shards, mesh=mesh, in_specs=in_specs, out_specs=out_specs, check_vma=False)
```

```python
import jax
import jax.numpy as jnp
from jax import lax
from jax.experimental import pallas as pl
from jax.experimental.pallas import tpu as pltpu
from jax.sharding import PartitionSpec as P

BLOCK = 128
K = 8
NOTE = 16
VMEM_LIMIT = 24 * 1024 * 1024


def pack_index(touched, width_slots, fill_value):
    homes, count = touched.shape
    rank = jnp.cumsum(touched.astype(jnp.int32), axis=1) - 1
    place = jnp.where(touched, rank, width_slots)
    home_ids = jnp.broadcast_to(jnp.arange(homes, dtype=jnp.int32)[:, None], touched.shape)
    row_ids = jnp.broadcast_to(jnp.arange(count, dtype=jnp.int32)[None, :], touched.shape)
    table = (
        jnp.full((homes, width_slots + 1), fill_value, jnp.int32).at[home_ids, place].set(row_ids)
    )
    return table[:, :width_slots]


def sparse_shards(queries, label_weights, sibling_blocks, positive_slot):
    width = queries.shape[1]
    qcount = sibling_blocks.shape[0]
    lab_dev = label_weights.shape[0]
    blocks_dev = lab_dev // BLOCK
    first = lax.axis_index("lab") * blocks_dev
    local_ids = first + jnp.arange(blocks_dev, dtype=jnp.int32)
    pblock = jnp.take_along_axis(sibling_blocks, (positive_slot // BLOCK)[:, None], axis=1)[:, 0]
    positive = pblock * BLOCK + positive_slot % BLOCK
    label_ids = local_ids[:, None] * BLOCK + jnp.arange(BLOCK, dtype=jnp.int32)[None, :]
    chosen_all = jnp.any(sibling_blocks[:, :, None] == local_ids[None, None, :], axis=1)
    piece = lax.all_gather(queries, "lab", axis=0, tiled=True)
    count = piece.shape[0]
    scores = jnp.dot(piece, label_weights.T, preferred_element_type=jnp.float32)
    scores = scores.reshape(count, blocks_dev, BLOCK)
    target = (label_ids[None, :, :] == positive[:, None, None]).astype(jnp.float32)
    slope = jnp.where(chosen_all[:, :, None], jax.nn.sigmoid(scores) - target, 0.0)
    slope = slope.astype(jnp.bfloat16).reshape(count, lab_dev)
    dq_all = jnp.dot(slope, label_weights, preferred_element_type=jnp.float32)
    w_acc = lax.dot_general(
        slope, piece, (((0,), (0,)), ((), ())), preferred_element_type=jnp.float32
    )
    homes = lax.axis_size("lab")
    q_home = qcount // homes
    slots = q_home * K // homes
    touched = jnp.any(chosen_all, axis=1).reshape(homes, q_home)
    send_idx = pack_index(touched, slots, q_home)
    padded = jnp.concatenate(
        [dq_all.reshape(homes, q_home, width), jnp.zeros((homes, 1, width), jnp.float32)], axis=1
    )
    outgoing = jnp.take_along_axis(padded, send_idx[:, :, None], axis=1)
    incoming = lax.all_to_all(outgoing, "lab", split_axis=0, concat_axis=0, tiled=True)
    own_blocks = lax.dynamic_slice_in_dim(sibling_blocks, lax.axis_index("lab") * q_home, q_home, 0)
    source_ids = jnp.arange(homes, dtype=jnp.int32)
    own_touch = jnp.any(
        (own_blocks // blocks_dev)[:, :, None] == source_ids[None, None, :], axis=1
    ).T
    recv_idx = pack_index(own_touch, slots, q_home)
    query_grad = (
        jnp.zeros((q_home + 1, width), jnp.float32)
        .at[recv_idx.reshape(-1)]
        .add(incoming.reshape(-1, width))[:q_home]
    )
    groups = lax.axis_size("pb")
    total = lax.psum(w_acc, "pb")
    weight_grad = (total / groups).astype(jnp.bfloat16)
    return (query_grad, weight_grad)


def swap(value, axis, bit):
    count = lax.axis_size(axis)
    return lax.ppermute(value, axis, [(i, i ^ bit) for i in range(count)])


def diagonal(value, group_bit, home_bit):
    groups, homes = lax.axis_size("pb"), lax.axis_size("lab")
    pairs = [
        (g * homes + h, (g ^ group_bit) * homes + (h ^ home_bit))
        for g in range(groups)
        for h in range(homes)
    ]
    return lax.ppermute(value, ("pb", "lab"), pairs)


def local_call(body, outs, args, flops=0, follows=()):
    specs = [
        pl.BlockSpec(memory_space=pltpu.SMEM if arg.dtype == jnp.int32 else pltpu.VMEM)
        for arg in args
    ]
    given, later = len(args), len(args) + len(follows)
    return pl.pallas_call(
        lambda *refs: body(*refs[:given], *refs[later:]),
        out_shape=outs,
        in_specs=specs + [pl.BlockSpec(memory_space=pl.ANY)] * len(follows),
        out_specs=[pl.BlockSpec(memory_space=pltpu.VMEM)] * len(outs),
        cost_estimate=pl.CostEstimate(flops=flops, bytes_accessed=0, transcendentals=0),
        compiler_params=pltpu.CompilerParams(vmem_limit_bytes=VMEM_LIMIT),
    )(*args, *follows)


def like(rows, width, dtype):
    return jax.ShapeDtypeStruct((rows, width), dtype)


def join_body(place_ref, own_ref, *refs):
    *came_refs, note_ref, out_ref, noted_ref = refs
    rows, place = own_ref.shape[0], place_ref[0]
    for step, ref in enumerate([own_ref, *came_refs]):
        start = pl.multiple_of((place ^ step) * rows, rows)
        out_ref[pl.ds(start, rows), :] = ref[...]
    half = out_ref.shape[0]
    noted_ref[:half, :] = out_ref[...]
    noted_ref[half:, :] = note_ref[...]


def hold_body(*refs):
    for source, held in zip(refs[: len(refs) // 2], refs[len(refs) // 2 :]):
        held[...] = source[...]


def slope_of(rows, weights, chosen, place):
    count, blocks = rows.shape[0], weights.shape[0] // BLOCK
    scores = lax.dot_general(
        weights, rows, (((1,), (1,)), ((), ())), preferred_element_type=jnp.float32
    )
    named = jnp.zeros((BLOCK, count), jnp.float32)
    for block in range(blocks):
        named = jnp.where(chosen == block, scores[block * BLOCK : (block + 1) * BLOCK], named)
    ids = lax.broadcasted_iota(jnp.int32, (BLOCK, count), 0)
    return (jax.nn.sigmoid(named) - jnp.where(ids == place, 1.0, 0.0)).astype(jnp.bfloat16)


def spread(slope, chosen, blocks):
    wide = slope.astype(jnp.float32)
    parts = [jnp.where(chosen == block, wide, 0.0).astype(slope.dtype) for block in blocks]
    return jnp.concatenate(parts, axis=0)


def read_note(note, which, count):
    chosen = note[2 * which : 2 * which + 1, :count].astype(jnp.int32)
    place = note[2 * which + 1 : 2 * which + 2, :count].astype(jnp.int32)
    return chosen, place


def grad_body(which, rows_ref, weights_ref, note_ref, dq_ref, slope_ref):
    rows, weights = rows_ref[...], weights_ref[...]
    note = note_ref[...].astype(jnp.float32)
    chosen, place = read_note(note, which, rows.shape[0])
    slope = slope_of(rows, weights, chosen, place)
    slope_ref[:BLOCK, :] = slope
    slope_ref[BLOCK:, :] = jnp.broadcast_to(chosen, (NOTE, rows.shape[0])).astype(slope.dtype)
    dq = lax.dot_general(
        spread(slope, chosen, range(weights.shape[0] // BLOCK)),
        weights,
        (((0,), (0,)), ((), ())),
        preferred_element_type=jnp.float32,
    )
    dq_ref[...] = dq.astype(dq_ref.dtype)


def near_body(rows_ref, weights_ref, note_ref, dq_ref, slope_ref, copy_ref):
    copy_ref[...] = rows_ref[...]
    grad_body(0, rows_ref, weights_ref, note_ref, dq_ref, slope_ref)


def far_body(rows_ref, weights_ref, note_ref, dq_ref, slope_ref):
    grad_body(1, rows_ref, weights_ref, note_ref, dq_ref, slope_ref)


def fold_body(place_ref, near_ref, came_ref, kept_ref, *send_refs):
    rows, place = kept_ref.shape[0], place_ref[0]
    for step, ref in enumerate([kept_ref, *send_refs]):
        part = pl.ds(pl.multiple_of((place ^ step) * rows, rows), rows)
        ref[...] = (near_ref[part, :] + came_ref[part, :].astype(jnp.float32)).astype(ref.dtype)


def sum_body(kept_ref, *refs):
    *term_refs, out_ref = refs
    total = kept_ref[...]
    for ref in term_refs:
        total = total + ref[...].astype(jnp.float32)
    out_ref[...] = total


def stack_body(*refs):
    *came_refs, out_ref = refs
    start = 0
    for ref in came_refs:
        out_ref[start : start + ref.shape[0], : ref.shape[1]] = ref[...]
        start += ref.shape[0]


def read_slope(slope):
    chosen = slope[BLOCK : BLOCK + 1].astype(jnp.float32).astype(jnp.int32)
    return slope[:BLOCK], chosen


def own_body(near_ref, far_ref, near_slope_ref, far_slope_ref, acc_ref, set_ref):
    rows = jnp.concatenate([near_ref[...], far_ref[...]], axis=0)
    slope = jnp.concatenate([near_slope_ref[...], far_slope_ref[...]], axis=1)
    count = rows.shape[0]
    set_ref[:count, :] = rows
    set_ref[count:, :count] = slope
    wide = spread(*read_slope(slope), range(acc_ref.shape[0] // BLOCK))
    acc_ref[...] = jnp.dot(wide, rows, preferred_element_type=jnp.float32)


def mate_body(set_ref, acc_ref, out_ref):
    count = set_ref.shape[0] - BLOCK - NOTE
    slope, chosen = read_slope(set_ref[count:, :count])
    wide = spread(slope, chosen, range(acc_ref.shape[0] // BLOCK))
    out_ref[...] = acc_ref[...] + jnp.dot(
        wide, set_ref[:count, :], preferred_element_type=jnp.float32
    )


def set_slope(set_ref, weights):
    half = (set_ref.shape[0] - NOTE) // 2
    rows = jnp.concatenate([set_ref[:half, :], set_ref[half + NOTE :, :]], axis=0)
    note = set_ref[half : half + NOTE, :].astype(jnp.float32)
    codes = [read_note(note, which, half) for which in range(2)]
    chosen = jnp.concatenate([codes[0][0], codes[1][0]], axis=1)
    place = jnp.concatenate([codes[0][1], codes[1][1]], axis=1)
    return rows, slope_of(rows, weights, chosen, place), chosen


def cross_body(set_ref, weights_ref, acc_ref, out_ref):
    rows, slope, chosen = set_slope(set_ref, weights_ref[...])
    wide = spread(slope, chosen, range(acc_ref.shape[0] // BLOCK))
    out_ref[...] = acc_ref[...] + jnp.dot(wide, rows, preferred_element_type=jnp.float32)


def late_body(groups, set_ref, weights_ref, acc_ref, out_ref, mark_ref, held, sems):
    mark_ref[...] = jnp.zeros_like(mark_ref)
    rows, slope, chosen = set_slope(set_ref, weights_ref[...])
    blocks = acc_ref.shape[0] // BLOCK
    chunk = blocks // sems.shape[0]
    copies = []
    for part in range(sems.shape[0]):
        here = pl.ds(part * chunk * BLOCK, chunk * BLOCK)
        wide = spread(slope, chosen, range(part * chunk, (part + 1) * chunk))
        total = acc_ref[here, :] + jnp.dot(wide, rows, preferred_element_type=jnp.float32)
        held[here, :] = (total / groups).astype(held.dtype)
        copy = pltpu.make_async_copy(held.at[here, :], out_ref.at[here, :], sems.at[part])
        copy.start()
        copies.append(copy)
    for copy in copies:
        copy.wait()


def late(groups, crossed, weights, acc):
    out = like(*weights.shape, weights.dtype)
    chunks = 4
    return pl.pallas_call(
        lambda *refs: late_body(groups, *refs),
        out_shape=[out, like(1, BLOCK, jnp.int32)],
        in_specs=[pl.BlockSpec(memory_space=pltpu.VMEM)] * 3,
        out_specs=[pl.BlockSpec(memory_space=pl.ANY), pl.BlockSpec(memory_space=pltpu.VMEM)],
        scratch_shapes=[pltpu.VMEM(out.shape, out.dtype), pltpu.SemaphoreType.DMA((chunks,))],
        cost_estimate=pl.CostEstimate(flops=0, bytes_accessed=0, transcendentals=0),
        compiler_params=pltpu.CompilerParams(vmem_limit_bytes=VMEM_LIMIT),
    )(crossed, weights, acc)


def note_body(blocks_dev, q_home, me_ref, choice_ref, note_ref):
    choice = choice_ref[...].astype(jnp.int32)
    me, picks, count = me_ref[0], choice.shape[0] - 1, choice.shape[1]
    local, slot = choice[:picks] - me * blocks_dev, choice[picks:]
    inside = (local >= 0) & (local < blocks_dev)
    chosen = jnp.max(jnp.where(inside, local, -1), axis=0, keepdims=True)
    steps = lax.broadcasted_iota(jnp.int32, local.shape, 0)
    named = steps == lax.shift_right_logical(slot, BLOCK.bit_length() - 1)
    pblock = jnp.sum(jnp.where(named, local, 0), axis=0, keepdims=True)
    place = jnp.where(pblock == chosen, slot & (BLOCK - 1), -1)
    row = lax.broadcasted_iota(jnp.int32, (NOTE, count), 0)
    code = jnp.where(row == 0, chosen, jnp.where(row == 1, place, 0))
    half = count // 2
    lane = lax.broadcasted_iota(jnp.int32, (count, count), 1)
    source = lax.broadcasted_iota(jnp.int32, (count, count), 0)
    plane = (lane >= half).astype(jnp.int32) ^ (me & 1)
    step = lax.shift_right_logical(lane & (half - 1), q_home.bit_length() - 1)
    wanted = (2 * step + plane) * q_home + (lane & (q_home - 1))
    order = jnp.where(source == wanted, 1.0, 0.0).astype(jnp.bfloat16)
    code = jnp.dot(code.astype(jnp.bfloat16), order, preferred_element_type=jnp.float32)
    rest = jnp.zeros((NOTE - 4, half), jnp.float32)
    note = jnp.concatenate([code[:2, :half], code[:2, half:], rest], axis=0)
    note_ref[...] = jnp.zeros_like(note_ref)
    note_ref[:, :half] = note.astype(note_ref.dtype)


def dense_shards(queries, label_weights, sibling_blocks, positive_slot):
    q_home, width = queries.shape
    qcount = sibling_blocks.shape[0]
    half = qcount // 2
    lab_dev = label_weights.shape[0]
    homes = lax.axis_size("lab")
    groups = lax.axis_size("pb")
    me = lax.axis_index("lab")
    f32, bf16 = jnp.float32, jnp.bfloat16

    place = jnp.reshape(me // 2, (1,)).astype(jnp.int32)
    far_bit = groups // 2
    came = [swap(queries, "lab", 2 * step) for step in range(1, homes // 2)]
    held, weights = local_call(
        hold_body,
        [like(q_home, width, bf16), like(lab_dev, width, bf16)],
        [queries, label_weights],
    )
    choice = jnp.concatenate([sibling_blocks.T, positive_slot[None]], axis=0).astype(f32)
    note = local_call(
        lambda *refs: note_body(lab_dev // BLOCK, q_home, *refs),
        [like(NOTE, width, bf16)],
        [jnp.reshape(me, (1,)).astype(jnp.int32), choice],
    )[0]
    near, noted = local_call(
        join_body,
        [like(half, width, bf16), like(half + NOTE, width, bf16)],
        [place, held, *came, note],
        0,
        [weights],
    )
    far = swap(near, "lab", 1)
    work = 4 * half * lab_dev * width
    slope_like = like(BLOCK + NOTE, half, bf16)
    near_dq, near_slope, near_copy = local_call(
        near_body,
        [like(half, width, f32), slope_like, like(half, width, bf16)],
        [near, weights, note],
        work,
    )
    cross_near = swap(noted, "pb", far_bit)
    cross_far = diagonal(near_copy, far_bit, 1)
    far_dq, far_slope = local_call(
        far_body,
        [like(half, width, bf16), slope_like],
        [far, weights, note],
        work,
        [near_dq],
    )
    came = swap(far_dq, "lab", 1)
    acc, own = local_call(
        own_body,
        [like(lab_dev, width, f32), like(qcount + BLOCK + NOTE, width, bf16)],
        [near, far, near_slope, far_slope],
        work,
    )
    mate = swap(own, "pb", 1)
    cross = local_call(
        stack_body, [like(qcount + NOTE, width, bf16)], [cross_near, cross_far], 0, []
    )[0]
    cross_mate = swap(cross, "pb", 1)
    grown = like(lab_dev, width, f32)
    acc = local_call(cross_body, [grown], [cross, weights, acc], 20 * work)[0]
    acc = local_call(mate_body, [grown], [mate, acc], work)[0]
    kept, *terms = local_call(
        fold_body,
        [like(q_home, width, f32)] + [like(q_home, width, bf16)] * (homes // 2 - 1),
        [place, near_dq, came],
        0,
        [acc],
    )
    terms = [swap(term, "lab", 2 * step) for step, term in enumerate(terms, 1)]
    weight_grad, mark = late(groups, cross_mate, weights, acc)
    query_grad = local_call(
        sum_body, [like(q_home, width, f32)], [kept, *terms], 0, [mark]
    )[0]
    return (query_grad, weight_grad)


def solution(mesh):
    groups, homes = mesh.shape["pb"], mesh.shape["lab"]

    def shards(queries, label_weights, sibling_blocks, positive_slot):
        every_row_everywhere = homes == K
        few = groups * sibling_blocks.shape[0] <= 2 * label_weights.shape[0]
        paired = groups == 4 and homes & (homes - 1) == 0
        one_block = label_weights.shape[0] // BLOCK <= K
        plan = dense_shards if every_row_everywhere and few and paired and one_block else sparse_shards
        return plan(queries, label_weights, sibling_blocks, positive_slot)

    in_specs = (P(("pb", "lab"), None), P("lab", None), P("pb", None), P("pb"))
    out_specs = (P(("pb", "lab"), None), P("lab", None))
    return jax.shard_map(shards, mesh=mesh, in_specs=in_specs, out_specs=out_specs, check_vma=False)
```

```python
import jax
import jax.numpy as jnp
from jax import lax
from jax.experimental import pallas as pl
from jax.experimental.pallas import tpu as pltpu
from jax.sharding import PartitionSpec as P

BLOCK = 128
K = 8
NOTE = 16
VMEM_LIMIT = 24 * 1024 * 1024


def pack_index(touched, width_slots, fill_value):
    homes, count = touched.shape
    rank = jnp.cumsum(touched.astype(jnp.int32), axis=1) - 1
    place = jnp.where(touched, rank, width_slots)
    home_ids = jnp.broadcast_to(jnp.arange(homes, dtype=jnp.int32)[:, None], touched.shape)
    row_ids = jnp.broadcast_to(jnp.arange(count, dtype=jnp.int32)[None, :], touched.shape)
    table = (
        jnp.full((homes, width_slots + 1), fill_value, jnp.int32).at[home_ids, place].set(row_ids)
    )
    return table[:, :width_slots]


def sparse_shards(queries, label_weights, sibling_blocks, positive_slot):
    width = queries.shape[1]
    qcount = sibling_blocks.shape[0]
    lab_dev = label_weights.shape[0]
    blocks_dev = lab_dev // BLOCK
    first = lax.axis_index("lab") * blocks_dev
    local_ids = first + jnp.arange(blocks_dev, dtype=jnp.int32)
    pblock = jnp.take_along_axis(sibling_blocks, (positive_slot // BLOCK)[:, None], axis=1)[:, 0]
    positive = pblock * BLOCK + positive_slot % BLOCK
    label_ids = local_ids[:, None] * BLOCK + jnp.arange(BLOCK, dtype=jnp.int32)[None, :]
    chosen_all = jnp.any(sibling_blocks[:, :, None] == local_ids[None, None, :], axis=1)
    piece = lax.all_gather(queries, "lab", axis=0, tiled=True)
    count = piece.shape[0]
    scores = jnp.dot(piece, label_weights.T, preferred_element_type=jnp.float32)
    scores = scores.reshape(count, blocks_dev, BLOCK)
    target = (label_ids[None, :, :] == positive[:, None, None]).astype(jnp.float32)
    slope = jnp.where(chosen_all[:, :, None], jax.nn.sigmoid(scores) - target, 0.0)
    slope = slope.astype(jnp.bfloat16).reshape(count, lab_dev)
    dq_all = jnp.dot(slope, label_weights, preferred_element_type=jnp.float32)
    w_acc = lax.dot_general(
        slope, piece, (((0,), (0,)), ((), ())), preferred_element_type=jnp.float32
    )
    homes = lax.axis_size("lab")
    q_home = qcount // homes
    slots = q_home * K // homes
    touched = jnp.any(chosen_all, axis=1).reshape(homes, q_home)
    send_idx = pack_index(touched, slots, q_home)
    padded = jnp.concatenate(
        [dq_all.reshape(homes, q_home, width), jnp.zeros((homes, 1, width), jnp.float32)], axis=1
    )
    outgoing = jnp.take_along_axis(padded, send_idx[:, :, None], axis=1)
    incoming = lax.all_to_all(outgoing, "lab", split_axis=0, concat_axis=0, tiled=True)
    own_blocks = lax.dynamic_slice_in_dim(sibling_blocks, lax.axis_index("lab") * q_home, q_home, 0)
    source_ids = jnp.arange(homes, dtype=jnp.int32)
    own_touch = jnp.any(
        (own_blocks // blocks_dev)[:, :, None] == source_ids[None, None, :], axis=1
    ).T
    recv_idx = pack_index(own_touch, slots, q_home)
    query_grad = (
        jnp.zeros((q_home + 1, width), jnp.float32)
        .at[recv_idx.reshape(-1)]
        .add(incoming.reshape(-1, width))[:q_home]
    )
    groups = lax.axis_size("pb")
    total = lax.psum(w_acc, "pb")
    weight_grad = (total / groups).astype(jnp.bfloat16)
    return (query_grad, weight_grad)


def swap(value, axis, bit):
    count = lax.axis_size(axis)
    return lax.ppermute(value, axis, [(i, i ^ bit) for i in range(count)])


def diagonal(value, group_bit, home_bit):
    groups, homes = lax.axis_size("pb"), lax.axis_size("lab")
    pairs = [
        (g * homes + h, (g ^ group_bit) * homes + (h ^ home_bit))
        for g in range(groups)
        for h in range(homes)
    ]
    return lax.ppermute(value, ("pb", "lab"), pairs)


def local_call(body, outs, args, flops=0, follows=()):
    specs = [
        pl.BlockSpec(memory_space=pltpu.SMEM if arg.dtype == jnp.int32 else pltpu.VMEM)
        for arg in args
    ]
    given, later = len(args), len(args) + len(follows)
    return pl.pallas_call(
        lambda *refs: body(*refs[:given], *refs[later:]),
        out_shape=outs,
        in_specs=specs + [pl.BlockSpec(memory_space=pl.ANY)] * len(follows),
        out_specs=[pl.BlockSpec(memory_space=pltpu.VMEM)] * len(outs),
        cost_estimate=pl.CostEstimate(flops=flops, bytes_accessed=0, transcendentals=0),
        compiler_params=pltpu.CompilerParams(vmem_limit_bytes=VMEM_LIMIT),
    )(*args, *follows)


def like(rows, width, dtype):
    return jax.ShapeDtypeStruct((rows, width), dtype)


def join_body(place_ref, own_ref, *refs):
    *came_refs, note_ref, out_ref, noted_ref = refs
    rows, place = own_ref.shape[0], place_ref[0]
    for step, ref in enumerate([own_ref, *came_refs]):
        start = pl.multiple_of((place ^ step) * rows, rows)
        out_ref[pl.ds(start, rows), :] = ref[...]
    half = out_ref.shape[0]
    noted_ref[:half, :] = out_ref[...]
    noted_ref[half:, :] = note_ref[...]


def hold_body(*refs):
    for source, held in zip(refs[: len(refs) // 2], refs[len(refs) // 2 :]):
        held[...] = source[...]


def slope_of(rows, weights, chosen, place):
    count, blocks = rows.shape[0], weights.shape[0] // BLOCK
    scores = lax.dot_general(
        weights, rows, (((1,), (1,)), ((), ())), preferred_element_type=jnp.float32
    )
    named = jnp.zeros((BLOCK, count), jnp.float32)
    for block in range(blocks):
        named = jnp.where(chosen == block, scores[block * BLOCK : (block + 1) * BLOCK], named)
    ids = lax.broadcasted_iota(jnp.int32, (BLOCK, count), 0)
    return (jax.nn.sigmoid(named) - jnp.where(ids == place, 1.0, 0.0)).astype(jnp.bfloat16)


def spread(slope, chosen, blocks):
    wide = slope.astype(jnp.float32)
    parts = [jnp.where(chosen == block, wide, 0.0).astype(slope.dtype) for block in blocks]
    return jnp.concatenate(parts, axis=0)


def read_note(note, which, count):
    chosen = note[2 * which : 2 * which + 1, :count].astype(jnp.int32)
    place = note[2 * which + 1 : 2 * which + 2, :count].astype(jnp.int32)
    return chosen, place


def grad_body(which, rows_ref, weights_ref, note_ref, dq_ref, slope_ref):
    rows, weights = rows_ref[...], weights_ref[...]
    note = note_ref[...].astype(jnp.float32)
    chosen, place = read_note(note, which, rows.shape[0])
    slope = slope_of(rows, weights, chosen, place)
    slope_ref[:BLOCK, :] = slope
    slope_ref[BLOCK:, :] = jnp.broadcast_to(chosen, (NOTE, rows.shape[0])).astype(slope.dtype)
    dq = lax.dot_general(
        spread(slope, chosen, range(weights.shape[0] // BLOCK)),
        weights,
        (((0,), (0,)), ((), ())),
        preferred_element_type=jnp.float32,
    )
    q_home = dq_ref.shape[1]
    for z in range(dq_ref.shape[0]):
        dq_ref[z] = dq[z * q_home : (z + 1) * q_home].astype(dq_ref.dtype)


def write_home(plane, staged, out_ref, sems):
    copies = [
        pltpu.make_async_copy(staged.at[z], out_ref.at[2 * z + plane], sems.at[z])
        for z in range(staged.shape[0])
    ]
    for copy in copies:
        copy.start()
    for copy in copies:
        copy.wait()


def near_body(side_ref, rows_ref, weights_ref, note_ref, slope_ref, copy_ref, out_ref, staged, sems):
    copy_ref[...] = rows_ref[...]
    grad_body(0, rows_ref, weights_ref, note_ref, staged, slope_ref)
    write_home(side_ref[0], staged, out_ref, sems)


def far_body(side_ref, rows_ref, weights_ref, note_ref, near_ref, slope_ref, out_ref, staged, sems):
    del near_ref
    grad_body(1, rows_ref, weights_ref, note_ref, staged, slope_ref)
    write_home(1 - side_ref[0], staged, out_ref, sems)


def grad_call(body, homes, q_home, outs, args, aliases, flops):
    width = args[1].shape[1]
    vmem = pl.BlockSpec(memory_space=pltpu.VMEM)
    specs = [pl.BlockSpec(memory_space=pltpu.SMEM), vmem, vmem, vmem]
    return pl.pallas_call(
        body,
        out_shape=outs + [jax.ShapeDtypeStruct((homes, q_home, width), jnp.bfloat16)],
        in_specs=specs + [pl.BlockSpec(memory_space=pl.ANY)] * len(aliases),
        out_specs=[vmem] * len(outs) + [pl.BlockSpec(memory_space=pl.ANY)],
        scratch_shapes=[
            pltpu.VMEM((homes // 2, q_home, width), jnp.bfloat16),
            pltpu.SemaphoreType.DMA((homes // 2,)),
        ],
        input_output_aliases=aliases,
        cost_estimate=pl.CostEstimate(flops=flops, bytes_accessed=0, transcendentals=0),
        compiler_params=pltpu.CompilerParams(vmem_limit_bytes=VMEM_LIMIT),
    )(*args)


def sum_body(terms_ref, out_ref):
    total = terms_ref[0].astype(jnp.float32)
    for source in range(1, terms_ref.shape[0]):
        total = total + terms_ref[source].astype(jnp.float32)
    out_ref[...] = total


def stack_body(*refs):
    *came_refs, out_ref = refs
    start = 0
    for ref in came_refs:
        out_ref[start : start + ref.shape[0], : ref.shape[1]] = ref[...]
        start += ref.shape[0]


def read_slope(slope):
    chosen = slope[BLOCK : BLOCK + 1].astype(jnp.float32).astype(jnp.int32)
    return slope[:BLOCK], chosen


def own_body(near_ref, far_ref, near_slope_ref, far_slope_ref, acc_ref, set_ref):
    rows = jnp.concatenate([near_ref[...], far_ref[...]], axis=0)
    slope = jnp.concatenate([near_slope_ref[...], far_slope_ref[...]], axis=1)
    count = rows.shape[0]
    set_ref[:count, :] = rows
    set_ref[count:, :count] = slope
    wide = spread(*read_slope(slope), range(acc_ref.shape[0] // BLOCK))
    acc_ref[...] = jnp.dot(wide, rows, preferred_element_type=jnp.float32)


def mate_body(set_ref, acc_ref, out_ref):
    count = set_ref.shape[0] - BLOCK - NOTE
    slope, chosen = read_slope(set_ref[count:, :count])
    wide = spread(slope, chosen, range(acc_ref.shape[0] // BLOCK))
    out_ref[...] = acc_ref[...] + jnp.dot(
        wide, set_ref[:count, :], preferred_element_type=jnp.float32
    )


def set_slope(set_ref, weights):
    half = (set_ref.shape[0] - NOTE) // 2
    rows = jnp.concatenate([set_ref[:half, :], set_ref[half + NOTE :, :]], axis=0)
    note = set_ref[half : half + NOTE, :].astype(jnp.float32)
    codes = [read_note(note, which, half) for which in range(2)]
    chosen = jnp.concatenate([codes[0][0], codes[1][0]], axis=1)
    place = jnp.concatenate([codes[0][1], codes[1][1]], axis=1)
    return rows, slope_of(rows, weights, chosen, place), chosen


def cross_body(set_ref, weights_ref, acc_ref, out_ref):
    rows, slope, chosen = set_slope(set_ref, weights_ref[...])
    wide = spread(slope, chosen, range(acc_ref.shape[0] // BLOCK))
    out_ref[...] = acc_ref[...] + jnp.dot(wide, rows, preferred_element_type=jnp.float32)


def late_body(groups, set_ref, weights_ref, acc_ref, out_ref, mark_ref, held, sems):
    mark_ref[...] = jnp.zeros_like(mark_ref)
    rows, slope, chosen = set_slope(set_ref, weights_ref[...])
    blocks = acc_ref.shape[0] // BLOCK
    chunk = blocks // sems.shape[0]
    copies = []
    for part in range(sems.shape[0]):
        here = pl.ds(part * chunk * BLOCK, chunk * BLOCK)
        wide = spread(slope, chosen, range(part * chunk, (part + 1) * chunk))
        total = acc_ref[here, :] + jnp.dot(wide, rows, preferred_element_type=jnp.float32)
        held[here, :] = (total / groups).astype(held.dtype)
        copy = pltpu.make_async_copy(held.at[here, :], out_ref.at[here, :], sems.at[part])
        copy.start()
        copies.append(copy)
    for copy in copies:
        copy.wait()


def late(groups, crossed, weights, acc):
    out = like(*weights.shape, weights.dtype)
    chunks = 4
    return pl.pallas_call(
        lambda *refs: late_body(groups, *refs),
        out_shape=[out, like(1, BLOCK, jnp.int32)],
        in_specs=[pl.BlockSpec(memory_space=pltpu.VMEM)] * 3,
        out_specs=[pl.BlockSpec(memory_space=pl.ANY), pl.BlockSpec(memory_space=pltpu.VMEM)],
        scratch_shapes=[pltpu.VMEM(out.shape, out.dtype), pltpu.SemaphoreType.DMA((chunks,))],
        cost_estimate=pl.CostEstimate(flops=0, bytes_accessed=0, transcendentals=0),
        compiler_params=pltpu.CompilerParams(vmem_limit_bytes=VMEM_LIMIT),
    )(crossed, weights, acc)


def note_body(blocks_dev, q_home, me_ref, choice_ref, note_ref):
    choice = choice_ref[...].astype(jnp.int32)
    me, picks, count = me_ref[0], choice.shape[0] - 1, choice.shape[1]
    local, slot = choice[:picks] - me * blocks_dev, choice[picks:]
    inside = (local >= 0) & (local < blocks_dev)
    chosen = jnp.max(jnp.where(inside, local, -1), axis=0, keepdims=True)
    steps = lax.broadcasted_iota(jnp.int32, local.shape, 0)
    named = steps == lax.shift_right_logical(slot, BLOCK.bit_length() - 1)
    pblock = jnp.sum(jnp.where(named, local, 0), axis=0, keepdims=True)
    place = jnp.where(pblock == chosen, slot & (BLOCK - 1), -1)
    row = lax.broadcasted_iota(jnp.int32, (NOTE, count), 0)
    code = jnp.where(row == 0, chosen, jnp.where(row == 1, place, 0))
    half = count // 2
    lane = lax.broadcasted_iota(jnp.int32, (count, count), 1)
    source = lax.broadcasted_iota(jnp.int32, (count, count), 0)
    plane = (lane >= half).astype(jnp.int32) ^ (me & 1)
    step = lax.shift_right_logical(lane & (half - 1), q_home.bit_length() - 1)
    wanted = (2 * step + plane) * q_home + (lane & (q_home - 1))
    order = jnp.where(source == wanted, 1.0, 0.0).astype(jnp.bfloat16)
    code = jnp.dot(code.astype(jnp.bfloat16), order, preferred_element_type=jnp.float32)
    rest = jnp.zeros((NOTE - 4, half), jnp.float32)
    note = jnp.concatenate([code[:2, :half], code[:2, half:], rest], axis=0)
    note_ref[...] = jnp.zeros_like(note_ref)
    note_ref[:, :half] = note.astype(note_ref.dtype)


def dense_shards(queries, label_weights, sibling_blocks, positive_slot):
    q_home, width = queries.shape
    qcount = sibling_blocks.shape[0]
    half = qcount // 2
    lab_dev = label_weights.shape[0]
    homes = lax.axis_size("lab")
    groups = lax.axis_size("pb")
    me = lax.axis_index("lab")
    f32, bf16 = jnp.float32, jnp.bfloat16

    place = jnp.reshape(me // 2, (1,)).astype(jnp.int32)
    side = jnp.reshape(me % 2, (1,)).astype(jnp.int32)
    far_bit = groups // 2
    came = [swap(queries, "lab", 2 * step) for step in range(1, homes // 2)]
    held, weights = local_call(
        hold_body,
        [like(q_home, width, bf16), like(lab_dev, width, bf16)],
        [queries, label_weights],
    )
    choice = jnp.concatenate([sibling_blocks.T, positive_slot[None]], axis=0).astype(f32)
    note = local_call(
        lambda *refs: note_body(lab_dev // BLOCK, q_home, *refs),
        [like(NOTE, width, bf16)],
        [jnp.reshape(me, (1,)).astype(jnp.int32), choice],
    )[0]
    near, noted = local_call(
        join_body,
        [like(half, width, bf16), like(half + NOTE, width, bf16)],
        [place, held, *came, note],
        0,
        [weights],
    )
    far = swap(near, "lab", 1)
    work = 4 * half * lab_dev * width
    slope_like = like(BLOCK + NOTE, half, bf16)
    near_slope, near_copy, dq = grad_call(
        near_body,
        homes,
        q_home,
        [slope_like, like(half, width, bf16)],
        [side, near, weights, note],
        {},
        work,
    )
    cross_near = swap(noted, "pb", far_bit)
    cross_far = diagonal(near_copy, far_bit, 1)
    far_slope, dq = grad_call(
        far_body, homes, q_home, [slope_like], [side, far, weights, note, dq], {4: 1}, work
    )
    terms = lax.all_to_all(dq, "lab", split_axis=0, concat_axis=0, tiled=True)
    acc, own = local_call(
        own_body,
        [like(lab_dev, width, f32), like(qcount + BLOCK + NOTE, width, bf16)],
        [near, far, near_slope, far_slope],
        work,
    )
    mate = swap(own, "pb", 1)
    cross = local_call(
        stack_body, [like(qcount + NOTE, width, bf16)], [cross_near, cross_far], 0, [acc]
    )[0]
    cross_mate = swap(cross, "pb", 1)
    grown = like(lab_dev, width, f32)
    acc = local_call(cross_body, [grown], [cross, weights, acc], 20 * work)[0]
    acc = local_call(mate_body, [grown], [mate, acc], work)[0]
    weight_grad, mark = late(groups, cross_mate, weights, acc)
    query_grad = local_call(sum_body, [like(q_home, width, f32)], [terms], 0, [mark])[0]
    return (query_grad, weight_grad)


def solution(mesh):
    groups, homes = mesh.shape["pb"], mesh.shape["lab"]

    def shards(queries, label_weights, sibling_blocks, positive_slot):
        every_row_everywhere = homes == K
        few = groups * sibling_blocks.shape[0] <= 2 * label_weights.shape[0]
        paired = groups == 4 and homes & (homes - 1) == 0
        one_block = label_weights.shape[0] // BLOCK <= K
        plan = dense_shards if every_row_everywhere and few and paired and one_block else sparse_shards
        return plan(queries, label_weights, sibling_blocks, positive_slot)

    in_specs = (P(("pb", "lab"), None), P("lab", None), P("pb", None), P("pb"))
    out_specs = (P(("pb", "lab"), None), P("lab", None))
    return jax.shard_map(shards, mesh=mesh, in_specs=in_specs, out_specs=out_specs, check_vma=False)
```

```python
import jax
import jax.numpy as jnp
from jax import lax
from jax.experimental import pallas as pl
from jax.experimental.pallas import tpu as pltpu
from jax.sharding import PartitionSpec as P

BLOCK = 128
K = 8
NOTE = 16
VMEM_LIMIT = 24 * 1024 * 1024


def pack_index(touched, width_slots, fill_value):
    homes, count = touched.shape
    rank = jnp.cumsum(touched.astype(jnp.int32), axis=1) - 1
    place = jnp.where(touched, rank, width_slots)
    home_ids = jnp.broadcast_to(jnp.arange(homes, dtype=jnp.int32)[:, None], touched.shape)
    row_ids = jnp.broadcast_to(jnp.arange(count, dtype=jnp.int32)[None, :], touched.shape)
    table = (
        jnp.full((homes, width_slots + 1), fill_value, jnp.int32).at[home_ids, place].set(row_ids)
    )
    return table[:, :width_slots]


def sparse_shards(queries, label_weights, sibling_blocks, positive_slot):
    width = queries.shape[1]
    qcount = sibling_blocks.shape[0]
    lab_dev = label_weights.shape[0]
    blocks_dev = lab_dev // BLOCK
    first = lax.axis_index("lab") * blocks_dev
    local_ids = first + jnp.arange(blocks_dev, dtype=jnp.int32)
    pblock = jnp.take_along_axis(sibling_blocks, (positive_slot // BLOCK)[:, None], axis=1)[:, 0]
    positive = pblock * BLOCK + positive_slot % BLOCK
    label_ids = local_ids[:, None] * BLOCK + jnp.arange(BLOCK, dtype=jnp.int32)[None, :]
    chosen_all = jnp.any(sibling_blocks[:, :, None] == local_ids[None, None, :], axis=1)
    piece = lax.all_gather(queries, "lab", axis=0, tiled=True)
    count = piece.shape[0]
    scores = jnp.dot(piece, label_weights.T, preferred_element_type=jnp.float32)
    scores = scores.reshape(count, blocks_dev, BLOCK)
    target = (label_ids[None, :, :] == positive[:, None, None]).astype(jnp.float32)
    slope = jnp.where(chosen_all[:, :, None], jax.nn.sigmoid(scores) - target, 0.0)
    slope = slope.astype(jnp.bfloat16).reshape(count, lab_dev)
    dq_all = jnp.dot(slope, label_weights, preferred_element_type=jnp.float32)
    w_acc = lax.dot_general(
        slope, piece, (((0,), (0,)), ((), ())), preferred_element_type=jnp.float32
    )
    homes = lax.axis_size("lab")
    q_home = qcount // homes
    slots = q_home * K // homes
    touched = jnp.any(chosen_all, axis=1).reshape(homes, q_home)
    send_idx = pack_index(touched, slots, q_home)
    padded = jnp.concatenate(
        [dq_all.reshape(homes, q_home, width), jnp.zeros((homes, 1, width), jnp.float32)], axis=1
    )
    outgoing = jnp.take_along_axis(padded, send_idx[:, :, None], axis=1)
    incoming = lax.all_to_all(outgoing, "lab", split_axis=0, concat_axis=0, tiled=True)
    own_blocks = lax.dynamic_slice_in_dim(sibling_blocks, lax.axis_index("lab") * q_home, q_home, 0)
    source_ids = jnp.arange(homes, dtype=jnp.int32)
    own_touch = jnp.any(
        (own_blocks // blocks_dev)[:, :, None] == source_ids[None, None, :], axis=1
    ).T
    recv_idx = pack_index(own_touch, slots, q_home)
    query_grad = (
        jnp.zeros((q_home + 1, width), jnp.float32)
        .at[recv_idx.reshape(-1)]
        .add(incoming.reshape(-1, width))[:q_home]
    )
    groups = lax.axis_size("pb")
    total = lax.psum(w_acc, "pb")
    weight_grad = (total / groups).astype(jnp.bfloat16)
    return (query_grad, weight_grad)


def swap(value, axis, bit):
    count = lax.axis_size(axis)
    return lax.ppermute(value, axis, [(i, i ^ bit) for i in range(count)])


def diagonal(value, group_bit, home_bit):
    groups, homes = lax.axis_size("pb"), lax.axis_size("lab")
    pairs = [
        (g * homes + h, (g ^ group_bit) * homes + (h ^ home_bit))
        for g in range(groups)
        for h in range(homes)
    ]
    return lax.ppermute(value, ("pb", "lab"), pairs)


def local_call(body, outs, args, flops=0, follows=()):
    specs = [
        pl.BlockSpec(memory_space=pltpu.SMEM if arg.dtype == jnp.int32 else pltpu.VMEM)
        for arg in args
    ]
    given, later = len(args), len(args) + len(follows)
    return pl.pallas_call(
        lambda *refs: body(*refs[:given], *refs[later:]),
        out_shape=outs,
        in_specs=specs + [pl.BlockSpec(memory_space=pl.ANY)] * len(follows),
        out_specs=[pl.BlockSpec(memory_space=pltpu.VMEM)] * len(outs),
        cost_estimate=pl.CostEstimate(flops=flops, bytes_accessed=0, transcendentals=0),
        compiler_params=pltpu.CompilerParams(vmem_limit_bytes=VMEM_LIMIT),
    )(*args, *follows)


def like(rows, width, dtype):
    return jax.ShapeDtypeStruct((rows, width), dtype)


def join_body(*refs):
    *came_refs, note_ref, out_ref, noted_ref, others_ref = refs
    stack_body(*came_refs, out_ref)
    stack_body(*came_refs, note_ref, noted_ref)
    stack_body(*came_refs[1:], others_ref)


def hold_body(*refs):
    for source, held in zip(refs[: len(refs) // 2], refs[len(refs) // 2 :]):
        held[...] = source[...]


def slope_of(rows, weights, chosen, place):
    count, blocks = rows.shape[0], weights.shape[0] // BLOCK
    scores = lax.dot_general(
        weights, rows, (((1,), (1,)), ((), ())), preferred_element_type=jnp.float32
    )
    named = jnp.zeros((BLOCK, count), jnp.float32)
    for block in range(blocks):
        named = jnp.where(chosen == block, scores[block * BLOCK : (block + 1) * BLOCK], named)
    ids = lax.broadcasted_iota(jnp.int32, (BLOCK, count), 0)
    return (jax.nn.sigmoid(named) - jnp.where(ids == place, 1.0, 0.0)).astype(jnp.bfloat16)


def spread(slope, chosen, blocks):
    wide = slope.astype(jnp.float32)
    parts = [jnp.where(chosen == block, wide, 0.0).astype(slope.dtype) for block in blocks]
    return jnp.concatenate(parts, axis=0)


def read_note(note, which, count):
    chosen = note[2 * which : 2 * which + 1, :count].astype(jnp.int32)
    place = note[2 * which + 1 : 2 * which + 2, :count].astype(jnp.int32)
    return chosen, place


def grad_body(which, rows, weights_ref, note_ref, dq_ref, slope_ref):
    weights = weights_ref[...]
    note = note_ref[...].astype(jnp.float32)
    chosen, place = read_note(note, which, rows.shape[0])
    slope = slope_of(rows, weights, chosen, place)
    slope_ref[:BLOCK, :] = slope
    slope_ref[BLOCK:, :] = jnp.broadcast_to(chosen, (NOTE, rows.shape[0])).astype(slope.dtype)
    dq = lax.dot_general(
        spread(slope, chosen, range(weights.shape[0] // BLOCK)),
        weights,
        (((0,), (0,)), ((), ())),
        preferred_element_type=jnp.float32,
    )
    q_home = dq_ref.shape[1]
    for step in range(dq_ref.shape[0]):
        dq_ref[step] = dq[step * q_home : (step + 1) * q_home].astype(dq_ref.dtype)


def near_body(rows_ref, weights_ref, note_ref, dq_ref, slope_ref, copy_ref):
    copy_ref[...] = rows_ref[...]
    grad_body(0, rows_ref[...], weights_ref, note_ref, dq_ref, slope_ref)


def far_body(
    me_ref, near_ref, first_ref, others_ref, weights_ref, note_ref, slope_ref, out_ref, staged, sems
):
    me, steps = me_ref[0], near_ref.shape[0]
    near = [
        pltpu.make_async_copy(near_ref.at[step], out_ref.at[me ^ (2 * step)], sems.at[0, step])
        for step in range(steps)
    ]
    for copy in near:
        copy.start()
    rows = jnp.concatenate([first_ref[...], others_ref[...]], axis=0)
    grad_body(1, rows, weights_ref, note_ref, staged, slope_ref)
    far = [
        pltpu.make_async_copy(staged.at[step], out_ref.at[me ^ (2 * step + 1)], sems.at[1, step])
        for step in range(steps)
    ]
    for copy in far:
        copy.start()
    for copy in near + far:
        copy.wait()


def far_call(slope_like, args, flops):
    steps, q_home, width = args[1].shape
    vmem = pl.BlockSpec(memory_space=pltpu.VMEM)
    return pl.pallas_call(
        far_body,
        out_shape=[slope_like, jax.ShapeDtypeStruct((2 * steps, q_home, width), jnp.bfloat16)],
        in_specs=[pl.BlockSpec(memory_space=pltpu.SMEM)] + [vmem] * (len(args) - 1),
        out_specs=[vmem, pl.BlockSpec(memory_space=pl.ANY)],
        scratch_shapes=[
            pltpu.VMEM((steps, q_home, width), jnp.bfloat16),
            pltpu.SemaphoreType.DMA((2, steps)),
        ],
        cost_estimate=pl.CostEstimate(flops=flops, bytes_accessed=0, transcendentals=0),
        compiler_params=pltpu.CompilerParams(vmem_limit_bytes=VMEM_LIMIT),
    )(*args)


def sum_body(terms_ref, out_ref):
    total = terms_ref[0].astype(jnp.float32)
    for source in range(1, terms_ref.shape[0]):
        total = total + terms_ref[source].astype(jnp.float32)
    out_ref[...] = total


def stack_body(*refs):
    *came_refs, out_ref = refs
    start = 0
    for ref in came_refs:
        out_ref[start : start + ref.shape[0], : ref.shape[1]] = ref[...]
        start += ref.shape[0]


def read_slope(slope):
    chosen = slope[BLOCK : BLOCK + 1].astype(jnp.float32).astype(jnp.int32)
    return slope[:BLOCK], chosen


def own_body(near_ref, first_ref, others_ref, near_slope_ref, far_slope_ref, acc_ref, set_ref):
    rows = jnp.concatenate([near_ref[...], first_ref[...], others_ref[...]], axis=0)
    slope = jnp.concatenate([near_slope_ref[...], far_slope_ref[...]], axis=1)
    count = rows.shape[0]
    set_ref[:count, :] = rows
    set_ref[count:, :count] = slope
    wide = spread(*read_slope(slope), range(acc_ref.shape[0] // BLOCK))
    acc_ref[...] = jnp.dot(wide, rows, preferred_element_type=jnp.float32)


def mate_body(set_ref, acc_ref, out_ref):
    count = set_ref.shape[0] - BLOCK - NOTE
    slope, chosen = read_slope(set_ref[count:, :count])
    wide = spread(slope, chosen, range(acc_ref.shape[0] // BLOCK))
    out_ref[...] = acc_ref[...] + jnp.dot(
        wide, set_ref[:count, :], preferred_element_type=jnp.float32
    )


def set_slope(set_ref, weights):
    half = (set_ref.shape[0] - NOTE) // 2
    rows = jnp.concatenate([set_ref[:half, :], set_ref[half + NOTE :, :]], axis=0)
    note = set_ref[half : half + NOTE, :].astype(jnp.float32)
    codes = [read_note(note, which, half) for which in range(2)]
    chosen = jnp.concatenate([codes[0][0], codes[1][0]], axis=1)
    place = jnp.concatenate([codes[0][1], codes[1][1]], axis=1)
    return rows, slope_of(rows, weights, chosen, place), chosen


def cross_body(set_ref, weights_ref, acc_ref, out_ref):
    rows, slope, chosen = set_slope(set_ref, weights_ref[...])
    wide = spread(slope, chosen, range(acc_ref.shape[0] // BLOCK))
    out_ref[...] = acc_ref[...] + jnp.dot(wide, rows, preferred_element_type=jnp.float32)


def late_body(groups, set_ref, weights_ref, acc_ref, out_ref, mark_ref, held, sems):
    mark_ref[...] = jnp.zeros_like(mark_ref)
    rows, slope, chosen = set_slope(set_ref, weights_ref[...])
    blocks = acc_ref.shape[0] // BLOCK
    chunk = blocks // sems.shape[0]
    copies = []
    for part in range(sems.shape[0]):
        here = pl.ds(part * chunk * BLOCK, chunk * BLOCK)
        wide = spread(slope, chosen, range(part * chunk, (part + 1) * chunk))
        total = acc_ref[here, :] + jnp.dot(wide, rows, preferred_element_type=jnp.float32)
        held[here, :] = (total / groups).astype(held.dtype)
        copy = pltpu.make_async_copy(held.at[here, :], out_ref.at[here, :], sems.at[part])
        copy.start()
        copies.append(copy)
    for copy in copies:
        copy.wait()


def late(groups, crossed, weights, acc):
    out = like(*weights.shape, weights.dtype)
    chunks = 4
    return pl.pallas_call(
        lambda *refs: late_body(groups, *refs),
        out_shape=[out, like(1, BLOCK, jnp.int32)],
        in_specs=[pl.BlockSpec(memory_space=pltpu.VMEM)] * 3,
        out_specs=[pl.BlockSpec(memory_space=pl.ANY), pl.BlockSpec(memory_space=pltpu.VMEM)],
        scratch_shapes=[pltpu.VMEM(out.shape, out.dtype), pltpu.SemaphoreType.DMA((chunks,))],
        cost_estimate=pl.CostEstimate(flops=0, bytes_accessed=0, transcendentals=0),
        compiler_params=pltpu.CompilerParams(vmem_limit_bytes=VMEM_LIMIT),
    )(crossed, weights, acc)


def note_body(blocks_dev, q_home, me_ref, choice_ref, note_ref):
    choice = choice_ref[...].astype(jnp.int32)
    me, picks, count = me_ref[0], choice.shape[0] - 1, choice.shape[1]
    local, slot = choice[:picks] - me * blocks_dev, choice[picks:]
    inside = (local >= 0) & (local < blocks_dev)
    chosen = jnp.max(jnp.where(inside, local, -1), axis=0, keepdims=True)
    steps = lax.broadcasted_iota(jnp.int32, local.shape, 0)
    named = steps == lax.shift_right_logical(slot, BLOCK.bit_length() - 1)
    pblock = jnp.sum(jnp.where(named, local, 0), axis=0, keepdims=True)
    place = jnp.where(pblock == chosen, slot & (BLOCK - 1), -1)
    row = lax.broadcasted_iota(jnp.int32, (NOTE, count), 0)
    code = jnp.where(row == 0, chosen, jnp.where(row == 1, place, 0))
    half = count // 2
    lane = lax.broadcasted_iota(jnp.int32, (count, count), 1)
    source = lax.broadcasted_iota(jnp.int32, (count, count), 0)
    plane = (lane >= half).astype(jnp.int32)
    step = lax.shift_right_logical(lane & (half - 1), q_home.bit_length() - 1)
    wanted = ((2 * step + plane) ^ me) * q_home + (lane & (q_home - 1))
    order = jnp.where(source == wanted, 1.0, 0.0).astype(jnp.bfloat16)
    code = jnp.dot(code.astype(jnp.bfloat16), order, preferred_element_type=jnp.float32)
    rest = jnp.zeros((NOTE - 4, half), jnp.float32)
    note = jnp.concatenate([code[:2, :half], code[:2, half:], rest], axis=0)
    note_ref[...] = jnp.zeros_like(note_ref)
    note_ref[:, :half] = note.astype(note_ref.dtype)


def dense_shards(queries, label_weights, sibling_blocks, positive_slot):
    q_home, width = queries.shape
    qcount = sibling_blocks.shape[0]
    half = qcount // 2
    lab_dev = label_weights.shape[0]
    homes = lax.axis_size("lab")
    groups = lax.axis_size("pb")
    f32, bf16 = jnp.float32, jnp.bfloat16
    me = jnp.reshape(lax.axis_index("lab"), (1,)).astype(jnp.int32)
    far_bit = groups // 2
    came = [swap(queries, "lab", step) for step in range(2, homes, 2)]
    far_first = swap(queries, "lab", 1)
    held, weights = local_call(
        hold_body,
        [like(q_home, width, bf16), like(lab_dev, width, bf16)],
        [queries, label_weights],
    )
    choice = jnp.concatenate([sibling_blocks.T, positive_slot[None]], axis=0).astype(f32)
    note = local_call(
        lambda *refs: note_body(lab_dev // BLOCK, q_home, *refs),
        [like(NOTE, width, bf16)],
        [me, choice],
    )[0]
    near, noted, others = local_call(
        join_body,
        [like(half, width, bf16), like(half + NOTE, width, bf16), like(half - q_home, width, bf16)],
        [held, *came, note],
        0,
        [weights, far_first],
    )
    far_others = swap(others, "lab", 1)
    work = 4 * half * lab_dev * width
    slope_like = like(BLOCK + NOTE, half, bf16)
    near_dq, near_slope, near_copy = local_call(
        near_body,
        [
            jax.ShapeDtypeStruct((homes // 2, q_home, width), bf16),
            slope_like,
            like(half, width, bf16),
        ],
        [near, weights, note],
        work,
    )
    cross_near = swap(noted, "pb", far_bit)
    cross_far = diagonal(near_copy, far_bit, 1)
    far_slope, dq = far_call(
        slope_like, [me, near_dq, far_first, far_others, weights, note], work
    )
    terms = lax.all_to_all(dq, "lab", split_axis=0, concat_axis=0, tiled=True)
    acc, own = local_call(
        own_body,
        [like(lab_dev, width, f32), like(qcount + BLOCK + NOTE, width, bf16)],
        [near, far_first, far_others, near_slope, far_slope],
        work,
    )
    mate = swap(own, "pb", 1)
    cross = local_call(
        stack_body, [like(qcount + NOTE, width, bf16)], [cross_near, cross_far], 0, [acc]
    )[0]
    cross_mate = swap(cross, "pb", 1)
    grown = like(lab_dev, width, f32)
    acc = local_call(cross_body, [grown], [cross, weights, acc], 20 * work)[0]
    acc = local_call(mate_body, [grown], [mate, acc], work)[0]
    weight_grad, mark = late(groups, cross_mate, weights, acc)
    query_grad = local_call(sum_body, [like(q_home, width, f32)], [terms], 0, [mark])[0]
    return (query_grad, weight_grad)


def solution(mesh):
    groups, homes = mesh.shape["pb"], mesh.shape["lab"]

    def shards(queries, label_weights, sibling_blocks, positive_slot):
        every_row_everywhere = homes == K
        few = groups * sibling_blocks.shape[0] <= 2 * label_weights.shape[0]
        paired = groups == 4 and homes & (homes - 1) == 0
        one_block = label_weights.shape[0] // BLOCK <= K
        plan = dense_shards if every_row_everywhere and few and paired and one_block else sparse_shards
        return plan(queries, label_weights, sibling_blocks, positive_slot)

    in_specs = (P(("pb", "lab"), None), P("lab", None), P("pb", None), P("pb"))
    out_specs = (P(("pb", "lab"), None), P("lab", None))
    return jax.shard_map(shards, mesh=mesh, in_specs=in_specs, out_specs=out_specs, check_vma=False)
```

```python
import jax
import jax.numpy as jnp
from jax import lax
from jax.experimental import pallas as pl
from jax.experimental.pallas import tpu as pltpu
from jax.sharding import PartitionSpec as P

BLOCK = 128
K = 8
NOTE = 16
VMEM_LIMIT = 24 * 1024 * 1024


def pack_index(touched, width_slots, fill_value):
    homes, count = touched.shape
    rank = jnp.cumsum(touched.astype(jnp.int32), axis=1) - 1
    place = jnp.where(touched, rank, width_slots)
    home_ids = jnp.broadcast_to(jnp.arange(homes, dtype=jnp.int32)[:, None], touched.shape)
    row_ids = jnp.broadcast_to(jnp.arange(count, dtype=jnp.int32)[None, :], touched.shape)
    table = (
        jnp.full((homes, width_slots + 1), fill_value, jnp.int32).at[home_ids, place].set(row_ids)
    )
    return table[:, :width_slots]


def sparse_shards(queries, label_weights, sibling_blocks, positive_slot):
    width = queries.shape[1]
    qcount = sibling_blocks.shape[0]
    lab_dev = label_weights.shape[0]
    blocks_dev = lab_dev // BLOCK
    first = lax.axis_index("lab") * blocks_dev
    local_ids = first + jnp.arange(blocks_dev, dtype=jnp.int32)
    pblock = jnp.take_along_axis(sibling_blocks, (positive_slot // BLOCK)[:, None], axis=1)[:, 0]
    positive = pblock * BLOCK + positive_slot % BLOCK
    label_ids = local_ids[:, None] * BLOCK + jnp.arange(BLOCK, dtype=jnp.int32)[None, :]
    chosen_all = jnp.any(sibling_blocks[:, :, None] == local_ids[None, None, :], axis=1)
    piece = lax.all_gather(queries, "lab", axis=0, tiled=True)
    count = piece.shape[0]
    scores = jnp.dot(piece, label_weights.T, preferred_element_type=jnp.float32)
    scores = scores.reshape(count, blocks_dev, BLOCK)
    target = (label_ids[None, :, :] == positive[:, None, None]).astype(jnp.float32)
    slope = jnp.where(chosen_all[:, :, None], jax.nn.sigmoid(scores) - target, 0.0)
    slope = slope.astype(jnp.bfloat16).reshape(count, lab_dev)
    dq_all = jnp.dot(slope, label_weights, preferred_element_type=jnp.float32)
    w_acc = lax.dot_general(
        slope, piece, (((0,), (0,)), ((), ())), preferred_element_type=jnp.float32
    )
    homes = lax.axis_size("lab")
    q_home = qcount // homes
    slots = q_home * K // homes
    touched = jnp.any(chosen_all, axis=1).reshape(homes, q_home)
    send_idx = pack_index(touched, slots, q_home)
    padded = jnp.concatenate(
        [dq_all.reshape(homes, q_home, width), jnp.zeros((homes, 1, width), jnp.float32)], axis=1
    )
    outgoing = jnp.take_along_axis(padded, send_idx[:, :, None], axis=1)
    incoming = lax.all_to_all(outgoing, "lab", split_axis=0, concat_axis=0, tiled=True)
    own_blocks = lax.dynamic_slice_in_dim(sibling_blocks, lax.axis_index("lab") * q_home, q_home, 0)
    source_ids = jnp.arange(homes, dtype=jnp.int32)
    own_touch = jnp.any(
        (own_blocks // blocks_dev)[:, :, None] == source_ids[None, None, :], axis=1
    ).T
    recv_idx = pack_index(own_touch, slots, q_home)
    query_grad = (
        jnp.zeros((q_home + 1, width), jnp.float32)
        .at[recv_idx.reshape(-1)]
        .add(incoming.reshape(-1, width))[:q_home]
    )
    groups = lax.axis_size("pb")
    total = lax.psum(w_acc, "pb")
    weight_grad = (total / groups).astype(jnp.bfloat16)
    return (query_grad, weight_grad)


def swap(value, axis, bit):
    count = lax.axis_size(axis)
    return lax.ppermute(value, axis, [(i, i ^ bit) for i in range(count)])


def diagonal(value, group_bit, home_bit):
    groups, homes = lax.axis_size("pb"), lax.axis_size("lab")
    pairs = [
        (g * homes + h, (g ^ group_bit) * homes + (h ^ home_bit))
        for g in range(groups)
        for h in range(homes)
    ]
    return lax.ppermute(value, ("pb", "lab"), pairs)


def local_call(body, outs, args, flops=0, follows=()):
    specs = [
        pl.BlockSpec(memory_space=pltpu.SMEM if arg.dtype == jnp.int32 else pltpu.VMEM)
        for arg in args
    ]
    given, later = len(args), len(args) + len(follows)
    return pl.pallas_call(
        lambda *refs: body(*refs[:given], *refs[later:]),
        out_shape=outs,
        in_specs=specs + [pl.BlockSpec(memory_space=pl.ANY)] * len(follows),
        out_specs=[pl.BlockSpec(memory_space=pltpu.VMEM)] * len(outs),
        cost_estimate=pl.CostEstimate(flops=flops, bytes_accessed=0, transcendentals=0),
        compiler_params=pltpu.CompilerParams(vmem_limit_bytes=VMEM_LIMIT),
    )(*args, *follows)


def like(rows, width, dtype):
    return jax.ShapeDtypeStruct((rows, width), dtype)


def join_body(*refs):
    *came_refs, note_ref, out_ref, noted_ref = refs
    stack_body(*came_refs, out_ref)
    stack_body(*came_refs, note_ref, noted_ref)


def hold_body(*refs):
    for source, held in zip(refs[: len(refs) // 2], refs[len(refs) // 2 :]):
        held[...] = source[...]


def slope_of(rows, weights, chosen, place):
    count, blocks = rows.shape[0], weights.shape[0] // BLOCK
    scores = lax.dot_general(
        weights, rows, (((1,), (1,)), ((), ())), preferred_element_type=jnp.float32
    )
    named = jnp.zeros((BLOCK, count), jnp.float32)
    for block in range(blocks):
        named = jnp.where(chosen == block, scores[block * BLOCK : (block + 1) * BLOCK], named)
    ids = lax.broadcasted_iota(jnp.int32, (BLOCK, count), 0)
    return (jax.nn.sigmoid(named) - jnp.where(ids == place, 1.0, 0.0)).astype(jnp.bfloat16)


def spread(slope, chosen, blocks):
    wide = slope.astype(jnp.float32)
    parts = [jnp.where(chosen == block, wide, 0.0).astype(slope.dtype) for block in blocks]
    return jnp.concatenate(parts, axis=0)


def read_note(note, which, count):
    chosen = note[2 * which : 2 * which + 1, :count].astype(jnp.int32)
    place = note[2 * which + 1 : 2 * which + 2, :count].astype(jnp.int32)
    return chosen, place


def grad_body(which, rows_ref, weights_ref, note_ref, kept_ref, sent_ref, slope_ref):
    rows, weights = rows_ref[...], weights_ref[...]
    note = note_ref[...].astype(jnp.float32)
    chosen, place = read_note(note, which, rows.shape[0])
    slope = slope_of(rows, weights, chosen, place)
    slope_ref[:BLOCK, :] = slope
    slope_ref[BLOCK:, :] = jnp.broadcast_to(chosen, (NOTE, rows.shape[0])).astype(slope.dtype)
    dq = lax.dot_general(
        spread(slope, chosen, range(weights.shape[0] // BLOCK)),
        weights,
        (((0,), (0,)), ((), ())),
        preferred_element_type=jnp.float32,
    )
    halve(dq, kept_ref, sent_ref, kept_ref.shape[0] // 2)


def halve(terms, kept_ref, sent_ref, span):
    for start in range(0, kept_ref.shape[0], span):
        kept_ref[start : start + span, :] = terms[2 * start : 2 * start + span]
        sent = terms[2 * start + span : 2 * start + 2 * span]
        sent_ref[start : start + span, :] = sent.astype(sent_ref.dtype)


def near_body(rows_ref, weights_ref, note_ref, kept_ref, sent_ref, slope_ref, copy_ref):
    copy_ref[...] = rows_ref[...]
    grad_body(0, rows_ref, weights_ref, note_ref, kept_ref, sent_ref, slope_ref)


def far_body(rows_ref, weights_ref, note_ref, kept_ref, sent_ref, slope_ref):
    grad_body(1, rows_ref, weights_ref, note_ref, kept_ref, sent_ref, slope_ref)


def fold_body(terms_ref, came_ref, kept_ref, sent_ref):
    terms = terms_ref[...] + came_ref[...].astype(jnp.float32)
    halve(terms, kept_ref, sent_ref, kept_ref.shape[0])


def sum_body(kept_ref, *refs):
    *term_refs, out_ref = refs
    total = kept_ref[...]
    for ref in term_refs:
        total = total + ref[...].astype(jnp.float32)
    out_ref[...] = total.astype(out_ref.dtype)


def stack_body(*refs):
    *came_refs, out_ref = refs
    start = 0
    for ref in came_refs:
        out_ref[start : start + ref.shape[0], : ref.shape[1]] = ref[...]
        start += ref.shape[0]


def read_slope(slope):
    chosen = slope[BLOCK : BLOCK + 1].astype(jnp.float32).astype(jnp.int32)
    return slope[:BLOCK], chosen


def own_body(near_ref, far_ref, near_slope_ref, far_slope_ref, acc_ref, set_ref):
    rows = jnp.concatenate([near_ref[...], far_ref[...]], axis=0)
    slope = jnp.concatenate([near_slope_ref[...], far_slope_ref[...]], axis=1)
    count = rows.shape[0]
    set_ref[:count, :] = rows
    set_ref[count:, :count] = slope
    wide = spread(*read_slope(slope), range(acc_ref.shape[0] // BLOCK))
    acc_ref[...] = jnp.dot(wide, rows, preferred_element_type=jnp.float32)


def mate_body(set_ref, acc_ref, out_ref):
    count = set_ref.shape[0] - BLOCK - NOTE
    slope, chosen = read_slope(set_ref[count:, :count])
    wide = spread(slope, chosen, range(acc_ref.shape[0] // BLOCK))
    out_ref[...] = acc_ref[...] + jnp.dot(
        wide, set_ref[:count, :], preferred_element_type=jnp.float32
    )


def set_slope(set_ref, weights):
    half = (set_ref.shape[0] - NOTE) // 2
    rows = jnp.concatenate([set_ref[:half, :], set_ref[half + NOTE :, :]], axis=0)
    note = set_ref[half : half + NOTE, :].astype(jnp.float32)
    codes = [read_note(note, which, half) for which in range(2)]
    chosen = jnp.concatenate([codes[0][0], codes[1][0]], axis=1)
    place = jnp.concatenate([codes[0][1], codes[1][1]], axis=1)
    return rows, slope_of(rows, weights, chosen, place), chosen


def cross_body(set_ref, weights_ref, acc_ref, out_ref):
    rows, slope, chosen = set_slope(set_ref, weights_ref[...])
    wide = spread(slope, chosen, range(acc_ref.shape[0] // BLOCK))
    out_ref[...] = acc_ref[...] + jnp.dot(wide, rows, preferred_element_type=jnp.float32)


def late_body(groups, set_ref, weights_ref, acc_ref, out_ref, mark_ref, held, sems):
    mark_ref[...] = jnp.zeros_like(mark_ref)
    rows, slope, chosen = set_slope(set_ref, weights_ref[...])
    blocks = acc_ref.shape[0] // BLOCK
    chunk = blocks // sems.shape[0]
    copies = []
    for part in range(sems.shape[0]):
        here = pl.ds(part * chunk * BLOCK, chunk * BLOCK)
        wide = spread(slope, chosen, range(part * chunk, (part + 1) * chunk))
        total = acc_ref[here, :] + jnp.dot(wide, rows, preferred_element_type=jnp.float32)
        held[here, :] = (total / groups).astype(held.dtype)
        copy = pltpu.make_async_copy(held.at[here, :], out_ref.at[here, :], sems.at[part])
        copy.start()
        copies.append(copy)
    for copy in copies:
        copy.wait()


def late(groups, crossed, weights, acc):
    out = like(*weights.shape, weights.dtype)
    chunks = 4
    return pl.pallas_call(
        lambda *refs: late_body(groups, *refs),
        out_shape=[out, like(1, BLOCK, jnp.int32)],
        in_specs=[pl.BlockSpec(memory_space=pltpu.VMEM)] * 3,
        out_specs=[pl.BlockSpec(memory_space=pl.ANY), pl.BlockSpec(memory_space=pltpu.VMEM)],
        scratch_shapes=[pltpu.VMEM(out.shape, out.dtype), pltpu.SemaphoreType.DMA((chunks,))],
        cost_estimate=pl.CostEstimate(flops=0, bytes_accessed=0, transcendentals=0),
        compiler_params=pltpu.CompilerParams(vmem_limit_bytes=VMEM_LIMIT),
    )(crossed, weights, acc)


def note_body(blocks_dev, q_home, me_ref, choice_ref, note_ref):
    choice = choice_ref[...].astype(jnp.int32)
    me, picks, count = me_ref[0], choice.shape[0] - 1, choice.shape[1]
    local, slot = choice[:picks] - me * blocks_dev, choice[picks:]
    inside = (local >= 0) & (local < blocks_dev)
    chosen = jnp.max(jnp.where(inside, local, -1), axis=0, keepdims=True)
    steps = lax.broadcasted_iota(jnp.int32, local.shape, 0)
    named = steps == lax.shift_right_logical(slot, BLOCK.bit_length() - 1)
    pblock = jnp.sum(jnp.where(named, local, 0), axis=0, keepdims=True)
    place = jnp.where(pblock == chosen, slot & (BLOCK - 1), -1)
    row = lax.broadcasted_iota(jnp.int32, (NOTE, count), 0)
    code = jnp.where(row == 0, chosen, jnp.where(row == 1, place, 0))
    half = count // 2
    lane = lax.broadcasted_iota(jnp.int32, (count, count), 1)
    source = lax.broadcasted_iota(jnp.int32, (count, count), 0)
    plane = (lane >= half).astype(jnp.int32)
    step = lax.shift_right_logical(lane & (half - 1), q_home.bit_length() - 1)
    wanted = ((2 * step + plane) ^ me) * q_home + (lane & (q_home - 1))
    order = jnp.where(source == wanted, 1.0, 0.0).astype(jnp.bfloat16)
    code = jnp.dot(code.astype(jnp.bfloat16), order, preferred_element_type=jnp.float32)
    rest = jnp.zeros((NOTE - 4, half), jnp.float32)
    note = jnp.concatenate([code[:2, :half], code[:2, half:], rest], axis=0)
    note_ref[...] = jnp.zeros_like(note_ref)
    note_ref[:, :half] = note.astype(note_ref.dtype)


def dense_shards(queries, label_weights, sibling_blocks, positive_slot):
    q_home, width = queries.shape
    qcount = sibling_blocks.shape[0]
    half = qcount // 2
    lab_dev = label_weights.shape[0]
    homes = lax.axis_size("lab")
    groups = lax.axis_size("pb")
    f32, bf16 = jnp.float32, jnp.bfloat16
    me = jnp.reshape(lax.axis_index("lab"), (1,)).astype(jnp.int32)
    far_bit = groups // 2
    came = [swap(queries, "lab", step) for step in range(2, homes, 2)]
    held, weights = local_call(
        hold_body,
        [like(q_home, width, bf16), like(lab_dev, width, bf16)],
        [queries, label_weights],
    )
    choice = jnp.concatenate([sibling_blocks.T, positive_slot[None]], axis=0).astype(f32)
    note = local_call(
        lambda *refs: note_body(lab_dev // BLOCK, q_home, *refs),
        [like(NOTE, width, bf16)],
        [me, choice],
    )[0]
    near, noted = local_call(
        join_body,
        [like(half, width, bf16), like(half + NOTE, width, bf16)],
        [held, *came, note],
        0,
        [weights],
    )
    far = swap(near, "lab", 1)
    work = 4 * half * lab_dev * width
    slope_like = like(BLOCK + NOTE, half, bf16)
    pair = [like(half // 2, width, f32), like(half // 2, width, bf16)]
    single = [like(q_home, width, f32), like(q_home, width, bf16)]
    near_kept, near_sent, near_slope, near_copy = local_call(
        near_body,
        pair + [slope_like, like(half, width, bf16)],
        [near, weights, note],
        work,
    )
    cross_near = swap(noted, "pb", far_bit)
    cross_far = diagonal(near_copy, far_bit, 1)
    far_kept, far_sent, far_slope = local_call(
        far_body, pair + [slope_like], [far, weights, note], work, [near_slope]
    )
    far_came, near_came = swap(far_sent, "lab", 2), swap(near_sent, "lab", 2)
    acc, own = local_call(
        own_body,
        [like(lab_dev, width, f32), like(qcount + BLOCK + NOTE, width, bf16)],
        [near, far, near_slope, far_slope],
        work,
    )
    mate = swap(own, "pb", 1)
    far_kept, far_sent = local_call(fold_body, single, [far_kept, far_came], 0, [acc])
    far_came = swap(far_sent, "lab", 4)
    near_kept, near_sent = local_call(fold_body, single, [near_kept, near_came], 0, [far_kept])
    near_came = swap(near_sent, "lab", 4)
    cross = local_call(
        stack_body, [like(qcount + NOTE, width, bf16)], [cross_near, cross_far], 0, [far_kept]
    )[0]
    cross_mate = swap(cross, "pb", 1)
    grown = like(lab_dev, width, f32)
    acc = local_call(cross_body, [grown], [cross, weights, acc], 20 * work, [near_kept])[0]
    far_sent = local_call(
        sum_body, [like(q_home, width, bf16)], [far_kept, far_came], 0, [acc]
    )[0]
    far_came = swap(far_sent, "lab", 1)
    acc = local_call(mate_body, [grown], [mate, acc], work, [far_sent])[0]
    weight_grad, mark = late(groups, cross_mate, weights, acc)
    query_grad = local_call(
        sum_body, [like(q_home, width, f32)], [near_kept, near_came, far_came], 0, [mark]
    )[0]
    return (query_grad, weight_grad)


def solution(mesh):
    groups, homes = mesh.shape["pb"], mesh.shape["lab"]

    def shards(queries, label_weights, sibling_blocks, positive_slot):
        every_row_everywhere = homes == K
        few = groups * sibling_blocks.shape[0] <= 2 * label_weights.shape[0]
        paired = groups == 4 and homes & (homes - 1) == 0
        one_block = label_weights.shape[0] // BLOCK <= K
        plan = dense_shards if every_row_everywhere and few and paired and one_block else sparse_shards
        return plan(queries, label_weights, sibling_blocks, positive_slot)

    in_specs = (P(("pb", "lab"), None), P("lab", None), P("pb", None), P("pb"))
    out_specs = (P(("pb", "lab"), None), P("lab", None))
    return jax.shard_map(shards, mesh=mesh, in_specs=in_specs, out_specs=out_specs, check_vma=False)
```

```python
import jax
import jax.numpy as jnp
from jax import lax
from jax.experimental import pallas as pl
from jax.experimental.pallas import tpu as pltpu
from jax.sharding import PartitionSpec as P

BLOCK = 128
K = 8
NOTE = 16
VMEM_LIMIT = 24 * 1024 * 1024


def pack_index(touched, width_slots, fill_value):
    homes, count = touched.shape
    rank = jnp.cumsum(touched.astype(jnp.int32), axis=1) - 1
    place = jnp.where(touched, rank, width_slots)
    home_ids = jnp.broadcast_to(jnp.arange(homes, dtype=jnp.int32)[:, None], touched.shape)
    row_ids = jnp.broadcast_to(jnp.arange(count, dtype=jnp.int32)[None, :], touched.shape)
    table = (
        jnp.full((homes, width_slots + 1), fill_value, jnp.int32).at[home_ids, place].set(row_ids)
    )
    return table[:, :width_slots]


def sparse_shards(queries, label_weights, sibling_blocks, positive_slot):
    width = queries.shape[1]
    qcount = sibling_blocks.shape[0]
    lab_dev = label_weights.shape[0]
    blocks_dev = lab_dev // BLOCK
    first = lax.axis_index("lab") * blocks_dev
    local_ids = first + jnp.arange(blocks_dev, dtype=jnp.int32)
    pblock = jnp.take_along_axis(sibling_blocks, (positive_slot // BLOCK)[:, None], axis=1)[:, 0]
    positive = pblock * BLOCK + positive_slot % BLOCK
    label_ids = local_ids[:, None] * BLOCK + jnp.arange(BLOCK, dtype=jnp.int32)[None, :]
    chosen_all = jnp.any(sibling_blocks[:, :, None] == local_ids[None, None, :], axis=1)
    piece = lax.all_gather(queries, "lab", axis=0, tiled=True)
    count = piece.shape[0]
    scores = jnp.dot(piece, label_weights.T, preferred_element_type=jnp.float32)
    scores = scores.reshape(count, blocks_dev, BLOCK)
    target = (label_ids[None, :, :] == positive[:, None, None]).astype(jnp.float32)
    slope = jnp.where(chosen_all[:, :, None], jax.nn.sigmoid(scores) - target, 0.0)
    slope = slope.astype(jnp.bfloat16).reshape(count, lab_dev)
    dq_all = jnp.dot(slope, label_weights, preferred_element_type=jnp.float32)
    w_acc = lax.dot_general(
        slope, piece, (((0,), (0,)), ((), ())), preferred_element_type=jnp.float32
    )
    homes = lax.axis_size("lab")
    q_home = qcount // homes
    slots = q_home * K // homes
    touched = jnp.any(chosen_all, axis=1).reshape(homes, q_home)
    send_idx = pack_index(touched, slots, q_home)
    padded = jnp.concatenate(
        [dq_all.reshape(homes, q_home, width), jnp.zeros((homes, 1, width), jnp.float32)], axis=1
    )
    outgoing = jnp.take_along_axis(padded, send_idx[:, :, None], axis=1)
    incoming = lax.all_to_all(outgoing, "lab", split_axis=0, concat_axis=0, tiled=True)
    own_blocks = lax.dynamic_slice_in_dim(sibling_blocks, lax.axis_index("lab") * q_home, q_home, 0)
    source_ids = jnp.arange(homes, dtype=jnp.int32)
    own_touch = jnp.any(
        (own_blocks // blocks_dev)[:, :, None] == source_ids[None, None, :], axis=1
    ).T
    recv_idx = pack_index(own_touch, slots, q_home)
    query_grad = (
        jnp.zeros((q_home + 1, width), jnp.float32)
        .at[recv_idx.reshape(-1)]
        .add(incoming.reshape(-1, width))[:q_home]
    )
    groups = lax.axis_size("pb")
    total = lax.psum(w_acc, "pb")
    weight_grad = (total / groups).astype(jnp.bfloat16)
    return (query_grad, weight_grad)


def swap(value, axis, bit):
    count = lax.axis_size(axis)
    return lax.ppermute(value, axis, [(i, i ^ bit) for i in range(count)])


def diagonal(value, group_bit, home_bit):
    groups, homes = lax.axis_size("pb"), lax.axis_size("lab")
    pairs = [
        (g * homes + h, (g ^ group_bit) * homes + (h ^ home_bit))
        for g in range(groups)
        for h in range(homes)
    ]
    return lax.ppermute(value, ("pb", "lab"), pairs)


def local_call(body, outs, args, flops=0, follows=()):
    specs = [
        pl.BlockSpec(memory_space=pltpu.SMEM if arg.dtype == jnp.int32 else pltpu.VMEM)
        for arg in args
    ]
    given, later = len(args), len(args) + len(follows)
    return pl.pallas_call(
        lambda *refs: body(*refs[:given], *refs[later:]),
        out_shape=outs,
        in_specs=specs + [pl.BlockSpec(memory_space=pl.ANY)] * len(follows),
        out_specs=[pl.BlockSpec(memory_space=pltpu.VMEM)] * len(outs),
        cost_estimate=pl.CostEstimate(flops=flops, bytes_accessed=0, transcendentals=0),
        compiler_params=pltpu.CompilerParams(vmem_limit_bytes=VMEM_LIMIT),
    )(*args, *follows)


def like(rows, width, dtype):
    return jax.ShapeDtypeStruct((rows, width), dtype)


def join_body(*refs):
    *came_refs, note_ref, out_ref, noted_ref = refs
    stack_body(*came_refs, out_ref)
    stack_body(*came_refs, note_ref, noted_ref)


def hold_body(*refs):
    for source, held in zip(refs[: len(refs) // 2], refs[len(refs) // 2 :]):
        held[...] = source[...]


def slope_of(rows, weights, chosen, place):
    count, blocks = rows.shape[0], weights.shape[0] // BLOCK
    scores = lax.dot_general(
        weights, rows, (((1,), (1,)), ((), ())), preferred_element_type=jnp.float32
    )
    named = jnp.zeros((BLOCK, count), jnp.float32)
    for block in range(blocks):
        named = jnp.where(chosen == block, scores[block * BLOCK : (block + 1) * BLOCK], named)
    ids = lax.broadcasted_iota(jnp.int32, (BLOCK, count), 0)
    return (jax.nn.sigmoid(named) - jnp.where(ids == place, 1.0, 0.0)).astype(jnp.bfloat16)


def spread(slope, chosen, blocks):
    wide = slope.astype(jnp.float32)
    parts = [jnp.where(chosen == block, wide, 0.0).astype(slope.dtype) for block in blocks]
    return jnp.concatenate(parts, axis=0)


def read_note(note, which, count):
    chosen = note[2 * which : 2 * which + 1, :count].astype(jnp.int32)
    place = note[2 * which + 1 : 2 * which + 2, :count].astype(jnp.int32)
    return chosen, place


def grad_body(which, rows_ref, weights_ref, note_ref, kept_ref, sent_ref, slope_ref):
    rows, weights = rows_ref[...], weights_ref[...]
    note = note_ref[...].astype(jnp.float32)
    chosen, place = read_note(note, which, rows.shape[0])
    slope = slope_of(rows, weights, chosen, place)
    slope_ref[:BLOCK, :] = slope
    slope_ref[BLOCK:, :] = jnp.broadcast_to(chosen, (NOTE, rows.shape[0])).astype(slope.dtype)
    dq = lax.dot_general(
        spread(slope, chosen, range(weights.shape[0] // BLOCK)),
        weights,
        (((0,), (0,)), ((), ())),
        preferred_element_type=jnp.float32,
    )
    halve(dq, kept_ref, sent_ref, kept_ref.shape[0] // 2)


def halve(terms, kept_ref, sent_ref, span):
    for start in range(0, kept_ref.shape[0], span):
        kept_ref[start : start + span, :] = terms[2 * start : 2 * start + span]
        sent = terms[2 * start + span : 2 * start + 2 * span]
        sent_ref[start : start + span, :] = sent.astype(sent_ref.dtype)


def near_body(rows_ref, weights_ref, note_ref, kept_ref, sent_ref, slope_ref, copy_ref):
    copy_ref[...] = rows_ref[...]
    grad_body(0, rows_ref, weights_ref, note_ref, kept_ref, sent_ref, slope_ref)


def far_body(rows_ref, weights_ref, note_ref, kept_ref, sent_ref, slope_ref):
    grad_body(1, rows_ref, weights_ref, note_ref, kept_ref, sent_ref, slope_ref)


def fold_body(far_ref, far_came_ref, near_ref, near_came_ref, far_kept, near_kept, sent_ref):
    span = far_kept.shape[0]
    far = far_ref[...] + far_came_ref[...].astype(jnp.float32)
    near = near_ref[...] + near_came_ref[...].astype(jnp.float32)
    halve(far, far_kept, sent_ref.at[:span], span)
    halve(near, near_kept, sent_ref.at[span:], span)


def home_body(far_ref, near_ref, came_ref, sent_ref, kept_ref):
    span = far_ref.shape[0]
    came = came_ref[...].astype(jnp.float32)
    sent_ref[...] = (far_ref[...] + came[:span]).astype(sent_ref.dtype)
    kept_ref[...] = near_ref[...] + came[span:]


def sum_body(kept_ref, *refs):
    *term_refs, out_ref = refs
    total = kept_ref[...]
    for ref in term_refs:
        total = total + ref[...].astype(jnp.float32)
    out_ref[...] = total.astype(out_ref.dtype)


def stack_body(*refs):
    *came_refs, out_ref = refs
    start = 0
    for ref in came_refs:
        out_ref[start : start + ref.shape[0], : ref.shape[1]] = ref[...]
        start += ref.shape[0]


def read_slope(slope):
    chosen = slope[BLOCK : BLOCK + 1].astype(jnp.float32).astype(jnp.int32)
    return slope[:BLOCK], chosen


def own_body(near_ref, far_ref, near_slope_ref, far_slope_ref, acc_ref, set_ref):
    rows = jnp.concatenate([near_ref[...], far_ref[...]], axis=0)
    slope = jnp.concatenate([near_slope_ref[...], far_slope_ref[...]], axis=1)
    count = rows.shape[0]
    set_ref[:count, :] = rows
    set_ref[count:, :count] = slope
    wide = spread(*read_slope(slope), range(acc_ref.shape[0] // BLOCK))
    acc_ref[...] = jnp.dot(wide, rows, preferred_element_type=jnp.float32)


def mate_body(set_ref, acc_ref, out_ref):
    count = set_ref.shape[0] - BLOCK - NOTE
    slope, chosen = read_slope(set_ref[count:, :count])
    wide = spread(slope, chosen, range(acc_ref.shape[0] // BLOCK))
    out_ref[...] = acc_ref[...] + jnp.dot(
        wide, set_ref[:count, :], preferred_element_type=jnp.float32
    )


def set_slope(set_ref, weights):
    half = (set_ref.shape[0] - NOTE) // 2
    rows = jnp.concatenate([set_ref[:half, :], set_ref[half + NOTE :, :]], axis=0)
    note = set_ref[half : half + NOTE, :].astype(jnp.float32)
    codes = [read_note(note, which, half) for which in range(2)]
    chosen = jnp.concatenate([codes[0][0], codes[1][0]], axis=1)
    place = jnp.concatenate([codes[0][1], codes[1][1]], axis=1)
    return rows, slope_of(rows, weights, chosen, place), chosen


def cross_body(set_ref, weights_ref, acc_ref, out_ref):
    rows, slope, chosen = set_slope(set_ref, weights_ref[...])
    wide = spread(slope, chosen, range(acc_ref.shape[0] // BLOCK))
    out_ref[...] = acc_ref[...] + jnp.dot(wide, rows, preferred_element_type=jnp.float32)


def late_body(groups, set_ref, weights_ref, acc_ref, out_ref, mark_ref, held, sems):
    mark_ref[...] = jnp.zeros_like(mark_ref)
    rows, slope, chosen = set_slope(set_ref, weights_ref[...])
    blocks = acc_ref.shape[0] // BLOCK
    chunk = blocks // sems.shape[0]
    copies = []
    for part in range(sems.shape[0]):
        here = pl.ds(part * chunk * BLOCK, chunk * BLOCK)
        wide = spread(slope, chosen, range(part * chunk, (part + 1) * chunk))
        total = acc_ref[here, :] + jnp.dot(wide, rows, preferred_element_type=jnp.float32)
        held[here, :] = (total / groups).astype(held.dtype)
        copy = pltpu.make_async_copy(held.at[here, :], out_ref.at[here, :], sems.at[part])
        copy.start()
        copies.append(copy)
    for copy in copies:
        copy.wait()


def late(groups, crossed, weights, acc):
    out = like(*weights.shape, weights.dtype)
    chunks = 4
    return pl.pallas_call(
        lambda *refs: late_body(groups, *refs),
        out_shape=[out, like(1, BLOCK, jnp.int32)],
        in_specs=[pl.BlockSpec(memory_space=pltpu.VMEM)] * 3,
        out_specs=[pl.BlockSpec(memory_space=pl.ANY), pl.BlockSpec(memory_space=pltpu.VMEM)],
        scratch_shapes=[pltpu.VMEM(out.shape, out.dtype), pltpu.SemaphoreType.DMA((chunks,))],
        cost_estimate=pl.CostEstimate(flops=0, bytes_accessed=0, transcendentals=0),
        compiler_params=pltpu.CompilerParams(vmem_limit_bytes=VMEM_LIMIT),
    )(crossed, weights, acc)


def note_body(blocks_dev, q_home, me_ref, choice_ref, note_ref):
    choice = choice_ref[...].astype(jnp.int32)
    me, picks, count = me_ref[0], choice.shape[0] - 1, choice.shape[1]
    local, slot = choice[:picks] - me * blocks_dev, choice[picks:]
    inside = (local >= 0) & (local < blocks_dev)
    chosen = jnp.max(jnp.where(inside, local, -1), axis=0, keepdims=True)
    steps = lax.broadcasted_iota(jnp.int32, local.shape, 0)
    named = steps == lax.shift_right_logical(slot, BLOCK.bit_length() - 1)
    pblock = jnp.sum(jnp.where(named, local, 0), axis=0, keepdims=True)
    place = jnp.where(pblock == chosen, slot & (BLOCK - 1), -1)
    row = lax.broadcasted_iota(jnp.int32, (NOTE, count), 0)
    code = jnp.where(row == 0, chosen, jnp.where(row == 1, place, 0))
    half = count // 2
    lane = lax.broadcasted_iota(jnp.int32, (count, count), 1)
    source = lax.broadcasted_iota(jnp.int32, (count, count), 0)
    plane = (lane >= half).astype(jnp.int32)
    step = lax.shift_right_logical(lane & (half - 1), q_home.bit_length() - 1)
    wanted = ((2 * step + plane) ^ me) * q_home + (lane & (q_home - 1))
    order = jnp.where(source == wanted, 1.0, 0.0).astype(jnp.bfloat16)
    code = jnp.dot(code.astype(jnp.bfloat16), order, preferred_element_type=jnp.float32)
    rest = jnp.zeros((NOTE - 4, half), jnp.float32)
    note = jnp.concatenate([code[:2, :half], code[:2, half:], rest], axis=0)
    note_ref[...] = jnp.zeros_like(note_ref)
    note_ref[:, :half] = note.astype(note_ref.dtype)


def dense_shards(queries, label_weights, sibling_blocks, positive_slot):
    q_home, width = queries.shape
    qcount = sibling_blocks.shape[0]
    half = qcount // 2
    lab_dev = label_weights.shape[0]
    homes = lax.axis_size("lab")
    groups = lax.axis_size("pb")
    f32, bf16 = jnp.float32, jnp.bfloat16
    me = jnp.reshape(lax.axis_index("lab"), (1,)).astype(jnp.int32)
    far_bit = groups // 2
    came = [swap(queries, "lab", step) for step in range(2, homes, 2)]
    held, weights = local_call(
        hold_body,
        [like(q_home, width, bf16), like(lab_dev, width, bf16)],
        [queries, label_weights],
    )
    choice = jnp.concatenate([sibling_blocks.T, positive_slot[None]], axis=0).astype(f32)
    note = local_call(
        lambda *refs: note_body(lab_dev // BLOCK, q_home, *refs),
        [like(NOTE, width, bf16)],
        [me, choice],
    )[0]
    near, noted = local_call(
        join_body,
        [like(half, width, bf16), like(half + NOTE, width, bf16)],
        [held, *came, note],
        0,
        [weights],
    )
    far = swap(near, "lab", 1)
    work = 4 * half * lab_dev * width
    slope_like = like(BLOCK + NOTE, half, bf16)
    pair = [like(half // 2, width, f32), like(half // 2, width, bf16)]
    near_kept, near_sent, near_slope, near_copy = local_call(
        near_body,
        pair + [slope_like, like(half, width, bf16)],
        [near, weights, note],
        work,
    )
    cross_near = swap(noted, "pb", far_bit)
    cross_far = diagonal(near_copy, far_bit, 1)
    far_kept, far_sent, far_slope = local_call(
        far_body, pair + [slope_like], [far, weights, note], work, [near_slope]
    )
    far_came, near_came = swap(far_sent, "lab", 2), swap(near_sent, "lab", 2)
    acc, own = local_call(
        own_body,
        [like(lab_dev, width, f32), like(qcount + BLOCK + NOTE, width, bf16)],
        [near, far, near_slope, far_slope],
        work,
    )
    mate = swap(own, "pb", 1)
    single = like(q_home, width, f32)
    far_kept, near_kept, sent = local_call(
        fold_body,
        [single, single, like(2 * q_home, width, bf16)],
        [far_kept, far_came, near_kept, near_came],
        0,
        [acc],
    )
    came = swap(sent, "lab", 4)
    cross = local_call(
        stack_body, [like(qcount + NOTE, width, bf16)], [cross_near, cross_far], 0, [far_kept]
    )[0]
    cross_mate = swap(cross, "pb", 1)
    grown = like(lab_dev, width, f32)
    acc = local_call(cross_body, [grown], [cross, weights, acc], 20 * work)[0]
    acc = local_call(mate_body, [grown], [mate, acc], work)[0]
    far_sent, kept = local_call(
        home_body, [like(q_home, width, bf16), single], [far_kept, near_kept, came], 0, [acc]
    )
    far_came = swap(far_sent, "lab", 1)
    weight_grad, mark = late(groups, cross_mate, weights, acc)
    query_grad = local_call(sum_body, [single], [kept, far_came], 0, [mark])[0]
    return (query_grad, weight_grad)


def solution(mesh):
    groups, homes = mesh.shape["pb"], mesh.shape["lab"]

    def shards(queries, label_weights, sibling_blocks, positive_slot):
        every_row_everywhere = homes == K
        few = groups * sibling_blocks.shape[0] <= 2 * label_weights.shape[0]
        paired = groups == 4 and homes & (homes - 1) == 0
        one_block = label_weights.shape[0] // BLOCK <= K
        plan = dense_shards if every_row_everywhere and few and paired and one_block else sparse_shards
        return plan(queries, label_weights, sibling_blocks, positive_slot)

    in_specs = (P(("pb", "lab"), None), P("lab", None), P("pb", None), P("pb"))
    out_specs = (P(("pb", "lab"), None), P("lab", None))
    return jax.shard_map(shards, mesh=mesh, in_specs=in_specs, out_specs=out_specs, check_vma=False)
```

```python
import jax
import jax.numpy as jnp
from jax import lax
from jax.experimental import pallas as pl
from jax.experimental.pallas import tpu as pltpu
from jax.sharding import PartitionSpec as P

BLOCK = 128
K = 8
NOTE = 16
VMEM_LIMIT = 24 * 1024 * 1024


def pack_index(touched, width_slots, fill_value):
    homes, count = touched.shape
    rank = jnp.cumsum(touched.astype(jnp.int32), axis=1) - 1
    place = jnp.where(touched, rank, width_slots)
    home_ids = jnp.broadcast_to(jnp.arange(homes, dtype=jnp.int32)[:, None], touched.shape)
    row_ids = jnp.broadcast_to(jnp.arange(count, dtype=jnp.int32)[None, :], touched.shape)
    table = (
        jnp.full((homes, width_slots + 1), fill_value, jnp.int32).at[home_ids, place].set(row_ids)
    )
    return table[:, :width_slots]


def sparse_shards(queries, label_weights, sibling_blocks, positive_slot):
    width = queries.shape[1]
    qcount = sibling_blocks.shape[0]
    lab_dev = label_weights.shape[0]
    blocks_dev = lab_dev // BLOCK
    first = lax.axis_index("lab") * blocks_dev
    local_ids = first + jnp.arange(blocks_dev, dtype=jnp.int32)
    pblock = jnp.take_along_axis(sibling_blocks, (positive_slot // BLOCK)[:, None], axis=1)[:, 0]
    positive = pblock * BLOCK + positive_slot % BLOCK
    label_ids = local_ids[:, None] * BLOCK + jnp.arange(BLOCK, dtype=jnp.int32)[None, :]
    chosen_all = jnp.any(sibling_blocks[:, :, None] == local_ids[None, None, :], axis=1)
    piece = lax.all_gather(queries, "lab", axis=0, tiled=True)
    count = piece.shape[0]
    scores = jnp.dot(piece, label_weights.T, preferred_element_type=jnp.float32)
    scores = scores.reshape(count, blocks_dev, BLOCK)
    target = (label_ids[None, :, :] == positive[:, None, None]).astype(jnp.float32)
    slope = jnp.where(chosen_all[:, :, None], jax.nn.sigmoid(scores) - target, 0.0)
    slope = slope.astype(jnp.bfloat16).reshape(count, lab_dev)
    dq_all = jnp.dot(slope, label_weights, preferred_element_type=jnp.float32)
    w_acc = lax.dot_general(
        slope, piece, (((0,), (0,)), ((), ())), preferred_element_type=jnp.float32
    )
    homes = lax.axis_size("lab")
    q_home = qcount // homes
    slots = q_home * K // homes
    touched = jnp.any(chosen_all, axis=1).reshape(homes, q_home)
    send_idx = pack_index(touched, slots, q_home)
    padded = jnp.concatenate(
        [dq_all.reshape(homes, q_home, width), jnp.zeros((homes, 1, width), jnp.float32)], axis=1
    )
    outgoing = jnp.take_along_axis(padded, send_idx[:, :, None], axis=1)
    incoming = lax.all_to_all(outgoing, "lab", split_axis=0, concat_axis=0, tiled=True)
    own_blocks = lax.dynamic_slice_in_dim(sibling_blocks, lax.axis_index("lab") * q_home, q_home, 0)
    source_ids = jnp.arange(homes, dtype=jnp.int32)
    own_touch = jnp.any(
        (own_blocks // blocks_dev)[:, :, None] == source_ids[None, None, :], axis=1
    ).T
    recv_idx = pack_index(own_touch, slots, q_home)
    query_grad = (
        jnp.zeros((q_home + 1, width), jnp.float32)
        .at[recv_idx.reshape(-1)]
        .add(incoming.reshape(-1, width))[:q_home]
    )
    groups = lax.axis_size("pb")
    total = lax.psum(w_acc, "pb")
    weight_grad = (total / groups).astype(jnp.bfloat16)
    return (query_grad, weight_grad)


def swap(value, axis, bit):
    count = lax.axis_size(axis)
    return lax.ppermute(value, axis, [(i, i ^ bit) for i in range(count)])


def diagonal(value, group_bit, home_bit):
    groups, homes = lax.axis_size("pb"), lax.axis_size("lab")
    pairs = [
        (g * homes + h, (g ^ group_bit) * homes + (h ^ home_bit))
        for g in range(groups)
        for h in range(homes)
    ]
    return lax.ppermute(value, ("pb", "lab"), pairs)


def local_call(body, outs, args, flops=0, follows=()):
    specs = [
        pl.BlockSpec(memory_space=pltpu.SMEM if arg.dtype == jnp.int32 else pltpu.VMEM)
        for arg in args
    ]
    given, later = len(args), len(args) + len(follows)
    return pl.pallas_call(
        lambda *refs: body(*refs[:given], *refs[later:]),
        out_shape=outs,
        in_specs=specs + [pl.BlockSpec(memory_space=pl.ANY)] * len(follows),
        out_specs=[pl.BlockSpec(memory_space=pltpu.VMEM)] * len(outs),
        cost_estimate=pl.CostEstimate(flops=flops, bytes_accessed=0, transcendentals=0),
        compiler_params=pltpu.CompilerParams(vmem_limit_bytes=VMEM_LIMIT),
    )(*args, *follows)


def like(rows, width, dtype):
    return jax.ShapeDtypeStruct((rows, width), dtype)


def join_body(*refs):
    *came_refs, note_ref, out_ref, noted_ref = refs
    stack_body(*came_refs, out_ref)
    stack_body(*came_refs, note_ref, noted_ref)


def hold_body(*refs):
    for source, held in zip(refs[: len(refs) // 2], refs[len(refs) // 2 :]):
        held[...] = source[...]


def slope_of(rows, weights, chosen, place):
    count, blocks = rows.shape[0], weights.shape[0] // BLOCK
    scores = lax.dot_general(
        weights, rows, (((1,), (1,)), ((), ())), preferred_element_type=jnp.float32
    )
    named = jnp.zeros((BLOCK, count), jnp.float32)
    for block in range(blocks):
        named = jnp.where(chosen == block, scores[block * BLOCK : (block + 1) * BLOCK], named)
    ids = lax.broadcasted_iota(jnp.int32, (BLOCK, count), 0)
    return (jax.nn.sigmoid(named) - jnp.where(ids == place, 1.0, 0.0)).astype(jnp.bfloat16)


def spread(slope, chosen, blocks):
    wide = slope.astype(jnp.float32)
    parts = [jnp.where(chosen == block, wide, 0.0).astype(slope.dtype) for block in blocks]
    return jnp.concatenate(parts, axis=0)


def read_note(note, which, count):
    chosen = note[2 * which : 2 * which + 1, :count].astype(jnp.int32)
    place = note[2 * which + 1 : 2 * which + 2, :count].astype(jnp.int32)
    return chosen, place


def grad_body(which, rows_ref, weights_ref, note_ref, kept_ref, sent_ref, slope_ref):
    rows, weights = rows_ref[...], weights_ref[...]
    note = note_ref[...].astype(jnp.float32)
    chosen, place = read_note(note, which, rows.shape[0])
    slope = slope_of(rows, weights, chosen, place)
    slope_ref[:BLOCK, :] = slope
    slope_ref[BLOCK:, :] = jnp.broadcast_to(chosen, (NOTE, rows.shape[0])).astype(slope.dtype)
    dq = lax.dot_general(
        spread(slope, chosen, range(weights.shape[0] // BLOCK)),
        weights,
        (((0,), (0,)), ((), ())),
        preferred_element_type=jnp.float32,
    )
    halve(dq, kept_ref, sent_ref, kept_ref.shape[0] // 2)


def halve(terms, kept_ref, sent_ref, span):
    for start in range(0, kept_ref.shape[0], span):
        kept_ref[start : start + span, :] = terms[2 * start : 2 * start + span]
        sent = terms[2 * start + span : 2 * start + 2 * span]
        sent_ref[start : start + span, :] = sent.astype(sent_ref.dtype)


def near_body(rows_ref, weights_ref, note_ref, kept_ref, sent_ref, slope_ref, copy_ref):
    copy_ref[...] = rows_ref[...]
    grad_body(0, rows_ref, weights_ref, note_ref, kept_ref, sent_ref, slope_ref)


def far_body(rows_ref, weights_ref, note_ref, kept_ref, sent_ref, slope_ref):
    grad_body(1, rows_ref, weights_ref, note_ref, kept_ref, sent_ref, slope_ref)


def fold_body(terms_ref, came_ref, kept_ref, sent_ref):
    terms = terms_ref[...] + came_ref[...].astype(jnp.float32)
    halve(terms, kept_ref, sent_ref, kept_ref.shape[0])


def sum_body(kept_ref, *refs):
    *term_refs, out_ref = refs
    total = kept_ref[...]
    for ref in term_refs:
        total = total + ref[...].astype(jnp.float32)
    out_ref[...] = total.astype(out_ref.dtype)


def stack_body(*refs):
    *came_refs, out_ref = refs
    start = 0
    for ref in came_refs:
        out_ref[start : start + ref.shape[0], : ref.shape[1]] = ref[...]
        start += ref.shape[0]


def read_slope(slope):
    chosen = slope[BLOCK : BLOCK + 1].astype(jnp.float32).astype(jnp.int32)
    return slope[:BLOCK], chosen


def own_body(near_ref, far_ref, near_slope_ref, far_slope_ref, acc_ref, set_ref):
    rows = jnp.concatenate([near_ref[...], far_ref[...]], axis=0)
    slope = jnp.concatenate([near_slope_ref[...], far_slope_ref[...]], axis=1)
    count = rows.shape[0]
    set_ref[:count, :] = rows
    set_ref[count:, :count] = slope
    wide = spread(*read_slope(slope), range(acc_ref.shape[0] // BLOCK))
    acc_ref[...] = jnp.dot(wide, rows, preferred_element_type=jnp.float32)


def mate_body(set_ref, acc_ref, out_ref):
    count = set_ref.shape[0] - BLOCK - NOTE
    slope, chosen = read_slope(set_ref[count:, :count])
    wide = spread(slope, chosen, range(acc_ref.shape[0] // BLOCK))
    out_ref[...] = acc_ref[...] + jnp.dot(
        wide, set_ref[:count, :], preferred_element_type=jnp.float32
    )


def set_slope(set_ref, weights):
    half = (set_ref.shape[0] - NOTE) // 2
    rows = jnp.concatenate([set_ref[:half, :], set_ref[half + NOTE :, :]], axis=0)
    note = set_ref[half : half + NOTE, :].astype(jnp.float32)
    codes = [read_note(note, which, half) for which in range(2)]
    chosen = jnp.concatenate([codes[0][0], codes[1][0]], axis=1)
    place = jnp.concatenate([codes[0][1], codes[1][1]], axis=1)
    return rows, slope_of(rows, weights, chosen, place), chosen


def cross_body(set_ref, weights_ref, acc_ref, out_ref):
    rows, slope, chosen = set_slope(set_ref, weights_ref[...])
    wide = spread(slope, chosen, range(acc_ref.shape[0] // BLOCK))
    out_ref[...] = acc_ref[...] + jnp.dot(wide, rows, preferred_element_type=jnp.float32)


def late_body(groups, set_ref, weights_ref, acc_ref, out_ref, mark_ref, held, sems):
    mark_ref[...] = jnp.zeros_like(mark_ref)
    rows, slope, chosen = set_slope(set_ref, weights_ref[...])
    blocks = acc_ref.shape[0] // BLOCK
    chunk = blocks // sems.shape[0]
    copies = []
    for part in range(sems.shape[0]):
        here = pl.ds(part * chunk * BLOCK, chunk * BLOCK)
        wide = spread(slope, chosen, range(part * chunk, (part + 1) * chunk))
        total = acc_ref[here, :] + jnp.dot(wide, rows, preferred_element_type=jnp.float32)
        held[here, :] = (total / groups).astype(held.dtype)
        copy = pltpu.make_async_copy(held.at[here, :], out_ref.at[here, :], sems.at[part])
        copy.start()
        copies.append(copy)
    for copy in copies:
        copy.wait()


def late(groups, crossed, weights, acc):
    out = like(*weights.shape, weights.dtype)
    chunks = 4
    return pl.pallas_call(
        lambda *refs: late_body(groups, *refs),
        out_shape=[out, like(1, BLOCK, jnp.int32)],
        in_specs=[pl.BlockSpec(memory_space=pltpu.VMEM)] * 3,
        out_specs=[pl.BlockSpec(memory_space=pl.ANY), pl.BlockSpec(memory_space=pltpu.VMEM)],
        scratch_shapes=[pltpu.VMEM(out.shape, out.dtype), pltpu.SemaphoreType.DMA((chunks,))],
        cost_estimate=pl.CostEstimate(flops=0, bytes_accessed=0, transcendentals=0),
        compiler_params=pltpu.CompilerParams(vmem_limit_bytes=VMEM_LIMIT),
    )(crossed, weights, acc)


def note_body(blocks_dev, q_home, me_ref, choice_ref, note_ref):
    choice = choice_ref[...].astype(jnp.int32)
    me, picks, count = me_ref[0], choice.shape[0] - 1, choice.shape[1]
    local, slot = choice[:picks] - me * blocks_dev, choice[picks:]
    inside = (local >= 0) & (local < blocks_dev)
    chosen = jnp.max(jnp.where(inside, local, -1), axis=0, keepdims=True)
    steps = lax.broadcasted_iota(jnp.int32, local.shape, 0)
    named = steps == lax.shift_right_logical(slot, BLOCK.bit_length() - 1)
    pblock = jnp.sum(jnp.where(named, local, 0), axis=0, keepdims=True)
    place = jnp.where(pblock == chosen, slot & (BLOCK - 1), -1)
    row = lax.broadcasted_iota(jnp.int32, (NOTE, count), 0)
    code = jnp.where(row == 0, chosen, jnp.where(row == 1, place, 0))
    half = count // 2
    lane = lax.broadcasted_iota(jnp.int32, (count, count), 1)
    source = lax.broadcasted_iota(jnp.int32, (count, count), 0)
    plane = (lane >= half).astype(jnp.int32)
    step = lax.shift_right_logical(lane & (half - 1), q_home.bit_length() - 1)
    wanted = ((2 * step + plane) ^ me) * q_home + (lane & (q_home - 1))
    order = jnp.where(source == wanted, 1.0, 0.0).astype(jnp.bfloat16)
    code = jnp.dot(code.astype(jnp.bfloat16), order, preferred_element_type=jnp.float32)
    rest = jnp.zeros((NOTE - 4, half), jnp.float32)
    note = jnp.concatenate([code[:2, :half], code[:2, half:], rest], axis=0)
    note_ref[...] = jnp.zeros_like(note_ref)
    note_ref[:, :half] = note.astype(note_ref.dtype)


def dense_shards(queries, label_weights, sibling_blocks, positive_slot):
    q_home, width = queries.shape
    qcount = sibling_blocks.shape[0]
    half = qcount // 2
    lab_dev = label_weights.shape[0]
    homes = lax.axis_size("lab")
    groups = lax.axis_size("pb")
    f32, bf16 = jnp.float32, jnp.bfloat16
    me = jnp.reshape(lax.axis_index("lab"), (1,)).astype(jnp.int32)
    far_bit = groups // 2
    came = [swap(queries, "lab", step) for step in range(2, homes, 2)]
    held, weights = local_call(
        hold_body,
        [like(q_home, width, bf16), like(lab_dev, width, bf16)],
        [queries, label_weights],
    )
    choice = jnp.concatenate([sibling_blocks.T, positive_slot[None]], axis=0).astype(f32)
    note = local_call(
        lambda *refs: note_body(lab_dev // BLOCK, q_home, *refs),
        [like(NOTE, width, bf16)],
        [me, choice],
    )[0]
    near, noted = local_call(
        join_body,
        [like(half, width, bf16), like(half + NOTE, width, bf16)],
        [held, *came, note],
        0,
        [weights],
    )
    far = swap(near, "lab", 1)
    work = 4 * half * lab_dev * width
    slope_like = like(BLOCK + NOTE, half, bf16)
    pair = [like(half // 2, width, f32), like(half // 2, width, bf16)]
    single = [like(q_home, width, f32), like(q_home, width, bf16)]
    near_kept, near_sent, near_slope, near_copy = local_call(
        near_body,
        pair + [slope_like, like(half, width, bf16)],
        [near, weights, note],
        work,
    )
    cross_near = swap(noted, "pb", far_bit)
    cross_far = diagonal(near_copy, far_bit, 1)
    far_kept, far_sent, far_slope = local_call(
        far_body, pair + [slope_like], [far, weights, note], work, [near_slope]
    )
    far_came, near_came = swap(far_sent, "lab", 2), swap(near_sent, "lab", 2)
    acc, own = local_call(
        own_body,
        [like(lab_dev, width, f32), like(qcount + BLOCK + NOTE, width, bf16)],
        [near, far, near_slope, far_slope],
        work,
    )
    mate = swap(own, "pb", 1)
    far_kept, far_sent = local_call(fold_body, single, [far_kept, far_came], 0, [acc])
    far_came = swap(far_sent, "lab", 4)
    near_kept, near_sent = local_call(fold_body, single, [near_kept, near_came], 0, [far_kept])
    near_came = swap(near_sent, "lab", 4)
    cross = local_call(
        stack_body, [like(qcount + NOTE, width, bf16)], [cross_near, cross_far], 0, [far_kept]
    )[0]
    cross_mate = swap(cross, "pb", 1)
    grown = like(lab_dev, width, f32)
    acc = local_call(cross_body, [grown], [cross, weights, acc], 20 * work, [near_kept])[0]
    far_sent = local_call(
        sum_body, [like(q_home, width, bf16)], [far_kept, far_came], 0, [acc]
    )[0]
    far_came = swap(far_sent, "lab", 1)
    near_most = local_call(
        sum_body, [like(q_home, width, f32)], [near_kept, near_came], 0, [far_sent]
    )[0]
    acc = local_call(mate_body, [grown], [mate, acc], work, [near_most])[0]
    weight_grad, mark = late(groups, cross_mate, weights, acc)
    query_grad = local_call(
        sum_body, [like(q_home, width, f32)], [near_most, far_came], 0, [mark]
    )[0]
    return (query_grad, weight_grad)


def solution(mesh):
    groups, homes = mesh.shape["pb"], mesh.shape["lab"]

    def shards(queries, label_weights, sibling_blocks, positive_slot):
        every_row_everywhere = homes == K
        few = groups * sibling_blocks.shape[0] <= 2 * label_weights.shape[0]
        paired = groups == 4 and homes & (homes - 1) == 0
        one_block = label_weights.shape[0] // BLOCK <= K
        plan = dense_shards if every_row_everywhere and few and paired and one_block else sparse_shards
        return plan(queries, label_weights, sibling_blocks, positive_slot)

    in_specs = (P(("pb", "lab"), None), P("lab", None), P("pb", None), P("pb"))
    out_specs = (P(("pb", "lab"), None), P("lab", None))
    return jax.shard_map(shards, mesh=mesh, in_specs=in_specs, out_specs=out_specs, check_vma=False)
```

```python
import jax
import jax.numpy as jnp
from jax import lax
from jax.experimental import pallas as pl
from jax.experimental.pallas import tpu as pltpu
from jax.sharding import PartitionSpec as P

BLOCK = 128
K = 8
NOTE = 16
VMEM_LIMIT = 24 * 1024 * 1024


def pack_index(touched, width_slots, fill_value):
    homes, count = touched.shape
    rank = jnp.cumsum(touched.astype(jnp.int32), axis=1) - 1
    place = jnp.where(touched, rank, width_slots)
    home_ids = jnp.broadcast_to(jnp.arange(homes, dtype=jnp.int32)[:, None], touched.shape)
    row_ids = jnp.broadcast_to(jnp.arange(count, dtype=jnp.int32)[None, :], touched.shape)
    table = (
        jnp.full((homes, width_slots + 1), fill_value, jnp.int32).at[home_ids, place].set(row_ids)
    )
    return table[:, :width_slots]


def sparse_shards(queries, label_weights, sibling_blocks, positive_slot):
    width = queries.shape[1]
    qcount = sibling_blocks.shape[0]
    lab_dev = label_weights.shape[0]
    blocks_dev = lab_dev // BLOCK
    first = lax.axis_index("lab") * blocks_dev
    local_ids = first + jnp.arange(blocks_dev, dtype=jnp.int32)
    pblock = jnp.take_along_axis(sibling_blocks, (positive_slot // BLOCK)[:, None], axis=1)[:, 0]
    positive = pblock * BLOCK + positive_slot % BLOCK
    label_ids = local_ids[:, None] * BLOCK + jnp.arange(BLOCK, dtype=jnp.int32)[None, :]
    chosen_all = jnp.any(sibling_blocks[:, :, None] == local_ids[None, None, :], axis=1)
    piece = lax.all_gather(queries, "lab", axis=0, tiled=True)
    count = piece.shape[0]
    scores = jnp.dot(piece, label_weights.T, preferred_element_type=jnp.float32)
    scores = scores.reshape(count, blocks_dev, BLOCK)
    target = (label_ids[None, :, :] == positive[:, None, None]).astype(jnp.float32)
    slope = jnp.where(chosen_all[:, :, None], jax.nn.sigmoid(scores) - target, 0.0)
    slope = slope.astype(jnp.bfloat16).reshape(count, lab_dev)
    dq_all = jnp.dot(slope, label_weights, preferred_element_type=jnp.float32)
    w_acc = lax.dot_general(
        slope, piece, (((0,), (0,)), ((), ())), preferred_element_type=jnp.float32
    )
    homes = lax.axis_size("lab")
    q_home = qcount // homes
    slots = q_home * K // homes
    touched = jnp.any(chosen_all, axis=1).reshape(homes, q_home)
    send_idx = pack_index(touched, slots, q_home)
    padded = jnp.concatenate(
        [dq_all.reshape(homes, q_home, width), jnp.zeros((homes, 1, width), jnp.float32)], axis=1
    )
    outgoing = jnp.take_along_axis(padded, send_idx[:, :, None], axis=1)
    incoming = lax.all_to_all(outgoing, "lab", split_axis=0, concat_axis=0, tiled=True)
    own_blocks = lax.dynamic_slice_in_dim(sibling_blocks, lax.axis_index("lab") * q_home, q_home, 0)
    source_ids = jnp.arange(homes, dtype=jnp.int32)
    own_touch = jnp.any(
        (own_blocks // blocks_dev)[:, :, None] == source_ids[None, None, :], axis=1
    ).T
    recv_idx = pack_index(own_touch, slots, q_home)
    query_grad = (
        jnp.zeros((q_home + 1, width), jnp.float32)
        .at[recv_idx.reshape(-1)]
        .add(incoming.reshape(-1, width))[:q_home]
    )
    groups = lax.axis_size("pb")
    total = lax.psum(w_acc, "pb")
    weight_grad = (total / groups).astype(jnp.bfloat16)
    return (query_grad, weight_grad)


def swap(value, axis, bit):
    count = lax.axis_size(axis)
    return lax.ppermute(value, axis, [(i, i ^ bit) for i in range(count)])


def diagonal(value, group_bit, home_bit):
    groups, homes = lax.axis_size("pb"), lax.axis_size("lab")
    pairs = [
        (g * homes + h, (g ^ group_bit) * homes + (h ^ home_bit))
        for g in range(groups)
        for h in range(homes)
    ]
    return lax.ppermute(value, ("pb", "lab"), pairs)


def local_call(body, outs, args, flops=0, follows=()):
    specs = [
        pl.BlockSpec(memory_space=pltpu.SMEM if arg.dtype == jnp.int32 else pltpu.VMEM)
        for arg in args
    ]
    given, later = len(args), len(args) + len(follows)
    return pl.pallas_call(
        lambda *refs: body(*refs[:given], *refs[later:]),
        out_shape=outs,
        in_specs=specs + [pl.BlockSpec(memory_space=pl.ANY)] * len(follows),
        out_specs=[pl.BlockSpec(memory_space=pltpu.VMEM)] * len(outs),
        cost_estimate=pl.CostEstimate(flops=flops, bytes_accessed=0, transcendentals=0),
        compiler_params=pltpu.CompilerParams(vmem_limit_bytes=VMEM_LIMIT),
    )(*args, *follows)


def like(rows, width, dtype):
    return jax.ShapeDtypeStruct((rows, width), dtype)


def join_body(*refs):
    *came_refs, note_ref, out_ref, noted_ref = refs
    stack_body(*came_refs, out_ref)
    stack_body(*came_refs, note_ref, noted_ref)


def hold_body(*refs):
    for source, held in zip(refs[: len(refs) // 2], refs[len(refs) // 2 :]):
        held[...] = source[...]


def slope_of(rows, weights, chosen, place):
    count, blocks = rows.shape[0], weights.shape[0] // BLOCK
    scores = lax.dot_general(
        weights, rows, (((1,), (1,)), ((), ())), preferred_element_type=jnp.float32
    )
    named = jnp.zeros((BLOCK, count), jnp.float32)
    for block in range(blocks):
        named = jnp.where(chosen == block, scores[block * BLOCK : (block + 1) * BLOCK], named)
    ids = lax.broadcasted_iota(jnp.int32, (BLOCK, count), 0)
    return (jax.nn.sigmoid(named) - jnp.where(ids == place, 1.0, 0.0)).astype(jnp.bfloat16)


def spread(slope, chosen, blocks):
    wide = slope.astype(jnp.float32)
    parts = [jnp.where(chosen == block, wide, 0.0).astype(slope.dtype) for block in blocks]
    return jnp.concatenate(parts, axis=0)


def read_note(note, which, count):
    chosen = note[2 * which : 2 * which + 1, :count].astype(jnp.int32)
    place = note[2 * which + 1 : 2 * which + 2, :count].astype(jnp.int32)
    return chosen, place


def grad_body(which, rows_ref, weights_ref, note_ref, kept_ref, sent_ref, slope_ref):
    rows, weights = rows_ref[...], weights_ref[...]
    note = note_ref[...].astype(jnp.float32)
    chosen, place = read_note(note, which, rows.shape[0])
    slope = slope_of(rows, weights, chosen, place)
    slope_ref[:BLOCK, :] = slope
    slope_ref[BLOCK:, :] = jnp.broadcast_to(chosen, (NOTE, rows.shape[0])).astype(slope.dtype)
    dq = lax.dot_general(
        spread(slope, chosen, range(weights.shape[0] // BLOCK)),
        weights,
        (((0,), (0,)), ((), ())),
        preferred_element_type=jnp.float32,
    )
    halve(dq, kept_ref, sent_ref, kept_ref.shape[0] // 2)


def halve(terms, kept_ref, sent_ref, span):
    for start in range(0, kept_ref.shape[0], span):
        kept_ref[start : start + span, :] = terms[2 * start : 2 * start + span]
        sent = terms[2 * start + span : 2 * start + 2 * span]
        sent_ref[start : start + span, :] = sent.astype(sent_ref.dtype)


def near_body(rows_ref, weights_ref, note_ref, kept_ref, sent_ref, slope_ref, copy_ref):
    copy_ref[...] = rows_ref[...]
    grad_body(0, rows_ref, weights_ref, note_ref, kept_ref, sent_ref, slope_ref)


def far_body(rows_ref, weights_ref, note_ref, kept_ref, sent_ref, slope_ref):
    grad_body(1, rows_ref, weights_ref, note_ref, kept_ref, sent_ref, slope_ref)


def fold_body(terms_ref, came_ref, kept_ref, sent_ref):
    terms = terms_ref[...] + came_ref[...].astype(jnp.float32)
    halve(terms, kept_ref, sent_ref, kept_ref.shape[0])


def sum_body(kept_ref, *refs):
    *term_refs, out_ref = refs
    total = kept_ref[...]
    for ref in term_refs:
        total = total + ref[...].astype(jnp.float32)
    out_ref[...] = total.astype(out_ref.dtype)


def stack_body(*refs):
    *came_refs, out_ref = refs
    start = 0
    for ref in came_refs:
        out_ref[start : start + ref.shape[0], : ref.shape[1]] = ref[...]
        start += ref.shape[0]


def read_slope(slope):
    chosen = slope[BLOCK : BLOCK + 1].astype(jnp.float32).astype(jnp.int32)
    return slope[:BLOCK], chosen


def own_body(near_ref, far_ref, near_slope_ref, far_slope_ref, acc_ref, set_ref):
    rows = jnp.concatenate([near_ref[...], far_ref[...]], axis=0)
    slope = jnp.concatenate([near_slope_ref[...], far_slope_ref[...]], axis=1)
    count = rows.shape[0]
    set_ref[:count, :] = rows
    set_ref[count:, :count] = slope
    wide = spread(*read_slope(slope), range(acc_ref.shape[0] // BLOCK))
    acc_ref[...] = jnp.dot(wide, rows, preferred_element_type=jnp.float32)


def mate_body(set_ref, acc_ref, out_ref):
    count = set_ref.shape[0] - BLOCK - NOTE
    slope, chosen = read_slope(set_ref[count:, :count])
    wide = spread(slope, chosen, range(acc_ref.shape[0] // BLOCK))
    out_ref[...] = acc_ref[...] + jnp.dot(
        wide, set_ref[:count, :], preferred_element_type=jnp.float32
    )


def set_slope(set_ref, weights):
    half = (set_ref.shape[0] - NOTE) // 2
    rows = jnp.concatenate([set_ref[:half, :], set_ref[half + NOTE :, :]], axis=0)
    note = set_ref[half : half + NOTE, :].astype(jnp.float32)
    codes = [read_note(note, which, half) for which in range(2)]
    chosen = jnp.concatenate([codes[0][0], codes[1][0]], axis=1)
    place = jnp.concatenate([codes[0][1], codes[1][1]], axis=1)
    return rows, slope_of(rows, weights, chosen, place), chosen


def cross_body(set_ref, weights_ref, acc_ref, out_ref):
    rows, slope, chosen = set_slope(set_ref, weights_ref[...])
    wide = spread(slope, chosen, range(acc_ref.shape[0] // BLOCK))
    out_ref[...] = acc_ref[...] + jnp.dot(wide, rows, preferred_element_type=jnp.float32)


def late_body(groups, set_ref, weights_ref, acc_ref, out_ref, mark_ref, held, sems):
    mark_ref[...] = jnp.zeros_like(mark_ref)
    rows, slope, chosen = set_slope(set_ref, weights_ref[...])
    blocks = acc_ref.shape[0] // BLOCK
    chunk = blocks // sems.shape[0]
    copies = []
    for part in range(sems.shape[0]):
        here = pl.ds(part * chunk * BLOCK, chunk * BLOCK)
        wide = spread(slope, chosen, range(part * chunk, (part + 1) * chunk))
        total = acc_ref[here, :] + jnp.dot(wide, rows, preferred_element_type=jnp.float32)
        held[here, :] = (total / groups).astype(held.dtype)
        copy = pltpu.make_async_copy(held.at[here, :], out_ref.at[here, :], sems.at[part])
        copy.start()
        copies.append(copy)
    for copy in copies:
        copy.wait()


def late(groups, crossed, weights, acc):
    out = like(*weights.shape, weights.dtype)
    chunks = 4
    return pl.pallas_call(
        lambda *refs: late_body(groups, *refs),
        out_shape=[out, like(1, BLOCK, jnp.int32)],
        in_specs=[pl.BlockSpec(memory_space=pltpu.VMEM)] * 3,
        out_specs=[pl.BlockSpec(memory_space=pl.ANY), pl.BlockSpec(memory_space=pltpu.VMEM)],
        scratch_shapes=[pltpu.VMEM(out.shape, out.dtype), pltpu.SemaphoreType.DMA((chunks,))],
        cost_estimate=pl.CostEstimate(flops=0, bytes_accessed=0, transcendentals=0),
        compiler_params=pltpu.CompilerParams(vmem_limit_bytes=VMEM_LIMIT),
    )(crossed, weights, acc)


def note_body(blocks_dev, q_home, me_ref, choice_ref, note_ref):
    choice = choice_ref[...].astype(jnp.int32)
    me, picks, count = me_ref[0], choice.shape[0] - 1, choice.shape[1]
    local, slot = choice[:picks] - me * blocks_dev, choice[picks:]
    inside = (local >= 0) & (local < blocks_dev)
    chosen = jnp.max(jnp.where(inside, local, -1), axis=0, keepdims=True)
    steps = lax.broadcasted_iota(jnp.int32, local.shape, 0)
    named = steps == lax.shift_right_logical(slot, BLOCK.bit_length() - 1)
    pblock = jnp.sum(jnp.where(named, local, 0), axis=0, keepdims=True)
    place = jnp.where(pblock == chosen, slot & (BLOCK - 1), -1)
    row = lax.broadcasted_iota(jnp.int32, (NOTE, count), 0)
    code = jnp.where(row == 0, chosen, jnp.where(row == 1, place, 0))
    half = count // 2
    lane = lax.broadcasted_iota(jnp.int32, (count, count), 1)
    source = lax.broadcasted_iota(jnp.int32, (count, count), 0)
    plane = (lane >= half).astype(jnp.int32)
    step = lax.shift_right_logical(lane & (half - 1), q_home.bit_length() - 1)
    wanted = ((2 * step + plane) ^ me) * q_home + (lane & (q_home - 1))
    order = jnp.where(source == wanted, 1.0, 0.0).astype(jnp.bfloat16)
    code = jnp.dot(code.astype(jnp.bfloat16), order, preferred_element_type=jnp.float32)
    rest = jnp.zeros((NOTE - 4, half), jnp.float32)
    note = jnp.concatenate([code[:2, :half], code[:2, half:], rest], axis=0)
    note_ref[...] = jnp.zeros_like(note_ref)
    note_ref[:, :half] = note.astype(note_ref.dtype)


def dense_shards(queries, label_weights, sibling_blocks, positive_slot):
    q_home, width = queries.shape
    qcount = sibling_blocks.shape[0]
    half = qcount // 2
    lab_dev = label_weights.shape[0]
    homes = lax.axis_size("lab")
    groups = lax.axis_size("pb")
    f32, bf16 = jnp.float32, jnp.bfloat16
    me = jnp.reshape(lax.axis_index("lab"), (1,)).astype(jnp.int32)
    far_bit = groups // 2
    came = [swap(queries, "lab", step) for step in range(2, homes, 2)]
    held, weights = local_call(
        hold_body,
        [like(q_home, width, bf16), like(lab_dev, width, bf16)],
        [queries, label_weights],
    )
    choice = jnp.concatenate([sibling_blocks.T, positive_slot[None]], axis=0).astype(f32)
    note = local_call(
        lambda *refs: note_body(lab_dev // BLOCK, q_home, *refs),
        [like(NOTE, width, bf16)],
        [me, choice],
    )[0]
    near, noted = local_call(
        join_body,
        [like(half, width, bf16), like(half + NOTE, width, bf16)],
        [held, *came, note],
        0,
        [weights],
    )
    far = swap(near, "lab", 1)
    work = 4 * half * lab_dev * width
    slope_like = like(BLOCK + NOTE, half, bf16)
    pair = [like(half // 2, width, f32), like(half // 2, width, bf16)]
    single = [like(q_home, width, f32), like(q_home, width, bf16)]
    near_kept, near_sent, near_slope, near_copy = local_call(
        near_body,
        pair + [slope_like, like(half, width, bf16)],
        [near, weights, note],
        work,
    )
    cross_near = swap(noted, "pb", far_bit)
    cross_far = diagonal(near_copy, far_bit, 1)
    far_kept, far_sent, far_slope = local_call(
        far_body, pair + [slope_like], [far, weights, note], work, [near_slope]
    )
    far_came, near_came = swap(far_sent, "lab", 2), swap(near_sent, "lab", 2)
    acc, own = local_call(
        own_body,
        [like(lab_dev, width, f32), like(qcount + BLOCK + NOTE, width, bf16)],
        [near, far, near_slope, far_slope],
        work,
    )
    mate = swap(own, "pb", 1)
    near_kept, near_sent = local_call(fold_body, single, [near_kept, near_came], 0, [acc])
    near_came = swap(near_sent, "lab", 4)
    far_kept, far_sent = local_call(
        fold_body, single, [far_kept, far_came], 0, [near_kept, acc]
    )
    far_came = swap(far_sent, "lab", 4)
    near_most = local_call(
        sum_body, [like(q_home, width, f32)], [near_kept, near_came], 0, [far_kept]
    )[0]
    cross = local_call(
        stack_body, [like(qcount + NOTE, width, bf16)], [cross_near, cross_far], 0, [far_kept]
    )[0]
    cross_mate = swap(cross, "pb", 1)
    grown = like(lab_dev, width, f32)
    acc = local_call(cross_body, [grown], [cross, weights, acc], 20 * work, [near_most])[0]
    acc = local_call(mate_body, [grown], [mate, acc], work)[0]
    far_sent = local_call(
        sum_body, [like(q_home, width, bf16)], [far_kept, far_came], 0, [acc]
    )[0]
    far_came = swap(far_sent, "lab", 1)
    weight_grad, mark = late(groups, cross_mate, weights, acc)
    query_grad = local_call(
        sum_body, [like(q_home, width, f32)], [near_most, far_came], 0, [mark]
    )[0]
    return (query_grad, weight_grad)


def solution(mesh):
    groups, homes = mesh.shape["pb"], mesh.shape["lab"]

    def shards(queries, label_weights, sibling_blocks, positive_slot):
        every_row_everywhere = homes == K
        few = groups * sibling_blocks.shape[0] <= 2 * label_weights.shape[0]
        paired = groups == 4 and homes & (homes - 1) == 0
        one_block = label_weights.shape[0] // BLOCK <= K
        plan = dense_shards if every_row_everywhere and few and paired and one_block else sparse_shards
        return plan(queries, label_weights, sibling_blocks, positive_slot)

    in_specs = (P(("pb", "lab"), None), P("lab", None), P("pb", None), P("pb"))
    out_specs = (P(("pb", "lab"), None), P("lab", None))
    return jax.shard_map(shards, mesh=mesh, in_specs=in_specs, out_specs=out_specs, check_vma=False)
```

```python
import jax
import jax.numpy as jnp
from jax import lax
from jax.experimental import pallas as pl
from jax.experimental.pallas import tpu as pltpu
from jax.sharding import PartitionSpec as P

BLOCK = 128
K = 8
NOTE = 16
VMEM_LIMIT = 24 * 1024 * 1024


def pack_index(touched, width_slots, fill_value):
    homes, count = touched.shape
    rank = jnp.cumsum(touched.astype(jnp.int32), axis=1) - 1
    place = jnp.where(touched, rank, width_slots)
    home_ids = jnp.broadcast_to(jnp.arange(homes, dtype=jnp.int32)[:, None], touched.shape)
    row_ids = jnp.broadcast_to(jnp.arange(count, dtype=jnp.int32)[None, :], touched.shape)
    table = (
        jnp.full((homes, width_slots + 1), fill_value, jnp.int32).at[home_ids, place].set(row_ids)
    )
    return table[:, :width_slots]


def sparse_shards(queries, label_weights, sibling_blocks, positive_slot):
    width = queries.shape[1]
    qcount = sibling_blocks.shape[0]
    lab_dev = label_weights.shape[0]
    blocks_dev = lab_dev // BLOCK
    first = lax.axis_index("lab") * blocks_dev
    local_ids = first + jnp.arange(blocks_dev, dtype=jnp.int32)
    pblock = jnp.take_along_axis(sibling_blocks, (positive_slot // BLOCK)[:, None], axis=1)[:, 0]
    positive = pblock * BLOCK + positive_slot % BLOCK
    label_ids = local_ids[:, None] * BLOCK + jnp.arange(BLOCK, dtype=jnp.int32)[None, :]
    chosen_all = jnp.any(sibling_blocks[:, :, None] == local_ids[None, None, :], axis=1)
    piece = lax.all_gather(queries, "lab", axis=0, tiled=True)
    count = piece.shape[0]
    scores = jnp.dot(piece, label_weights.T, preferred_element_type=jnp.float32)
    scores = scores.reshape(count, blocks_dev, BLOCK)
    target = (label_ids[None, :, :] == positive[:, None, None]).astype(jnp.float32)
    slope = jnp.where(chosen_all[:, :, None], jax.nn.sigmoid(scores) - target, 0.0)
    slope = slope.astype(jnp.bfloat16).reshape(count, lab_dev)
    dq_all = jnp.dot(slope, label_weights, preferred_element_type=jnp.float32)
    w_acc = lax.dot_general(
        slope, piece, (((0,), (0,)), ((), ())), preferred_element_type=jnp.float32
    )
    homes = lax.axis_size("lab")
    q_home = qcount // homes
    slots = q_home * K // homes
    touched = jnp.any(chosen_all, axis=1).reshape(homes, q_home)
    send_idx = pack_index(touched, slots, q_home)
    padded = jnp.concatenate(
        [dq_all.reshape(homes, q_home, width), jnp.zeros((homes, 1, width), jnp.float32)], axis=1
    )
    outgoing = jnp.take_along_axis(padded, send_idx[:, :, None], axis=1)
    incoming = lax.all_to_all(outgoing, "lab", split_axis=0, concat_axis=0, tiled=True)
    own_blocks = lax.dynamic_slice_in_dim(sibling_blocks, lax.axis_index("lab") * q_home, q_home, 0)
    source_ids = jnp.arange(homes, dtype=jnp.int32)
    own_touch = jnp.any(
        (own_blocks // blocks_dev)[:, :, None] == source_ids[None, None, :], axis=1
    ).T
    recv_idx = pack_index(own_touch, slots, q_home)
    query_grad = (
        jnp.zeros((q_home + 1, width), jnp.float32)
        .at[recv_idx.reshape(-1)]
        .add(incoming.reshape(-1, width))[:q_home]
    )
    groups = lax.axis_size("pb")
    total = lax.psum(w_acc, "pb")
    weight_grad = (total / groups).astype(jnp.bfloat16)
    return (query_grad, weight_grad)


def swap(value, axis, bit):
    count = lax.axis_size(axis)
    return lax.ppermute(value, axis, [(i, i ^ bit) for i in range(count)])


def diagonal(value, group_bit, home_bit):
    groups, homes = lax.axis_size("pb"), lax.axis_size("lab")
    pairs = [
        (g * homes + h, (g ^ group_bit) * homes + (h ^ home_bit))
        for g in range(groups)
        for h in range(homes)
    ]
    return lax.ppermute(value, ("pb", "lab"), pairs)


def local_call(body, outs, args, flops=0, follows=()):
    specs = [
        pl.BlockSpec(memory_space=pltpu.SMEM if arg.dtype == jnp.int32 else pltpu.VMEM)
        for arg in args
    ]
    given, later = len(args), len(args) + len(follows)
    return pl.pallas_call(
        lambda *refs: body(*refs[:given], *refs[later:]),
        out_shape=outs,
        in_specs=specs + [pl.BlockSpec(memory_space=pl.ANY)] * len(follows),
        out_specs=[pl.BlockSpec(memory_space=pltpu.VMEM)] * len(outs),
        cost_estimate=pl.CostEstimate(flops=flops, bytes_accessed=0, transcendentals=0),
        compiler_params=pltpu.CompilerParams(vmem_limit_bytes=VMEM_LIMIT),
    )(*args, *follows)


def like(rows, width, dtype):
    return jax.ShapeDtypeStruct((rows, width), dtype)


def join_body(*refs):
    own_ref, first_ref, *rest, note_ref, out_ref, noted_ref = refs
    came_refs = [own_ref, first_ref, *rest[::-1]]
    stack_body(*came_refs, out_ref)
    stack_body(*came_refs, note_ref, noted_ref)


def hold_body(*refs):
    for source, held in zip(refs[: len(refs) // 2], refs[len(refs) // 2 :]):
        held[...] = source[...]


def slope_of(rows, weights, chosen, place):
    count, blocks = rows.shape[0], weights.shape[0] // BLOCK
    scores = lax.dot_general(
        weights, rows, (((1,), (1,)), ((), ())), preferred_element_type=jnp.float32
    )
    named = jnp.zeros((BLOCK, count), jnp.float32)
    for block in range(blocks):
        named = jnp.where(chosen == block, scores[block * BLOCK : (block + 1) * BLOCK], named)
    ids = lax.broadcasted_iota(jnp.int32, (BLOCK, count), 0)
    return (jax.nn.sigmoid(named) - jnp.where(ids == place, 1.0, 0.0)).astype(jnp.bfloat16)


def spread(slope, chosen, blocks):
    wide = slope.astype(jnp.float32)
    parts = [jnp.where(chosen == block, wide, 0.0).astype(slope.dtype) for block in blocks]
    return jnp.concatenate(parts, axis=0)


def read_note(note, which, count):
    chosen = note[2 * which : 2 * which + 1, :count].astype(jnp.int32)
    place = note[2 * which + 1 : 2 * which + 2, :count].astype(jnp.int32)
    return chosen, place


def grad_body(which, rows_ref, weights_ref, note_ref, kept_ref, sent_ref, slope_ref):
    rows, weights = rows_ref[...], weights_ref[...]
    note = note_ref[...].astype(jnp.float32)
    chosen, place = read_note(note, which, rows.shape[0])
    slope = slope_of(rows, weights, chosen, place)
    slope_ref[:BLOCK, :] = slope
    slope_ref[BLOCK:, :] = jnp.broadcast_to(chosen, (NOTE, rows.shape[0])).astype(slope.dtype)
    dq = lax.dot_general(
        spread(slope, chosen, range(weights.shape[0] // BLOCK)),
        weights,
        (((0,), (0,)), ((), ())),
        preferred_element_type=jnp.float32,
    )
    halve(dq, kept_ref, sent_ref, kept_ref.shape[0] // 2)


def halve(terms, kept_ref, sent_ref, span):
    for start in range(0, kept_ref.shape[0], span):
        kept_ref[start : start + span, :] = terms[2 * start : 2 * start + span]
        sent = terms[2 * start + span : 2 * start + 2 * span]
        sent_ref[start : start + span, :] = sent.astype(sent_ref.dtype)


def near_body(rows_ref, weights_ref, note_ref, kept_ref, sent_ref, slope_ref, copy_ref):
    copy_ref[...] = rows_ref[...]
    grad_body(0, rows_ref, weights_ref, note_ref, kept_ref, sent_ref, slope_ref)


def far_body(rows_ref, weights_ref, note_ref, kept_ref, sent_ref, slope_ref):
    grad_body(1, rows_ref, weights_ref, note_ref, kept_ref, sent_ref, slope_ref)


def fold_body(terms_ref, came_ref, kept_ref, sent_ref):
    terms = terms_ref[...] + came_ref[...].astype(jnp.float32)
    halve(terms, kept_ref, sent_ref, kept_ref.shape[0])


def sum_body(kept_ref, *refs):
    *term_refs, out_ref = refs
    total = kept_ref[...]
    for ref in term_refs:
        total = total + ref[...].astype(jnp.float32)
    out_ref[...] = total.astype(out_ref.dtype)


def stack_body(*refs):
    *came_refs, out_ref = refs
    start = 0
    for ref in came_refs:
        out_ref[start : start + ref.shape[0], : ref.shape[1]] = ref[...]
        start += ref.shape[0]


def read_slope(slope):
    chosen = slope[BLOCK : BLOCK + 1].astype(jnp.float32).astype(jnp.int32)
    return slope[:BLOCK], chosen


def own_body(near_ref, far_ref, near_slope_ref, far_slope_ref, acc_ref, set_ref):
    rows = jnp.concatenate([near_ref[...], far_ref[...]], axis=0)
    slope = jnp.concatenate([near_slope_ref[...], far_slope_ref[...]], axis=1)
    count = rows.shape[0]
    set_ref[:count, :] = rows
    set_ref[count:, :count] = slope
    wide = spread(*read_slope(slope), range(acc_ref.shape[0] // BLOCK))
    acc_ref[...] = jnp.dot(wide, rows, preferred_element_type=jnp.float32)


def mate_body(set_ref, acc_ref, out_ref):
    count = set_ref.shape[0] - BLOCK - NOTE
    slope, chosen = read_slope(set_ref[count:, :count])
    wide = spread(slope, chosen, range(acc_ref.shape[0] // BLOCK))
    out_ref[...] = acc_ref[...] + jnp.dot(
        wide, set_ref[:count, :], preferred_element_type=jnp.float32
    )


def set_slope(set_ref, weights):
    half = (set_ref.shape[0] - NOTE) // 2
    rows = jnp.concatenate([set_ref[:half, :], set_ref[half + NOTE :, :]], axis=0)
    note = set_ref[half : half + NOTE, :].astype(jnp.float32)
    codes = [read_note(note, which, half) for which in range(2)]
    chosen = jnp.concatenate([codes[0][0], codes[1][0]], axis=1)
    place = jnp.concatenate([codes[0][1], codes[1][1]], axis=1)
    return rows, slope_of(rows, weights, chosen, place), chosen


def cross_body(set_ref, weights_ref, acc_ref, out_ref):
    rows, slope, chosen = set_slope(set_ref, weights_ref[...])
    wide = spread(slope, chosen, range(acc_ref.shape[0] // BLOCK))
    out_ref[...] = acc_ref[...] + jnp.dot(wide, rows, preferred_element_type=jnp.float32)


def late_body(groups, set_ref, weights_ref, acc_ref, out_ref, mark_ref, held, sems):
    mark_ref[...] = jnp.zeros_like(mark_ref)
    rows, slope, chosen = set_slope(set_ref, weights_ref[...])
    blocks = acc_ref.shape[0] // BLOCK
    chunk = blocks // sems.shape[0]
    copies = []
    for part in range(sems.shape[0]):
        here = pl.ds(part * chunk * BLOCK, chunk * BLOCK)
        wide = spread(slope, chosen, range(part * chunk, (part + 1) * chunk))
        total = acc_ref[here, :] + jnp.dot(wide, rows, preferred_element_type=jnp.float32)
        held[here, :] = (total / groups).astype(held.dtype)
        copy = pltpu.make_async_copy(held.at[here, :], out_ref.at[here, :], sems.at[part])
        copy.start()
        copies.append(copy)
    for copy in copies:
        copy.wait()


def late(groups, crossed, weights, acc):
    out = like(*weights.shape, weights.dtype)
    chunks = 4
    return pl.pallas_call(
        lambda *refs: late_body(groups, *refs),
        out_shape=[out, like(1, BLOCK, jnp.int32)],
        in_specs=[pl.BlockSpec(memory_space=pltpu.VMEM)] * 3,
        out_specs=[pl.BlockSpec(memory_space=pl.ANY), pl.BlockSpec(memory_space=pltpu.VMEM)],
        scratch_shapes=[pltpu.VMEM(out.shape, out.dtype), pltpu.SemaphoreType.DMA((chunks,))],
        cost_estimate=pl.CostEstimate(flops=0, bytes_accessed=0, transcendentals=0),
        compiler_params=pltpu.CompilerParams(vmem_limit_bytes=VMEM_LIMIT),
    )(crossed, weights, acc)


def note_body(blocks_dev, q_home, me_ref, choice_ref, note_ref):
    choice = choice_ref[...].astype(jnp.int32)
    me, picks, count = me_ref[0], choice.shape[0] - 1, choice.shape[1]
    local, slot = choice[:picks] - me * blocks_dev, choice[picks:]
    inside = (local >= 0) & (local < blocks_dev)
    chosen = jnp.max(jnp.where(inside, local, -1), axis=0, keepdims=True)
    steps = lax.broadcasted_iota(jnp.int32, local.shape, 0)
    named = steps == lax.shift_right_logical(slot, BLOCK.bit_length() - 1)
    pblock = jnp.sum(jnp.where(named, local, 0), axis=0, keepdims=True)
    place = jnp.where(pblock == chosen, slot & (BLOCK - 1), -1)
    row = lax.broadcasted_iota(jnp.int32, (NOTE, count), 0)
    code = jnp.where(row == 0, chosen, jnp.where(row == 1, place, 0))
    half = count // 2
    lane = lax.broadcasted_iota(jnp.int32, (count, count), 1)
    source = lax.broadcasted_iota(jnp.int32, (count, count), 0)
    plane = (lane >= half).astype(jnp.int32)
    step = lax.shift_right_logical(lane & (half - 1), q_home.bit_length() - 1)
    wanted = ((2 * step + plane) ^ me) * q_home + (lane & (q_home - 1))
    order = jnp.where(source == wanted, 1.0, 0.0).astype(jnp.bfloat16)
    code = jnp.dot(code.astype(jnp.bfloat16), order, preferred_element_type=jnp.float32)
    rest = jnp.zeros((NOTE - 4, half), jnp.float32)
    note = jnp.concatenate([code[:2, :half], code[:2, half:], rest], axis=0)
    note_ref[...] = jnp.zeros_like(note_ref)
    note_ref[:, :half] = note.astype(note_ref.dtype)


def dense_shards(queries, label_weights, sibling_blocks, positive_slot):
    q_home, width = queries.shape
    qcount = sibling_blocks.shape[0]
    half = qcount // 2
    lab_dev = label_weights.shape[0]
    homes = lax.axis_size("lab")
    groups = lax.axis_size("pb")
    f32, bf16 = jnp.float32, jnp.bfloat16
    me = jnp.reshape(lax.axis_index("lab"), (1,)).astype(jnp.int32)
    far_bit = groups // 2
    came = [swap(queries, "lab", step) for step in range(2, homes, 2)]
    held, weights = local_call(
        hold_body,
        [like(q_home, width, bf16), like(lab_dev, width, bf16)],
        [queries, label_weights],
    )
    choice = jnp.concatenate([sibling_blocks.T, positive_slot[None]], axis=0).astype(f32)
    note = local_call(
        lambda *refs: note_body(lab_dev // BLOCK, q_home, *refs),
        [like(NOTE, width, bf16)],
        [me, choice],
    )[0]
    near, noted = local_call(
        join_body,
        [like(half, width, bf16), like(half + NOTE, width, bf16)],
        [held, came[0], *came[:0:-1], note],
        0,
        [weights],
    )
    far = swap(near, "lab", 1)
    work = 4 * half * lab_dev * width
    slope_like = like(BLOCK + NOTE, half, bf16)
    pair = [like(half // 2, width, f32), like(half // 2, width, bf16)]
    single = [like(q_home, width, f32), like(q_home, width, bf16)]
    near_kept, near_sent, near_slope, near_copy = local_call(
        near_body,
        pair + [slope_like, like(half, width, bf16)],
        [near, weights, note],
        work,
    )
    cross_near = swap(noted, "pb", far_bit)
    cross_far = diagonal(near_copy, far_bit, 1)
    far_kept, far_sent, far_slope = local_call(
        far_body, pair + [slope_like], [far, weights, note], work, [near_slope]
    )
    far_came, near_came = swap(far_sent, "lab", 2), swap(near_sent, "lab", 2)
    acc, own = local_call(
        own_body,
        [like(lab_dev, width, f32), like(qcount + BLOCK + NOTE, width, bf16)],
        [near, far, near_slope, far_slope],
        work,
    )
    mate = swap(own, "pb", 1)
    near_kept, near_sent = local_call(fold_body, single, [near_kept, near_came], 0, [acc])
    near_came = swap(near_sent, "lab", 4)
    far_kept, far_sent = local_call(
        fold_body, single, [far_kept, far_came], 0, [near_kept, acc]
    )
    far_came = swap(far_sent, "lab", 4)
    near_most = local_call(
        sum_body, [like(q_home, width, f32)], [near_kept, near_came], 0, [far_kept]
    )[0]
    cross = local_call(
        stack_body, [like(qcount + NOTE, width, bf16)], [cross_near, cross_far], 0, [far_kept]
    )[0]
    cross_mate = swap(cross, "pb", 1)
    grown = like(lab_dev, width, f32)
    acc = local_call(cross_body, [grown], [cross, weights, acc], 20 * work, [far_kept])[0]
    acc = local_call(mate_body, [grown], [mate, acc], work, [near_most])[0]
    far_sent = local_call(
        sum_body, [like(q_home, width, bf16)], [far_kept, far_came], 0, [acc]
    )[0]
    far_came = swap(far_sent, "lab", 1)
    weight_grad, mark = late(groups, cross_mate, weights, acc)
    query_grad = local_call(
        sum_body, [like(q_home, width, f32)], [near_most, far_came], 0, [mark]
    )[0]
    return (query_grad, weight_grad)


def solution(mesh):
    groups, homes = mesh.shape["pb"], mesh.shape["lab"]

    def shards(queries, label_weights, sibling_blocks, positive_slot):
        every_row_everywhere = homes == K
        few = groups * sibling_blocks.shape[0] <= 2 * label_weights.shape[0]
        paired = groups == 4 and homes & (homes - 1) == 0
        one_block = label_weights.shape[0] // BLOCK <= K
        plan = dense_shards if every_row_everywhere and few and paired and one_block else sparse_shards
        return plan(queries, label_weights, sibling_blocks, positive_slot)

    in_specs = (P(("pb", "lab"), None), P("lab", None), P("pb", None), P("pb"))
    out_specs = (P(("pb", "lab"), None), P("lab", None))
    return jax.shard_map(shards, mesh=mesh, in_specs=in_specs, out_specs=out_specs, check_vma=False)
```

```python
import jax
import jax.numpy as jnp
from jax import lax
from jax.experimental import pallas as pl
from jax.experimental.pallas import tpu as pltpu
from jax.sharding import PartitionSpec as P

BLOCK = 128
K = 8
NOTE = 16
VMEM_LIMIT = 24 * 1024 * 1024


def pack_index(touched, width_slots, fill_value):
    homes, count = touched.shape
    rank = jnp.cumsum(touched.astype(jnp.int32), axis=1) - 1
    place = jnp.where(touched, rank, width_slots)
    home_ids = jnp.broadcast_to(jnp.arange(homes, dtype=jnp.int32)[:, None], touched.shape)
    row_ids = jnp.broadcast_to(jnp.arange(count, dtype=jnp.int32)[None, :], touched.shape)
    table = (
        jnp.full((homes, width_slots + 1), fill_value, jnp.int32).at[home_ids, place].set(row_ids)
    )
    return table[:, :width_slots]


def sparse_shards(queries, label_weights, sibling_blocks, positive_slot):
    width = queries.shape[1]
    qcount = sibling_blocks.shape[0]
    lab_dev = label_weights.shape[0]
    blocks_dev = lab_dev // BLOCK
    first = lax.axis_index("lab") * blocks_dev
    local_ids = first + jnp.arange(blocks_dev, dtype=jnp.int32)
    pblock = jnp.take_along_axis(sibling_blocks, (positive_slot // BLOCK)[:, None], axis=1)[:, 0]
    positive = pblock * BLOCK + positive_slot % BLOCK
    label_ids = local_ids[:, None] * BLOCK + jnp.arange(BLOCK, dtype=jnp.int32)[None, :]
    chosen_all = jnp.any(sibling_blocks[:, :, None] == local_ids[None, None, :], axis=1)
    piece = lax.all_gather(queries, "lab", axis=0, tiled=True)
    count = piece.shape[0]
    scores = jnp.dot(piece, label_weights.T, preferred_element_type=jnp.float32)
    scores = scores.reshape(count, blocks_dev, BLOCK)
    target = (label_ids[None, :, :] == positive[:, None, None]).astype(jnp.float32)
    slope = jnp.where(chosen_all[:, :, None], jax.nn.sigmoid(scores) - target, 0.0)
    slope = slope.astype(jnp.bfloat16).reshape(count, lab_dev)
    dq_all = jnp.dot(slope, label_weights, preferred_element_type=jnp.float32)
    w_acc = lax.dot_general(
        slope, piece, (((0,), (0,)), ((), ())), preferred_element_type=jnp.float32
    )
    homes = lax.axis_size("lab")
    q_home = qcount // homes
    slots = q_home * K // homes
    touched = jnp.any(chosen_all, axis=1).reshape(homes, q_home)
    send_idx = pack_index(touched, slots, q_home)
    padded = jnp.concatenate(
        [dq_all.reshape(homes, q_home, width), jnp.zeros((homes, 1, width), jnp.float32)], axis=1
    )
    outgoing = jnp.take_along_axis(padded, send_idx[:, :, None], axis=1)
    incoming = lax.all_to_all(outgoing, "lab", split_axis=0, concat_axis=0, tiled=True)
    own_blocks = lax.dynamic_slice_in_dim(sibling_blocks, lax.axis_index("lab") * q_home, q_home, 0)
    source_ids = jnp.arange(homes, dtype=jnp.int32)
    own_touch = jnp.any(
        (own_blocks // blocks_dev)[:, :, None] == source_ids[None, None, :], axis=1
    ).T
    recv_idx = pack_index(own_touch, slots, q_home)
    query_grad = (
        jnp.zeros((q_home + 1, width), jnp.float32)
        .at[recv_idx.reshape(-1)]
        .add(incoming.reshape(-1, width))[:q_home]
    )
    groups = lax.axis_size("pb")
    total = lax.psum(w_acc, "pb")
    weight_grad = (total / groups).astype(jnp.bfloat16)
    return (query_grad, weight_grad)


def swap(value, axis, bit):
    count = lax.axis_size(axis)
    return lax.ppermute(value, axis, [(i, i ^ bit) for i in range(count)])


def diagonal(value, group_bit, home_bit):
    groups, homes = lax.axis_size("pb"), lax.axis_size("lab")
    pairs = [
        (g * homes + h, (g ^ group_bit) * homes + (h ^ home_bit))
        for g in range(groups)
        for h in range(homes)
    ]
    return lax.ppermute(value, ("pb", "lab"), pairs)


def local_call(body, outs, args, flops=0, follows=()):
    specs = [
        pl.BlockSpec(memory_space=pltpu.SMEM if arg.dtype == jnp.int32 else pltpu.VMEM)
        for arg in args
    ]
    given, later = len(args), len(args) + len(follows)
    return pl.pallas_call(
        lambda *refs: body(*refs[:given], *refs[later:]),
        out_shape=outs,
        in_specs=specs + [pl.BlockSpec(memory_space=pl.ANY)] * len(follows),
        out_specs=[pl.BlockSpec(memory_space=pltpu.VMEM)] * len(outs),
        cost_estimate=pl.CostEstimate(flops=flops, bytes_accessed=0, transcendentals=0),
        compiler_params=pltpu.CompilerParams(vmem_limit_bytes=VMEM_LIMIT),
    )(*args, *follows)


def like(rows, width, dtype):
    return jax.ShapeDtypeStruct((rows, width), dtype)


def join_body(*refs):
    *came_refs, note_ref, out_ref, noted_ref = refs
    stack_body(*came_refs, out_ref)
    stack_body(*came_refs, note_ref, noted_ref)


def hold_body(*refs):
    for source, held in zip(refs[: len(refs) // 2], refs[len(refs) // 2 :]):
        held[...] = source[...]


def slope_of(rows, weights, chosen, place):
    count, blocks = rows.shape[0], weights.shape[0] // BLOCK
    scores = lax.dot_general(
        weights, rows, (((1,), (1,)), ((), ())), preferred_element_type=jnp.float32
    )
    named = jnp.zeros((BLOCK, count), jnp.float32)
    for block in range(blocks):
        named = jnp.where(chosen == block, scores[block * BLOCK : (block + 1) * BLOCK], named)
    ids = lax.broadcasted_iota(jnp.int32, (BLOCK, count), 0)
    return (jax.nn.sigmoid(named) - jnp.where(ids == place, 1.0, 0.0)).astype(jnp.bfloat16)


def spread(slope, chosen, blocks):
    wide = slope.astype(jnp.float32)
    parts = [jnp.where(chosen == block, wide, 0.0).astype(slope.dtype) for block in blocks]
    return jnp.concatenate(parts, axis=0)


def read_note(note, which, count):
    chosen = note[2 * which : 2 * which + 1, :count].astype(jnp.int32)
    place = note[2 * which + 1 : 2 * which + 2, :count].astype(jnp.int32)
    return chosen, place


def grad_body(which, rows_ref, weights_ref, note_ref, kept_ref, sent_ref, slope_ref):
    rows, weights = rows_ref[...], weights_ref[...]
    note = note_ref[...].astype(jnp.float32)
    chosen, place = read_note(note, which, rows.shape[0])
    slope = slope_of(rows, weights, chosen, place)
    slope_ref[:BLOCK, :] = slope
    slope_ref[BLOCK:, :] = jnp.broadcast_to(chosen, (NOTE, rows.shape[0])).astype(slope.dtype)
    dq = lax.dot_general(
        spread(slope, chosen, range(weights.shape[0] // BLOCK)),
        weights,
        (((0,), (0,)), ((), ())),
        preferred_element_type=jnp.float32,
    )
    halve(dq, kept_ref, sent_ref, kept_ref.shape[0] // 2)


def halve(terms, kept_ref, sent_ref, span):
    for start in range(0, kept_ref.shape[0], span):
        kept_ref[start : start + span, :] = terms[2 * start : 2 * start + span]
        sent = terms[2 * start + span : 2 * start + 2 * span]
        sent_ref[start : start + span, :] = sent.astype(sent_ref.dtype)


def near_body(rows_ref, weights_ref, note_ref, kept_ref, sent_ref, slope_ref, copy_ref):
    copy_ref[...] = rows_ref[...]
    grad_body(0, rows_ref, weights_ref, note_ref, kept_ref, sent_ref, slope_ref)


def far_body(rows_ref, weights_ref, note_ref, kept_ref, sent_ref, slope_ref):
    grad_body(1, rows_ref, weights_ref, note_ref, kept_ref, sent_ref, slope_ref)


def fold_body(terms_ref, came_ref, first_ref, second_ref):
    terms = terms_ref[...] + came_ref[...].astype(jnp.float32)
    span = first_ref.shape[0]
    first_ref[...] = terms[:span].astype(first_ref.dtype)
    second_ref[...] = terms[span:].astype(second_ref.dtype)


def sum_body(kept_ref, *refs):
    *term_refs, out_ref = refs
    total = kept_ref[...]
    for ref in term_refs:
        total = total + ref[...].astype(jnp.float32)
    out_ref[...] = total.astype(out_ref.dtype)


def stack_body(*refs):
    *came_refs, out_ref = refs
    start = 0
    for ref in came_refs:
        out_ref[start : start + ref.shape[0], : ref.shape[1]] = ref[...]
        start += ref.shape[0]


def read_slope(slope):
    chosen = slope[BLOCK : BLOCK + 1].astype(jnp.float32).astype(jnp.int32)
    return slope[:BLOCK], chosen


def own_body(near_ref, far_ref, near_slope_ref, far_slope_ref, acc_ref, set_ref):
    rows = jnp.concatenate([near_ref[...], far_ref[...]], axis=0)
    slope = jnp.concatenate([near_slope_ref[...], far_slope_ref[...]], axis=1)
    count = rows.shape[0]
    set_ref[:count, :] = rows
    set_ref[count:, :count] = slope
    wide = spread(*read_slope(slope), range(acc_ref.shape[0] // BLOCK))
    acc_ref[...] = jnp.dot(wide, rows, preferred_element_type=jnp.float32)


def mate_body(set_ref, acc_ref, out_ref):
    count = set_ref.shape[0] - BLOCK - NOTE
    slope, chosen = read_slope(set_ref[count:, :count])
    wide = spread(slope, chosen, range(acc_ref.shape[0] // BLOCK))
    out_ref[...] = acc_ref[...] + jnp.dot(
        wide, set_ref[:count, :], preferred_element_type=jnp.float32
    )


def set_slope(set_ref, weights):
    half = (set_ref.shape[0] - NOTE) // 2
    rows = jnp.concatenate([set_ref[:half, :], set_ref[half + NOTE :, :]], axis=0)
    note = set_ref[half : half + NOTE, :].astype(jnp.float32)
    codes = [read_note(note, which, half) for which in range(2)]
    chosen = jnp.concatenate([codes[0][0], codes[1][0]], axis=1)
    place = jnp.concatenate([codes[0][1], codes[1][1]], axis=1)
    return rows, slope_of(rows, weights, chosen, place), chosen


def cross_body(set_ref, weights_ref, acc_ref, out_ref):
    rows, slope, chosen = set_slope(set_ref, weights_ref[...])
    wide = spread(slope, chosen, range(acc_ref.shape[0] // BLOCK))
    out_ref[...] = acc_ref[...] + jnp.dot(wide, rows, preferred_element_type=jnp.float32)


def late_body(groups, set_ref, weights_ref, acc_ref, out_ref, mark_ref, held, sems):
    mark_ref[...] = jnp.zeros_like(mark_ref)
    rows, slope, chosen = set_slope(set_ref, weights_ref[...])
    blocks = acc_ref.shape[0] // BLOCK
    chunk = blocks // sems.shape[0]
    copies = []
    for part in range(sems.shape[0]):
        here = pl.ds(part * chunk * BLOCK, chunk * BLOCK)
        wide = spread(slope, chosen, range(part * chunk, (part + 1) * chunk))
        total = acc_ref[here, :] + jnp.dot(wide, rows, preferred_element_type=jnp.float32)
        held[here, :] = (total / groups).astype(held.dtype)
        copy = pltpu.make_async_copy(held.at[here, :], out_ref.at[here, :], sems.at[part])
        copy.start()
        copies.append(copy)
    for copy in copies:
        copy.wait()


def late(groups, crossed, weights, acc):
    out = like(*weights.shape, weights.dtype)
    chunks = 4
    return pl.pallas_call(
        lambda *refs: late_body(groups, *refs),
        out_shape=[out, like(1, BLOCK, jnp.int32)],
        in_specs=[pl.BlockSpec(memory_space=pltpu.VMEM)] * 3,
        out_specs=[pl.BlockSpec(memory_space=pl.ANY), pl.BlockSpec(memory_space=pltpu.VMEM)],
        scratch_shapes=[pltpu.VMEM(out.shape, out.dtype), pltpu.SemaphoreType.DMA((chunks,))],
        cost_estimate=pl.CostEstimate(flops=0, bytes_accessed=0, transcendentals=0),
        compiler_params=pltpu.CompilerParams(vmem_limit_bytes=VMEM_LIMIT),
    )(crossed, weights, acc)


def note_body(blocks_dev, q_home, me_ref, choice_ref, note_ref):
    choice = choice_ref[...].astype(jnp.int32)
    me, picks, count = me_ref[0], choice.shape[0] - 1, choice.shape[1]
    local, slot = choice[:picks] - me * blocks_dev, choice[picks:]
    inside = (local >= 0) & (local < blocks_dev)
    chosen = jnp.max(jnp.where(inside, local, -1), axis=0, keepdims=True)
    steps = lax.broadcasted_iota(jnp.int32, local.shape, 0)
    named = steps == lax.shift_right_logical(slot, BLOCK.bit_length() - 1)
    pblock = jnp.sum(jnp.where(named, local, 0), axis=0, keepdims=True)
    place = jnp.where(pblock == chosen, slot & (BLOCK - 1), -1)
    row = lax.broadcasted_iota(jnp.int32, (NOTE, count), 0)
    code = jnp.where(row == 0, chosen, jnp.where(row == 1, place, 0))
    half = count // 2
    lane = lax.broadcasted_iota(jnp.int32, (count, count), 1)
    source = lax.broadcasted_iota(jnp.int32, (count, count), 0)
    plane = (lane >= half).astype(jnp.int32)
    step = lax.shift_right_logical(lane & (half - 1), q_home.bit_length() - 1)
    wanted = ((2 * step + plane) ^ me) * q_home + (lane & (q_home - 1))
    order = jnp.where(source == wanted, 1.0, 0.0).astype(jnp.bfloat16)
    code = jnp.dot(code.astype(jnp.bfloat16), order, preferred_element_type=jnp.float32)
    rest = jnp.zeros((NOTE - 4, half), jnp.float32)
    note = jnp.concatenate([code[:2, :half], code[:2, half:], rest], axis=0)
    note_ref[...] = jnp.zeros_like(note_ref)
    note_ref[:, :half] = note.astype(note_ref.dtype)


def dense_shards(queries, label_weights, sibling_blocks, positive_slot):
    q_home, width = queries.shape
    qcount = sibling_blocks.shape[0]
    half = qcount // 2
    lab_dev = label_weights.shape[0]
    homes = lax.axis_size("lab")
    groups = lax.axis_size("pb")
    f32, bf16 = jnp.float32, jnp.bfloat16
    me = jnp.reshape(lax.axis_index("lab"), (1,)).astype(jnp.int32)
    far_bit = groups // 2
    came = [swap(queries, "lab", step) for step in range(2, homes, 2)]
    held, weights = local_call(
        hold_body,
        [like(q_home, width, bf16), like(lab_dev, width, bf16)],
        [queries, label_weights],
    )
    choice = jnp.concatenate([sibling_blocks.T, positive_slot[None]], axis=0).astype(f32)
    note = local_call(
        lambda *refs: note_body(lab_dev // BLOCK, q_home, *refs),
        [like(NOTE, width, bf16)],
        [me, choice],
    )[0]
    near, noted = local_call(
        join_body,
        [like(half, width, bf16), like(half + NOTE, width, bf16)],
        [held, *came, note],
        0,
        [weights],
    )
    far = swap(near, "lab", 1)
    work = 4 * half * lab_dev * width
    slope_like = like(BLOCK + NOTE, half, bf16)
    pair = [like(half // 2, width, f32), like(half // 2, width, bf16)]
    near_kept, near_sent, near_slope, near_copy = local_call(
        near_body,
        pair + [slope_like, like(half, width, bf16)],
        [near, weights, note],
        work,
    )
    cross_near = swap(noted, "pb", far_bit)
    cross_far = diagonal(near_copy, far_bit, 1)
    far_kept, far_sent, far_slope = local_call(
        far_body, pair + [slope_like], [far, weights, note], work, [near_slope]
    )
    far_came, near_came = swap(far_sent, "lab", 2), swap(near_sent, "lab", 2)
    acc, own = local_call(
        own_body,
        [like(lab_dev, width, f32), like(qcount + BLOCK + NOTE, width, bf16)],
        [near, far, near_slope, far_slope],
        work,
    )
    mate = swap(own, "pb", 1)
    home, sent = like(q_home, width, f32), like(q_home, width, bf16)
    near_kept, near_sent = local_call(
        fold_body, [home, sent], [near_kept, near_came], 0, [acc]
    )
    near_came = swap(near_sent, "lab", 4)
    far_sent, far_across = local_call(
        fold_body, [sent, sent], [far_kept, far_came], 0, [near_kept, acc]
    )
    far_came, far_across = swap(far_sent, "lab", 1), swap(far_across, "lab", 5)
    cross = local_call(
        stack_body, [like(qcount + NOTE, width, bf16)], [cross_near, cross_far], 0, [far_sent]
    )[0]
    cross_mate = swap(cross, "pb", 1)
    grown = like(lab_dev, width, f32)
    acc = local_call(cross_body, [grown], [cross, weights, acc], 20 * work)[0]
    acc = local_call(mate_body, [grown], [mate, acc], work)[0]
    weight_grad, mark = late(groups, cross_mate, weights, acc)
    query_grad = local_call(
        sum_body, [home], [near_kept, near_came, far_came, far_across], 0, [mark]
    )[0]
    return (query_grad, weight_grad)


def solution(mesh):
    groups, homes = mesh.shape["pb"], mesh.shape["lab"]

    def shards(queries, label_weights, sibling_blocks, positive_slot):
        every_row_everywhere = homes == K
        few = groups * sibling_blocks.shape[0] <= 2 * label_weights.shape[0]
        paired = groups == 4 and homes & (homes - 1) == 0
        one_block = label_weights.shape[0] // BLOCK <= K
        plan = dense_shards if every_row_everywhere and few and paired and one_block else sparse_shards
        return plan(queries, label_weights, sibling_blocks, positive_slot)

    in_specs = (P(("pb", "lab"), None), P("lab", None), P("pb", None), P("pb"))
    out_specs = (P(("pb", "lab"), None), P("lab", None))
    return jax.shard_map(shards, mesh=mesh, in_specs=in_specs, out_specs=out_specs, check_vma=False)
```

```python
import jax
import jax.numpy as jnp
from jax import lax
from jax.experimental import pallas as pl
from jax.experimental.pallas import tpu as pltpu
from jax.sharding import PartitionSpec as P

BLOCK = 128
K = 8
NOTE = 16
VMEM_LIMIT = 24 * 1024 * 1024


def pack_index(touched, width_slots, fill_value):
    homes, count = touched.shape
    rank = jnp.cumsum(touched.astype(jnp.int32), axis=1) - 1
    place = jnp.where(touched, rank, width_slots)
    home_ids = jnp.broadcast_to(jnp.arange(homes, dtype=jnp.int32)[:, None], touched.shape)
    row_ids = jnp.broadcast_to(jnp.arange(count, dtype=jnp.int32)[None, :], touched.shape)
    table = (
        jnp.full((homes, width_slots + 1), fill_value, jnp.int32).at[home_ids, place].set(row_ids)
    )
    return table[:, :width_slots]


def sparse_shards(queries, label_weights, sibling_blocks, positive_slot):
    width = queries.shape[1]
    qcount = sibling_blocks.shape[0]
    lab_dev = label_weights.shape[0]
    blocks_dev = lab_dev // BLOCK
    first = lax.axis_index("lab") * blocks_dev
    local_ids = first + jnp.arange(blocks_dev, dtype=jnp.int32)
    pblock = jnp.take_along_axis(sibling_blocks, (positive_slot // BLOCK)[:, None], axis=1)[:, 0]
    positive = pblock * BLOCK + positive_slot % BLOCK
    label_ids = local_ids[:, None] * BLOCK + jnp.arange(BLOCK, dtype=jnp.int32)[None, :]
    chosen_all = jnp.any(sibling_blocks[:, :, None] == local_ids[None, None, :], axis=1)
    piece = lax.all_gather(queries, "lab", axis=0, tiled=True)
    count = piece.shape[0]
    scores = jnp.dot(piece, label_weights.T, preferred_element_type=jnp.float32)
    scores = scores.reshape(count, blocks_dev, BLOCK)
    target = (label_ids[None, :, :] == positive[:, None, None]).astype(jnp.float32)
    slope = jnp.where(chosen_all[:, :, None], jax.nn.sigmoid(scores) - target, 0.0)
    slope = slope.astype(jnp.bfloat16).reshape(count, lab_dev)
    dq_all = jnp.dot(slope, label_weights, preferred_element_type=jnp.float32)
    w_acc = lax.dot_general(
        slope, piece, (((0,), (0,)), ((), ())), preferred_element_type=jnp.float32
    )
    homes = lax.axis_size("lab")
    q_home = qcount // homes
    slots = q_home * K // homes
    touched = jnp.any(chosen_all, axis=1).reshape(homes, q_home)
    send_idx = pack_index(touched, slots, q_home)
    padded = jnp.concatenate(
        [dq_all.reshape(homes, q_home, width), jnp.zeros((homes, 1, width), jnp.float32)], axis=1
    )
    outgoing = jnp.take_along_axis(padded, send_idx[:, :, None], axis=1)
    incoming = lax.all_to_all(outgoing, "lab", split_axis=0, concat_axis=0, tiled=True)
    own_blocks = lax.dynamic_slice_in_dim(sibling_blocks, lax.axis_index("lab") * q_home, q_home, 0)
    source_ids = jnp.arange(homes, dtype=jnp.int32)
    own_touch = jnp.any(
        (own_blocks // blocks_dev)[:, :, None] == source_ids[None, None, :], axis=1
    ).T
    recv_idx = pack_index(own_touch, slots, q_home)
    query_grad = (
        jnp.zeros((q_home + 1, width), jnp.float32)
        .at[recv_idx.reshape(-1)]
        .add(incoming.reshape(-1, width))[:q_home]
    )
    groups = lax.axis_size("pb")
    total = lax.psum(w_acc, "pb")
    weight_grad = (total / groups).astype(jnp.bfloat16)
    return (query_grad, weight_grad)


def swap(value, axis, bit):
    count = lax.axis_size(axis)
    return lax.ppermute(value, axis, [(i, i ^ bit) for i in range(count)])


def diagonal(value, group_bit, home_bit):
    groups, homes = lax.axis_size("pb"), lax.axis_size("lab")
    pairs = [
        (g * homes + h, (g ^ group_bit) * homes + (h ^ home_bit))
        for g in range(groups)
        for h in range(homes)
    ]
    return lax.ppermute(value, ("pb", "lab"), pairs)


def local_call(body, outs, args, flops=0, follows=()):
    specs = [
        pl.BlockSpec(memory_space=pltpu.SMEM if arg.dtype == jnp.int32 else pltpu.VMEM)
        for arg in args
    ]
    given, later = len(args), len(args) + len(follows)
    return pl.pallas_call(
        lambda *refs: body(*refs[:given], *refs[later:]),
        out_shape=outs,
        in_specs=specs + [pl.BlockSpec(memory_space=pl.ANY)] * len(follows),
        out_specs=[pl.BlockSpec(memory_space=pltpu.VMEM)] * len(outs),
        cost_estimate=pl.CostEstimate(flops=flops, bytes_accessed=0, transcendentals=0),
        compiler_params=pltpu.CompilerParams(vmem_limit_bytes=VMEM_LIMIT),
    )(*args, *follows)


def like(rows, width, dtype):
    return jax.ShapeDtypeStruct((rows, width), dtype)


def join_body(*refs):
    *came_refs, note_ref, out_ref, noted_ref = refs
    stack_body(*came_refs, out_ref)
    stack_body(*came_refs, note_ref, noted_ref)


def hold_body(*refs):
    for source, held in zip(refs[: len(refs) // 2], refs[len(refs) // 2 :]):
        held[...] = source[...]


def slope_of(rows, weights, chosen, place):
    count, blocks = rows.shape[0], weights.shape[0] // BLOCK
    scores = lax.dot_general(
        weights, rows, (((1,), (1,)), ((), ())), preferred_element_type=jnp.float32
    )
    named = jnp.zeros((BLOCK, count), jnp.float32)
    for block in range(blocks):
        named = jnp.where(chosen == block, scores[block * BLOCK : (block + 1) * BLOCK], named)
    ids = lax.broadcasted_iota(jnp.int32, (BLOCK, count), 0)
    return (jax.nn.sigmoid(named) - jnp.where(ids == place, 1.0, 0.0)).astype(jnp.bfloat16)


def spread(slope, chosen, blocks):
    wide = slope.astype(jnp.float32)
    parts = [jnp.where(chosen == block, wide, 0.0).astype(slope.dtype) for block in blocks]
    return jnp.concatenate(parts, axis=0)


def read_note(note, which, count):
    chosen = note[2 * which : 2 * which + 1, :count].astype(jnp.int32)
    place = note[2 * which + 1 : 2 * which + 2, :count].astype(jnp.int32)
    return chosen, place


def grad_body(which, rows_ref, weights_ref, note_ref, kept_ref, sent_ref, slope_ref):
    rows, weights = rows_ref[...], weights_ref[...]
    note = note_ref[...].astype(jnp.float32)
    chosen, place = read_note(note, which, rows.shape[0])
    slope = slope_of(rows, weights, chosen, place)
    slope_ref[:BLOCK, :] = slope
    slope_ref[BLOCK:, :] = jnp.broadcast_to(chosen, (NOTE, rows.shape[0])).astype(slope.dtype)
    dq = lax.dot_general(
        spread(slope, chosen, range(weights.shape[0] // BLOCK)),
        weights,
        (((0,), (0,)), ((), ())),
        preferred_element_type=jnp.float32,
    )
    halve(dq, kept_ref, sent_ref, kept_ref.shape[0] // 2)


def halve(terms, kept_ref, sent_ref, span):
    for start in range(0, kept_ref.shape[0], span):
        kept_ref[start : start + span, :] = terms[2 * start : 2 * start + span]
        sent = terms[2 * start + span : 2 * start + 2 * span]
        sent_ref[start : start + span, :] = sent.astype(sent_ref.dtype)


def near_body(rows_ref, weights_ref, note_ref, kept_ref, sent_ref, slope_ref, copy_ref):
    copy_ref[...] = rows_ref[...]
    grad_body(0, rows_ref, weights_ref, note_ref, kept_ref, sent_ref, slope_ref)


def far_body(rows_ref, weights_ref, note_ref, kept_ref, sent_ref, slope_ref):
    grad_body(1, rows_ref, weights_ref, note_ref, kept_ref, sent_ref, slope_ref)


def fold_body(terms_ref, came_ref, first_ref, second_ref):
    terms = terms_ref[...] + came_ref[...].astype(jnp.float32)
    span = first_ref.shape[0]
    first_ref[...] = terms[:span].astype(first_ref.dtype)
    second_ref[...] = terms[span:].astype(second_ref.dtype)


def sum_body(kept_ref, *refs):
    *term_refs, out_ref = refs
    total = kept_ref[...]
    for ref in term_refs:
        total = total + ref[...].astype(jnp.float32)
    out_ref[...] = total.astype(out_ref.dtype)


def stack_body(*refs):
    *came_refs, out_ref = refs
    start = 0
    for ref in came_refs:
        out_ref[start : start + ref.shape[0], : ref.shape[1]] = ref[...]
        start += ref.shape[0]


def read_slope(slope):
    chosen = slope[BLOCK : BLOCK + 1].astype(jnp.float32).astype(jnp.int32)
    return slope[:BLOCK], chosen


def own_body(near_ref, far_ref, near_slope_ref, far_slope_ref, acc_ref, set_ref):
    rows = jnp.concatenate([near_ref[...], far_ref[...]], axis=0)
    slope = jnp.concatenate([near_slope_ref[...], far_slope_ref[...]], axis=1)
    count = rows.shape[0]
    set_ref[:count, :] = rows
    set_ref[count:, :count] = slope
    wide = spread(*read_slope(slope), range(acc_ref.shape[0] // BLOCK))
    acc_ref[...] = jnp.dot(wide, rows, preferred_element_type=jnp.float32)


def set_slope(set_ref, weights):
    half = (set_ref.shape[0] - NOTE) // 2
    rows = jnp.concatenate([set_ref[:half, :], set_ref[half + NOTE :, :]], axis=0)
    note = set_ref[half : half + NOTE, :].astype(jnp.float32)
    codes = [read_note(note, which, half) for which in range(2)]
    chosen = jnp.concatenate([codes[0][0], codes[1][0]], axis=1)
    place = jnp.concatenate([codes[0][1], codes[1][1]], axis=1)
    return rows, slope_of(rows, weights, chosen, place), chosen


def cross_body(set_ref, weights_ref, acc_ref, out_ref):
    rows, slope, chosen = set_slope(set_ref, weights_ref[...])
    wide = spread(slope, chosen, range(acc_ref.shape[0] // BLOCK))
    out_ref[...] = acc_ref[...] + jnp.dot(wide, rows, preferred_element_type=jnp.float32)


def late_body(groups, set_ref, mate_ref, weights_ref, acc_ref, out_ref, mark_ref, held, sems):
    mark_ref[...] = jnp.zeros_like(mark_ref)
    rows, slope, chosen = set_slope(set_ref, weights_ref[...])
    count = mate_ref.shape[0] - BLOCK - NOTE
    mate_slope, mate_chosen = read_slope(mate_ref[count:, :count])
    rows = jnp.concatenate([rows, mate_ref[:count, :]], axis=0)
    slope = jnp.concatenate([slope, mate_slope], axis=1)
    chosen = jnp.concatenate([chosen, mate_chosen], axis=1)
    blocks = acc_ref.shape[0] // BLOCK
    chunk = blocks // sems.shape[0]
    copies = []
    for part in range(sems.shape[0]):
        here = pl.ds(part * chunk * BLOCK, chunk * BLOCK)
        wide = spread(slope, chosen, range(part * chunk, (part + 1) * chunk))
        total = acc_ref[here, :] + jnp.dot(wide, rows, preferred_element_type=jnp.float32)
        held[here, :] = (total / groups).astype(held.dtype)
        copy = pltpu.make_async_copy(held.at[here, :], out_ref.at[here, :], sems.at[part])
        copy.start()
        copies.append(copy)
    for copy in copies:
        copy.wait()


def late(groups, crossed, mate, weights, acc):
    out = like(*weights.shape, weights.dtype)
    chunks = 4
    return pl.pallas_call(
        lambda *refs: late_body(groups, *refs),
        out_shape=[out, like(1, BLOCK, jnp.int32)],
        in_specs=[pl.BlockSpec(memory_space=pltpu.VMEM)] * 4,
        out_specs=[pl.BlockSpec(memory_space=pl.ANY), pl.BlockSpec(memory_space=pltpu.VMEM)],
        scratch_shapes=[pltpu.VMEM(out.shape, out.dtype), pltpu.SemaphoreType.DMA((chunks,))],
        cost_estimate=pl.CostEstimate(flops=0, bytes_accessed=0, transcendentals=0),
        compiler_params=pltpu.CompilerParams(vmem_limit_bytes=VMEM_LIMIT),
    )(crossed, mate, weights, acc)


def note_body(blocks_dev, q_home, me_ref, choice_ref, note_ref):
    choice = choice_ref[...].astype(jnp.int32)
    me, picks, count = me_ref[0], choice.shape[0] - 1, choice.shape[1]
    local, slot = choice[:picks] - me * blocks_dev, choice[picks:]
    inside = (local >= 0) & (local < blocks_dev)
    chosen = jnp.max(jnp.where(inside, local, -1), axis=0, keepdims=True)
    steps = lax.broadcasted_iota(jnp.int32, local.shape, 0)
    named = steps == lax.shift_right_logical(slot, BLOCK.bit_length() - 1)
    pblock = jnp.sum(jnp.where(named, local, 0), axis=0, keepdims=True)
    place = jnp.where(pblock == chosen, slot & (BLOCK - 1), -1)
    row = lax.broadcasted_iota(jnp.int32, (NOTE, count), 0)
    code = jnp.where(row == 0, chosen, jnp.where(row == 1, place, 0))
    half = count // 2
    lane = lax.broadcasted_iota(jnp.int32, (count, count), 1)
    source = lax.broadcasted_iota(jnp.int32, (count, count), 0)
    plane = (lane >= half).astype(jnp.int32)
    step = lax.shift_right_logical(lane & (half - 1), q_home.bit_length() - 1)
    wanted = ((2 * step + plane) ^ me) * q_home + (lane & (q_home - 1))
    order = jnp.where(source == wanted, 1.0, 0.0).astype(jnp.bfloat16)
    code = jnp.dot(code.astype(jnp.bfloat16), order, preferred_element_type=jnp.float32)
    rest = jnp.zeros((NOTE - 4, half), jnp.float32)
    note = jnp.concatenate([code[:2, :half], code[:2, half:], rest], axis=0)
    note_ref[...] = jnp.zeros_like(note_ref)
    note_ref[:, :half] = note.astype(note_ref.dtype)


def dense_shards(queries, label_weights, sibling_blocks, positive_slot):
    q_home, width = queries.shape
    qcount = sibling_blocks.shape[0]
    half = qcount // 2
    lab_dev = label_weights.shape[0]
    homes = lax.axis_size("lab")
    groups = lax.axis_size("pb")
    f32, bf16 = jnp.float32, jnp.bfloat16
    me = jnp.reshape(lax.axis_index("lab"), (1,)).astype(jnp.int32)
    far_bit = groups // 2
    came = [swap(queries, "lab", step) for step in range(2, homes, 2)]
    held, weights = local_call(
        hold_body,
        [like(q_home, width, bf16), like(lab_dev, width, bf16)],
        [queries, label_weights],
    )
    choice = jnp.concatenate([sibling_blocks.T, positive_slot[None]], axis=0).astype(f32)
    note = local_call(
        lambda *refs: note_body(lab_dev // BLOCK, q_home, *refs),
        [like(NOTE, width, bf16)],
        [me, choice],
    )[0]
    near, noted = local_call(
        join_body,
        [like(half, width, bf16), like(half + NOTE, width, bf16)],
        [held, *came, note],
        0,
        [weights],
    )
    far = swap(near, "lab", 1)
    work = 4 * half * lab_dev * width
    slope_like = like(BLOCK + NOTE, half, bf16)
    pair = [like(half // 2, width, f32), like(half // 2, width, bf16)]
    near_kept, near_sent, near_slope, near_copy = local_call(
        near_body,
        pair + [slope_like, like(half, width, bf16)],
        [near, weights, note],
        work,
    )
    cross_near = swap(noted, "pb", far_bit)
    cross_far = diagonal(near_copy, far_bit, 1)
    far_kept, far_sent, far_slope = local_call(
        far_body, pair + [slope_like], [far, weights, note], work, [near_slope]
    )
    far_came, near_came = swap(far_sent, "lab", 2), swap(near_sent, "lab", 2)
    acc, own = local_call(
        own_body,
        [like(lab_dev, width, f32), like(qcount + BLOCK + NOTE, width, bf16)],
        [near, far, near_slope, far_slope],
        work,
    )
    mate = swap(own, "pb", 1)
    home, sent = like(q_home, width, f32), like(q_home, width, bf16)
    near_kept, near_sent = local_call(
        fold_body, [home, sent], [near_kept, near_came], 0, [acc]
    )
    near_came = swap(near_sent, "lab", 4)
    far_sent, far_across = local_call(
        fold_body, [sent, sent], [far_kept, far_came], 0, [near_kept, acc]
    )
    far_came, far_across = swap(far_sent, "lab", 1), swap(far_across, "lab", 5)
    cross = local_call(
        stack_body, [like(qcount + NOTE, width, bf16)], [cross_near, cross_far], 0, [far_sent]
    )[0]
    cross_mate = swap(cross, "pb", 1)
    grown = like(lab_dev, width, f32)
    acc = local_call(cross_body, [grown], [cross, weights, acc], 20 * work)[0]
    weight_grad, mark = late(groups, cross_mate, mate, weights, acc)
    query_grad = local_call(
        sum_body, [home], [near_kept, near_came, far_came, far_across], 0, [mark]
    )[0]
    return (query_grad, weight_grad)


def solution(mesh):
    groups, homes = mesh.shape["pb"], mesh.shape["lab"]

    def shards(queries, label_weights, sibling_blocks, positive_slot):
        every_row_everywhere = homes == K
        few = groups * sibling_blocks.shape[0] <= 2 * label_weights.shape[0]
        paired = groups == 4 and homes & (homes - 1) == 0
        one_block = label_weights.shape[0] // BLOCK <= K
        plan = dense_shards if every_row_everywhere and few and paired and one_block else sparse_shards
        return plan(queries, label_weights, sibling_blocks, positive_slot)

    in_specs = (P(("pb", "lab"), None), P("lab", None), P("pb", None), P("pb"))
    out_specs = (P(("pb", "lab"), None), P("lab", None))
    return jax.shard_map(shards, mesh=mesh, in_specs=in_specs, out_specs=out_specs, check_vma=False)
```

```python
import jax
import jax.numpy as jnp
from jax import lax
from jax.experimental import pallas as pl
from jax.experimental.pallas import tpu as pltpu
from jax.sharding import PartitionSpec as P

BLOCK = 128
K = 8
NOTE = 16
VMEM_LIMIT = 24 * 1024 * 1024


def pack_index(touched, width_slots, fill_value):
    homes, count = touched.shape
    rank = jnp.cumsum(touched.astype(jnp.int32), axis=1) - 1
    place = jnp.where(touched, rank, width_slots)
    home_ids = jnp.broadcast_to(jnp.arange(homes, dtype=jnp.int32)[:, None], touched.shape)
    row_ids = jnp.broadcast_to(jnp.arange(count, dtype=jnp.int32)[None, :], touched.shape)
    table = (
        jnp.full((homes, width_slots + 1), fill_value, jnp.int32).at[home_ids, place].set(row_ids)
    )
    return table[:, :width_slots]


def sparse_shards(queries, label_weights, sibling_blocks, positive_slot):
    width = queries.shape[1]
    qcount = sibling_blocks.shape[0]
    lab_dev = label_weights.shape[0]
    blocks_dev = lab_dev // BLOCK
    first = lax.axis_index("lab") * blocks_dev
    local_ids = first + jnp.arange(blocks_dev, dtype=jnp.int32)
    pblock = jnp.take_along_axis(sibling_blocks, (positive_slot // BLOCK)[:, None], axis=1)[:, 0]
    positive = pblock * BLOCK + positive_slot % BLOCK
    label_ids = local_ids[:, None] * BLOCK + jnp.arange(BLOCK, dtype=jnp.int32)[None, :]
    chosen_all = jnp.any(sibling_blocks[:, :, None] == local_ids[None, None, :], axis=1)
    piece = lax.all_gather(queries, "lab", axis=0, tiled=True)
    count = piece.shape[0]
    scores = jnp.dot(piece, label_weights.T, preferred_element_type=jnp.float32)
    scores = scores.reshape(count, blocks_dev, BLOCK)
    target = (label_ids[None, :, :] == positive[:, None, None]).astype(jnp.float32)
    slope = jnp.where(chosen_all[:, :, None], jax.nn.sigmoid(scores) - target, 0.0)
    slope = slope.astype(jnp.bfloat16).reshape(count, lab_dev)
    dq_all = jnp.dot(slope, label_weights, preferred_element_type=jnp.float32)
    w_acc = lax.dot_general(
        slope, piece, (((0,), (0,)), ((), ())), preferred_element_type=jnp.float32
    )
    homes = lax.axis_size("lab")
    q_home = qcount // homes
    slots = q_home * K // homes
    touched = jnp.any(chosen_all, axis=1).reshape(homes, q_home)
    send_idx = pack_index(touched, slots, q_home)
    padded = jnp.concatenate(
        [dq_all.reshape(homes, q_home, width), jnp.zeros((homes, 1, width), jnp.float32)], axis=1
    )
    outgoing = jnp.take_along_axis(padded, send_idx[:, :, None], axis=1)
    incoming = lax.all_to_all(outgoing, "lab", split_axis=0, concat_axis=0, tiled=True)
    own_blocks = lax.dynamic_slice_in_dim(sibling_blocks, lax.axis_index("lab") * q_home, q_home, 0)
    source_ids = jnp.arange(homes, dtype=jnp.int32)
    own_touch = jnp.any(
        (own_blocks // blocks_dev)[:, :, None] == source_ids[None, None, :], axis=1
    ).T
    recv_idx = pack_index(own_touch, slots, q_home)
    query_grad = (
        jnp.zeros((q_home + 1, width), jnp.float32)
        .at[recv_idx.reshape(-1)]
        .add(incoming.reshape(-1, width))[:q_home]
    )
    groups = lax.axis_size("pb")
    total = lax.psum(w_acc, "pb")
    weight_grad = (total / groups).astype(jnp.bfloat16)
    return (query_grad, weight_grad)


def swap(value, axis, bit):
    count = lax.axis_size(axis)
    return lax.ppermute(value, axis, [(i, i ^ bit) for i in range(count)])


def diagonal(value, group_bit, home_bit):
    groups, homes = lax.axis_size("pb"), lax.axis_size("lab")
    pairs = [
        (g * homes + h, (g ^ group_bit) * homes + (h ^ home_bit))
        for g in range(groups)
        for h in range(homes)
    ]
    return lax.ppermute(value, ("pb", "lab"), pairs)


def local_call(body, outs, args, flops=0, follows=()):
    specs = [
        pl.BlockSpec(memory_space=pltpu.SMEM if arg.dtype == jnp.int32 else pltpu.VMEM)
        for arg in args
    ]
    given, later = len(args), len(args) + len(follows)
    return pl.pallas_call(
        lambda *refs: body(*refs[:given], *refs[later:]),
        out_shape=outs,
        in_specs=specs + [pl.BlockSpec(memory_space=pl.ANY)] * len(follows),
        out_specs=[pl.BlockSpec(memory_space=pltpu.VMEM)] * len(outs),
        cost_estimate=pl.CostEstimate(flops=flops, bytes_accessed=0, transcendentals=0),
        compiler_params=pltpu.CompilerParams(vmem_limit_bytes=VMEM_LIMIT),
    )(*args, *follows)


def like(rows, width, dtype):
    return jax.ShapeDtypeStruct((rows, width), dtype)


def join_body(*refs):
    *came_refs, note_ref, out_ref, noted_ref = refs
    stack_body(*came_refs, out_ref)
    stack_body(*came_refs, note_ref, noted_ref)


def hold_body(*refs):
    for source, held in zip(refs[: len(refs) // 2], refs[len(refs) // 2 :]):
        held[...] = source[...]


def slope_of(rows, weights, chosen, place):
    count, blocks = rows.shape[0], weights.shape[0] // BLOCK
    scores = lax.dot_general(
        weights, rows, (((1,), (1,)), ((), ())), preferred_element_type=jnp.float32
    )
    named = jnp.zeros((BLOCK, count), jnp.float32)
    for block in range(blocks):
        named = jnp.where(chosen == block, scores[block * BLOCK : (block + 1) * BLOCK], named)
    ids = lax.broadcasted_iota(jnp.int32, (BLOCK, count), 0)
    return (jax.nn.sigmoid(named) - jnp.where(ids == place, 1.0, 0.0)).astype(jnp.bfloat16)


def spread(slope, chosen, blocks):
    wide = slope.astype(jnp.float32)
    parts = [jnp.where(chosen == block, wide, 0.0).astype(slope.dtype) for block in blocks]
    return jnp.concatenate(parts, axis=0)


def read_note(note, which, count):
    chosen = note[2 * which : 2 * which + 1, :count].astype(jnp.int32)
    place = note[2 * which + 1 : 2 * which + 2, :count].astype(jnp.int32)
    return chosen, place


def grad_body(which, rows_ref, weights_ref, note_ref, kept_ref, sent_ref, slope_ref):
    rows, weights = rows_ref[...], weights_ref[...]
    note = note_ref[...].astype(jnp.float32)
    chosen, place = read_note(note, which, rows.shape[0])
    slope = slope_of(rows, weights, chosen, place)
    slope_ref[:BLOCK, :] = slope
    slope_ref[BLOCK:, :] = jnp.broadcast_to(chosen, (NOTE, rows.shape[0])).astype(slope.dtype)
    dq = lax.dot_general(
        spread(slope, chosen, range(weights.shape[0] // BLOCK)),
        weights,
        (((0,), (0,)), ((), ())),
        preferred_element_type=jnp.float32,
    )
    halve(dq, kept_ref, sent_ref, kept_ref.shape[0] // 2)


def halve(terms, kept_ref, sent_ref, span):
    for start in range(0, kept_ref.shape[0], span):
        kept_ref[start : start + span, :] = terms[2 * start : 2 * start + span]
        sent = terms[2 * start + span : 2 * start + 2 * span]
        sent_ref[start : start + span, :] = sent.astype(sent_ref.dtype)


def near_body(rows_ref, weights_ref, note_ref, kept_ref, sent_ref, slope_ref, copy_ref):
    copy_ref[...] = rows_ref[...]
    grad_body(0, rows_ref, weights_ref, note_ref, kept_ref, sent_ref, slope_ref)


def far_body(rows_ref, weights_ref, note_ref, kept_ref, sent_ref, slope_ref):
    grad_body(1, rows_ref, weights_ref, note_ref, kept_ref, sent_ref, slope_ref)


def fold_body(terms_ref, came_ref, first_ref, second_ref):
    terms = terms_ref[...] + came_ref[...].astype(jnp.float32)
    span = first_ref.shape[0]
    first_ref[...] = terms[:span].astype(first_ref.dtype)
    second_ref[...] = terms[span:].astype(second_ref.dtype)


def stack_body(*refs):
    *came_refs, out_ref = refs
    start = 0
    for ref in came_refs:
        out_ref[start : start + ref.shape[0], : ref.shape[1]] = ref[...]
        start += ref.shape[0]


def read_slope(slope):
    chosen = slope[BLOCK : BLOCK + 1].astype(jnp.float32).astype(jnp.int32)
    return slope[:BLOCK], chosen


def own_body(near_ref, far_ref, near_slope_ref, far_slope_ref, acc_ref, set_ref):
    rows = jnp.concatenate([near_ref[...], far_ref[...]], axis=0)
    slope = jnp.concatenate([near_slope_ref[...], far_slope_ref[...]], axis=1)
    count = rows.shape[0]
    set_ref[:count, :] = rows
    set_ref[count:, :count] = slope
    wide = spread(*read_slope(slope), range(acc_ref.shape[0] // BLOCK))
    acc_ref[...] = jnp.dot(wide, rows, preferred_element_type=jnp.float32)


def set_slope(set_ref, weights):
    half = (set_ref.shape[0] - NOTE) // 2
    rows = jnp.concatenate([set_ref[:half, :], set_ref[half + NOTE :, :]], axis=0)
    note = set_ref[half : half + NOTE, :].astype(jnp.float32)
    codes = [read_note(note, which, half) for which in range(2)]
    chosen = jnp.concatenate([codes[0][0], codes[1][0]], axis=1)
    place = jnp.concatenate([codes[0][1], codes[1][1]], axis=1)
    return rows, slope_of(rows, weights, chosen, place), chosen


def cross_body(set_ref, weights_ref, acc_ref, out_ref):
    rows, slope, chosen = set_slope(set_ref, weights_ref[...])
    wide = spread(slope, chosen, range(acc_ref.shape[0] // BLOCK))
    out_ref[...] = acc_ref[...] + jnp.dot(wide, rows, preferred_element_type=jnp.float32)


def cross_slope_body(set_ref, weights_ref, slope_ref):
    _, slope, chosen = set_slope(set_ref, weights_ref[...])
    slope_ref[:BLOCK, :] = slope
    slope_ref[BLOCK:, :] = jnp.broadcast_to(chosen, (NOTE, chosen.shape[1])).astype(slope.dtype)


def late_body(
    groups, set_ref, slope_ref, mate_ref, acc_ref, kept_ref, *refs
):
    *term_refs, out_ref, home_ref, held, total, sems, home_sem = refs
    gathered = kept_ref[...]
    for ref in term_refs:
        gathered = gathered + ref[...].astype(jnp.float32)
    total[...] = gathered
    copies = [pltpu.make_async_copy(total, home_ref, home_sem)]
    copies[0].start()
    half = (set_ref.shape[0] - NOTE) // 2
    count = mate_ref.shape[0] - BLOCK - NOTE
    rows = jnp.concatenate(
        [set_ref[:half, :], set_ref[half + NOTE :, :], mate_ref[:count, :]], axis=0
    )
    slope = jnp.concatenate([slope_ref[...], mate_ref[count:, :count]], axis=1)
    slope, chosen = read_slope(slope)
    blocks = acc_ref.shape[0] // BLOCK
    chunk = blocks // sems.shape[0]
    for part in range(sems.shape[0]):
        here = pl.ds(part * chunk * BLOCK, chunk * BLOCK)
        wide = spread(slope, chosen, range(part * chunk, (part + 1) * chunk))
        sums = acc_ref[here, :] + jnp.dot(wide, rows, preferred_element_type=jnp.float32)
        held[here, :] = (sums / groups).astype(held.dtype)
        copy = pltpu.make_async_copy(held.at[here, :], out_ref.at[here, :], sems.at[part])
        copy.start()
        copies.append(copy)
    for copy in copies:
        copy.wait()


def late(groups, crossed, slope, mate, acc, kept, terms):
    out = like(*acc.shape, crossed.dtype)
    args = [crossed, slope, mate, acc, kept, *terms]
    chunks = 4
    return pl.pallas_call(
        lambda *refs: late_body(groups, *refs),
        out_shape=[out, like(*kept.shape, kept.dtype)],
        in_specs=[pl.BlockSpec(memory_space=pltpu.VMEM)] * len(args),
        out_specs=[pl.BlockSpec(memory_space=pl.ANY)] * 2,
        scratch_shapes=[
            pltpu.VMEM(out.shape, out.dtype),
            pltpu.VMEM(kept.shape, kept.dtype),
            pltpu.SemaphoreType.DMA((chunks,)),
            pltpu.SemaphoreType.DMA,
        ],
        cost_estimate=pl.CostEstimate(flops=0, bytes_accessed=0, transcendentals=0),
        compiler_params=pltpu.CompilerParams(vmem_limit_bytes=VMEM_LIMIT),
    )(*args)


def note_body(blocks_dev, q_home, me_ref, choice_ref, note_ref):
    choice = choice_ref[...].astype(jnp.int32)
    me, picks, count = me_ref[0], choice.shape[0] - 1, choice.shape[1]
    local, slot = choice[:picks] - me * blocks_dev, choice[picks:]
    inside = (local >= 0) & (local < blocks_dev)
    chosen = jnp.max(jnp.where(inside, local, -1), axis=0, keepdims=True)
    steps = lax.broadcasted_iota(jnp.int32, local.shape, 0)
    named = steps == lax.shift_right_logical(slot, BLOCK.bit_length() - 1)
    pblock = jnp.sum(jnp.where(named, local, 0), axis=0, keepdims=True)
    place = jnp.where(pblock == chosen, slot & (BLOCK - 1), -1)
    row = lax.broadcasted_iota(jnp.int32, (NOTE, count), 0)
    code = jnp.where(row == 0, chosen, jnp.where(row == 1, place, 0))
    half = count // 2
    lane = lax.broadcasted_iota(jnp.int32, (count, count), 1)
    source = lax.broadcasted_iota(jnp.int32, (count, count), 0)
    plane = (lane >= half).astype(jnp.int32)
    step = lax.shift_right_logical(lane & (half - 1), q_home.bit_length() - 1)
    wanted = ((2 * step + plane) ^ me) * q_home + (lane & (q_home - 1))
    order = jnp.where(source == wanted, 1.0, 0.0).astype(jnp.bfloat16)
    code = jnp.dot(code.astype(jnp.bfloat16), order, preferred_element_type=jnp.float32)
    rest = jnp.zeros((NOTE - 4, half), jnp.float32)
    note = jnp.concatenate([code[:2, :half], code[:2, half:], rest], axis=0)
    note_ref[...] = jnp.zeros_like(note_ref)
    note_ref[:, :half] = note.astype(note_ref.dtype)


def dense_shards(queries, label_weights, sibling_blocks, positive_slot):
    q_home, width = queries.shape
    qcount = sibling_blocks.shape[0]
    half = qcount // 2
    lab_dev = label_weights.shape[0]
    homes = lax.axis_size("lab")
    groups = lax.axis_size("pb")
    f32, bf16 = jnp.float32, jnp.bfloat16
    me = jnp.reshape(lax.axis_index("lab"), (1,)).astype(jnp.int32)
    far_bit = groups // 2
    came = [swap(queries, "lab", step) for step in range(2, homes, 2)]
    held, weights = local_call(
        hold_body,
        [like(q_home, width, bf16), like(lab_dev, width, bf16)],
        [queries, label_weights],
    )
    choice = jnp.concatenate([sibling_blocks.T, positive_slot[None]], axis=0).astype(f32)
    note = local_call(
        lambda *refs: note_body(lab_dev // BLOCK, q_home, *refs),
        [like(NOTE, width, bf16)],
        [me, choice],
    )[0]
    near, noted = local_call(
        join_body,
        [like(half, width, bf16), like(half + NOTE, width, bf16)],
        [held, *came, note],
        0,
        [weights],
    )
    far = swap(near, "lab", 1)
    work = 4 * half * lab_dev * width
    slope_like = like(BLOCK + NOTE, half, bf16)
    pair = [like(half // 2, width, f32), like(half // 2, width, bf16)]
    near_kept, near_sent, near_slope, near_copy = local_call(
        near_body,
        pair + [slope_like, like(half, width, bf16)],
        [near, weights, note],
        work,
    )
    cross_near = swap(noted, "pb", far_bit)
    cross_far = diagonal(near_copy, far_bit, 1)
    far_kept, far_sent, far_slope = local_call(
        far_body, pair + [slope_like], [far, weights, note], work, [near_slope]
    )
    far_came, near_came = swap(far_sent, "lab", 2), swap(near_sent, "lab", 2)
    acc, own = local_call(
        own_body,
        [like(lab_dev, width, f32), like(qcount + BLOCK + NOTE, width, bf16)],
        [near, far, near_slope, far_slope],
        work,
    )
    mate = swap(own, "pb", 1)
    home, sent = like(q_home, width, f32), like(q_home, width, bf16)
    near_kept, near_sent = local_call(
        fold_body, [home, sent], [near_kept, near_came], 0, [acc]
    )
    near_came = swap(near_sent, "lab", 4)
    far_sent, far_across = local_call(
        fold_body, [sent, sent], [far_kept, far_came], 0, [near_kept, acc]
    )
    far_came, far_across = swap(far_sent, "lab", 1), swap(far_across, "lab", 5)
    cross = local_call(
        stack_body, [like(qcount + NOTE, width, bf16)], [cross_near, cross_far], 0, [far_sent]
    )[0]
    cross_mate = swap(cross, "pb", 1)
    grown = like(lab_dev, width, f32)
    acc = local_call(cross_body, [grown], [cross, weights, acc], 20 * work)[0]
    slope = local_call(
        cross_slope_body,
        [like(BLOCK + NOTE, qcount, bf16)],
        [cross_mate, weights],
        2 * work,
        [acc],
    )[0]
    weight_grad, query_grad = late(
        groups, cross_mate, slope, mate, acc, near_kept, [near_came, far_came, far_across]
    )
    return (query_grad, weight_grad)


def solution(mesh):
    groups, homes = mesh.shape["pb"], mesh.shape["lab"]

    def shards(queries, label_weights, sibling_blocks, positive_slot):
        every_row_everywhere = homes == K
        few = groups * sibling_blocks.shape[0] <= 2 * label_weights.shape[0]
        paired = groups == 4 and homes & (homes - 1) == 0
        one_block = label_weights.shape[0] // BLOCK <= K
        plan = dense_shards if every_row_everywhere and few and paired and one_block else sparse_shards
        return plan(queries, label_weights, sibling_blocks, positive_slot)

    in_specs = (P(("pb", "lab"), None), P("lab", None), P("pb", None), P("pb"))
    out_specs = (P(("pb", "lab"), None), P("lab", None))
    return jax.shard_map(shards, mesh=mesh, in_specs=in_specs, out_specs=out_specs, check_vma=False)
```

```python
import jax
import jax.numpy as jnp
from jax import lax
from jax.experimental import pallas as pl
from jax.experimental.pallas import tpu as pltpu
from jax.sharding import PartitionSpec as P

BLOCK = 128
K = 8
NOTE = 16
VMEM_LIMIT = 24 * 1024 * 1024


def pack_index(touched, width_slots, fill_value):
    homes, count = touched.shape
    rank = jnp.cumsum(touched.astype(jnp.int32), axis=1) - 1
    place = jnp.where(touched, rank, width_slots)
    home_ids = jnp.broadcast_to(jnp.arange(homes, dtype=jnp.int32)[:, None], touched.shape)
    row_ids = jnp.broadcast_to(jnp.arange(count, dtype=jnp.int32)[None, :], touched.shape)
    table = (
        jnp.full((homes, width_slots + 1), fill_value, jnp.int32).at[home_ids, place].set(row_ids)
    )
    return table[:, :width_slots]


def sparse_shards(queries, label_weights, sibling_blocks, positive_slot):
    width = queries.shape[1]
    qcount = sibling_blocks.shape[0]
    lab_dev = label_weights.shape[0]
    blocks_dev = lab_dev // BLOCK
    first = lax.axis_index("lab") * blocks_dev
    local_ids = first + jnp.arange(blocks_dev, dtype=jnp.int32)
    pblock = jnp.take_along_axis(sibling_blocks, (positive_slot // BLOCK)[:, None], axis=1)[:, 0]
    positive = pblock * BLOCK + positive_slot % BLOCK
    label_ids = local_ids[:, None] * BLOCK + jnp.arange(BLOCK, dtype=jnp.int32)[None, :]
    chosen_all = jnp.any(sibling_blocks[:, :, None] == local_ids[None, None, :], axis=1)
    piece = lax.all_gather(queries, "lab", axis=0, tiled=True)
    count = piece.shape[0]
    scores = jnp.dot(piece, label_weights.T, preferred_element_type=jnp.float32)
    scores = scores.reshape(count, blocks_dev, BLOCK)
    target = (label_ids[None, :, :] == positive[:, None, None]).astype(jnp.float32)
    slope = jnp.where(chosen_all[:, :, None], jax.nn.sigmoid(scores) - target, 0.0)
    slope = slope.astype(jnp.bfloat16).reshape(count, lab_dev)
    dq_all = jnp.dot(slope, label_weights, preferred_element_type=jnp.float32)
    w_acc = lax.dot_general(
        slope, piece, (((0,), (0,)), ((), ())), preferred_element_type=jnp.float32
    )
    homes = lax.axis_size("lab")
    q_home = qcount // homes
    slots = q_home * K // homes
    touched = jnp.any(chosen_all, axis=1).reshape(homes, q_home)
    send_idx = pack_index(touched, slots, q_home)
    padded = jnp.concatenate(
        [dq_all.reshape(homes, q_home, width), jnp.zeros((homes, 1, width), jnp.float32)], axis=1
    )
    outgoing = jnp.take_along_axis(padded, send_idx[:, :, None], axis=1)
    incoming = lax.all_to_all(outgoing, "lab", split_axis=0, concat_axis=0, tiled=True)
    own_blocks = lax.dynamic_slice_in_dim(sibling_blocks, lax.axis_index("lab") * q_home, q_home, 0)
    source_ids = jnp.arange(homes, dtype=jnp.int32)
    own_touch = jnp.any(
        (own_blocks // blocks_dev)[:, :, None] == source_ids[None, None, :], axis=1
    ).T
    recv_idx = pack_index(own_touch, slots, q_home)
    query_grad = (
        jnp.zeros((q_home + 1, width), jnp.float32)
        .at[recv_idx.reshape(-1)]
        .add(incoming.reshape(-1, width))[:q_home]
    )
    groups = lax.axis_size("pb")
    total = lax.psum(w_acc, "pb")
    weight_grad = (total / groups).astype(jnp.bfloat16)
    return (query_grad, weight_grad)


def swap(value, axis, bit):
    count = lax.axis_size(axis)
    return lax.ppermute(value, axis, [(i, i ^ bit) for i in range(count)])


def diagonal(value, group_bit, home_bit):
    groups, homes = lax.axis_size("pb"), lax.axis_size("lab")
    pairs = [
        (g * homes + h, (g ^ group_bit) * homes + (h ^ home_bit))
        for g in range(groups)
        for h in range(homes)
    ]
    return lax.ppermute(value, ("pb", "lab"), pairs)


def local_call(body, outs, args, flops=0, follows=()):
    specs = [
        pl.BlockSpec(memory_space=pltpu.SMEM if arg.dtype == jnp.int32 else pltpu.VMEM)
        for arg in args
    ]
    given, later = len(args), len(args) + len(follows)
    return pl.pallas_call(
        lambda *refs: body(*refs[:given], *refs[later:]),
        out_shape=outs,
        in_specs=specs + [pl.BlockSpec(memory_space=pl.ANY)] * len(follows),
        out_specs=[pl.BlockSpec(memory_space=pltpu.VMEM)] * len(outs),
        cost_estimate=pl.CostEstimate(flops=flops, bytes_accessed=0, transcendentals=0),
        compiler_params=pltpu.CompilerParams(vmem_limit_bytes=VMEM_LIMIT),
    )(*args, *follows)


def like(rows, width, dtype):
    return jax.ShapeDtypeStruct((rows, width), dtype)


def join_body(*refs):
    own_ref, first_ref, *rest, note_ref, out_ref, noted_ref = refs
    came_refs = [own_ref, first_ref, *rest[::-1]]
    stack_body(*came_refs, out_ref)
    stack_body(*came_refs, note_ref, noted_ref)


def hold_body(*refs):
    for source, held in zip(refs[: len(refs) // 2], refs[len(refs) // 2 :]):
        held[...] = source[...]


def slope_of(rows, weights, chosen, place):
    count, blocks = rows.shape[0], weights.shape[0] // BLOCK
    scores = lax.dot_general(
        weights, rows, (((1,), (1,)), ((), ())), preferred_element_type=jnp.float32
    )
    named = jnp.zeros((BLOCK, count), jnp.float32)
    for block in range(blocks):
        named = jnp.where(chosen == block, scores[block * BLOCK : (block + 1) * BLOCK], named)
    ids = lax.broadcasted_iota(jnp.int32, (BLOCK, count), 0)
    return (jax.nn.sigmoid(named) - jnp.where(ids == place, 1.0, 0.0)).astype(jnp.bfloat16)


def spread(slope, chosen, blocks):
    wide = slope.astype(jnp.float32)
    parts = [jnp.where(chosen == block, wide, 0.0).astype(slope.dtype) for block in blocks]
    return jnp.concatenate(parts, axis=0)


def read_note(note, which, count):
    chosen = note[2 * which : 2 * which + 1, :count].astype(jnp.int32)
    place = note[2 * which + 1 : 2 * which + 2, :count].astype(jnp.int32)
    return chosen, place


def grad_body(which, rows_ref, weights_ref, note_ref, kept_ref, sent_ref, slope_ref):
    rows, weights = rows_ref[...], weights_ref[...]
    note = note_ref[...].astype(jnp.float32)
    chosen, place = read_note(note, which, rows.shape[0])
    slope = slope_of(rows, weights, chosen, place)
    slope_ref[:BLOCK, :] = slope
    slope_ref[BLOCK:, :] = jnp.broadcast_to(chosen, (NOTE, rows.shape[0])).astype(slope.dtype)
    dq = lax.dot_general(
        spread(slope, chosen, range(weights.shape[0] // BLOCK)),
        weights,
        (((0,), (0,)), ((), ())),
        preferred_element_type=jnp.float32,
    )
    halve(dq, kept_ref, sent_ref, kept_ref.shape[0] // 2)


def halve(terms, kept_ref, sent_ref, span):
    for start in range(0, kept_ref.shape[0], span):
        kept_ref[start : start + span, :] = terms[2 * start : 2 * start + span]
        sent = terms[2 * start + span : 2 * start + 2 * span]
        sent_ref[start : start + span, :] = sent.astype(sent_ref.dtype)


def near_body(rows_ref, weights_ref, note_ref, kept_ref, sent_ref, slope_ref, copy_ref):
    copy_ref[...] = rows_ref[...]
    grad_body(0, rows_ref, weights_ref, note_ref, kept_ref, sent_ref, slope_ref)


def far_body(rows_ref, weights_ref, note_ref, kept_ref, sent_ref, slope_ref):
    grad_body(1, rows_ref, weights_ref, note_ref, kept_ref, sent_ref, slope_ref)


def fold_body(terms_ref, came_ref, first_ref, second_ref):
    terms = terms_ref[...] + came_ref[...].astype(jnp.float32)
    span = first_ref.shape[0]
    first_ref[...] = terms[:span].astype(first_ref.dtype)
    second_ref[...] = terms[span:].astype(second_ref.dtype)


def stack_body(*refs):
    *came_refs, out_ref = refs
    start = 0
    for ref in came_refs:
        out_ref[start : start + ref.shape[0], : ref.shape[1]] = ref[...]
        start += ref.shape[0]


def read_slope(slope):
    chosen = slope[BLOCK : BLOCK + 1].astype(jnp.float32).astype(jnp.int32)
    return slope[:BLOCK], chosen


def own_body(near_ref, far_ref, near_slope_ref, far_slope_ref, acc_ref, set_ref):
    rows = jnp.concatenate([near_ref[...], far_ref[...]], axis=0)
    slope = jnp.concatenate([near_slope_ref[...], far_slope_ref[...]], axis=1)
    count = rows.shape[0]
    set_ref[:count, :] = rows
    set_ref[count:, :count] = slope
    wide = spread(*read_slope(slope), range(acc_ref.shape[0] // BLOCK))
    acc_ref[...] = jnp.dot(wide, rows, preferred_element_type=jnp.float32)


def set_slope(set_ref, weights):
    half = (set_ref.shape[0] - NOTE) // 2
    rows = jnp.concatenate([set_ref[:half, :], set_ref[half + NOTE :, :]], axis=0)
    note = set_ref[half : half + NOTE, :].astype(jnp.float32)
    codes = [read_note(note, which, half) for which in range(2)]
    chosen = jnp.concatenate([codes[0][0], codes[1][0]], axis=1)
    place = jnp.concatenate([codes[0][1], codes[1][1]], axis=1)
    return rows, slope_of(rows, weights, chosen, place), chosen


def cross_slope_body(set_ref, weights_ref, slope_ref):
    _, slope, chosen = set_slope(set_ref, weights_ref[...])
    slope_ref[:BLOCK, :] = slope
    slope_ref[BLOCK:, :] = jnp.broadcast_to(chosen, (NOTE, chosen.shape[1])).astype(slope.dtype)


def set_rows(set_ref):
    half = (set_ref.shape[0] - NOTE) // 2
    return jnp.concatenate([set_ref[:half, :], set_ref[half + NOTE :, :]], axis=0)


def sets_body(cross_ref, slope_ref, mate_ref, acc_ref, out_ref):
    count = mate_ref.shape[0] - BLOCK - NOTE
    rows = jnp.concatenate([set_rows(cross_ref), mate_ref[:count, :]], axis=0)
    slope = jnp.concatenate([slope_ref[...], mate_ref[count:, :count]], axis=1)
    wide = spread(*read_slope(slope), range(acc_ref.shape[0] // BLOCK))
    out_ref[...] = acc_ref[...] + jnp.dot(wide, rows, preferred_element_type=jnp.float32)


def late_body(groups, set_ref, slope_ref, acc_ref, out_ref, mark_ref, held, sems):
    mark_ref[...] = jnp.zeros_like(mark_ref)
    rows, (slope, chosen) = set_rows(set_ref), read_slope(slope_ref[...])
    blocks = acc_ref.shape[0] // BLOCK
    chunk = blocks // sems.shape[0]
    copies = []
    for part in range(sems.shape[0]):
        here = pl.ds(part * chunk * BLOCK, chunk * BLOCK)
        wide = spread(slope, chosen, range(part * chunk, (part + 1) * chunk))
        sums = acc_ref[here, :] + jnp.dot(wide, rows, preferred_element_type=jnp.float32)
        held[here, :] = (sums / groups).astype(held.dtype)
        copy = pltpu.make_async_copy(held.at[here, :], out_ref.at[here, :], sems.at[part])
        copy.start()
        copies.append(copy)
    for copy in copies:
        copy.wait()


def late(groups, crossed, slope, acc):
    out = like(*acc.shape, crossed.dtype)
    chunks = 4
    return pl.pallas_call(
        lambda *refs: late_body(groups, *refs),
        out_shape=[out, like(1, BLOCK, jnp.int32)],
        in_specs=[pl.BlockSpec(memory_space=pltpu.VMEM)] * 3,
        out_specs=[pl.BlockSpec(memory_space=pl.ANY), pl.BlockSpec(memory_space=pltpu.VMEM)],
        scratch_shapes=[pltpu.VMEM(out.shape, out.dtype), pltpu.SemaphoreType.DMA((chunks,))],
        cost_estimate=pl.CostEstimate(flops=0, bytes_accessed=0, transcendentals=0),
        compiler_params=pltpu.CompilerParams(vmem_limit_bytes=VMEM_LIMIT),
    )(crossed, slope, acc)


def sum_body(kept_ref, *refs):
    *term_refs, out_ref = refs
    total = kept_ref[...]
    for ref in term_refs:
        total = total + ref[...].astype(jnp.float32)
    out_ref[...] = total


def note_body(blocks_dev, q_home, me_ref, choice_ref, note_ref):
    choice = choice_ref[...].astype(jnp.int32)
    me, picks, count = me_ref[0], choice.shape[0] - 1, choice.shape[1]
    local, slot = choice[:picks] - me * blocks_dev, choice[picks:]
    inside = (local >= 0) & (local < blocks_dev)
    chosen = jnp.max(jnp.where(inside, local, -1), axis=0, keepdims=True)
    steps = lax.broadcasted_iota(jnp.int32, local.shape, 0)
    named = steps == lax.shift_right_logical(slot, BLOCK.bit_length() - 1)
    pblock = jnp.sum(jnp.where(named, local, 0), axis=0, keepdims=True)
    place = jnp.where(pblock == chosen, slot & (BLOCK - 1), -1)
    row = lax.broadcasted_iota(jnp.int32, (NOTE, count), 0)
    code = jnp.where(row == 0, chosen, jnp.where(row == 1, place, 0))
    half = count // 2
    lane = lax.broadcasted_iota(jnp.int32, (count, count), 1)
    source = lax.broadcasted_iota(jnp.int32, (count, count), 0)
    plane = (lane >= half).astype(jnp.int32)
    step = lax.shift_right_logical(lane & (half - 1), q_home.bit_length() - 1)
    wanted = ((2 * step + plane) ^ me) * q_home + (lane & (q_home - 1))
    order = jnp.where(source == wanted, 1.0, 0.0).astype(jnp.bfloat16)
    code = jnp.dot(code.astype(jnp.bfloat16), order, preferred_element_type=jnp.float32)
    rest = jnp.zeros((NOTE - 4, half), jnp.float32)
    note = jnp.concatenate([code[:2, :half], code[:2, half:], rest], axis=0)
    note_ref[...] = jnp.zeros_like(note_ref)
    note_ref[:, :half] = note.astype(note_ref.dtype)


def dense_shards(queries, label_weights, sibling_blocks, positive_slot):
    q_home, width = queries.shape
    qcount = sibling_blocks.shape[0]
    half = qcount // 2
    lab_dev = label_weights.shape[0]
    homes = lax.axis_size("lab")
    groups = lax.axis_size("pb")
    f32, bf16 = jnp.float32, jnp.bfloat16
    me = jnp.reshape(lax.axis_index("lab"), (1,)).astype(jnp.int32)
    far_bit = groups // 2
    came = [swap(queries, "lab", step) for step in range(2, homes, 2)]
    held, weights = local_call(
        hold_body,
        [like(q_home, width, bf16), like(lab_dev, width, bf16)],
        [queries, label_weights],
    )
    choice = jnp.concatenate([sibling_blocks.T, positive_slot[None]], axis=0).astype(f32)
    note = local_call(
        lambda *refs: note_body(lab_dev // BLOCK, q_home, *refs),
        [like(NOTE, width, bf16)],
        [me, choice],
    )[0]
    near, noted = local_call(
        join_body,
        [like(half, width, bf16), like(half + NOTE, width, bf16)],
        [held, came[0], *came[:0:-1], note],
        0,
        [weights],
    )
    far = swap(near, "lab", 1)
    work = 4 * half * lab_dev * width
    slope_like = like(BLOCK + NOTE, half, bf16)
    pair = [like(half // 2, width, f32), like(half // 2, width, bf16)]
    near_kept, near_sent, near_slope, near_copy = local_call(
        near_body,
        pair + [slope_like, like(half, width, bf16)],
        [near, weights, note],
        work,
    )
    cross_near = swap(noted, "pb", far_bit)
    cross_far = diagonal(near_copy, far_bit, 1)
    far_kept, far_sent, far_slope = local_call(
        far_body, pair + [slope_like], [far, weights, note], work, [near_slope]
    )
    far_came, near_came = swap(far_sent, "lab", 2), swap(near_sent, "lab", 2)
    acc, own = local_call(
        own_body,
        [like(lab_dev, width, f32), like(qcount + BLOCK + NOTE, width, bf16)],
        [near, far, near_slope, far_slope],
        work,
    )
    mate = swap(own, "pb", 1)
    home, sent = like(q_home, width, f32), like(q_home, width, bf16)
    near_kept, near_sent = local_call(
        fold_body, [home, sent], [near_kept, near_came], 0, [acc]
    )
    near_came = swap(near_sent, "lab", 4)
    far_sent, far_across = local_call(
        fold_body, [sent, sent], [far_kept, far_came], 0, [near_kept, acc]
    )
    far_came, far_across = swap(far_sent, "lab", 1), swap(far_across, "lab", 5)
    cross = local_call(
        stack_body, [like(qcount + NOTE, width, bf16)], [cross_near, cross_far], 0, [far_sent]
    )[0]
    cross_mate = swap(cross, "pb", 1)
    grown = like(lab_dev, width, f32)
    slope_like = like(BLOCK + NOTE, qcount, bf16)
    slope = local_call(
        cross_slope_body, [slope_like], [cross, weights], 20 * work, [acc]
    )[0]
    acc = local_call(sets_body, [grown], [cross, slope, mate, acc], work)[0]
    slope = local_call(
        cross_slope_body, [slope_like], [cross_mate, weights], work, [acc]
    )[0]
    weight_grad, mark = late(groups, cross_mate, slope, acc)
    query_grad = local_call(
        sum_body, [home], [near_kept, near_came, far_came, far_across], 0, [mark]
    )[0]
    return (query_grad, weight_grad)


def solution(mesh):
    groups, homes = mesh.shape["pb"], mesh.shape["lab"]

    def shards(queries, label_weights, sibling_blocks, positive_slot):
        every_row_everywhere = homes == K
        few = groups * sibling_blocks.shape[0] <= 2 * label_weights.shape[0]
        paired = groups == 4 and homes & (homes - 1) == 0
        one_block = label_weights.shape[0] // BLOCK <= K
        plan = dense_shards if every_row_everywhere and few and paired and one_block else sparse_shards
        return plan(queries, label_weights, sibling_blocks, positive_slot)

    in_specs = (P(("pb", "lab"), None), P("lab", None), P("pb", None), P("pb"))
    out_specs = (P(("pb", "lab"), None), P("lab", None))
    return jax.shard_map(shards, mesh=mesh, in_specs=in_specs, out_specs=out_specs, check_vma=False)
```

```python
import jax
import jax.numpy as jnp
from jax import lax
from jax.experimental import pallas as pl
from jax.experimental.pallas import tpu as pltpu
from jax.sharding import PartitionSpec as P

BLOCK = 128
K = 8
NOTE = 16
VMEM_LIMIT = 24 * 1024 * 1024


def pack_index(touched, width_slots, fill_value):
    homes, count = touched.shape
    rank = jnp.cumsum(touched.astype(jnp.int32), axis=1) - 1
    place = jnp.where(touched, rank, width_slots)
    home_ids = jnp.broadcast_to(jnp.arange(homes, dtype=jnp.int32)[:, None], touched.shape)
    row_ids = jnp.broadcast_to(jnp.arange(count, dtype=jnp.int32)[None, :], touched.shape)
    table = (
        jnp.full((homes, width_slots + 1), fill_value, jnp.int32).at[home_ids, place].set(row_ids)
    )
    return table[:, :width_slots]


def sparse_shards(queries, label_weights, sibling_blocks, positive_slot):
    width = queries.shape[1]
    qcount = sibling_blocks.shape[0]
    lab_dev = label_weights.shape[0]
    blocks_dev = lab_dev // BLOCK
    first = lax.axis_index("lab") * blocks_dev
    local_ids = first + jnp.arange(blocks_dev, dtype=jnp.int32)
    pblock = jnp.take_along_axis(sibling_blocks, (positive_slot // BLOCK)[:, None], axis=1)[:, 0]
    positive = pblock * BLOCK + positive_slot % BLOCK
    label_ids = local_ids[:, None] * BLOCK + jnp.arange(BLOCK, dtype=jnp.int32)[None, :]
    chosen_all = jnp.any(sibling_blocks[:, :, None] == local_ids[None, None, :], axis=1)
    piece = lax.all_gather(queries, "lab", axis=0, tiled=True)
    count = piece.shape[0]
    scores = jnp.dot(piece, label_weights.T, preferred_element_type=jnp.float32)
    scores = scores.reshape(count, blocks_dev, BLOCK)
    target = (label_ids[None, :, :] == positive[:, None, None]).astype(jnp.float32)
    slope = jnp.where(chosen_all[:, :, None], jax.nn.sigmoid(scores) - target, 0.0)
    slope = slope.astype(jnp.bfloat16).reshape(count, lab_dev)
    dq_all = jnp.dot(slope, label_weights, preferred_element_type=jnp.float32)
    w_acc = lax.dot_general(
        slope, piece, (((0,), (0,)), ((), ())), preferred_element_type=jnp.float32
    )
    homes = lax.axis_size("lab")
    q_home = qcount // homes
    slots = q_home * K // homes
    touched = jnp.any(chosen_all, axis=1).reshape(homes, q_home)
    send_idx = pack_index(touched, slots, q_home)
    padded = jnp.concatenate(
        [dq_all.reshape(homes, q_home, width), jnp.zeros((homes, 1, width), jnp.float32)], axis=1
    )
    outgoing = jnp.take_along_axis(padded, send_idx[:, :, None], axis=1)
    incoming = lax.all_to_all(outgoing, "lab", split_axis=0, concat_axis=0, tiled=True)
    own_blocks = lax.dynamic_slice_in_dim(sibling_blocks, lax.axis_index("lab") * q_home, q_home, 0)
    source_ids = jnp.arange(homes, dtype=jnp.int32)
    own_touch = jnp.any(
        (own_blocks // blocks_dev)[:, :, None] == source_ids[None, None, :], axis=1
    ).T
    recv_idx = pack_index(own_touch, slots, q_home)
    query_grad = (
        jnp.zeros((q_home + 1, width), jnp.float32)
        .at[recv_idx.reshape(-1)]
        .add(incoming.reshape(-1, width))[:q_home]
    )
    groups = lax.axis_size("pb")
    total = lax.psum(w_acc, "pb")
    weight_grad = (total / groups).astype(jnp.bfloat16)
    return (query_grad, weight_grad)


def swap(value, axis, bit):
    count = lax.axis_size(axis)
    return lax.ppermute(value, axis, [(i, i ^ bit) for i in range(count)])


def diagonal(value, group_bit, home_bit):
    groups, homes = lax.axis_size("pb"), lax.axis_size("lab")
    pairs = [
        (g * homes + h, (g ^ group_bit) * homes + (h ^ home_bit))
        for g in range(groups)
        for h in range(homes)
    ]
    return lax.ppermute(value, ("pb", "lab"), pairs)


def local_call(body, outs, args, flops=0, follows=()):
    specs = [
        pl.BlockSpec(memory_space=pltpu.SMEM if arg.dtype == jnp.int32 else pltpu.VMEM)
        for arg in args
    ]
    given, later = len(args), len(args) + len(follows)
    return pl.pallas_call(
        lambda *refs: body(*refs[:given], *refs[later:]),
        out_shape=outs,
        in_specs=specs + [pl.BlockSpec(memory_space=pl.ANY)] * len(follows),
        out_specs=[pl.BlockSpec(memory_space=pltpu.VMEM)] * len(outs),
        cost_estimate=pl.CostEstimate(flops=flops, bytes_accessed=0, transcendentals=0),
        compiler_params=pltpu.CompilerParams(vmem_limit_bytes=VMEM_LIMIT),
    )(*args, *follows)


def like(rows, width, dtype):
    return jax.ShapeDtypeStruct((rows, width), dtype)


def join_body(*refs):
    own_ref, first_ref, *rest, note_ref, out_ref, noted_ref = refs
    came_refs = [own_ref, first_ref, *rest[::-1]]
    stack_body(*came_refs, out_ref)
    stack_body(*came_refs, note_ref, noted_ref)


def hold_body(*refs):
    for source, held in zip(refs[: len(refs) // 2], refs[len(refs) // 2 :]):
        held[...] = source[...]


def slope_of(rows, weights, chosen, place):
    count, blocks = rows.shape[0], weights.shape[0] // BLOCK
    scores = lax.dot_general(
        weights, rows, (((1,), (1,)), ((), ())), preferred_element_type=jnp.float32
    )
    named = jnp.zeros((BLOCK, count), jnp.float32)
    for block in range(blocks):
        named = jnp.where(chosen == block, scores[block * BLOCK : (block + 1) * BLOCK], named)
    ids = lax.broadcasted_iota(jnp.int32, (BLOCK, count), 0)
    return (jax.nn.sigmoid(named) - jnp.where(ids == place, 1.0, 0.0)).astype(jnp.bfloat16)


def spread(slope, chosen, blocks):
    wide = slope.astype(jnp.float32)
    parts = [jnp.where(chosen == block, wide, 0.0).astype(slope.dtype) for block in blocks]
    return jnp.concatenate(parts, axis=0)


def read_note(note, which, count):
    chosen = note[2 * which : 2 * which + 1, :count].astype(jnp.int32)
    place = note[2 * which + 1 : 2 * which + 2, :count].astype(jnp.int32)
    return chosen, place


def grad_body(which, rows_ref, weights_ref, note_ref, kept_ref, sent_ref, slope_ref):
    rows, weights = rows_ref[...], weights_ref[...]
    note = note_ref[...].astype(jnp.float32)
    chosen, place = read_note(note, which, rows.shape[0])
    slope = slope_of(rows, weights, chosen, place)
    slope_ref[:BLOCK, :] = slope
    slope_ref[BLOCK:, :] = jnp.broadcast_to(chosen, (NOTE, rows.shape[0])).astype(slope.dtype)
    dq = lax.dot_general(
        spread(slope, chosen, range(weights.shape[0] // BLOCK)),
        weights,
        (((0,), (0,)), ((), ())),
        preferred_element_type=jnp.float32,
    )
    halve(dq, kept_ref, sent_ref, kept_ref.shape[0] // 2)


def halve(terms, kept_ref, sent_ref, span):
    for start in range(0, kept_ref.shape[0], span):
        kept_ref[start : start + span, :] = terms[2 * start : 2 * start + span]
        sent = terms[2 * start + span : 2 * start + 2 * span]
        sent_ref[start : start + span, :] = sent.astype(sent_ref.dtype)


def near_body(rows_ref, weights_ref, note_ref, kept_ref, sent_ref, slope_ref, copy_ref):
    copy_ref[...] = rows_ref[...]
    grad_body(0, rows_ref, weights_ref, note_ref, kept_ref, sent_ref, slope_ref)


def far_body(rows_ref, weights_ref, note_ref, kept_ref, sent_ref, slope_ref):
    grad_body(1, rows_ref, weights_ref, note_ref, kept_ref, sent_ref, slope_ref)


def fold_body(terms_ref, came_ref, first_ref, second_ref):
    terms = terms_ref[...] + came_ref[...].astype(jnp.float32)
    span = first_ref.shape[0]
    first_ref[...] = terms[:span].astype(first_ref.dtype)
    second_ref[...] = terms[span:].astype(second_ref.dtype)


def stack_body(*refs):
    *came_refs, out_ref = refs
    start = 0
    for ref in came_refs:
        out_ref[start : start + ref.shape[0], : ref.shape[1]] = ref[...]
        start += ref.shape[0]


def read_slope(slope):
    chosen = slope[BLOCK : BLOCK + 1].astype(jnp.float32).astype(jnp.int32)
    return slope[:BLOCK], chosen


def own_body(near_ref, far_ref, near_slope_ref, far_slope_ref, acc_ref, set_ref):
    rows = jnp.concatenate([near_ref[...], far_ref[...]], axis=0)
    slope = jnp.concatenate([near_slope_ref[...], far_slope_ref[...]], axis=1)
    count = rows.shape[0]
    set_ref[:count, :] = rows
    set_ref[count:, :count] = slope
    wide = spread(*read_slope(slope), range(acc_ref.shape[0] // BLOCK))
    acc_ref[...] = jnp.dot(wide, rows, preferred_element_type=jnp.float32)


def set_slope(set_ref, weights):
    half = (set_ref.shape[0] - NOTE) // 2
    rows = jnp.concatenate([set_ref[:half, :], set_ref[half + NOTE :, :]], axis=0)
    note = set_ref[half : half + NOTE, :].astype(jnp.float32)
    codes = [read_note(note, which, half) for which in range(2)]
    chosen = jnp.concatenate([codes[0][0], codes[1][0]], axis=1)
    place = jnp.concatenate([codes[0][1], codes[1][1]], axis=1)
    return rows, slope_of(rows, weights, chosen, place), chosen


def cross_slope_body(set_ref, weights_ref, slope_ref):
    _, slope, chosen = set_slope(set_ref, weights_ref[...])
    slope_ref[:BLOCK, :] = slope
    slope_ref[BLOCK:, :] = jnp.broadcast_to(chosen, (NOTE, chosen.shape[1])).astype(slope.dtype)


def set_rows(set_ref):
    half = (set_ref.shape[0] - NOTE) // 2
    return jnp.concatenate([set_ref[:half, :], set_ref[half + NOTE :, :]], axis=0)


def sets_body(cross_ref, slope_ref, mate_ref, acc_ref, out_ref):
    count = mate_ref.shape[0] - BLOCK - NOTE
    rows = jnp.concatenate([set_rows(cross_ref), mate_ref[:count, :]], axis=0)
    slope = jnp.concatenate([slope_ref[...], mate_ref[count:, :count]], axis=1)
    wide = spread(*read_slope(slope), range(acc_ref.shape[0] // BLOCK))
    out_ref[...] = acc_ref[...] + jnp.dot(wide, rows, preferred_element_type=jnp.float32)


def late_body(groups, set_ref, slope_ref, acc_ref, out_ref, mark_ref, held, sems):
    mark_ref[...] = jnp.zeros_like(mark_ref)
    rows, (slope, chosen) = set_rows(set_ref), read_slope(slope_ref[...])
    blocks = acc_ref.shape[0] // BLOCK
    chunk = blocks // sems.shape[0]
    copies = []
    for part in range(sems.shape[0]):
        here = pl.ds(part * chunk * BLOCK, chunk * BLOCK)
        wide = spread(slope, chosen, range(part * chunk, (part + 1) * chunk))
        sums = acc_ref[here, :] + jnp.dot(wide, rows, preferred_element_type=jnp.float32)
        held[here, :] = (sums / groups).astype(held.dtype)
        copy = pltpu.make_async_copy(held.at[here, :], out_ref.at[here, :], sems.at[part])
        copy.start()
        copies.append(copy)
    for copy in copies:
        copy.wait()


def late(groups, crossed, slope, acc):
    out = like(*acc.shape, crossed.dtype)
    chunks = 4
    return pl.pallas_call(
        lambda *refs: late_body(groups, *refs),
        out_shape=[out, like(1, BLOCK, jnp.int32)],
        in_specs=[pl.BlockSpec(memory_space=pltpu.VMEM)] * 3,
        out_specs=[pl.BlockSpec(memory_space=pl.ANY), pl.BlockSpec(memory_space=pltpu.VMEM)],
        scratch_shapes=[pltpu.VMEM(out.shape, out.dtype), pltpu.SemaphoreType.DMA((chunks,))],
        cost_estimate=pl.CostEstimate(flops=0, bytes_accessed=0, transcendentals=0),
        compiler_params=pltpu.CompilerParams(vmem_limit_bytes=VMEM_LIMIT),
    )(crossed, slope, acc)


def sum_body(kept_ref, *refs):
    *term_refs, out_ref = refs
    total = kept_ref[...]
    for ref in term_refs:
        total = total + ref[...].astype(jnp.float32)
    out_ref[...] = total


def note_body(blocks_dev, q_home, me_ref, choice_ref, note_ref):
    choice = choice_ref[...].astype(jnp.int32)
    me, picks, count = me_ref[0], choice.shape[0] - 1, choice.shape[1]
    local, slot = choice[:picks] - me * blocks_dev, choice[picks:]
    inside = (local >= 0) & (local < blocks_dev)
    chosen = jnp.max(jnp.where(inside, local, -1), axis=0, keepdims=True)
    steps = lax.broadcasted_iota(jnp.int32, local.shape, 0)
    named = steps == lax.shift_right_logical(slot, BLOCK.bit_length() - 1)
    pblock = jnp.sum(jnp.where(named, local, 0), axis=0, keepdims=True)
    place = jnp.where(pblock == chosen, slot & (BLOCK - 1), -1)
    row = lax.broadcasted_iota(jnp.int32, (NOTE, count), 0)
    code = jnp.where(row == 0, chosen, jnp.where(row == 1, place, 0))
    half = count // 2
    lane = lax.broadcasted_iota(jnp.int32, (count, count), 1)
    source = lax.broadcasted_iota(jnp.int32, (count, count), 0)
    plane = (lane >= half).astype(jnp.int32)
    step = lax.shift_right_logical(lane & (half - 1), q_home.bit_length() - 1)
    wanted = ((2 * step + plane) ^ me) * q_home + (lane & (q_home - 1))
    order = jnp.where(source == wanted, 1.0, 0.0).astype(jnp.bfloat16)
    code = jnp.dot(code.astype(jnp.bfloat16), order, preferred_element_type=jnp.float32)
    rest = jnp.zeros((NOTE - 4, half), jnp.float32)
    note = jnp.concatenate([code[:2, :half], code[:2, half:], rest], axis=0)
    note_ref[...] = jnp.zeros_like(note_ref)
    note_ref[:, :half] = note.astype(note_ref.dtype)


def dense_shards(queries, label_weights, sibling_blocks, positive_slot):
    q_home, width = queries.shape
    qcount = sibling_blocks.shape[0]
    half = qcount // 2
    lab_dev = label_weights.shape[0]
    homes = lax.axis_size("lab")
    groups = lax.axis_size("pb")
    f32, bf16 = jnp.float32, jnp.bfloat16
    me = jnp.reshape(lax.axis_index("lab"), (1,)).astype(jnp.int32)
    far_bit = groups // 2
    came = [swap(queries, "lab", step) for step in range(2, homes, 2)]
    held, weights = local_call(
        hold_body,
        [like(q_home, width, bf16), like(lab_dev, width, bf16)],
        [queries, label_weights],
    )
    choice = jnp.concatenate([sibling_blocks.T, positive_slot[None]], axis=0).astype(f32)
    note = local_call(
        lambda *refs: note_body(lab_dev // BLOCK, q_home, *refs),
        [like(NOTE, width, bf16)],
        [me, choice],
    )[0]
    near, noted = local_call(
        join_body,
        [like(half, width, bf16), like(half + NOTE, width, bf16)],
        [held, came[0], *came[:0:-1], note],
        0,
        [weights],
    )
    far = swap(near, "lab", 1)
    work = 4 * half * lab_dev * width
    slope_like = like(BLOCK + NOTE, half, bf16)
    pair = [like(half // 2, width, f32), like(half // 2, width, bf16)]
    near_kept, near_sent, near_slope, near_copy = local_call(
        near_body,
        pair + [slope_like, like(half, width, bf16)],
        [near, weights, note],
        work,
    )
    cross_near = swap(noted, "pb", far_bit)
    cross_far = diagonal(near_copy, far_bit, 1)
    far_kept, far_sent, far_slope = local_call(
        far_body, pair + [slope_like], [far, weights, note], work, [near_slope]
    )
    far_came, near_came = swap(far_sent, "lab", 2), swap(near_sent, "lab", 2)
    acc, own = local_call(
        own_body,
        [like(lab_dev, width, f32), like(qcount + BLOCK + NOTE, width, bf16)],
        [near, far, near_slope, far_slope],
        work,
    )
    mate = swap(own, "pb", 1)
    home, sent = like(q_home, width, f32), like(q_home, width, bf16)
    near_kept, near_sent = local_call(
        fold_body, [home, sent], [near_kept, near_came], 0, [acc]
    )
    near_came = swap(near_sent, "lab", 4)
    far_sent, far_across = local_call(
        fold_body, [sent, sent], [far_kept, far_came], 0, [near_kept, acc]
    )
    far_came, far_over = swap(far_sent, "lab", 1), swap(far_across, "lab", 5)
    cross = local_call(
        stack_body, [like(qcount + NOTE, width, bf16)], [cross_near, cross_far], 0, [far_across]
    )[0]
    cross_mate = swap(cross, "pb", 1)
    grown = like(lab_dev, width, f32)
    slope_like = like(BLOCK + NOTE, qcount, bf16)
    slope = local_call(
        cross_slope_body, [slope_like], [cross, weights], 20 * work, [acc]
    )[0]
    acc = local_call(sets_body, [grown], [cross, slope, mate, acc], work)[0]
    slope = local_call(
        cross_slope_body, [slope_like], [cross_mate, weights], work, [acc]
    )[0]
    weight_grad, mark = late(groups, cross_mate, slope, acc)
    query_grad = local_call(
        sum_body, [home], [near_kept, near_came, far_came, far_over], 0, [mark]
    )[0]
    return (query_grad, weight_grad)


def solution(mesh):
    groups, homes = mesh.shape["pb"], mesh.shape["lab"]

    def shards(queries, label_weights, sibling_blocks, positive_slot):
        every_row_everywhere = homes == K
        few = groups * sibling_blocks.shape[0] <= 2 * label_weights.shape[0]
        paired = groups == 4 and homes & (homes - 1) == 0
        one_block = label_weights.shape[0] // BLOCK <= K
        plan = dense_shards if every_row_everywhere and few and paired and one_block else sparse_shards
        return plan(queries, label_weights, sibling_blocks, positive_slot)

    in_specs = (P(("pb", "lab"), None), P("lab", None), P("pb", None), P("pb"))
    out_specs = (P(("pb", "lab"), None), P("lab", None))
    return jax.shard_map(shards, mesh=mesh, in_specs=in_specs, out_specs=out_specs, check_vma=False)
```

```python
import jax
import jax.numpy as jnp
from jax import lax
from jax.experimental import pallas as pl
from jax.experimental.pallas import tpu as pltpu
from jax.sharding import PartitionSpec as P

BLOCK = 128
K = 8
NOTE = 16
VMEM_LIMIT = 24 * 1024 * 1024


def pack_index(touched, width_slots, fill_value):
    homes, count = touched.shape
    rank = jnp.cumsum(touched.astype(jnp.int32), axis=1) - 1
    place = jnp.where(touched, rank, width_slots)
    home_ids = jnp.broadcast_to(jnp.arange(homes, dtype=jnp.int32)[:, None], touched.shape)
    row_ids = jnp.broadcast_to(jnp.arange(count, dtype=jnp.int32)[None, :], touched.shape)
    table = (
        jnp.full((homes, width_slots + 1), fill_value, jnp.int32).at[home_ids, place].set(row_ids)
    )
    return table[:, :width_slots]


def sparse_shards(queries, label_weights, sibling_blocks, positive_slot):
    width = queries.shape[1]
    qcount = sibling_blocks.shape[0]
    lab_dev = label_weights.shape[0]
    blocks_dev = lab_dev // BLOCK
    first = lax.axis_index("lab") * blocks_dev
    local_ids = first + jnp.arange(blocks_dev, dtype=jnp.int32)
    pblock = jnp.take_along_axis(sibling_blocks, (positive_slot // BLOCK)[:, None], axis=1)[:, 0]
    positive = pblock * BLOCK + positive_slot % BLOCK
    label_ids = local_ids[:, None] * BLOCK + jnp.arange(BLOCK, dtype=jnp.int32)[None, :]
    chosen_all = jnp.any(sibling_blocks[:, :, None] == local_ids[None, None, :], axis=1)
    piece = lax.all_gather(queries, "lab", axis=0, tiled=True)
    count = piece.shape[0]
    scores = jnp.dot(piece, label_weights.T, preferred_element_type=jnp.float32)
    scores = scores.reshape(count, blocks_dev, BLOCK)
    target = (label_ids[None, :, :] == positive[:, None, None]).astype(jnp.float32)
    slope = jnp.where(chosen_all[:, :, None], jax.nn.sigmoid(scores) - target, 0.0)
    slope = slope.astype(jnp.bfloat16).reshape(count, lab_dev)
    dq_all = jnp.dot(slope, label_weights, preferred_element_type=jnp.float32)
    w_acc = lax.dot_general(
        slope, piece, (((0,), (0,)), ((), ())), preferred_element_type=jnp.float32
    )
    homes = lax.axis_size("lab")
    q_home = qcount // homes
    slots = q_home * K // homes
    touched = jnp.any(chosen_all, axis=1).reshape(homes, q_home)
    send_idx = pack_index(touched, slots, q_home)
    padded = jnp.concatenate(
        [dq_all.reshape(homes, q_home, width), jnp.zeros((homes, 1, width), jnp.float32)], axis=1
    )
    outgoing = jnp.take_along_axis(padded, send_idx[:, :, None], axis=1)
    incoming = lax.all_to_all(outgoing, "lab", split_axis=0, concat_axis=0, tiled=True)
    own_blocks = lax.dynamic_slice_in_dim(sibling_blocks, lax.axis_index("lab") * q_home, q_home, 0)
    source_ids = jnp.arange(homes, dtype=jnp.int32)
    own_touch = jnp.any(
        (own_blocks // blocks_dev)[:, :, None] == source_ids[None, None, :], axis=1
    ).T
    recv_idx = pack_index(own_touch, slots, q_home)
    query_grad = (
        jnp.zeros((q_home + 1, width), jnp.float32)
        .at[recv_idx.reshape(-1)]
        .add(incoming.reshape(-1, width))[:q_home]
    )
    groups = lax.axis_size("pb")
    total = lax.psum(w_acc, "pb")
    weight_grad = (total / groups).astype(jnp.bfloat16)
    return (query_grad, weight_grad)


def swap(value, axis, bit):
    count = lax.axis_size(axis)
    return lax.ppermute(value, axis, [(i, i ^ bit) for i in range(count)])


def diagonal(value, group_bit, home_bit):
    groups, homes = lax.axis_size("pb"), lax.axis_size("lab")
    pairs = [
        (g * homes + h, (g ^ group_bit) * homes + (h ^ home_bit))
        for g in range(groups)
        for h in range(homes)
    ]
    return lax.ppermute(value, ("pb", "lab"), pairs)


def local_call(body, outs, args, flops=0, follows=()):
    specs = [
        pl.BlockSpec(memory_space=pltpu.SMEM if arg.dtype == jnp.int32 else pltpu.VMEM)
        for arg in args
    ]
    given, later = len(args), len(args) + len(follows)
    return pl.pallas_call(
        lambda *refs: body(*refs[:given], *refs[later:]),
        out_shape=outs,
        in_specs=specs + [pl.BlockSpec(memory_space=pl.ANY)] * len(follows),
        out_specs=[pl.BlockSpec(memory_space=pltpu.VMEM)] * len(outs),
        cost_estimate=pl.CostEstimate(flops=flops, bytes_accessed=0, transcendentals=0),
        compiler_params=pltpu.CompilerParams(vmem_limit_bytes=VMEM_LIMIT),
    )(*args, *follows)


def like(rows, width, dtype):
    return jax.ShapeDtypeStruct((rows, width), dtype)


def join_body(*refs):
    own_ref, *came_refs, note_ref, out_ref, noted_ref = refs
    came_refs = [own_ref, *came_refs[::-1]]
    stack_body(*came_refs, out_ref)
    stack_body(*came_refs, note_ref, noted_ref)


def hold_body(*refs):
    for source, held in zip(refs[: len(refs) // 2], refs[len(refs) // 2 :]):
        held[...] = source[...]


def slope_of(rows, weights, chosen, place):
    count, blocks = rows.shape[0], weights.shape[0] // BLOCK
    scores = lax.dot_general(
        weights, rows, (((1,), (1,)), ((), ())), preferred_element_type=jnp.float32
    )
    named = jnp.zeros((BLOCK, count), jnp.float32)
    for block in range(blocks):
        named = jnp.where(chosen == block, scores[block * BLOCK : (block + 1) * BLOCK], named)
    ids = lax.broadcasted_iota(jnp.int32, (BLOCK, count), 0)
    return (jax.nn.sigmoid(named) - jnp.where(ids == place, 1.0, 0.0)).astype(jnp.bfloat16)


def spread(slope, chosen, blocks):
    wide = slope.astype(jnp.float32)
    parts = [jnp.where(chosen == block, wide, 0.0).astype(slope.dtype) for block in blocks]
    return jnp.concatenate(parts, axis=0)


def read_note(note, which, count):
    chosen = note[2 * which : 2 * which + 1, :count].astype(jnp.int32)
    place = note[2 * which + 1 : 2 * which + 2, :count].astype(jnp.int32)
    return chosen, place


def grad_body(which, rows_ref, weights_ref, note_ref, kept_ref, sent_ref, slope_ref):
    rows, weights = rows_ref[...], weights_ref[...]
    note = note_ref[...].astype(jnp.float32)
    chosen, place = read_note(note, which, rows.shape[0])
    slope = slope_of(rows, weights, chosen, place)
    slope_ref[:BLOCK, :] = slope
    slope_ref[BLOCK:, :] = jnp.broadcast_to(chosen, (NOTE, rows.shape[0])).astype(slope.dtype)
    dq = lax.dot_general(
        spread(slope, chosen, range(weights.shape[0] // BLOCK)),
        weights,
        (((0,), (0,)), ((), ())),
        preferred_element_type=jnp.float32,
    )
    halve(dq, kept_ref, sent_ref, kept_ref.shape[0] // 2)


def halve(terms, kept_ref, sent_ref, span):
    for start in range(0, kept_ref.shape[0], span):
        kept_ref[start : start + span, :] = terms[2 * start : 2 * start + span]
        sent = terms[2 * start + span : 2 * start + 2 * span]
        sent_ref[start : start + span, :] = sent.astype(sent_ref.dtype)


def near_body(rows_ref, weights_ref, note_ref, kept_ref, sent_ref, slope_ref, copy_ref):
    copy_ref[...] = rows_ref[...]
    grad_body(0, rows_ref, weights_ref, note_ref, kept_ref, sent_ref, slope_ref)


def far_body(rows_ref, weights_ref, note_ref, kept_ref, sent_ref, slope_ref):
    grad_body(1, rows_ref, weights_ref, note_ref, kept_ref, sent_ref, slope_ref)


def fold_body(terms_ref, came_ref, first_ref, second_ref):
    terms = terms_ref[...] + came_ref[...].astype(jnp.float32)
    span = first_ref.shape[0]
    first_ref[...] = terms[:span].astype(first_ref.dtype)
    second_ref[...] = terms[span:].astype(second_ref.dtype)


def stack_body(*refs):
    *came_refs, out_ref = refs
    start = 0
    for ref in came_refs:
        out_ref[start : start + ref.shape[0], : ref.shape[1]] = ref[...]
        start += ref.shape[0]


def read_slope(slope):
    chosen = slope[BLOCK : BLOCK + 1].astype(jnp.float32).astype(jnp.int32)
    return slope[:BLOCK], chosen


def own_body(near_ref, far_ref, near_slope_ref, far_slope_ref, acc_ref, set_ref):
    rows = jnp.concatenate([near_ref[...], far_ref[...]], axis=0)
    slope = jnp.concatenate([near_slope_ref[...], far_slope_ref[...]], axis=1)
    count = rows.shape[0]
    set_ref[:count, :] = rows
    set_ref[count:, :count] = slope
    wide = spread(*read_slope(slope), range(acc_ref.shape[0] // BLOCK))
    acc_ref[...] = jnp.dot(wide, rows, preferred_element_type=jnp.float32)


def set_slope(set_ref, weights):
    half = (set_ref.shape[0] - NOTE) // 2
    rows = jnp.concatenate([set_ref[:half, :], set_ref[half + NOTE :, :]], axis=0)
    note = set_ref[half : half + NOTE, :].astype(jnp.float32)
    codes = [read_note(note, which, half) for which in range(2)]
    chosen = jnp.concatenate([codes[0][0], codes[1][0]], axis=1)
    place = jnp.concatenate([codes[0][1], codes[1][1]], axis=1)
    return rows, slope_of(rows, weights, chosen, place), chosen


def cross_slope_body(set_ref, weights_ref, slope_ref):
    _, slope, chosen = set_slope(set_ref, weights_ref[...])
    slope_ref[:BLOCK, :] = slope
    slope_ref[BLOCK:, :] = jnp.broadcast_to(chosen, (NOTE, chosen.shape[1])).astype(slope.dtype)


def set_rows(set_ref):
    half = (set_ref.shape[0] - NOTE) // 2
    return jnp.concatenate([set_ref[:half, :], set_ref[half + NOTE :, :]], axis=0)


def sets_body(cross_ref, slope_ref, mate_ref, acc_ref, out_ref):
    count = mate_ref.shape[0] - BLOCK - NOTE
    rows = jnp.concatenate([set_rows(cross_ref), mate_ref[:count, :]], axis=0)
    slope = jnp.concatenate([slope_ref[...], mate_ref[count:, :count]], axis=1)
    wide = spread(*read_slope(slope), range(acc_ref.shape[0] // BLOCK))
    out_ref[...] = acc_ref[...] + jnp.dot(wide, rows, preferred_element_type=jnp.float32)


def late_body(groups, set_ref, slope_ref, acc_ref, out_ref, mark_ref, held, sems):
    mark_ref[...] = jnp.zeros_like(mark_ref)
    rows, (slope, chosen) = set_rows(set_ref), read_slope(slope_ref[...])
    blocks = acc_ref.shape[0] // BLOCK
    chunk = blocks // sems.shape[0]
    copies = []
    for part in range(sems.shape[0]):
        here = pl.ds(part * chunk * BLOCK, chunk * BLOCK)
        wide = spread(slope, chosen, range(part * chunk, (part + 1) * chunk))
        sums = acc_ref[here, :] + jnp.dot(wide, rows, preferred_element_type=jnp.float32)
        held[here, :] = (sums / groups).astype(held.dtype)
        copy = pltpu.make_async_copy(held.at[here, :], out_ref.at[here, :], sems.at[part])
        copy.start()
        copies.append(copy)
    for copy in copies:
        copy.wait()


def late(groups, crossed, slope, acc):
    out = like(*acc.shape, crossed.dtype)
    chunks = 8
    return pl.pallas_call(
        lambda *refs: late_body(groups, *refs),
        out_shape=[out, like(1, BLOCK, jnp.int32)],
        in_specs=[pl.BlockSpec(memory_space=pltpu.VMEM)] * 3,
        out_specs=[pl.BlockSpec(memory_space=pl.ANY), pl.BlockSpec(memory_space=pltpu.VMEM)],
        scratch_shapes=[pltpu.VMEM(out.shape, out.dtype), pltpu.SemaphoreType.DMA((chunks,))],
        cost_estimate=pl.CostEstimate(flops=0, bytes_accessed=0, transcendentals=0),
        compiler_params=pltpu.CompilerParams(vmem_limit_bytes=VMEM_LIMIT),
    )(crossed, slope, acc)


def sum_body(kept_ref, *refs):
    *term_refs, out_ref = refs
    total = kept_ref[...]
    for ref in term_refs:
        total = total + ref[...].astype(jnp.float32)
    out_ref[...] = total


def note_body(blocks_dev, q_home, me_ref, choice_ref, note_ref):
    choice = choice_ref[...].astype(jnp.int32)
    me, picks, count = me_ref[0], choice.shape[0] - 1, choice.shape[1]
    local, slot = choice[:picks] - me * blocks_dev, choice[picks:]
    inside = (local >= 0) & (local < blocks_dev)
    chosen = jnp.max(jnp.where(inside, local, -1), axis=0, keepdims=True)
    steps = lax.broadcasted_iota(jnp.int32, local.shape, 0)
    named = steps == lax.shift_right_logical(slot, BLOCK.bit_length() - 1)
    pblock = jnp.sum(jnp.where(named, local, 0), axis=0, keepdims=True)
    place = jnp.where(pblock == chosen, slot & (BLOCK - 1), -1)
    row = lax.broadcasted_iota(jnp.int32, (NOTE, count), 0)
    code = jnp.where(row == 0, chosen, jnp.where(row == 1, place, 0))
    half = count // 2
    lane = lax.broadcasted_iota(jnp.int32, (count, count), 1)
    source = lax.broadcasted_iota(jnp.int32, (count, count), 0)
    plane = (lane >= half).astype(jnp.int32)
    step = lax.shift_right_logical(lane & (half - 1), q_home.bit_length() - 1)
    wanted = ((2 * step + plane) ^ me) * q_home + (lane & (q_home - 1))
    order = jnp.where(source == wanted, 1.0, 0.0).astype(jnp.bfloat16)
    code = jnp.dot(code.astype(jnp.bfloat16), order, preferred_element_type=jnp.float32)
    rest = jnp.zeros((NOTE - 4, half), jnp.float32)
    note = jnp.concatenate([code[:2, :half], code[:2, half:], rest], axis=0)
    note_ref[...] = jnp.zeros_like(note_ref)
    note_ref[:, :half] = note.astype(note_ref.dtype)


def dense_shards(queries, label_weights, sibling_blocks, positive_slot):
    q_home, width = queries.shape
    qcount = sibling_blocks.shape[0]
    half = qcount // 2
    lab_dev = label_weights.shape[0]
    homes = lax.axis_size("lab")
    groups = lax.axis_size("pb")
    f32, bf16 = jnp.float32, jnp.bfloat16
    me = jnp.reshape(lax.axis_index("lab"), (1,)).astype(jnp.int32)
    far_bit, next_bit, wide_bit = groups // 2, homes // 4, homes // 2
    came = [swap(queries, "lab", step) for step in range(2, homes, 2)]
    held, weights = local_call(
        hold_body,
        [like(q_home, width, bf16), like(lab_dev, width, bf16)],
        [queries, label_weights],
    )
    choice = jnp.concatenate([sibling_blocks.T, positive_slot[None]], axis=0).astype(f32)
    note = local_call(
        lambda *refs: note_body(lab_dev // BLOCK, q_home, *refs),
        [like(NOTE, width, bf16)],
        [me, choice],
    )[0]
    near, noted = local_call(
        join_body,
        [like(half, width, bf16), like(half + NOTE, width, bf16)],
        [held, *came[::-1], note],
        0,
        [weights],
    )
    far = swap(near, "lab", 1)
    work = 4 * half * lab_dev * width
    slope_like = like(BLOCK + NOTE, half, bf16)
    pair = [like(half // 2, width, f32), like(half // 2, width, bf16)]
    near_kept, near_sent, near_slope, near_copy = local_call(
        near_body,
        pair + [slope_like, like(half, width, bf16)],
        [near, weights, note],
        work,
    )
    cross_near = swap(noted, "pb", far_bit)
    cross_far = diagonal(near_copy, far_bit, 1)
    far_kept, far_sent, far_slope = local_call(
        far_body, pair + [slope_like], [far, weights, note], work, [near_slope]
    )
    far_came, near_came = swap(far_sent, "lab", next_bit), swap(near_sent, "lab", next_bit)
    acc, own = local_call(
        own_body,
        [like(lab_dev, width, f32), like(qcount + BLOCK + NOTE, width, bf16)],
        [near, far, near_slope, far_slope],
        work,
    )
    mate = swap(own, "pb", 1)
    home, sent = like(q_home, width, f32), like(q_home, width, bf16)
    near_kept, near_sent = local_call(
        fold_body, [home, sent], [near_kept, near_came], 0, [acc]
    )
    near_came = swap(near_sent, "lab", wide_bit)
    far_sent, far_across = local_call(
        fold_body, [sent, sent], [far_kept, far_came], 0, [near_kept, acc]
    )
    far_came, far_over = swap(far_sent, "lab", 1), swap(far_across, "lab", wide_bit + 1)
    cross = local_call(
        stack_body, [like(qcount + NOTE, width, bf16)], [cross_near, cross_far], 0, [far_across]
    )[0]
    cross_mate = swap(cross, "pb", 1)
    grown = like(lab_dev, width, f32)
    slope_like = like(BLOCK + NOTE, qcount, bf16)
    slope = local_call(
        cross_slope_body, [slope_like], [cross, weights], 20 * work, [acc]
    )[0]
    acc = local_call(sets_body, [grown], [cross, slope, mate, acc], work)[0]
    slope = local_call(
        cross_slope_body, [slope_like], [cross_mate, weights], work, [acc]
    )[0]
    weight_grad, mark = late(groups, cross_mate, slope, acc)
    query_grad = local_call(
        sum_body, [home], [near_kept, near_came, far_came, far_over], 0, [mark]
    )[0]
    return (query_grad, weight_grad)


def solution(mesh):
    groups, homes = mesh.shape["pb"], mesh.shape["lab"]

    def shards(queries, label_weights, sibling_blocks, positive_slot):
        every_row_everywhere = homes == K
        few = groups * sibling_blocks.shape[0] <= 2 * label_weights.shape[0]
        paired = groups == 4 and homes & (homes - 1) == 0
        one_block = label_weights.shape[0] // BLOCK <= K
        plan = dense_shards if every_row_everywhere and few and paired and one_block else sparse_shards
        return plan(queries, label_weights, sibling_blocks, positive_slot)

    in_specs = (P(("pb", "lab"), None), P("lab", None), P("pb", None), P("pb"))
    out_specs = (P(("pb", "lab"), None), P("lab", None))
    return jax.shard_map(shards, mesh=mesh, in_specs=in_specs, out_specs=out_specs, check_vma=False)
```

```python
import jax
import jax.numpy as jnp
from jax import lax
from jax.experimental import pallas as pl
from jax.experimental.pallas import tpu as pltpu
from jax.sharding import PartitionSpec as P

BLOCK = 128
K = 8
NOTE = 16
VMEM_LIMIT = 24 * 1024 * 1024


def pack_index(touched, width_slots, fill_value):
    homes, count = touched.shape
    rank = jnp.cumsum(touched.astype(jnp.int32), axis=1) - 1
    place = jnp.where(touched, rank, width_slots)
    home_ids = jnp.broadcast_to(jnp.arange(homes, dtype=jnp.int32)[:, None], touched.shape)
    row_ids = jnp.broadcast_to(jnp.arange(count, dtype=jnp.int32)[None, :], touched.shape)
    table = (
        jnp.full((homes, width_slots + 1), fill_value, jnp.int32).at[home_ids, place].set(row_ids)
    )
    return table[:, :width_slots]


def sparse_shards(queries, label_weights, sibling_blocks, positive_slot):
    width = queries.shape[1]
    qcount = sibling_blocks.shape[0]
    lab_dev = label_weights.shape[0]
    blocks_dev = lab_dev // BLOCK
    first = lax.axis_index("lab") * blocks_dev
    local_ids = first + jnp.arange(blocks_dev, dtype=jnp.int32)
    pblock = jnp.take_along_axis(sibling_blocks, (positive_slot // BLOCK)[:, None], axis=1)[:, 0]
    positive = pblock * BLOCK + positive_slot % BLOCK
    label_ids = local_ids[:, None] * BLOCK + jnp.arange(BLOCK, dtype=jnp.int32)[None, :]
    chosen_all = jnp.any(sibling_blocks[:, :, None] == local_ids[None, None, :], axis=1)
    piece = lax.all_gather(queries, "lab", axis=0, tiled=True)
    count = piece.shape[0]
    scores = jnp.dot(piece, label_weights.T, preferred_element_type=jnp.float32)
    scores = scores.reshape(count, blocks_dev, BLOCK)
    target = (label_ids[None, :, :] == positive[:, None, None]).astype(jnp.float32)
    slope = jnp.where(chosen_all[:, :, None], jax.nn.sigmoid(scores) - target, 0.0)
    slope = slope.astype(jnp.bfloat16).reshape(count, lab_dev)
    dq_all = jnp.dot(slope, label_weights, preferred_element_type=jnp.float32)
    w_acc = lax.dot_general(
        slope, piece, (((0,), (0,)), ((), ())), preferred_element_type=jnp.float32
    )
    homes = lax.axis_size("lab")
    q_home = qcount // homes
    slots = q_home * K // homes
    touched = jnp.any(chosen_all, axis=1).reshape(homes, q_home)
    send_idx = pack_index(touched, slots, q_home)
    padded = jnp.concatenate(
        [dq_all.reshape(homes, q_home, width), jnp.zeros((homes, 1, width), jnp.float32)], axis=1
    )
    outgoing = jnp.take_along_axis(padded, send_idx[:, :, None], axis=1)
    incoming = lax.all_to_all(outgoing, "lab", split_axis=0, concat_axis=0, tiled=True)
    own_blocks = lax.dynamic_slice_in_dim(sibling_blocks, lax.axis_index("lab") * q_home, q_home, 0)
    source_ids = jnp.arange(homes, dtype=jnp.int32)
    own_touch = jnp.any(
        (own_blocks // blocks_dev)[:, :, None] == source_ids[None, None, :], axis=1
    ).T
    recv_idx = pack_index(own_touch, slots, q_home)
    query_grad = (
        jnp.zeros((q_home + 1, width), jnp.float32)
        .at[recv_idx.reshape(-1)]
        .add(incoming.reshape(-1, width))[:q_home]
    )
    groups = lax.axis_size("pb")
    total = lax.psum(w_acc, "pb")
    weight_grad = (total / groups).astype(jnp.bfloat16)
    return (query_grad, weight_grad)


def swap(value, axis, bit):
    count = lax.axis_size(axis)
    return lax.ppermute(value, axis, [(i, i ^ bit) for i in range(count)])


def diagonal(value, group_bit, home_bit):
    groups, homes = lax.axis_size("pb"), lax.axis_size("lab")
    pairs = [
        (g * homes + h, (g ^ group_bit) * homes + (h ^ home_bit))
        for g in range(groups)
        for h in range(homes)
    ]
    return lax.ppermute(value, ("pb", "lab"), pairs)


def local_call(body, outs, args, flops=0, follows=()):
    specs = [
        pl.BlockSpec(memory_space=pltpu.SMEM if arg.dtype == jnp.int32 else pltpu.VMEM)
        for arg in args
    ]
    given, later = len(args), len(args) + len(follows)
    return pl.pallas_call(
        lambda *refs: body(*refs[:given], *refs[later:]),
        out_shape=outs,
        in_specs=specs + [pl.BlockSpec(memory_space=pl.ANY)] * len(follows),
        out_specs=[pl.BlockSpec(memory_space=pltpu.VMEM)] * len(outs),
        cost_estimate=pl.CostEstimate(flops=flops, bytes_accessed=0, transcendentals=0),
        compiler_params=pltpu.CompilerParams(vmem_limit_bytes=VMEM_LIMIT),
    )(*args, *follows)


def like(rows, width, dtype):
    return jax.ShapeDtypeStruct((rows, width), dtype)


def join_body(*refs):
    own_ref, *came_refs, note_ref, out_ref, noted_ref = refs
    came_refs = [own_ref, *came_refs[1:], came_refs[0]]
    stack_body(*came_refs, out_ref)
    stack_body(*came_refs, note_ref, noted_ref)


def hold_body(*refs):
    for source, held in zip(refs[: len(refs) // 2], refs[len(refs) // 2 :]):
        held[...] = source[...]


def slope_of(rows, weights, chosen, place):
    count, blocks = rows.shape[0], weights.shape[0] // BLOCK
    scores = lax.dot_general(
        weights, rows, (((1,), (1,)), ((), ())), preferred_element_type=jnp.float32
    )
    named = jnp.zeros((BLOCK, count), jnp.float32)
    for block in range(blocks):
        named = jnp.where(chosen == block, scores[block * BLOCK : (block + 1) * BLOCK], named)
    ids = lax.broadcasted_iota(jnp.int32, (BLOCK, count), 0)
    return (jax.nn.sigmoid(named) - jnp.where(ids == place, 1.0, 0.0)).astype(jnp.bfloat16)


def spread(slope, chosen, blocks):
    wide = slope.astype(jnp.float32)
    parts = [jnp.where(chosen == block, wide, 0.0).astype(slope.dtype) for block in blocks]
    return jnp.concatenate(parts, axis=0)


def read_note(note, which, count):
    chosen = note[2 * which : 2 * which + 1, :count].astype(jnp.int32)
    place = note[2 * which + 1 : 2 * which + 2, :count].astype(jnp.int32)
    return chosen, place


def grad_body(which, rows_ref, weights_ref, note_ref, kept_ref, sent_ref, slope_ref):
    rows, weights = rows_ref[...], weights_ref[...]
    note = note_ref[...].astype(jnp.float32)
    chosen, place = read_note(note, which, rows.shape[0])
    slope = slope_of(rows, weights, chosen, place)
    slope_ref[:BLOCK, :] = slope
    slope_ref[BLOCK:, :] = jnp.broadcast_to(chosen, (NOTE, rows.shape[0])).astype(slope.dtype)
    dq = lax.dot_general(
        spread(slope, chosen, range(weights.shape[0] // BLOCK)),
        weights,
        (((0,), (0,)), ((), ())),
        preferred_element_type=jnp.float32,
    )
    halve(dq, kept_ref, sent_ref, kept_ref.shape[0] // 2)


def halve(terms, kept_ref, sent_ref, span):
    for start in range(0, kept_ref.shape[0], span):
        kept_ref[start : start + span, :] = terms[2 * start : 2 * start + span]
        sent = terms[2 * start + span : 2 * start + 2 * span]
        sent_ref[start : start + span, :] = sent.astype(sent_ref.dtype)


def near_body(rows_ref, weights_ref, note_ref, kept_ref, sent_ref, slope_ref, copy_ref):
    copy_ref[...] = rows_ref[...]
    grad_body(0, rows_ref, weights_ref, note_ref, kept_ref, sent_ref, slope_ref)


def far_body(rows_ref, weights_ref, note_ref, kept_ref, sent_ref, slope_ref):
    grad_body(1, rows_ref, weights_ref, note_ref, kept_ref, sent_ref, slope_ref)


def fold_body(terms_ref, came_ref, first_ref, second_ref):
    terms = terms_ref[...] + came_ref[...].astype(jnp.float32)
    span = first_ref.shape[0]
    first_ref[...] = terms[:span].astype(first_ref.dtype)
    second_ref[...] = terms[span:].astype(second_ref.dtype)


def stack_body(*refs):
    *came_refs, out_ref = refs
    start = 0
    for ref in came_refs:
        out_ref[start : start + ref.shape[0], : ref.shape[1]] = ref[...]
        start += ref.shape[0]


def read_slope(slope):
    chosen = slope[BLOCK : BLOCK + 1].astype(jnp.float32).astype(jnp.int32)
    return slope[:BLOCK], chosen


def own_body(near_ref, far_ref, near_slope_ref, far_slope_ref, acc_ref, set_ref):
    rows = jnp.concatenate([near_ref[...], far_ref[...]], axis=0)
    slope = jnp.concatenate([near_slope_ref[...], far_slope_ref[...]], axis=1)
    count = rows.shape[0]
    set_ref[:count, :] = rows
    set_ref[count:, :count] = slope
    wide = spread(*read_slope(slope), range(acc_ref.shape[0] // BLOCK))
    acc_ref[...] = jnp.dot(wide, rows, preferred_element_type=jnp.float32)


def set_slope(set_ref, weights):
    half = (set_ref.shape[0] - NOTE) // 2
    rows = jnp.concatenate([set_ref[:half, :], set_ref[half + NOTE :, :]], axis=0)
    note = set_ref[half : half + NOTE, :].astype(jnp.float32)
    codes = [read_note(note, which, half) for which in range(2)]
    chosen = jnp.concatenate([codes[0][0], codes[1][0]], axis=1)
    place = jnp.concatenate([codes[0][1], codes[1][1]], axis=1)
    return rows, slope_of(rows, weights, chosen, place), chosen


def cross_slope_body(set_ref, weights_ref, slope_ref):
    _, slope, chosen = set_slope(set_ref, weights_ref[...])
    slope_ref[:BLOCK, :] = slope
    slope_ref[BLOCK:, :] = jnp.broadcast_to(chosen, (NOTE, chosen.shape[1])).astype(slope.dtype)


def set_rows(set_ref):
    half = (set_ref.shape[0] - NOTE) // 2
    return jnp.concatenate([set_ref[:half, :], set_ref[half + NOTE :, :]], axis=0)


def sets_body(cross_ref, slope_ref, mate_ref, acc_ref, out_ref):
    count = mate_ref.shape[0] - BLOCK - NOTE
    rows = jnp.concatenate([set_rows(cross_ref), mate_ref[:count, :]], axis=0)
    slope = jnp.concatenate([slope_ref[...], mate_ref[count:, :count]], axis=1)
    wide = spread(*read_slope(slope), range(acc_ref.shape[0] // BLOCK))
    out_ref[...] = acc_ref[...] + jnp.dot(wide, rows, preferred_element_type=jnp.float32)


def late_body(groups, set_ref, slope_ref, acc_ref, out_ref, mark_ref, held, sems):
    mark_ref[...] = jnp.zeros_like(mark_ref)
    rows, (slope, chosen) = set_rows(set_ref), read_slope(slope_ref[...])
    blocks = acc_ref.shape[0] // BLOCK
    chunk = blocks // sems.shape[0]
    copies = []
    for part in range(sems.shape[0]):
        here = pl.ds(part * chunk * BLOCK, chunk * BLOCK)
        wide = spread(slope, chosen, range(part * chunk, (part + 1) * chunk))
        sums = acc_ref[here, :] + jnp.dot(wide, rows, preferred_element_type=jnp.float32)
        held[here, :] = (sums / groups).astype(held.dtype)
        copy = pltpu.make_async_copy(held.at[here, :], out_ref.at[here, :], sems.at[part])
        copy.start()
        copies.append(copy)
    for copy in copies:
        copy.wait()


def late(groups, crossed, slope, acc):
    out = like(*acc.shape, crossed.dtype)
    chunks = 4
    return pl.pallas_call(
        lambda *refs: late_body(groups, *refs),
        out_shape=[out, like(1, BLOCK, jnp.int32)],
        in_specs=[pl.BlockSpec(memory_space=pltpu.VMEM)] * 3,
        out_specs=[pl.BlockSpec(memory_space=pl.ANY), pl.BlockSpec(memory_space=pltpu.VMEM)],
        scratch_shapes=[pltpu.VMEM(out.shape, out.dtype), pltpu.SemaphoreType.DMA((chunks,))],
        cost_estimate=pl.CostEstimate(flops=0, bytes_accessed=0, transcendentals=0),
        compiler_params=pltpu.CompilerParams(vmem_limit_bytes=VMEM_LIMIT),
    )(crossed, slope, acc)


def sum_body(kept_ref, *refs):
    *term_refs, out_ref = refs
    total = kept_ref[...]
    for ref in term_refs:
        total = total + ref[...].astype(jnp.float32)
    out_ref[...] = total


def note_body(blocks_dev, q_home, me_ref, choice_ref, note_ref):
    choice = choice_ref[...].astype(jnp.int32)
    me, picks, count = me_ref[0], choice.shape[0] - 1, choice.shape[1]
    local, slot = choice[:picks] - me * blocks_dev, choice[picks:]
    inside = (local >= 0) & (local < blocks_dev)
    chosen = jnp.max(jnp.where(inside, local, -1), axis=0, keepdims=True)
    steps = lax.broadcasted_iota(jnp.int32, local.shape, 0)
    named = steps == lax.shift_right_logical(slot, BLOCK.bit_length() - 1)
    pblock = jnp.sum(jnp.where(named, local, 0), axis=0, keepdims=True)
    place = jnp.where(pblock == chosen, slot & (BLOCK - 1), -1)
    row = lax.broadcasted_iota(jnp.int32, (NOTE, count), 0)
    code = jnp.where(row == 0, chosen, jnp.where(row == 1, place, 0))
    half = count // 2
    lane = lax.broadcasted_iota(jnp.int32, (count, count), 1)
    source = lax.broadcasted_iota(jnp.int32, (count, count), 0)
    plane = (lane >= half).astype(jnp.int32)
    step = lax.shift_right_logical(lane & (half - 1), q_home.bit_length() - 1)
    wanted = ((2 * step + plane) ^ me) * q_home + (lane & (q_home - 1))
    order = jnp.where(source == wanted, 1.0, 0.0).astype(jnp.bfloat16)
    code = jnp.dot(code.astype(jnp.bfloat16), order, preferred_element_type=jnp.float32)
    rest = jnp.zeros((NOTE - 4, half), jnp.float32)
    note = jnp.concatenate([code[:2, :half], code[:2, half:], rest], axis=0)
    note_ref[...] = jnp.zeros_like(note_ref)
    note_ref[:, :half] = note.astype(note_ref.dtype)


def dense_shards(queries, label_weights, sibling_blocks, positive_slot):
    q_home, width = queries.shape
    qcount = sibling_blocks.shape[0]
    half = qcount // 2
    lab_dev = label_weights.shape[0]
    homes = lax.axis_size("lab")
    groups = lax.axis_size("pb")
    f32, bf16 = jnp.float32, jnp.bfloat16
    me = jnp.reshape(lax.axis_index("lab"), (1,)).astype(jnp.int32)
    far_bit, next_bit, wide_bit = groups // 2, homes // 4, homes // 2
    came = [swap(queries, "lab", step) for step in range(2, homes, 2)]
    held, weights = local_call(
        hold_body,
        [like(q_home, width, bf16), like(lab_dev, width, bf16)],
        [queries, label_weights],
    )
    choice = jnp.concatenate([sibling_blocks.T, positive_slot[None]], axis=0).astype(f32)
    note = local_call(
        lambda *refs: note_body(lab_dev // BLOCK, q_home, *refs),
        [like(NOTE, width, bf16)],
        [me, choice],
    )[0]
    near, noted = local_call(
        join_body,
        [like(half, width, bf16), like(half + NOTE, width, bf16)],
        [held, came[-1], *came[:-1], note],
        0,
        [weights],
    )
    far = swap(near, "lab", 1)
    work = 4 * half * lab_dev * width
    slope_like = like(BLOCK + NOTE, half, bf16)
    pair = [like(half // 2, width, f32), like(half // 2, width, bf16)]
    near_kept, near_sent, near_slope, near_copy = local_call(
        near_body,
        pair + [slope_like, like(half, width, bf16)],
        [near, weights, note],
        work,
    )
    cross_near = swap(noted, "pb", far_bit)
    cross_far = diagonal(near_copy, far_bit, 1)
    far_kept, far_sent, far_slope = local_call(
        far_body, pair + [slope_like], [far, weights, note], work, [near_slope]
    )
    far_came, near_came = swap(far_sent, "lab", next_bit), swap(near_sent, "lab", next_bit)
    acc, own = local_call(
        own_body,
        [like(lab_dev, width, f32), like(qcount + BLOCK + NOTE, width, bf16)],
        [near, far, near_slope, far_slope],
        work,
    )
    mate = swap(own, "pb", 1)
    home, sent = like(q_home, width, f32), like(q_home, width, bf16)
    near_kept, near_sent = local_call(
        fold_body, [home, sent], [near_kept, near_came], 0, [acc]
    )
    near_came = swap(near_sent, "lab", wide_bit)
    far_sent, far_across = local_call(
        fold_body, [sent, sent], [far_kept, far_came], 0, [near_kept, acc]
    )
    far_came, far_over = swap(far_sent, "lab", 1), swap(far_across, "lab", wide_bit + 1)
    cross = local_call(
        stack_body, [like(qcount + NOTE, width, bf16)], [cross_near, cross_far], 0, [far_across]
    )[0]
    cross_mate = swap(cross, "pb", 1)
    grown = like(lab_dev, width, f32)
    slope_like = like(BLOCK + NOTE, qcount, bf16)
    slope = local_call(
        cross_slope_body, [slope_like], [cross, weights], 20 * work, [acc]
    )[0]
    acc = local_call(sets_body, [grown], [cross, slope, mate, acc], work)[0]
    slope = local_call(
        cross_slope_body, [slope_like], [cross_mate, weights], work, [acc]
    )[0]
    weight_grad, mark = late(groups, cross_mate, slope, acc)
    query_grad = local_call(
        sum_body, [home], [near_kept, near_came, far_came, far_over], 0, [mark]
    )[0]
    return (query_grad, weight_grad)


def solution(mesh):
    groups, homes = mesh.shape["pb"], mesh.shape["lab"]

    def shards(queries, label_weights, sibling_blocks, positive_slot):
        every_row_everywhere = homes == K
        few = groups * sibling_blocks.shape[0] <= 2 * label_weights.shape[0]
        paired = groups == 4 and homes & (homes - 1) == 0
        one_block = label_weights.shape[0] // BLOCK <= K
        plan = dense_shards if every_row_everywhere and few and paired and one_block else sparse_shards
        return plan(queries, label_weights, sibling_blocks, positive_slot)

    in_specs = (P(("pb", "lab"), None), P("lab", None), P("pb", None), P("pb"))
    out_specs = (P(("pb", "lab"), None), P("lab", None))
    return jax.shard_map(shards, mesh=mesh, in_specs=in_specs, out_specs=out_specs, check_vma=False)
```
